128 devices in a mesh: dp: 16 (over z, y), vocab: 8 (over x, core).
Axes of the slice: x: 4, y: 4, z: 4, core: 2. Of those that a mesh axis runs over, the one named last changes fastest.
Arguments:
- token_ids: int32 [16384], P(('dp', 'vocab')), may hold values from 0 to 50303, as said below
- targets: int32 [16384], P(('dp', 'vocab')), may hold values from 0 to 50303, as said below
- lengths: int32 [16, 8, 3], P('dp'), may hold values from 1 to 80, 128 in all within a row
- embed_table: float32 [50304, 768], P(('dp', 'vocab')), may hold values from -0.3125 to 0.3125
- embed_moment: float32 [50304, 768], P(('dp', 'vocab')), may hold values from -9.536743e-06 to 9.536743e-06
- embed_average: float32 [50304, 768], P(('dp', 'vocab')), may hold values from -0.3125 to 0.3125
- blocks: float32 [2, 768, 9216], P(None, None, ('dp', 'vocab')), may hold values from -0.21875 to 0.21875
- block_moment: float32 [2, 768, 9216], P(None, None, ('dp', 'vocab')), may hold values from -9.536743e-06 to 9.536743e-06
- block_average: float32 [2, 768, 9216], P(None, None, ('dp', 'vocab')), may hold values from -0.21875 to 0.21875
- pos_table: float32 [80, 768], P(None, ('dp', 'vocab')), may hold values from -0.3125 to 0.3125
- pos_moment: float32 [80, 768], P(None, ('dp', 'vocab')), may hold values from -9.536743e-06 to 9.536743e-06
- pos_average: float32 [80, 768], P(None, ('dp', 'vocab')), may hold values from -0.3125 to 0.3125
- vectors: float32 [19968], P(('dp', 'vocab'))
- vector_moment: float32 [19968], P(('dp', 'vocab')), may hold values from -9.536743e-06 to 9.536743e-06
- vector_average: float32 [19968], P(('dp', 'vocab'))
Outputs:
- loss_sum: float32 [], replicated
- grad_norm: float32 [], replicated
- embed_moment_next: float32 [50304, 768], P(('dp', 'vocab'))
- embed_next: float32 [50304, 768], P(('dp', 'vocab'))
- embed_average_next: float32 [50304, 768], P(('dp', 'vocab'))
- embed_copy: bfloat16 [50304, 768], P(('dp', 'vocab'))
- block_moment_next: float32 [2, 768, 9216], P(None, None, ('dp', 'vocab'))
- blocks_next: float32 [2, 768, 9216], P(None, None, ('dp', 'vocab'))
- block_average_next: float32 [2, 768, 9216], P(None, None, ('dp', 'vocab'))
- block_copy: bfloat16 [2, 768, 9216], P(None, None, ('dp', 'vocab'))
- pos_moment_next: float32 [80, 768], P(None, ('dp', 'vocab'))
- pos_next: float32 [80, 768], P(None, ('dp', 'vocab'))
- pos_average_next: float32 [80, 768], P(None, ('dp', 'vocab'))
- pos_copy: bfloat16 [80, 768], P(None, ('dp', 'vocab'))
- vector_moment_next: float32 [19968], P(('dp', 'vocab'))
- vectors_next: float32 [19968], P(('dp', 'vocab'))
- vector_average_next: float32 [19968], P(('dp', 'vocab'))
- vector_copy: bfloat16 [19968], P(('dp', 'vocab'))
The draws below stay inside these ranges and needn't reach their ends.
Inputs may be any that keep to these rules, and one draw needn't show every extreme that they name: `token_ids`: among one device's 128 ids, at most 2 lie in any one block of 393 consecutive rows. Likewise for one device's targets. Each device's 3 lengths sum to 128.
All inputs are finite; a program needn't handle non-finite values.
Results may differ from the reference program's by a relative error of at most 0.018.
Values may be sent and summed in bfloat16 or wider, within the bound.
A program may use at most 320 MiB of HBM per device.

```python
import math
from functools import partial
import jax
import jax.numpy as jnp
import numpy as np
from jax import lax

D = 768
H = 12
FF = 3072
VOCAB = 50304
L = 2
TOK_DEV = 128
DOCS = 3
HD = 64
MOST = 80
CAP = 2
TOKENS = 16384
COLS = 9216
VW = 9216
VEC = 19968
N_DP = 16
N_VOCAB = 8


def route_ids(key):
    devices = TOKENS // TOK_DEV
    own_rows = VOCAB // devices
    slots = devices * CAP
    key_list = jax.random.split(key, 7)
    owner_heat = jax.random.randint(key_list[0], (devices,), 0, 3)
    common = jax.random.randint(key_list[1], (), 0, devices)
    favored = jax.random.randint(key_list[2], (devices, 1), 0, devices)
    noise_draw = jax.random.randint(key_list[3], (devices, slots), 0, 4096)
    slot_owner = jnp.arange(slots, dtype=jnp.int32) // CAP
    score = noise_draw + 2000 * owner_heat[slot_owner][None, :]
    score = score + 16384 * (slot_owner == common).astype(jnp.int32)[None, :]
    score = score + 8192 * (slot_owner[None, :] == favored).astype(jnp.int32)
    ranked = score * slots + jnp.arange(slots, dtype=jnp.int32)[None, :]
    unused, chosen = lax.top_k(ranked, TOK_DEV)
    owners = chosen // CAP
    first_draw = jax.random.randint(key_list[4], (devices, TOK_DEV), 0, own_rows)
    second_draw = jax.random.randint(key_list[5], (devices, TOK_DEV), 0, own_rows)
    token_rows = owners * own_rows + (own_rows - 1 - first_draw * second_draw // own_rows)
    orders = jax.vmap(jax.random.permutation, in_axes=(0, None))(jax.random.split(key_list[6], devices), TOK_DEV)
    token_rows = jnp.take_along_axis(token_rows, orders, 1)
    return token_rows.reshape(TOKENS).astype(jnp.int32)


def draw_token_ids(key, part):
    key = jax.random.fold_in(key, 11)
    return route_ids(key)


def draw_targets(key, part):
    key = jax.random.fold_in(key, 12)
    return route_ids(key)


def vector_law(key, spread):
    places = jnp.arange(VEC, dtype=jnp.int32)
    inner = places % VW
    in_tail = places >= L * VW
    tail_place = places - L * VW
    is_gain = jnp.where(in_tail, tail_place < D, (inner < D) | (inner >= 5 * D) & (inner < 6 * D))
    column = jnp.where(in_tail, tail_place % D, inner % D)
    rise = 0.5 + column.astype(jnp.float32) / D
    key_gain, key_shift = jax.random.split(key)
    gains = rise * jax.random.uniform(key_gain, (VEC,), jnp.float32, 0.8, 1.2)
    shifts = spread * jax.random.normal(key_shift, (VEC,), jnp.float32)
    return jnp.where(is_gain, gains, shifts).astype(jnp.float32)


def draw_vectors(key, part):
    key = jax.random.fold_in(key, 21)
    return vector_law(key, 0.2)


def draw_vector_average(key, part):
    key = jax.random.fold_in(key, 22)
    return vector_law(key, 0.2)


def steps_of(stream_key, extent, cuts, smallest, top_value):
    def one(dim, shards_of):
        draws = jax.random.uniform(jax.random.fold_in(jax.random.fold_in(stream_key, 6), dim), (shards_of,), jnp.float32, smallest / len(cuts), top_value / len(cuts))
        return jnp.repeat(jnp.exp(draws), extent[dim] // shards_of).reshape((-1,) + (1,) * (len(extent) - dim - 1))

    level = one(*cuts[0])
    for cut in cuts[1:]:
        level = level * one(*cut)
    return level


def split_up(amount, total, bound, lean):
    loads = [(1 << 20) // math.isqrt(standing ** lean) + 1 for standing in range(2, amount + 1)]
    spare, holding = total - bound - (amount - 1), [1] * (amount - 1)
    while spare > 0:
        free = [i for i in range(amount - 1) if holding[i] < bound]
        mass, budget = sum([loads[i] for i in free]), spare
        for i in free:
            more = min(bound - holding[i], max(1, budget * loads[i] // mass), spare)
            holding[i] = holding[i] + more
            spare = spare - more
    return np.array([bound] + holding)


def uneven_parts(stream_key, number_of, total, reach, skew):
    if number_of == 2:
        one = jax.random.randint(stream_key, (), max(1, total - reach), min(reach, total - 1) + 1)
        return jnp.stack([one, total - one])
    sizes = jnp.asarray(split_up(number_of, total, reach, skew), jnp.int32)
    couples = (number_of - 1) // 2
    source_of, taker = sizes[1:1 + 2 * couples:2], sizes[2:2 + 2 * couples:2]
    margin = jnp.minimum(source_of - 1, reach - taker)
    moved = jax.random.randint(jax.random.fold_in(stream_key, 1), (couples,), 0, 1 << 20) % (margin + 1)
    sizes = sizes.at[1:1 + 2 * couples:2].set(source_of - moved).at[2:2 + 2 * couples:2].set(taker + moved)
    return sizes[jax.random.permutation(jax.random.fold_in(stream_key, 2), number_of)]


def normal_values(own_key, dims, deviation, bound, pieces=(), kind=jnp.bfloat16):
    result = jax.random.normal(own_key, dims, jnp.float32) * deviation
    if len(pieces) > 0:
        result = steps_of(own_key, dims, pieces, -0.22, 0.18) * result
    return jnp.clip(result, min=-bound, max=bound).astype(kind)


def setup_inputs(seed: int = 0) -> dict:
    streams_of = jax.random.split(jax.random.key(seed), 16)
    token_ids = draw_token_ids(jax.random.fold_in(streams_of[15], 71), 0)
    targets = draw_targets(jax.random.fold_in(streams_of[15], 71), 0)
    lengths = jax.vmap(lambda own: uneven_parts(own, DOCS, TOK_DEV, MOST, 2))(jax.random.split(streams_of[2], N_DP * N_VOCAB)).reshape((N_DP, N_VOCAB, DOCS)).astype(jnp.int32)
    embed_table = normal_values(streams_of[3], (VOCAB, D), 0.05, 0.3125, ((0, 128),), jnp.float32)
    embed_moment = normal_values(streams_of[4], (VOCAB, D), 0.0000015, 9.5367431640625e-06, ((0, 128),), jnp.float32)
    embed_average = normal_values(streams_of[5], (VOCAB, D), 0.05, 0.3125, ((0, 128),), jnp.float32)
    blocks = normal_values(streams_of[6], (L, D, COLS), D ** -0.5, 0.21875, ((2, 128),), jnp.float32)
    block_moment = normal_values(streams_of[7], (L, D, COLS), 0.0000015, 9.5367431640625e-06, ((2, 128),), jnp.float32)
    block_average = normal_values(streams_of[8], (L, D, COLS), D ** -0.5, 0.21875, ((2, 128),), jnp.float32)
    pos_table = normal_values(streams_of[9], (MOST, D), 0.05, 0.3125, ((1, 128),), jnp.float32)
    pos_moment = normal_values(streams_of[10], (MOST, D), 0.0000015, 9.5367431640625e-06, ((1, 128),), jnp.float32)
    pos_average = normal_values(streams_of[11], (MOST, D), 0.05, 0.3125, ((1, 128),), jnp.float32)
    vectors = draw_vectors(jax.random.fold_in(streams_of[15], 71), 0)
    vector_moment = normal_values(streams_of[13], (VEC,), 0.0000015, 9.5367431640625e-06, ((0, 128),), jnp.float32)
    vector_average = draw_vector_average(jax.random.fold_in(streams_of[15], 71), 0)
    return {"token_ids": token_ids, "targets": targets, "lengths": lengths, "embed_table": embed_table, "embed_moment": embed_moment, "embed_average": embed_average, "blocks": blocks, "block_moment": block_moment, "block_average": block_average, "pos_table": pos_table, "pos_moment": pos_moment, "pos_average": pos_average, "vectors": vectors, "vector_moment": vector_moment, "vector_average": vector_average}


@jax.custom_vjp
def low(v):
    return lax.optimization_barrier(v.astype(jnp.bfloat16)).astype(jnp.float32)

@jax.custom_vjp
def low_back(v):
    return v

def low_keep(v):
    return (low(v), None)

def low_pass(kept, grad):
    return (grad,)

def back_keep(v):
    return (v, None)

def back_low(kept, grad):
    return (low(grad),)
low.defvjp(low_keep, low_pass)
low_back.defvjp(back_keep, back_low)
norm_eps = 1e-05
clip_bound = 0.01
learn_rate = 10000.0
momentum_coef = 0.5
ema_decay = 0.5

def matmul(left, right):
    return jnp.dot(left, right, precision=lax.Precision.HIGHEST)

def layer_norm(inputs, gain, shift):
    centered = inputs - lax.optimization_barrier(jnp.mean(inputs, -1, keepdims=True))
    spread = lax.optimization_barrier(jnp.mean(centered * centered, -1, keepdims=True))
    return centered * lax.rsqrt(spread + norm_eps) * gain + shift

def gelu_tanh(inputs):
    return jax.nn.gelu(inputs, approximate=True)

def doc_info(doc_lens, tok_count, total_docs):
    doc_ends = jnp.cumsum(doc_lens)
    places = jnp.arange(tok_count, dtype=jnp.int32)
    seg_ids = lax.optimization_barrier(jnp.sum((places[:, None] >= doc_ends[None, :]).astype(jnp.int32), 1))
    one_hot = seg_ids[:, None] == jnp.arange(doc_lens.shape[0], dtype=jnp.int32)[None, :]
    starts = doc_ends - doc_lens
    pos_ids = places - lax.optimization_barrier(jnp.sum(jnp.where(one_hot, starts[None, :], 0), 1))
    doc_len = lax.optimization_barrier(jnp.sum(jnp.where(one_hot, doc_lens[None, :], 0), 1))
    weights = 1.0 / (doc_len.astype(jnp.float32) * total_docs)
    return (seg_ids, pos_ids, weights)

def device_rise(first, count, devices):
    places = first + jnp.arange(count, dtype=jnp.int32)
    return 1.0 + 2.0 * places.astype(jnp.float32) / (devices - 1)

def block_layer(hidden, mats, vecs, attn_mask):
    batch, tok = (hidden.shape[0], hidden.shape[1])
    w_qkv = mats[:, :3 * D]
    w_proj = mats[:, 3 * D:4 * D]
    w_fc = mats[:, 4 * D:4 * D + FF]
    w_out = mats[:, 4 * D + FF:]
    normed = low(layer_norm(hidden, vecs[:D], vecs[D:2 * D]))
    bias_qkv = jnp.concatenate([vecs[2 * D:3 * D], jnp.zeros((D,), jnp.float32), vecs[3 * D:4 * D]])
    qkv_all = low(low_back(matmul(normed, w_qkv)) + bias_qkv).reshape(batch, tok, 3, H, HD)
    raw_scores = jnp.einsum('bthd,buhd->bhtu', qkv_all[:, :, 0], qkv_all[:, :, 1], precision=lax.Precision.HIGHEST)
    scores = jnp.where(attn_mask[:, None], low_back(raw_scores) * HD ** (-0.5), -1000000000.0)
    shifted = jnp.exp(scores - lax.optimization_barrier(jnp.max(scores, -1, keepdims=True)))
    attn_probs = shifted / lax.optimization_barrier(jnp.sum(shifted, -1, keepdims=True))
    attended = jnp.einsum('bhtu,buhd->bthd', low(attn_probs), qkv_all[:, :, 2], precision=lax.Precision.HIGHEST)
    attended = low_back(low(attended)).reshape(batch, tok, D)
    middle = hidden + low_back(matmul(attended, w_proj)) + vecs[4 * D:5 * D]
    normed_two = low(layer_norm(middle, vecs[5 * D:6 * D], vecs[6 * D:7 * D]))
    up_act = low_back(matmul(normed_two, w_fc)) + vecs[7 * D:7 * D + FF]
    activ = low(gelu_tanh(up_act))
    return middle + low_back(matmul(activ, w_out.T)) + vecs[7 * D + FF:8 * D + FF]

def loss_of(embed_table, blocks, pos_table, vectors, ids, target_ids, pos_ids, weights, attn_mask):
    embed_low = low(embed_table)
    mats = low(blocks)
    vec_low = low(vectors)
    hidden = embed_low[ids] + low(pos_table)[pos_ids]
    for layer in range(L):
        hidden = block_layer(hidden, mats[layer], vec_low[layer * VW:(layer + 1) * VW], attn_mask)
    tail = vec_low[L * VW:]
    final = low(layer_norm(hidden, tail[:D], tail[D:]))
    target_logit = lax.optimization_barrier(jnp.sum(final * embed_low[target_ids], -1))

    def group_lse(rows):
        logits = low_back(matmul(rows, embed_low.T))
        top = lax.optimization_barrier(jnp.max(logits, -1, keepdims=True))
        return top[:, 0] + jnp.log(lax.optimization_barrier(jnp.sum(jnp.exp(logits - top), -1)))
    lse = lax.map(jax.checkpoint(group_lse), final)
    return jnp.sum(weights * (lse - target_logit))

def renew(weight, moment, average, grad, factor):
    clipped = factor * grad
    moment_next = momentum_coef * moment + clipped
    weight_next = weight - learn_rate * (clipped + momentum_coef * moment_next)
    average_next = ema_decay * average + (1.0 - ema_decay) * weight_next
    return (moment_next, weight_next, average_next, weight_next.astype(jnp.bfloat16))

def reference(token_ids, targets, lengths, embed_table, embed_moment, embed_average, blocks, block_moment, block_average, pos_table, pos_moment, pos_average, vectors, vector_moment, vector_average):
    devices = N_DP * N_VOCAB
    doc_lens = lengths.reshape(devices, DOCS)
    seg_ids, pos_ids, weights = jax.vmap(partial(doc_info, tok_count=TOK_DEV, total_docs=DOCS * devices))(doc_lens)
    weights = weights * device_rise(0, devices, devices)[:, None]
    places = jnp.arange(TOK_DEV, dtype=jnp.int32)
    attn_mask = (seg_ids[:, :, None] == seg_ids[:, None, :]) & (places[None, None, :] <= places[None, :, None])
    ids = token_ids.reshape(devices, TOK_DEV)
    target_ids = targets.reshape(devices, TOK_DEV)

    def objective(table_now, blocks_now, pos_now, vectors_now):
        return loss_of(table_now, blocks_now, pos_now, vectors_now, ids, target_ids, pos_ids, weights, attn_mask)
    loss_sum, pullback = jax.vjp(objective, embed_table, blocks, pos_table, vectors)
    grads = pullback(jnp.ones((), jnp.float32))
    squares = jnp.sum(grads[0] * grads[0]) + jnp.sum(grads[1] * grads[1]) + jnp.sum(grads[2] * grads[2]) + jnp.sum(grads[3] * grads[3])
    grad_norm = jnp.sqrt(squares)
    factor = clip_bound / jnp.maximum(grad_norm, clip_bound)
    embed_out = renew(embed_table, embed_moment, embed_average, grads[0], factor)
    block_out = renew(blocks, block_moment, block_average, grads[1], factor)
    pos_out = renew(pos_table, pos_moment, pos_average, grads[2], factor)
    vector_out = renew(vectors, vector_moment, vector_average, grads[3], factor)
    return (loss_sum, grad_norm, embed_out[0], embed_out[1], embed_out[2], embed_out[3], block_out[0], block_out[1], block_out[2], block_out[3], pos_out[0], pos_out[1], pos_out[2], pos_out[3], vector_out[0], vector_out[1], vector_out[2], vector_out[3])
```

```python
from functools import partial

import jax
import jax.numpy as jnp
from jax import lax
from jax.experimental import pallas as pl
from jax.experimental.pallas import tpu as pltpu
from jax.sharding import PartitionSpec as P

H = 12
RING = 4
ORDERS = ((2, 1, 0), (1, 0, 2), (0, 2, 1))

norm_eps = 1e-05
clip_bound = 0.01
learn_rate = 10000.0
momentum_coef = 0.5
ema_decay = 0.5


def place():
    dp = lax.axis_index("dp")
    vocab = lax.axis_index("vocab")
    return (lax.div(dp, RING), lax.rem(dp, RING), lax.div(vocab, 2)), lax.rem(vocab, 2)


def device_at(at, core):
    return (at[0] * RING + at[1], at[2] * 2 + core)


def moved(at, axis, by):
    out = list(at)
    out[axis] = lax.rem(at[axis] + by, RING)
    return tuple(out)


class Wires:
    def __init__(self, send, recv):
        self.send, self.recv, self.count, self.live = send, recv, 0, []

    def copy(self, src, dst, device):
        number = self.count
        self.count += 1
        op = pltpu.make_async_remote_copy(
            src_ref=src,
            dst_ref=dst,
            send_sem=self.send.at[number],
            recv_sem=self.recv.at[number],
            device_id=device,
            device_id_type=pl.DeviceIdType.MESH,
        )
        op.start()
        self.live.append(op)
        return op

    def drain(self):
        for op in self.live:
            op.wait_send()


def greet(devices):
    barrier = pltpu.get_barrier_semaphore()
    for device in devices:
        pl.semaphore_signal(
            barrier, inc=1, device_id=device, device_id_type=pl.DeviceIdType.MESH
        )
    pl.semaphore_wait(barrier, len(devices))


def neighbours(at, core):
    near = [device_at(moved(at, axis, by), core) for axis in range(3) for by in (1, RING - 1)]
    return near + [device_at(at, 1 - core)]


def gather_kernel(
    mine_ref, small_ref, first_ref, second_ref, small_out, peer, block, send, recv, local
):
    at, core = place()
    out_refs = (first_ref, second_ref)
    rows, half = mine_ref.shape[1], mine_ref.shape[2] // 2
    part = 2 * rows // 3
    sibling = device_at(at, 1 - core)
    greet(neighbours(at, core))
    wires = Wires(send, recv)
    cols = pl.ds(pl.multiple_of(core * half, half), half)
    other = pl.ds(pl.multiple_of((1 - core) * half, half), half)

    swap = wires.copy(mine_ref.at[:, :, other], peer, sibling)
    small_local = pltpu.make_async_copy(small_ref, small_out.at[at[0], at[1], at[2], core], local.at[0])
    small_local.start()
    swap.wait_recv()
    for layer in range(2):
        own = jnp.where(core == 0, mine_ref[layer, :, :half], mine_ref[layer, :, half:])
        got = peer[layer]
        both = jnp.concatenate(
            [jnp.where(core == 0, own, got), jnp.where(core == 0, got, own)], 0
        )
        block[layer] = both.astype(jnp.bfloat16)
    block_local = []
    for layer in range(2):
        op = pltpu.make_async_copy(
            block.at[layer],
            out_refs[layer].at[at[0], at[1], at[2], :, cols],
            local.at[1 + layer],
        )
        op.start()
        block_local.append(op)

    def bundle(layer, p, phase, c, piece=None):
        order = ORDERS[p]
        index = list(at)
        index[order[phase]] = c
        for axis in order[:phase]:
            index[axis] = pl.ds(0, RING)
        first, count = p * part, part
        if piece is not None:
            if phase == 0:
                first, count = (first, 32) if piece == 0 else (first + 32, part - 32)
            else:
                index[order[0]] = pl.ds(2 * piece, 2)
        return out_refs[layer].at[index[0], index[1], index[2], pl.ds(first, count), cols]

    def small_bundle(phase, c):
        order = ORDERS[0]
        index = list(at)
        index[order[phase]] = c
        for axis in order[:phase]:
            index[axis] = pl.ds(0, RING)
        return small_out.at[index[0], index[1], index[2], core]

    def right(axis):
        return device_at(moved(at, axis, 1), core)

    def left(axis):
        return device_at(moved(at, axis, RING - 1), core)

    chains = [(layer, p) for layer in range(2) for p in range(3)]
    pending = []
    small_local.wait()
    for op in block_local:
        op.wait()
    for phase in range(3):
        steps = {}
        for key in chains:
            layer, p = key
            axis = ORDERS[p][phase]
            src = bundle(layer, p, phase, at[axis])
            if phase == 2:
                pending.append(wires.copy(src, src, sibling))
            steps[key] = (wires.copy(src, src, right(axis)), wires.copy(src, src, left(axis)))
        axis = ORDERS[0][phase]
        src = small_bundle(phase, at[axis])
        small_steps = (wires.copy(src, src, right(axis)), wires.copy(src, src, left(axis)))
        forwards = {}
        for key in chains:
            layer, p = key
            axis = ORDERS[p][phase]
            before, after = lax.rem(at[axis] + 3, RING), lax.rem(at[axis] + 1, RING)
            steps[key][0].wait_recv()
            src = bundle(layer, p, phase, before, 0)
            one = wires.copy(src, src, right(axis))
            steps[key][1].wait_recv()
            src = bundle(layer, p, phase, after, 1)
            two = wires.copy(src, src, left(axis))
            forwards[key] = (one, two)
            if phase == 2:
                for c in (before, after):
                    src = bundle(layer, p, phase, c)
                    pending.append(wires.copy(src, src, sibling))
        axis = ORDERS[0][phase]
        for op in small_steps:
            op.wait_recv()
        src = small_bundle(phase, lax.rem(at[axis] + 3, RING))
        small_forward = wires.copy(src, src, right(axis))
        for key in chains:
            layer, p = key
            axis = ORDERS[p][phase]
            across = lax.rem(at[axis] + 2, RING)
            for piece in range(2):
                forwards[key][piece].wait_recv()
                if phase == 2:
                    src = bundle(layer, p, phase, across, piece)
                    pending.append(wires.copy(src, src, sibling))
        small_forward.wait_recv()
    src = small_out.at[:, :, :, core]
    pending.append(wires.copy(src, src, sibling))
    for op in pending:
        op.wait_recv()
    wires.drain()


GATHER_COPIES = 1 + 3 * (6 * 4 + 3) + 6 * 5 + 1


def gather_weights(mine, small):
    layers, rows, width = mine.shape
    whole = jax.ShapeDtypeStruct((RING, RING, RING, 2 * rows, width), jnp.bfloat16)
    hbm = pl.BlockSpec(memory_space=pltpu.HBM)
    vmem = pl.BlockSpec(memory_space=pltpu.VMEM)
    first, second, small_all = pl.pallas_call(
        gather_kernel,
        out_shape=(
            whole,
            whole,
            jax.ShapeDtypeStruct((RING, RING, RING, 2) + small.shape, jnp.bfloat16),
        ),
        in_specs=[vmem, vmem],
        out_specs=(hbm, hbm, hbm),
        scratch_shapes=[
            pltpu.VMEM((layers, rows, width // 2), jnp.float32),
            pltpu.VMEM((layers, 2 * rows, width // 2), jnp.bfloat16),
            pltpu.SemaphoreType.DMA((GATHER_COPIES,)),
            pltpu.SemaphoreType.DMA((GATHER_COPIES,)),
            pltpu.SemaphoreType.DMA((3,)),
        ],
        compiler_params=pltpu.CompilerParams(
            collective_id=0, has_side_effects=True, vmem_limit_bytes=24 * 2**20
        ),
        name="gather_weights",
    )(mine, small)
    count = RING**3 * 2 * rows
    return (
        (first.reshape(count, width), second.reshape(count, width)),
        small_all.reshape((2 * RING**3,) + small.shape),
    )


def reduce_kernel(
    first_ref,
    second_ref,
    small_ref,
    out_ref,
    small_out,
    acc,
    sib,
    wide_half_0,
    wide_half_1,
    wide_half_2,
    wide_full,
    mid_half,
    mid_full,
    thin_half,
    thin_full,
    small_acc,
    small_sib,
    small_wide,
    small_mid,
    small_thin,
    final,
    final_peer,
    send,
    recv,
    local,
):
    at, core = place()
    grads = (first_ref, second_ref)
    rows, half = acc.shape[4], acc.shape[5]
    own_rows = rows // 2
    part = rows // 3
    sibling = device_at(at, 1 - core)
    cols = pl.ds(pl.multiple_of(core * half, half), half)
    other = pl.ds(pl.multiple_of((1 - core) * half, half), half)
    chains = [(layer, p) for layer in range(2) for p in range(3)]
    loads = {}
    number = 0
    near = (2, 1, 3, 0)

    def span(p, step, c, piece=None):
        order = ORDERS[p]
        index = list(at)
        index[order[2 - step]] = c
        for axis in order[: 2 - step]:
            index[axis] = pl.ds(0, RING)
        first, count = p * part, part
        if piece is not None:
            if step == 2:
                first, count = (first, 32) if piece == 0 else (first + 32, part - 32)
            else:
                index[order[0]] = pl.ds(2 * piece, 2)
        return index, pl.ds(first, count)

    for by in near:
        for key in chains:
            layer, p = key
            c = lax.rem(at[ORDERS[p][2]] + by, RING)
            index, where = span(p, 0, c)
            op = pltpu.make_async_copy(
                grads[layer].at[index[0], index[1], index[2], where, cols],
                acc.at[layer, index[0], index[1], index[2], where],
                local.at[number],
            )
            op.start()
            loads[key, by] = op
            number += 1
    small_load = pltpu.make_async_copy(small_ref.at[:, :, :, core], small_acc, local.at[number])
    small_load.start()

    greet(neighbours(at, core))
    wires = Wires(send, recv)
    swaps = {}
    small_swap = wires.copy(small_ref.at[:, :, :, 1 - core], small_sib, sibling)
    for by in near:
        for key in chains:
            layer, p = key
            c = lax.rem(at[ORDERS[p][2]] + by, RING)
            index, where = span(p, 0, c)
            swaps[key, by] = wires.copy(
                grads[layer].at[index[0], index[1], index[2], where, other],
                sib.at[layer, index[0], index[1], index[2], where],
                sibling,
            )

    def right(axis):
        return device_at(moved(at, axis, 1), core)

    def left(axis):
        return device_at(moved(at, axis, RING - 1), core)

    def add(layer, p, step, c, piece, terms, into=None):
        order = ORDERS[p]
        free = [axis for axis in range(3) if axis in order[: 2 - step]]
        sizes = [2 if piece is not None and axis == order[0] else RING for axis in free]
        index, where = span(p, step, c, piece)
        total = 1
        for size in sizes:
            total *= size

        def body(n, unused):
            spot = list(index)
            inner = []
            if len(free) == 2:
                inner = [lax.div(n, sizes[1]), lax.rem(n, sizes[1])]
            elif len(free) == 1:
                inner = [n]
            for axis, size, i in zip(free, sizes, inner):
                start = 2 * piece if size == 2 else 0
                spot[axis] = start + i
            here = (layer, spot[0], spot[1], spot[2], where)
            value = acc[here].astype(jnp.float32)
            for term in terms:
                value = value + term(inner, spot, where).astype(jnp.float32)
            if into is None:
                acc[here] = value.astype(jnp.bfloat16)
            else:
                into(value)
            return unused

        if total == 1:
            body(0, 0)
        else:
            lax.fori_loop(0, total, body, 0)

    def add_sibling(key, by):
        layer, p = key
        loads[key, by].wait()
        swaps[key, by].wait_recv()
        c = lax.rem(at[ORDERS[p][2]] + by, RING)
        add(
            layer,
            p,
            0,
            c,
            None,
            [lambda inner, spot, where: sib[layer, spot[0], spot[1], spot[2], where]],
        )

    wide_half = (wide_half_0, wide_half_1, wide_half_2)

    def half_slot(layer, p, step, side):
        if step == 0:
            return wide_half[p].at[layer, side]
        if step == 1:
            return mid_half.at[layer, p, side]
        return thin_half.at[layer, p, side, pl.ds(0, 32 if side == 0 else part - 32)]

    def full_slot(layer, p, step, side):
        return (wide_full, mid_full, thin_full)[step].at[layer, p, side]

    def read(slot):
        return lambda inner, spot, where: slot[tuple(inner) + (slice(None), slice(None))]

    def acc_view(layer, p, step, c, piece=None):
        index, where = span(p, step, c, piece)
        return acc.at[layer, index[0], index[1], index[2], where]

    small_order = ORDERS[0]
    small_slots = (small_wide, small_mid, small_thin)

    def small_view(step, c):
        index = list(at)
        index[small_order[2 - step]] = c
        for axis in small_order[: 2 - step]:
            index[axis] = slice(None)
        return tuple(index)

    def small_add(step, c, term):
        where = small_view(step, c)
        small_acc[where] = small_acc[where] + term

    for step in range(3):
        halves = {}
        for key in chains:
            layer, p = key
            axis = ORDERS[p][2 - step]
            if step == 0:
                add_sibling(key, 2)
            across = lax.rem(at[axis] + 2, RING)
            halves[key] = (
                wires.copy(
                    acc_view(layer, p, step, across, 0), half_slot(layer, p, step, 0), right(axis)
                ),
                wires.copy(
                    acc_view(layer, p, step, across, 1), half_slot(layer, p, step, 1), left(axis)
                ),
            )
        if step == 0:
            small_load.wait()
            small_swap.wait_recv()
            small_acc[...] = small_acc[...] + small_sib[...]
        axis = small_order[2 - step]
        across = lax.rem(at[axis] + 2, RING)
        small_half = wires.copy(
            small_acc.at[small_view(step, across)], small_slots[step].at[0], right(axis)
        )
        if step == 0:
            for key in chains:
                add_sibling(key, 1)
                add_sibling(key, 3)
        fulls = {}
        for key in chains:
            layer, p = key
            axis = ORDERS[p][2 - step]
            after, before = lax.rem(at[axis] + 1, RING), lax.rem(at[axis] + 3, RING)
            halves[key][0].wait_recv()
            add(layer, p, step, after, 0, [read(half_slot(layer, p, step, 0))])
            one = wires.copy(
                acc_view(layer, p, step, after), full_slot(layer, p, step, 0), right(axis)
            )
            halves[key][1].wait_recv()
            add(layer, p, step, before, 1, [read(half_slot(layer, p, step, 1))])
            two = wires.copy(
                acc_view(layer, p, step, before), full_slot(layer, p, step, 1), left(axis)
            )
            fulls[key] = (one, two)
        axis = small_order[2 - step]
        after, before = lax.rem(at[axis] + 1, RING), lax.rem(at[axis] + 3, RING)
        small_half.wait_recv()
        small_add(step, after, small_slots[step][0])
        small_full = (
            wires.copy(small_acc.at[small_view(step, after)], small_slots[step].at[1], right(axis)),
            wires.copy(small_acc.at[small_view(step, before)], small_slots[step].at[2], left(axis)),
        )
        for key in chains:
            layer, p = key
            axis = ORDERS[p][2 - step]
            if step == 0:
                add_sibling(key, 0)
            fulls[key][0].wait_recv()
            fulls[key][1].wait_recv()
            terms = [read(full_slot(layer, p, step, side)) for side in range(2)]
            if step < 2:
                add(layer, p, step, at[axis], None, terms)
            else:

                def keep(value, layer=layer, p=p):
                    final[layer, p * part : (p + 1) * part] = value

                add(layer, p, step, at[axis], None, terms, keep)
        axis = small_order[2 - step]
        for op in small_full:
            op.wait_recv()
        small_add(step, at[axis], small_slots[step][1] + small_slots[step][2])

    theirs = pl.ds(pl.multiple_of((1 - core) * own_rows, own_rows), own_rows)
    swap = wires.copy(final.at[:, theirs], final_peer, sibling)
    small_out[...] = small_acc[at]
    swap.wait_recv()
    for layer in range(2):
        own = jnp.where(core == 0, final[layer, :own_rows], final[layer, own_rows:])
        got = final_peer[layer]
        out_ref[layer, :, :half] = jnp.where(core == 0, own, got)
        out_ref[layer, :, half:] = jnp.where(core == 0, got, own)
    wires.drain()


REDUCE_COPIES = 1 + 24 + 3 * (6 * 4 + 3) + 1


def reduce_weights(first, second, small):
    count, width = first.shape
    rows, half = count // RING**3, width // 2
    part = rows // 3
    torus = (RING, RING, RING)
    small_shape = small.shape[1:]
    hbm = pl.BlockSpec(memory_space=pltpu.HBM)
    vmem = pl.BlockSpec(memory_space=pltpu.VMEM)
    low = jnp.bfloat16

    def wide_shape(p):
        order = ORDERS[p]
        free = [axis for axis in range(3) if axis in order[:2]]
        return tuple(2 if axis == order[0] else RING for axis in free)

    return pl.pallas_call(
        reduce_kernel,
        out_shape=(
            jax.ShapeDtypeStruct((2, rows // 2, width), jnp.float32),
            jax.ShapeDtypeStruct(small_shape, jnp.float32),
        ),
        in_specs=[hbm, hbm, hbm],
        out_specs=(vmem, vmem),
        scratch_shapes=[
            pltpu.VMEM((2,) + torus + (rows, half), low),
            pltpu.VMEM((2,) + torus + (rows, half), low),
        ]
        + [pltpu.VMEM((2, 2) + wide_shape(p) + (part, half), low) for p in range(3)]
        + [
            pltpu.VMEM((2, 3, 2, RING, RING, part, half), low),
            pltpu.VMEM((2, 3, 2, 2, part, half), low),
            pltpu.VMEM((2, 3, 2, RING, part, half), low),
            pltpu.VMEM((2, 3, 2, 32, half), low),
            pltpu.VMEM((2, 3, 2, part, half), low),
            pltpu.VMEM(torus + small_shape, jnp.float32),
            pltpu.VMEM(torus + small_shape, jnp.float32),
            pltpu.VMEM((3, RING, RING) + small_shape, jnp.float32),
            pltpu.VMEM((3, RING) + small_shape, jnp.float32),
            pltpu.VMEM((3,) + small_shape, jnp.float32),
            pltpu.VMEM((2, rows, half), jnp.float32),
            pltpu.VMEM((2, rows // 2, half), jnp.float32),
            pltpu.SemaphoreType.DMA((REDUCE_COPIES,)),
            pltpu.SemaphoreType.DMA((REDUCE_COPIES,)),
            pltpu.SemaphoreType.DMA((25,)),
        ],
        compiler_params=pltpu.CompilerParams(
            collective_id=1, has_side_effects=True, vmem_limit_bytes=58 * 2**20
        ),
        name="reduce_weights",
    )(
        first.reshape(torus + (rows, width)),
        second.reshape(torus + (rows, width)),
        small.reshape(torus + (2,) + small_shape),
    )


def sum_kernel(in_ref, out_ref, slots, send, recv):
    at, core = place()
    sibling = device_at(at, 1 - core)
    partners = [sibling] + [
        device_at(moved(at, axis, by), core) for axis in range(3) for by in range(1, RING)
    ]
    greet(partners)
    wires = Wires(send, recv)
    slots[0, core] = in_ref[...]
    swap = wires.copy(in_ref, slots.at[0, core], sibling)
    swap.wait_recv()
    value = slots[0, 0] + slots[0, 1]
    for axis in range(3):
        slots[1 + axis, at[axis]] = value
        ops = []
        for by in range(1, RING):
            ops.append(
                wires.copy(
                    slots.at[1 + axis, at[axis]],
                    slots.at[1 + axis, at[axis]],
                    device_at(moved(at, axis, by), core),
                )
            )
        for op in ops:
            op.wait_recv()
        value = slots[1 + axis, 0]
        for c in range(1, RING):
            value = value + slots[1 + axis, c]
    out_ref[...] = value
    wires.drain()


def sum_all(value):
    vmem = pl.BlockSpec(memory_space=pltpu.VMEM)
    return pl.pallas_call(
        sum_kernel,
        out_shape=jax.ShapeDtypeStruct(value.shape, jnp.float32),
        in_specs=[vmem],
        out_specs=vmem,
        scratch_shapes=[
            pltpu.VMEM((4, RING) + value.shape, jnp.float32),
            pltpu.SemaphoreType.DMA((10,)),
            pltpu.SemaphoreType.DMA((10,)),
        ],
        compiler_params=pltpu.CompilerParams(collective_id=2, has_side_effects=True),
        name="sum_all",
    )(value)


def layer_norm(inputs, gain, shift):
    centered = inputs - jnp.mean(inputs, -1, keepdims=True)
    spread = jnp.mean(centered * centered, -1, keepdims=True)
    return centered * lax.rsqrt(spread + norm_eps) * gain + shift


def gelu_tanh(inputs):
    return jax.nn.gelu(inputs, approximate=True)


def doc_info(doc_lens, tok_count, total_docs):
    doc_ends = jnp.cumsum(doc_lens)
    places = jnp.arange(tok_count, dtype=jnp.int32)
    seg_ids = jnp.sum((places[:, None] >= doc_ends[None, :]).astype(jnp.int32), 1)
    one_hot = seg_ids[:, None] == jnp.arange(doc_lens.shape[0], dtype=jnp.int32)[None, :]
    starts = doc_ends - doc_lens
    pos_ids = places - jnp.sum(jnp.where(one_hot, starts[None, :], 0), 1)
    doc_len = jnp.sum(jnp.where(one_hot, doc_lens[None, :], 0), 1)
    weights = 1.0 / (doc_len.astype(jnp.float32) * total_docs)
    return (seg_ids, pos_ids, weights)


def device_rise(first, count, devices):
    places = first + jnp.arange(count, dtype=jnp.int32)
    return 1.0 + 2.0 * places.astype(jnp.float32) / (devices - 1)


def contract(left, right, left_dim, right_dim):
    return lax.dot_general(
        left, right, (((left_dim,), (right_dim,)), ((), ())), preferred_element_type=jnp.float32
    )


def split_vecs(vecs, width):
    pieces = [vecs[index * width : (index + 1) * width] for index in range(7)]
    ff_width = vecs.shape[0] - 8 * width
    pieces.append(vecs[7 * width : 7 * width + ff_width])
    pieces.append(vecs[7 * width + ff_width :])
    return pieces


def split_mats(mats, width):
    ff_width = (mats.shape[0] - 4 * width) // 2
    cuts = [0, 3 * width, 4 * width, 4 * width + ff_width, 4 * width + 2 * ff_width]
    return [mats[a:b] for a, b in zip(cuts[:-1], cuts[1:])]


def layer_forward(hidden, mats, vecs, attn_mask):
    tok, width = hidden.shape
    head_dim = width // H
    w_qkv, w_proj, w_fc, w_out = split_mats(mats, width)
    gain_one, shift_one, bias_q, bias_v, bias_proj, gain_two, shift_two, bias_fc, bias_out = (
        split_vecs(vecs, width)
    )
    normed_low = layer_norm(hidden, gain_one, shift_one).astype(jnp.bfloat16)
    bias_qkv = jnp.concatenate([bias_q, jnp.zeros_like(bias_q), bias_v])
    qkv_f = contract(normed_low, w_qkv, 1, 1) + bias_qkv
    qkv_low = qkv_f.astype(jnp.bfloat16).reshape(tok, 3, H, head_dim)
    scores = jnp.einsum(
        "thd,uhd->htu", qkv_low[:, 0], qkv_low[:, 1], preferred_element_type=jnp.float32
    ) * head_dim ** (-0.5)
    scores = jnp.where(attn_mask[None], scores, -1000000000.0)
    shifted = jnp.exp(scores - jnp.max(scores, -1, keepdims=True))
    attn_probs = shifted / jnp.sum(shifted, -1, keepdims=True)
    probs_low = attn_probs.astype(jnp.bfloat16)
    attended = jnp.einsum(
        "htu,uhd->thd", probs_low, qkv_low[:, 2], preferred_element_type=jnp.float32
    )
    attended = attended.reshape(tok, width).astype(jnp.bfloat16)
    middle = hidden + contract(attended, w_proj, 1, 1) + bias_proj
    two_low = layer_norm(middle, gain_two, shift_two).astype(jnp.bfloat16)
    up_act = contract(two_low, w_fc, 1, 1) + bias_fc
    activ_low = gelu_tanh(up_act).astype(jnp.bfloat16)
    output = middle + contract(activ_low, w_out, 1, 0) + bias_out
    saved = (
        hidden,
        normed_low,
        qkv_low,
        attn_probs,
        probs_low,
        attended,
        middle,
        two_low,
        up_act,
        activ_low,
    )
    return (output, saved)


def layer_backward(saved, mats, vecs, grad_out):
    hidden, normed_low, qkv_low, attn_probs, probs_low, attended, middle, two_low, up_act, activ_low = saved
    tok, width = hidden.shape
    head_dim = width // H
    w_qkv, w_proj, w_fc, w_out = split_mats(mats, width)
    gain_one, shift_one, bias_q, bias_v, bias_proj, gain_two, shift_two, bias_fc, bias_out = (
        split_vecs(vecs, width)
    )
    low = jnp.bfloat16
    out_low = grad_out.astype(low)
    grad_wout = contract(activ_low, out_low, 0, 0).astype(low)
    grad_bout = jnp.sum(grad_out, 0)
    grad_act = contract(out_low, w_out, 1, 1)
    unused_up, gelu_pull = jax.vjp(gelu_tanh, up_act)
    grad_up = gelu_pull(grad_act)[0]
    up_low = grad_up.astype(low)
    grad_wfc = contract(up_low, two_low, 0, 0).astype(low)
    grad_bfc = jnp.sum(grad_up, 0)
    grad_two = contract(up_low, w_fc, 1, 0)
    unused_two, norm_pull = jax.vjp(layer_norm, middle, gain_two, shift_two)
    grad_mid_norm, grad_g2, grad_s2 = norm_pull(grad_two)
    grad_mid = grad_out + grad_mid_norm
    mid_low = grad_mid.astype(low)
    grad_wproj = contract(mid_low, attended, 0, 0).astype(low)
    grad_bproj = jnp.sum(grad_mid, 0)
    grad_att = contract(mid_low, w_proj, 1, 0).astype(low).reshape(tok, H, head_dim)
    grad_probs = jnp.einsum(
        "thd,uhd->htu", grad_att, qkv_low[:, 2], preferred_element_type=jnp.float32
    )
    grad_vals = jnp.einsum("htu,thd->uhd", probs_low, grad_att, preferred_element_type=jnp.float32)
    grad_scores = attn_probs * (grad_probs - jnp.sum(attn_probs * grad_probs, -1, keepdims=True))
    score_low = (grad_scores * head_dim ** (-0.5)).astype(low)
    grad_q = jnp.einsum(
        "htu,uhd->thd", score_low, qkv_low[:, 1], preferred_element_type=jnp.float32
    )
    grad_k = jnp.einsum(
        "htu,thd->uhd", score_low, qkv_low[:, 0], preferred_element_type=jnp.float32
    )
    grad_qkv = jnp.stack([grad_q, grad_k, grad_vals], 1).reshape(tok, 3 * width)
    qkv_grad_low = grad_qkv.astype(low)
    grad_wqkv = contract(qkv_grad_low, normed_low, 0, 0).astype(low)
    grad_normed = contract(qkv_grad_low, w_qkv, 1, 0)
    unused_one, first_pull = jax.vjp(layer_norm, hidden, gain_one, shift_one)
    grad_in_norm, grad_g1, grad_s1 = first_pull(grad_normed)
    grad_in = grad_mid + grad_in_norm
    grad_mats = jnp.concatenate([grad_wqkv, grad_wproj, grad_wfc, grad_wout], 0)
    grad_vecs = jnp.concatenate(
        [
            grad_g1,
            grad_s1,
            jnp.sum(grad_q, 0).reshape(width),
            jnp.sum(grad_vals, 0).reshape(width),
            grad_bproj,
            grad_g2,
            grad_s2,
            grad_bfc,
            grad_bout,
        ]
    )
    return (grad_in, grad_mats, grad_vecs)


def renew(weight, moment, average, grad, factor):
    clipped = factor * grad
    moment_next = momentum_coef * moment + clipped
    weight_next = weight - learn_rate * (clipped + momentum_coef * moment_next)
    average_next = ema_decay * average + (1.0 - ema_decay) * weight_next
    return (moment_next, weight_next, average_next, weight_next.astype(jnp.bfloat16))


SMALL_ROWS, LANES = 16, 128


def pack_small(values):
    room = SMALL_ROWS * LANES - values.shape[-1]
    pads = [(0, 0)] * (values.ndim - 1) + [(0, room)]
    return jnp.pad(values, pads).reshape(values.shape[:-1] + (SMALL_ROWS, LANES))


def per_device(
    token_ids,
    targets,
    lengths,
    embed_table,
    embed_moment,
    embed_average,
    blocks,
    block_moment,
    block_average,
    pos_table,
    pos_moment,
    pos_average,
    vectors,
    vector_moment,
    vector_average,
):
    devices = lax.axis_size(("dp", "vocab"))
    vocab_count = lax.axis_size("vocab")
    dp_count = lax.axis_size("dp")
    vocab_at = lax.axis_index("vocab")
    data_at = lax.axis_index("dp")
    tok = token_ids.shape[0]
    own_rows, width = embed_table.shape
    layers = blocks.shape[0]
    capacity = max(2, 2 * tok // devices)
    low = jnp.bfloat16
    blocks, block_moment, block_average = (
        jnp.transpose(item, (0, 2, 1)) for item in (blocks, block_moment, block_average)
    )
    pos_rows, pos_cols = pos_table.shape
    vec_own = vectors.shape[0]
    table_low = embed_table.astype(low)
    pad_rows = -own_rows % 16
    table_padded = jnp.pad(table_low, ((0, pad_rows), (0, 0)))
    slot_rows = own_rows + pad_rows

    both_ids = jnp.stack([token_ids, targets])
    owners = both_ids // own_rows
    hits = owners[:, :, None] == jnp.arange(devices, dtype=jnp.int32)[None, None, :]
    tokens = jnp.arange(tok, dtype=jnp.int32)
    earlier = jnp.sum(
        (owners[:, :, None] == owners[:, None, :]) & (tokens[None, None, :] < tokens[None, :, None]), 2
    )
    slot_hot = hits[:, :, :, None] & (
        earlier[:, :, None, None] == jnp.arange(capacity, dtype=jnp.int32)[None, None, None, :]
    )
    send_rows = jnp.sum(
        jnp.where(slot_hot, (both_ids % own_rows)[:, :, None, None], 0), 1
    )
    slot_hot = slot_hot.reshape(2, tok, devices * capacity).astype(low)
    local_rows = lax.all_to_all(send_rows, ("dp", "vocab"), split_axis=1, concat_axis=1, tiled=True)
    asked = (
        local_rows.reshape(-1)[:, None] == jnp.arange(own_rows, dtype=jnp.int32)[None, :]
    ).astype(low)
    fetched = jnp.dot(asked, table_low, preferred_element_type=jnp.float32).astype(low)
    returned_rows = lax.all_to_all(
        fetched.reshape(2, devices, capacity, width),
        ("dp", "vocab"),
        split_axis=1,
        concat_axis=1,
        tiled=True,
    ).reshape(2, devices * capacity, width)

    small = pack_small(
        jnp.concatenate([jnp.transpose(pos_table).reshape(-1), vectors]).astype(low)
    )
    mats_all, small_all = gather_weights(blocks, small)
    small_all = small_all.reshape(devices, -1)
    pos_low_t = small_all[:, : pos_rows * pos_cols].reshape(width, pos_rows)
    vecs_all = (
        small_all[:, pos_rows * pos_cols : pos_rows * pos_cols + vec_own]
        .reshape(-1)
        .astype(jnp.float32)
    )
    vec_width = (vecs_all.shape[0] - 2 * width) // layers

    lens_group = lengths[0]
    seg_group, pos_group, weight_group = jax.vmap(
        partial(doc_info, tok_count=tok, total_docs=devices * lens_group.shape[1])
    )(lens_group)
    weight_group = weight_group * device_rise(data_at * vocab_count, vocab_count, devices)[:, None]
    seg_ids = lax.dynamic_index_in_dim(seg_group, vocab_at, 0, keepdims=False)
    pos_ids = lax.dynamic_index_in_dim(pos_group, vocab_at, 0, keepdims=False)
    own_weight = lax.dynamic_index_in_dim(weight_group, vocab_at, 0, keepdims=False)
    places = jnp.arange(tok, dtype=jnp.int32)
    attn_mask = (seg_ids[:, None] == seg_ids[None, :]) & (places[None, :] <= places[:, None])

    gotten = jnp.einsum(
        "ktr,krd->ktd", slot_hot, returned_rows, preferred_element_type=jnp.float32
    )
    pos_hot = (pos_ids[:, None] == jnp.arange(pos_rows, dtype=jnp.int32)[None, :]).astype(low)
    hidden = gotten[0] + contract(pos_hot, pos_low_t, 1, 1)
    kept = []
    for layer in range(layers):
        hidden, saved = layer_forward(
            hidden,
            mats_all[layer],
            vecs_all[layer * vec_width : (layer + 1) * vec_width],
            attn_mask,
        )
        kept.append(saved)
    tail = vecs_all[layers * vec_width :]
    final_low = layer_norm(hidden, tail[:width], tail[width:]).astype(low)
    group_rows = lax.all_gather(final_low, "vocab", axis=0, tiled=True)
    table_blocks = lax.all_gather(table_padded, "dp", axis=0)
    group_weight = weight_group.reshape(-1)
    group_count = group_rows.shape[0]
    real = jnp.arange(slot_rows, dtype=jnp.int32) < own_rows

    def forward_block(carry, piece):
        top, total = carry
        logits = jnp.where(real[None, :], contract(group_rows, piece, 1, 1), -1e30)
        new_top = jnp.maximum(top, jnp.max(logits, 1))
        total = total * jnp.exp(top - new_top) + jnp.sum(jnp.exp(logits - new_top[:, None]), 1)
        return ((new_top, total), None)

    start_top = jnp.full((group_count,), -1e30, jnp.float32)
    (row_top, row_total), unused = lax.scan(
        forward_block, (start_top, jnp.zeros((group_count,), jnp.float32)), table_blocks
    )
    tops, totals = lax.all_gather(jnp.stack([row_top, row_total]), "vocab", axis=1)
    peak = jnp.max(tops, 0)
    group_lse = peak + jnp.log(jnp.sum(totals * jnp.exp(tops - peak[None]), 0))
    own_lse = lax.dynamic_slice_in_dim(group_lse, vocab_at * tok, tok)
    target_rows = gotten[1]
    final_f = final_low.astype(jnp.float32)
    loss_part = jnp.sum(own_weight * (own_lse - jnp.sum(final_f * target_rows, 1)))

    def backward_block(acc, piece):
        logits = jnp.where(real[None, :], contract(group_rows, piece, 1, 1), -1e30)
        grad_low = (group_weight[:, None] * jnp.exp(logits - group_lse[:, None])).astype(low)
        return (
            acc + jnp.dot(grad_low, piece, preferred_element_type=jnp.float32),
            contract(grad_low, group_rows, 0, 0).astype(low),
        )

    group_grad, term = lax.scan(
        backward_block, jnp.zeros((group_count, width), jnp.float32), table_blocks
    )
    own_grad = lax.psum_scatter(
        group_grad.astype(low), "vocab", scatter_dimension=0, tiled=True
    ).astype(jnp.float32)
    table_grad = lax.psum_scatter(
        term.reshape(slot_rows * dp_count, width), "dp", scatter_dimension=0, tiled=True
    )[:own_rows].astype(jnp.float32)
    grad_final = own_grad - own_weight[:, None] * target_rows
    target_grad = -own_weight[:, None] * final_f
    unused_final, final_pull = jax.vjp(layer_norm, hidden, tail[:width], tail[width:])
    grad_hidden, grad_gf, grad_sf = final_pull(grad_final)
    mats_parts = [None] * layers
    vec_parts = [None] * layers
    for layer in reversed(range(layers)):
        grad_hidden, mats_parts[layer], vec_parts[layer] = layer_backward(
            kept[layer],
            mats_all[layer],
            vecs_all[layer * vec_width : (layer + 1) * vec_width],
            grad_hidden,
        )
    grad_vec_all = jnp.concatenate(vec_parts + [grad_gf, grad_sf])
    grad_pos = lax.dot_general(
        grad_hidden,
        pos_hot.astype(jnp.float32),
        (((0,), (0,)), ((), ())),
        precision=lax.Precision.HIGHEST,
    )
    send_grads = jnp.einsum(
        "ktr,ktd->krd",
        slot_hot,
        jnp.stack([grad_hidden, target_grad]).astype(low),
        preferred_element_type=jnp.float32,
    ).astype(low)
    back_grads = lax.all_to_all(
        send_grads.reshape(2, devices, capacity, width),
        ("dp", "vocab"),
        split_axis=1,
        concat_axis=1,
        tiled=True,
    ).reshape(-1, width)
    small_grads = pack_small(
        jnp.concatenate(
            [grad_pos.reshape(devices, -1), grad_vec_all.reshape(devices, -1)], 1
        )
    )
    mats_shard, small_shard = reduce_weights(mats_parts[0], mats_parts[1], small_grads)
    small_shard = small_shard.reshape(-1)
    pos_shard = small_shard[: pos_rows * pos_cols].reshape(pos_cols, pos_rows)
    vec_shard = small_shard[pos_rows * pos_cols : pos_rows * pos_cols + vec_own]
    table_grad = table_grad + contract(asked, back_grads, 0, 0)
    local_squares = (
        jnp.sum(table_grad * table_grad)
        + jnp.sum(mats_shard * mats_shard)
        + jnp.sum(pos_shard * pos_shard)
        + jnp.sum(vec_shard * vec_shard)
    )
    both_sums = sum_all(
        jnp.broadcast_to(jnp.pad(jnp.stack([loss_part, local_squares]), (0, 6))[:, None], (8, LANES))
    )
    loss_sum, squares = both_sums[0, 0], both_sums[1, 0]
    grad_norm = jnp.sqrt(squares)
    factor = clip_bound / jnp.maximum(grad_norm, clip_bound)
    embed_out = renew(embed_table, embed_moment, embed_average, table_grad, factor)
    block_out = renew(blocks, block_moment, block_average, mats_shard, factor)
    block_out = tuple(jnp.transpose(item, (0, 2, 1)) for item in block_out)
    pos_out = renew(
        jnp.transpose(pos_table),
        jnp.transpose(pos_moment),
        jnp.transpose(pos_average),
        pos_shard,
        factor,
    )
    pos_out = tuple(jnp.transpose(item) for item in pos_out)
    vector_out = renew(vectors, vector_moment, vector_average, vec_shard, factor)
    return (loss_sum, grad_norm) + embed_out + block_out + pos_out + vector_out


def solution(mesh):
    table = P(("dp", "vocab"), None)
    cols = P(None, None, ("dp", "vocab"))
    pos = P(None, ("dp", "vocab"))
    vec = P(("dp", "vocab"))
    return jax.shard_map(
        per_device,
        mesh=mesh,
        in_specs=(vec, vec, P("dp", None, None))
        + (table,) * 3
        + (cols,) * 3
        + (pos,) * 3
        + (vec,) * 3,
        out_specs=(P(), P()) + (table,) * 4 + (cols,) * 4 + (pos,) * 4 + (vec,) * 4,
        check_vma=False,
    )
```

```python
from functools import partial

import jax
import jax.numpy as jnp
from jax import lax
from jax.experimental import pallas as pl
from jax.experimental.pallas import tpu as pltpu
from jax.sharding import PartitionSpec as P

H = 12
RING = 4
ORDERS = ((2, 1, 0), (1, 0, 2), (0, 2, 1))

norm_eps = 1e-05
clip_bound = 0.01
learn_rate = 10000.0
momentum_coef = 0.5
ema_decay = 0.5


def place():
    dp = lax.axis_index("dp")
    vocab = lax.axis_index("vocab")
    return (lax.div(dp, RING), lax.rem(dp, RING), lax.div(vocab, 2)), lax.rem(vocab, 2)


def device_at(at, core):
    return (at[0] * RING + at[1], at[2] * 2 + core)


def moved(at, axis, by):
    out = list(at)
    out[axis] = lax.rem(at[axis] + by, RING)
    return tuple(out)


class Wires:
    def __init__(self, send, recv):
        self.send, self.recv, self.count, self.live = send, recv, 0, []

    def copy(self, src, dst, device):
        number = self.count
        self.count += 1
        op = pltpu.make_async_remote_copy(
            src_ref=src,
            dst_ref=dst,
            send_sem=self.send.at[number],
            recv_sem=self.recv.at[number],
            device_id=device,
            device_id_type=pl.DeviceIdType.MESH,
        )
        op.start()
        self.live.append(op)
        return op

    def drain(self):
        for op in self.live:
            op.wait_send()


def greet(devices):
    barrier = pltpu.get_barrier_semaphore()
    for device in devices:
        pl.semaphore_signal(
            barrier, inc=1, device_id=device, device_id_type=pl.DeviceIdType.MESH
        )
    pl.semaphore_wait(barrier, len(devices))


def neighbours(at, core):
    near = [device_at(moved(at, axis, by), core) for axis in range(3) for by in (1, RING - 1)]
    return near + [device_at(at, 1 - core)]


def gather_kernel(
    mine_ref, small_ref, first_ref, second_ref, small_out, peer, block, send, recv, local
):
    at, core = place()
    out_refs = (first_ref, second_ref)
    rows, half = mine_ref.shape[1], mine_ref.shape[2] // 2
    part = 2 * rows // 3
    sibling = device_at(at, 1 - core)
    greet(neighbours(at, core))
    wires = Wires(send, recv)
    cols = pl.ds(pl.multiple_of(core * half, half), half)
    other = pl.ds(pl.multiple_of((1 - core) * half, half), half)

    swap = wires.copy(mine_ref.at[:, :, other], peer, sibling)
    small_local = pltpu.make_async_copy(small_ref, small_out.at[at[0], at[1], at[2], core], local.at[0])
    small_local.start()
    swap.wait_recv()
    for layer in range(2):
        own = jnp.where(core == 0, mine_ref[layer, :, :half], mine_ref[layer, :, half:])
        got = peer[layer]
        both = jnp.concatenate(
            [jnp.where(core == 0, own, got), jnp.where(core == 0, got, own)], 0
        )
        block[layer] = both.astype(jnp.bfloat16)
    block_local = []
    for layer in range(2):
        op = pltpu.make_async_copy(
            block.at[layer],
            out_refs[layer].at[at[0], at[1], at[2], :, cols],
            local.at[1 + layer],
        )
        op.start()
        block_local.append(op)

    def bundle(layer, p, phase, c, piece=None):
        order = ORDERS[p]
        index = list(at)
        index[order[phase]] = c
        for axis in order[:phase]:
            index[axis] = pl.ds(0, RING)
        first, count = p * part, part
        if piece is not None:
            if phase == 0:
                first, count = (first, 32) if piece == 0 else (first + 32, part - 32)
            else:
                index[order[0]] = pl.ds(2 * piece, 2)
        return out_refs[layer].at[index[0], index[1], index[2], pl.ds(first, count), cols]

    def small_bundle(phase, c):
        order = ORDERS[0]
        index = list(at)
        index[order[phase]] = c
        for axis in order[:phase]:
            index[axis] = pl.ds(0, RING)
        return small_out.at[index[0], index[1], index[2], core]

    def right(axis):
        return device_at(moved(at, axis, 1), core)

    def left(axis):
        return device_at(moved(at, axis, RING - 1), core)

    chains = [(layer, p) for layer in range(2) for p in range(3)]
    pending = []
    small_local.wait()
    for op in block_local:
        op.wait()
    for phase in range(3):
        steps = {}
        for key in chains:
            layer, p = key
            axis = ORDERS[p][phase]
            src = bundle(layer, p, phase, at[axis])
            if phase == 2:
                pending.append(wires.copy(src, src, sibling))
            steps[key] = (wires.copy(src, src, right(axis)), wires.copy(src, src, left(axis)))
        axis = ORDERS[0][phase]
        src = small_bundle(phase, at[axis])
        small_steps = (wires.copy(src, src, right(axis)), wires.copy(src, src, left(axis)))
        forwards = {}
        for key in chains:
            layer, p = key
            axis = ORDERS[p][phase]
            before, after = lax.rem(at[axis] + 3, RING), lax.rem(at[axis] + 1, RING)
            steps[key][0].wait_recv()
            src = bundle(layer, p, phase, before, 0)
            one = wires.copy(src, src, right(axis))
            steps[key][1].wait_recv()
            src = bundle(layer, p, phase, after, 1)
            two = wires.copy(src, src, left(axis))
            forwards[key] = (one, two)
            if phase == 2:
                for c in (before, after):
                    src = bundle(layer, p, phase, c)
                    pending.append(wires.copy(src, src, sibling))
        axis = ORDERS[0][phase]
        for op in small_steps:
            op.wait_recv()
        src = small_bundle(phase, lax.rem(at[axis] + 3, RING))
        small_forward = wires.copy(src, src, right(axis))
        for key in chains:
            layer, p = key
            axis = ORDERS[p][phase]
            across = lax.rem(at[axis] + 2, RING)
            for piece in range(2):
                forwards[key][piece].wait_recv()
                if phase == 2:
                    src = bundle(layer, p, phase, across, piece)
                    pending.append(wires.copy(src, src, sibling))
        small_forward.wait_recv()
    src = small_out.at[:, :, :, core]
    pending.append(wires.copy(src, src, sibling))
    for op in pending:
        op.wait_recv()
    wires.drain()


GATHER_COPIES = 1 + 3 * (6 * 4 + 3) + 6 * 5 + 1


def gather_weights(mine, small):
    layers, rows, width = mine.shape
    whole = jax.ShapeDtypeStruct((RING, RING, RING, 2 * rows, width), jnp.bfloat16)
    hbm = pl.BlockSpec(memory_space=pltpu.HBM)
    vmem = pl.BlockSpec(memory_space=pltpu.VMEM)
    first, second, small_all = pl.pallas_call(
        gather_kernel,
        out_shape=(
            whole,
            whole,
            jax.ShapeDtypeStruct((RING, RING, RING, 2) + small.shape, jnp.bfloat16),
        ),
        in_specs=[vmem, vmem],
        out_specs=(hbm, hbm, hbm),
        scratch_shapes=[
            pltpu.VMEM((layers, rows, width // 2), jnp.float32),
            pltpu.VMEM((layers, 2 * rows, width // 2), jnp.bfloat16),
            pltpu.SemaphoreType.DMA((GATHER_COPIES,)),
            pltpu.SemaphoreType.DMA((GATHER_COPIES,)),
            pltpu.SemaphoreType.DMA((3,)),
        ],
        compiler_params=pltpu.CompilerParams(
            collective_id=0, has_side_effects=True, vmem_limit_bytes=58 * 2**20
        ),
        name="gather_weights",
    )(mine, small)
    count = RING**3 * 2 * rows
    return (
        (first.reshape(count, width), second.reshape(count, width)),
        small_all.reshape((2 * RING**3,) + small.shape),
    )


def reduce_kernel(
    first_ref,
    second_ref,
    small_ref,
    out_ref,
    small_out,
    acc,
    sib,
    wide_half_0,
    wide_half_1,
    wide_half_2,
    wide_full,
    mid_half,
    mid_full,
    thin_half,
    thin_full,
    small_acc,
    small_sib,
    small_wide,
    small_mid,
    small_thin,
    final,
    final_peer,
    send,
    recv,
    local,
):
    at, core = place()
    grads = (first_ref, second_ref)
    rows, half = acc.shape[4], acc.shape[5]
    own_rows = rows // 2
    part = rows // 3
    sibling = device_at(at, 1 - core)
    cols = pl.ds(pl.multiple_of(core * half, half), half)
    other = pl.ds(pl.multiple_of((1 - core) * half, half), half)
    chains = [(layer, p) for layer in range(2) for p in range(3)]
    loads = {}
    number = 0
    near = (2, 1, 3, 0)

    def span(p, step, c, piece=None):
        order = ORDERS[p]
        index = list(at)
        index[order[2 - step]] = c
        for axis in order[: 2 - step]:
            index[axis] = pl.ds(0, RING)
        first, count = p * part, part
        if piece is not None:
            if step == 2:
                first, count = (first, 32) if piece == 0 else (first + 32, part - 32)
            else:
                index[order[0]] = pl.ds(2 * piece, 2)
        return index, pl.ds(first, count)

    for by in near:
        for key in chains:
            layer, p = key
            c = lax.rem(at[ORDERS[p][2]] + by, RING)
            index, where = span(p, 0, c)
            op = pltpu.make_async_copy(
                grads[layer].at[index[0], index[1], index[2], where, cols],
                acc.at[layer, index[0], index[1], index[2], where],
                local.at[number],
            )
            op.start()
            loads[key, by] = op
            number += 1
    small_load = pltpu.make_async_copy(small_ref.at[:, :, :, core], small_acc, local.at[number])
    small_load.start()

    greet(neighbours(at, core))
    wires = Wires(send, recv)
    swaps = {}
    small_swap = wires.copy(small_ref.at[:, :, :, 1 - core], small_sib, sibling)
    for by in near:
        for key in chains:
            layer, p = key
            c = lax.rem(at[ORDERS[p][2]] + by, RING)
            index, where = span(p, 0, c)
            swaps[key, by] = wires.copy(
                grads[layer].at[index[0], index[1], index[2], where, other],
                sib.at[layer, index[0], index[1], index[2], where],
                sibling,
            )

    def right(axis):
        return device_at(moved(at, axis, 1), core)

    def left(axis):
        return device_at(moved(at, axis, RING - 1), core)

    def add(layer, p, step, c, piece, terms, into=None):
        order = ORDERS[p]
        free = [axis for axis in range(3) if axis in order[: 2 - step]]
        sizes = [2 if piece is not None and axis == order[0] else RING for axis in free]
        index, where = span(p, step, c, piece)
        total = 1
        for size in sizes:
            total *= size

        def body(n, unused):
            spot = list(index)
            inner = []
            if len(free) == 2:
                inner = [lax.div(n, sizes[1]), lax.rem(n, sizes[1])]
            elif len(free) == 1:
                inner = [n]
            for axis, size, i in zip(free, sizes, inner):
                start = 2 * piece if size == 2 else 0
                spot[axis] = start + i
            here = (layer, spot[0], spot[1], spot[2], where)
            value = acc[here].astype(jnp.float32)
            for term in terms:
                value = value + term(inner, spot, where).astype(jnp.float32)
            if into is None:
                acc[here] = value.astype(jnp.bfloat16)
            else:
                into(value)
            return unused

        if total == 1:
            body(0, 0)
        else:
            lax.fori_loop(0, total, body, 0)

    def add_sibling(key, by):
        layer, p = key
        loads[key, by].wait()
        swaps[key, by].wait_recv()
        c = lax.rem(at[ORDERS[p][2]] + by, RING)
        add(
            layer,
            p,
            0,
            c,
            None,
            [lambda inner, spot, where: sib[layer, spot[0], spot[1], spot[2], where]],
        )

    wide_half = (wide_half_0, wide_half_1, wide_half_2)

    def half_slot(layer, p, step, side):
        if step == 0:
            return wide_half[p].at[layer, side]
        if step == 1:
            return mid_half.at[layer, p, side]
        return thin_half.at[layer, p, side, pl.ds(0, 32 if side == 0 else part - 32)]

    def full_slot(layer, p, step, side):
        return (wide_full, mid_full, thin_full)[step].at[layer, p, side]

    def read(slot):
        return lambda inner, spot, where: slot[tuple(inner) + (slice(None), slice(None))]

    def acc_view(layer, p, step, c, piece=None):
        index, where = span(p, step, c, piece)
        return acc.at[layer, index[0], index[1], index[2], where]

    small_order = ORDERS[0]
    small_slots = (small_wide, small_mid, small_thin)

    def small_view(step, c):
        index = list(at)
        index[small_order[2 - step]] = c
        for axis in small_order[: 2 - step]:
            index[axis] = slice(None)
        return tuple(index)

    def small_add(step, c, term):
        where = small_view(step, c)
        small_acc[where] = small_acc[where] + term

    for step in range(3):
        halves = {}
        for key in chains:
            layer, p = key
            axis = ORDERS[p][2 - step]
            if step == 0:
                add_sibling(key, 2)
            across = lax.rem(at[axis] + 2, RING)
            halves[key] = (
                wires.copy(
                    acc_view(layer, p, step, across, 0), half_slot(layer, p, step, 0), right(axis)
                ),
                wires.copy(
                    acc_view(layer, p, step, across, 1), half_slot(layer, p, step, 1), left(axis)
                ),
            )
        if step == 0:
            small_load.wait()
            small_swap.wait_recv()
            small_acc[...] = small_acc[...] + small_sib[...]
        axis = small_order[2 - step]
        across = lax.rem(at[axis] + 2, RING)
        small_half = wires.copy(
            small_acc.at[small_view(step, across)], small_slots[step].at[0], right(axis)
        )
        if step == 0:
            for key in chains:
                add_sibling(key, 1)
                add_sibling(key, 3)
        fulls = {}
        for key in chains:
            layer, p = key
            axis = ORDERS[p][2 - step]
            after, before = lax.rem(at[axis] + 1, RING), lax.rem(at[axis] + 3, RING)
            halves[key][0].wait_recv()
            add(layer, p, step, after, 0, [read(half_slot(layer, p, step, 0))])
            one = wires.copy(
                acc_view(layer, p, step, after), full_slot(layer, p, step, 0), right(axis)
            )
            halves[key][1].wait_recv()
            add(layer, p, step, before, 1, [read(half_slot(layer, p, step, 1))])
            two = wires.copy(
                acc_view(layer, p, step, before), full_slot(layer, p, step, 1), left(axis)
            )
            fulls[key] = (one, two)
        axis = small_order[2 - step]
        after, before = lax.rem(at[axis] + 1, RING), lax.rem(at[axis] + 3, RING)
        small_half.wait_recv()
        small_add(step, after, small_slots[step][0])
        small_full = (
            wires.copy(small_acc.at[small_view(step, after)], small_slots[step].at[1], right(axis)),
            wires.copy(small_acc.at[small_view(step, before)], small_slots[step].at[2], left(axis)),
        )
        for key in chains:
            layer, p = key
            axis = ORDERS[p][2 - step]
            if step == 0:
                add_sibling(key, 0)
            fulls[key][0].wait_recv()
            fulls[key][1].wait_recv()
            terms = [read(full_slot(layer, p, step, side)) for side in range(2)]
            if step < 2:
                add(layer, p, step, at[axis], None, terms)
            else:

                def keep(value, layer=layer, p=p):
                    final[layer, p * part : (p + 1) * part] = value

                add(layer, p, step, at[axis], None, terms, keep)
        axis = small_order[2 - step]
        for op in small_full:
            op.wait_recv()
        small_add(step, at[axis], small_slots[step][1] + small_slots[step][2])

    theirs = pl.ds(pl.multiple_of((1 - core) * own_rows, own_rows), own_rows)
    swap = wires.copy(final.at[:, theirs], final_peer, sibling)
    small_out[...] = small_acc[at]
    swap.wait_recv()
    for layer in range(2):
        own = jnp.where(core == 0, final[layer, :own_rows], final[layer, own_rows:])
        got = final_peer[layer]
        out_ref[layer, :, :half] = jnp.where(core == 0, own, got)
        out_ref[layer, :, half:] = jnp.where(core == 0, got, own)
    wires.drain()


REDUCE_COPIES = 1 + 24 + 3 * (6 * 4 + 3) + 1


def reduce_weights(first, second, small):
    count, width = first.shape
    rows, half = count // RING**3, width // 2
    part = rows // 3
    torus = (RING, RING, RING)
    small_shape = small.shape[1:]
    hbm = pl.BlockSpec(memory_space=pltpu.HBM)
    vmem = pl.BlockSpec(memory_space=pltpu.VMEM)
    low = jnp.bfloat16

    def wide_shape(p):
        order = ORDERS[p]
        free = [axis for axis in range(3) if axis in order[:2]]
        return tuple(2 if axis == order[0] else RING for axis in free)

    return pl.pallas_call(
        reduce_kernel,
        out_shape=(
            jax.ShapeDtypeStruct((2, rows // 2, width), jnp.float32),
            jax.ShapeDtypeStruct(small_shape, jnp.float32),
        ),
        in_specs=[hbm, hbm, hbm],
        out_specs=(vmem, vmem),
        scratch_shapes=[
            pltpu.VMEM((2,) + torus + (rows, half), low),
            pltpu.VMEM((2,) + torus + (rows, half), low),
        ]
        + [pltpu.VMEM((2, 2) + wide_shape(p) + (part, half), low) for p in range(3)]
        + [
            pltpu.VMEM((2, 3, 2, RING, RING, part, half), low),
            pltpu.VMEM((2, 3, 2, 2, part, half), low),
            pltpu.VMEM((2, 3, 2, RING, part, half), low),
            pltpu.VMEM((2, 3, 2, 32, half), low),
            pltpu.VMEM((2, 3, 2, part, half), low),
            pltpu.VMEM(torus + small_shape, jnp.float32),
            pltpu.VMEM(torus + small_shape, jnp.float32),
            pltpu.VMEM((3, RING, RING) + small_shape, jnp.float32),
            pltpu.VMEM((3, RING) + small_shape, jnp.float32),
            pltpu.VMEM((3,) + small_shape, jnp.float32),
            pltpu.VMEM((2, rows, half), jnp.float32),
            pltpu.VMEM((2, rows // 2, half), jnp.float32),
            pltpu.SemaphoreType.DMA((REDUCE_COPIES,)),
            pltpu.SemaphoreType.DMA((REDUCE_COPIES,)),
            pltpu.SemaphoreType.DMA((25,)),
        ],
        compiler_params=pltpu.CompilerParams(
            collective_id=1, has_side_effects=True, vmem_limit_bytes=58 * 2**20
        ),
        cost_estimate=pl.CostEstimate(flops=0, bytes_accessed=280 * 10**6, transcendentals=0),
        name="reduce_weights",
    )(
        first.reshape(torus + (rows, width)),
        second.reshape(torus + (rows, width)),
        small.reshape(torus + (2,) + small_shape),
    )


def sum_kernel(in_ref, out_ref, slots, send, recv):
    at, core = place()
    sibling = device_at(at, 1 - core)
    partners = [sibling] + [
        device_at(moved(at, axis, by), core) for axis in range(3) for by in range(1, RING)
    ]
    greet(partners)
    wires = Wires(send, recv)
    slots[0, core] = in_ref[...]
    swap = wires.copy(in_ref, slots.at[0, core], sibling)
    swap.wait_recv()
    value = slots[0, 0] + slots[0, 1]
    for axis in range(3):
        slots[1 + axis, at[axis]] = value
        ops = []
        for by in range(1, RING):
            ops.append(
                wires.copy(
                    slots.at[1 + axis, at[axis]],
                    slots.at[1 + axis, at[axis]],
                    device_at(moved(at, axis, by), core),
                )
            )
        for op in ops:
            op.wait_recv()
        value = slots[1 + axis, 0]
        for c in range(1, RING):
            value = value + slots[1 + axis, c]
    out_ref[...] = value
    wires.drain()


def sum_all(value):
    vmem = pl.BlockSpec(memory_space=pltpu.VMEM)
    return pl.pallas_call(
        sum_kernel,
        out_shape=jax.ShapeDtypeStruct(value.shape, jnp.float32),
        in_specs=[vmem],
        out_specs=vmem,
        scratch_shapes=[
            pltpu.VMEM((4, RING) + value.shape, jnp.float32),
            pltpu.SemaphoreType.DMA((10,)),
            pltpu.SemaphoreType.DMA((10,)),
        ],
        compiler_params=pltpu.CompilerParams(collective_id=2, has_side_effects=True),
        name="sum_all",
    )(value)


TILE = 800


def head_kernel(
    f_ref,
    code_ref,
    weight_ref,
    table_ref,
    grad_out,
    dtable_ref,
    loss_ref,
    f_all,
    codes,
    table,
    logits,
    probs,
    tops,
    stats,
    df,
    df_send,
    df_sib,
    ring,
    ring_half,
    ring_full,
    staged,
    send,
    recv,
    load,
    store,
):
    at, core = place()
    x = at[2]
    dp, vocab = lax.axis_index("dp"), lax.axis_index("vocab")
    tok, width = f_ref.shape
    group = f_all.shape[0]
    members = group // tok
    tiles = table.shape[0] // TILE
    low, f32 = jnp.bfloat16, jnp.float32

    def tile_rows(t):
        return pl.ds(pl.multiple_of(t * TILE, TILE), TILE)

    loads = []
    for t in range(tiles):
        op = pltpu.make_async_copy(
            table_ref.at[pl.ds(t * TILE, TILE)], table.at[pl.ds(t * TILE, TILE)], load.at[t]
        )
        op.start()
        loads.append(op)

    peers = [(dp, lax.rem(vocab + by, members)) for by in range(1, members)]
    greet(peers)
    wires = Wires(send, recv)
    sibling = device_at(at, 1 - core)
    right, left = device_at(moved(at, 2, 1), core), device_at(moved(at, 2, 3), core)
    before, after, across = lax.rem(x + 3, RING), lax.rem(x + 1, RING), lax.rem(x + 2, RING)

    def rows_of(at_x, piece=None):
        first = (at_x * 2 + core) * tok
        if piece is None:
            return f_all.at[pl.ds(pl.multiple_of(first, tok), tok)]
        half = tok // 2
        return f_all.at[pl.ds(pl.multiple_of(first + piece * half, half), half)]

    f_all[pl.ds(pl.multiple_of(vocab * tok, tok), tok), :] = f_ref[...]
    own = rows_of(x)
    one, two = wires.copy(own, own, right), wires.copy(own, own, left)
    pending = [wires.copy(own, own, sibling)]
    codes[vocab] = code_ref[...]
    for peer in peers:
        pending.append(wires.copy(codes.at[vocab], codes.at[vocab], peer))
    one.wait_recv()
    one_on = wires.copy(rows_of(before, 0), rows_of(before, 0), right)
    pending.append(wires.copy(rows_of(before), rows_of(before), sibling))
    two.wait_recv()
    two_on = wires.copy(rows_of(after, 1), rows_of(after, 1), left)
    pending.append(wires.copy(rows_of(after), rows_of(after), sibling))
    one_on.wait_recv()
    pending.append(wires.copy(rows_of(across, 0), rows_of(across, 0), sibling))
    two_on.wait_recv()
    pending.append(wires.copy(rows_of(across, 1), rows_of(across, 1), sibling))
    for op in pending:
        op.wait_recv()

    code_row = jnp.concatenate([codes[m, 0:1, :] for m in range(members)], 1) - vocab * table.shape[0]
    code8 = jnp.broadcast_to(code_row, (8, group))
    code16 = jnp.broadcast_to(code_row, (16, group))
    rows8 = lax.broadcasted_iota(jnp.int32, (8, group), 0)
    rows16 = lax.broadcasted_iota(jnp.int32, (16, group), 0)
    slot = TILE // 2
    real = slot - 7
    steps8, steps16 = 5, 5

    def first_pass(t, carry):
        top, total, target = carry
        here = tile_rows(t)
        logits[...] = lax.dot_general(
            table[here, :], f_all[...], (((1,), (1,)), ((), ())), preferred_element_type=f32
        )
        for part in range(2):
            last = pl.ds((part + 1) * slot - 8, 8)
            logits[last, :] = jnp.where(rows8 < 1, logits[last, :], -1e30)

        def look(i, state):
            high, hit = state
            for u in range(steps8):
                first = (i * steps8 + u) * 8
                value = logits[pl.ds(pl.multiple_of(first, 8), 8), :]
                high = jnp.maximum(high, value)
                hit = hit + jnp.where(rows8 + (first + t * TILE) == code8, value, 0.0)
            return high, hit

        high, hit = lax.fori_loop(
            0,
            TILE // (8 * steps8),
            look,
            (jnp.full((8, group), -1e30, f32), jnp.zeros((8, group), f32)),
        )
        top_next = jnp.maximum(top, jnp.max(high, 0, keepdims=True))
        target = target + jnp.sum(hit, 0, keepdims=True)

        def lift(i, acc):
            for u in range(steps16):
                first = (i * steps16 + u) * 16
                value = jnp.exp(logits[pl.ds(pl.multiple_of(first, 16), 16), :] - top_next)
                acc = acc + value
                probs[pl.ds(pl.multiple_of(t * TILE + first, 16), 16), :] = value.astype(low)
            return acc

        acc = lax.fori_loop(
            0, TILE // (16 * steps16), lift, jnp.zeros((16, group), f32)
        )
        total = total * jnp.exp(top - top_next) + jnp.sum(acc, 0, keepdims=True)
        tops[t] = top_next
        return top_next, total, target

    for op in loads:
        op.wait()
    start = (jnp.full((1, group), -1e30, f32), jnp.zeros((1, group), f32), jnp.zeros((1, group), f32))
    found = lax.fori_loop(0, tiles, first_pass, start)
    for k in range(3):
        for m in range(members):
            stats[vocab, k, m : m + 1, :] = found[k][:, m * tok : (m + 1) * tok]
    pending = [wires.copy(stats.at[vocab], stats.at[vocab], peer) for peer in peers]
    for op in pending:
        op.wait_recv()
    peak = stats[0, 0]
    for m in range(1, members):
        peak = jnp.maximum(peak, stats[m, 0])
    total, target = jnp.zeros_like(peak), jnp.zeros_like(peak)
    for m in range(members):
        total = total + stats[m, 1] * jnp.exp(stats[m, 0] - peak)
        target = target + stats[m, 2]
    lse = peak + jnp.log(total)
    weight = weight_ref[...]
    mine = lax.broadcasted_iota(jnp.int32, (members, tok), 0) == vocab
    loss_ref[...] = jnp.where(mine, weight * (lse - target), 0.0)
    lse_row = jnp.concatenate([lse[m : m + 1, :] for m in range(members)], 1)
    weight_row = jnp.concatenate([weight[m : m + 1, :] for m in range(members)], 1)

    df[...] = jnp.zeros_like(df)

    def second_pass(t, unused):
        scale = weight_row * jnp.exp(tops[t] - lse_row)

        def turn(i, unused):
            for u in range(steps16):
                first = t * TILE + (i * steps16 + u) * 16
                here = pl.ds(pl.multiple_of(first, 16), 16)
                value = probs[here, :].astype(f32) * scale
                value = value - jnp.where(rows16 + first == code16, weight_row, 0.0)
                probs[here, :] = value.astype(low)
            return unused

        lax.fori_loop(0, TILE // (16 * steps16), turn, 0)
        here = tile_rows(t)
        df[...] += lax.dot_general(
            probs[here, :], table[here, :], (((0,), (0,)), ((), ())), preferred_element_type=f32
        )
        return unused

    lax.fori_loop(0, tiles, second_pass, 0)

    def third_pass(t):
        if t >= 2:
            stores[t - 2].wait()
        staged[t % 2] = jnp.dot(
            probs[t * TILE : (t + 1) * TILE, :], f_all[...], preferred_element_type=f32
        ).astype(low)
        op = pltpu.make_async_copy(
            staged.at[t % 2], dtable_ref.at[pl.ds(t * TILE, TILE)], store.at[t]
        )
        op.start()
        stores.append(op)

    stores = []
    for m in range(members):
        df_send[m % 2, m // 2] = df[m * tok : (m + 1) * tok, :].astype(low)
    swap = wires.copy(df_send.at[1 - core], df_sib, sibling)
    third_pass(0)
    third_pass(1)
    swap.wait_recv()
    for k in range(RING):
        first = pl.multiple_of((2 * k + core) * tok, tok)
        ring[k] = (df[pl.ds(first, tok), :] + df_sib[k].astype(f32)).astype(low)
    half = tok // 2
    one = wires.copy(ring.at[across, pl.ds(0, half)], ring_half.at[0], right)
    two = wires.copy(ring.at[across, pl.ds(half, half)], ring_half.at[1], left)
    third_pass(2)
    third_pass(3)
    one.wait_recv()
    ring[after, :half] = (ring[after, :half].astype(f32) + ring_half[0].astype(f32)).astype(low)
    one = wires.copy(ring.at[after], ring_full.at[0], right)
    two.wait_recv()
    ring[before, half:] = (ring[before, half:].astype(f32) + ring_half[1].astype(f32)).astype(low)
    two = wires.copy(ring.at[before], ring_full.at[1], left)
    for t in range(4, tiles):
        third_pass(t)
    one.wait_recv()
    two.wait_recv()
    grad_out[...] = ring[x].astype(f32) + ring_full[0].astype(f32) + ring_full[1].astype(f32)
    for op in stores[-2:]:
        op.wait()
    wires.drain()


HEAD_COPIES = 9 + 7 + 7 + 5


def head(final_low, codes, weights, table):
    tok, width = final_low.shape
    rows = table.shape[0]
    members = weights.shape[0]
    group = members * tok
    tiles = rows // TILE
    hbm = pl.BlockSpec(memory_space=pltpu.HBM)
    vmem = pl.BlockSpec(memory_space=pltpu.VMEM)
    low, f32 = jnp.bfloat16, jnp.float32
    return pl.pallas_call(
        head_kernel,
        out_shape=(
            jax.ShapeDtypeStruct((tok, width), f32),
            jax.ShapeDtypeStruct((rows, width), low),
            jax.ShapeDtypeStruct((members, tok), f32),
        ),
        in_specs=[vmem, vmem, vmem, hbm],
        out_specs=(vmem, hbm, vmem),
        scratch_shapes=[
            pltpu.VMEM((group, width), low),
            pltpu.VMEM((members, 8, tok), jnp.int32),
            pltpu.VMEM((rows, width), low),
            pltpu.VMEM((TILE, group), f32),
            pltpu.VMEM((rows, group), low),
            pltpu.VMEM((tiles, 1, group), f32),
            pltpu.VMEM((members, 3, members, tok), f32),
            pltpu.VMEM((group, width), f32),
            pltpu.VMEM((2, RING, tok, width), low),
            pltpu.VMEM((RING, tok, width), low),
            pltpu.VMEM((RING, tok, width), low),
            pltpu.VMEM((2, tok // 2, width), low),
            pltpu.VMEM((2, tok, width), low),
            pltpu.VMEM((2, TILE, width), low),
            pltpu.SemaphoreType.DMA((HEAD_COPIES,)),
            pltpu.SemaphoreType.DMA((HEAD_COPIES,)),
            pltpu.SemaphoreType.DMA((tiles,)),
            pltpu.SemaphoreType.DMA((tiles,)),
        ],
        compiler_params=pltpu.CompilerParams(
            collective_id=3, has_side_effects=True, vmem_limit_bytes=58 * 2**20
        ),
        cost_estimate=pl.CostEstimate(
            flops=6 * group * rows * width, bytes_accessed=4 * rows * width, transcendentals=group * rows
        ),
        name="head",
    )(final_low, codes, weights, table)


def grads_kernel(dqkv_ref, dmid_ref, dup_ref, act_ref, a_ref, o_ref, m_ref, dz_ref, out_ref):
    step = pl.program_id(0)

    def put(left, right):
        out_ref[...] = lax.dot_general(
            left[...], right[...], (((0,), (0,)), ((), ())), preferred_element_type=jnp.float32
        ).astype(out_ref.dtype)

    pl.when(step < 3)(lambda: put(dqkv_ref, a_ref))
    pl.when(step == 3)(lambda: put(dmid_ref, o_ref))
    pl.when((step >= 4) & (step < 8))(lambda: put(dup_ref, m_ref))
    pl.when(step >= 8)(lambda: put(act_ref, dz_ref))


def weight_grads(dqkv, dmid, dup, act, a, o, m, dz):
    tok, width = a.shape

    def piece(first, count):
        return pl.BlockSpec((tok, width), lambda i: (0, jnp.clip(i - first, 0, count - 1)))

    whole = pl.BlockSpec((tok, width), lambda i: (0, 0))
    steps = 12
    return pl.pallas_call(
        grads_kernel,
        grid=(steps,),
        out_shape=jax.ShapeDtypeStruct((steps * width, width), jnp.bfloat16),
        in_specs=[piece(0, 3), piece(3, 1), piece(4, 4), piece(8, 4)] + [whole] * 4,
        out_specs=pl.BlockSpec((width, width), lambda i: (i, 0)),
        cost_estimate=pl.CostEstimate(
            flops=2 * tok * steps * width * width,
            bytes_accessed=2 * steps * width * width,
            transcendentals=0,
        ),
        name="weight_grads",
    )(dqkv, dmid, dup, act, a, o, m, dz)


def layer_norm(inputs, gain, shift):
    centered = inputs - jnp.mean(inputs, -1, keepdims=True)
    spread = jnp.mean(centered * centered, -1, keepdims=True)
    return centered * lax.rsqrt(spread + norm_eps) * gain + shift


def gelu_tanh(inputs):
    return jax.nn.gelu(inputs, approximate=True)


def doc_info(doc_lens, tok_count, total_docs):
    doc_ends = jnp.cumsum(doc_lens)
    places = jnp.arange(tok_count, dtype=jnp.int32)
    seg_ids = jnp.sum((places[:, None] >= doc_ends[None, :]).astype(jnp.int32), 1)
    one_hot = seg_ids[:, None] == jnp.arange(doc_lens.shape[0], dtype=jnp.int32)[None, :]
    starts = doc_ends - doc_lens
    pos_ids = places - jnp.sum(jnp.where(one_hot, starts[None, :], 0), 1)
    doc_len = jnp.sum(jnp.where(one_hot, doc_lens[None, :], 0), 1)
    weights = 1.0 / (doc_len.astype(jnp.float32) * total_docs)
    return (seg_ids, pos_ids, weights)


def device_rise(first, count, devices):
    places = first + jnp.arange(count, dtype=jnp.int32)
    return 1.0 + 2.0 * places.astype(jnp.float32) / (devices - 1)


def contract(left, right, left_dim, right_dim):
    return lax.dot_general(
        left, right, (((left_dim,), (right_dim,)), ((), ())), preferred_element_type=jnp.float32
    )


def split_vecs(vecs, width):
    pieces = [vecs[index * width : (index + 1) * width] for index in range(7)]
    ff_width = vecs.shape[0] - 8 * width
    pieces.append(vecs[7 * width : 7 * width + ff_width])
    pieces.append(vecs[7 * width + ff_width :])
    return pieces


def split_mats(mats, width):
    ff_width = (mats.shape[0] - 4 * width) // 2
    cuts = [0, 3 * width, 4 * width, 4 * width + ff_width, 4 * width + 2 * ff_width]
    return [mats[a:b] for a, b in zip(cuts[:-1], cuts[1:])]


def layer_forward(hidden, mats, vecs, attn_mask):
    tok, width = hidden.shape
    head_dim = width // H
    w_qkv, w_proj, w_fc, w_out = split_mats(mats, width)
    gain_one, shift_one, bias_q, bias_v, bias_proj, gain_two, shift_two, bias_fc, bias_out = (
        split_vecs(vecs, width)
    )
    normed_low = layer_norm(hidden, gain_one, shift_one).astype(jnp.bfloat16)
    bias_qkv = jnp.concatenate([bias_q, jnp.zeros_like(bias_q), bias_v])
    qkv_f = contract(normed_low, w_qkv, 1, 1) + bias_qkv
    qkv_low = qkv_f.astype(jnp.bfloat16).reshape(tok, 3, H, head_dim)
    scores = jnp.einsum(
        "thd,uhd->htu", qkv_low[:, 0], qkv_low[:, 1], preferred_element_type=jnp.float32
    ) * head_dim ** (-0.5)
    scores = jnp.where(attn_mask[None], scores, -1000000000.0)
    shifted = jnp.exp(scores - jnp.max(scores, -1, keepdims=True))
    attn_probs = shifted / jnp.sum(shifted, -1, keepdims=True)
    probs_low = attn_probs.astype(jnp.bfloat16)
    attended = jnp.einsum(
        "htu,uhd->thd", probs_low, qkv_low[:, 2], preferred_element_type=jnp.float32
    )
    attended = attended.reshape(tok, width).astype(jnp.bfloat16)
    middle = hidden + contract(attended, w_proj, 1, 1) + bias_proj
    two_low = layer_norm(middle, gain_two, shift_two).astype(jnp.bfloat16)
    up_act = contract(two_low, w_fc, 1, 1) + bias_fc
    activ_low = gelu_tanh(up_act).astype(jnp.bfloat16)
    output = middle + contract(activ_low, w_out, 1, 0) + bias_out
    saved = (
        hidden,
        normed_low,
        qkv_low,
        attn_probs,
        probs_low,
        attended,
        middle,
        two_low,
        up_act,
        activ_low,
    )
    return (output, saved)


def layer_backward(saved, mats, vecs, grad_out):
    hidden, normed_low, qkv_low, attn_probs, probs_low, attended, middle, two_low, up_act, activ_low = saved
    tok, width = hidden.shape
    head_dim = width // H
    w_qkv, w_proj, w_fc, w_out = split_mats(mats, width)
    gain_one, shift_one, bias_q, bias_v, bias_proj, gain_two, shift_two, bias_fc, bias_out = (
        split_vecs(vecs, width)
    )
    low = jnp.bfloat16
    out_low = grad_out.astype(low)
    grad_bout = jnp.sum(grad_out, 0)
    grad_act = contract(out_low, w_out, 1, 1)
    unused_up, gelu_pull = jax.vjp(gelu_tanh, up_act)
    grad_up = gelu_pull(grad_act)[0]
    up_low = grad_up.astype(low)
    grad_bfc = jnp.sum(grad_up, 0)
    grad_two = contract(up_low, w_fc, 1, 0)
    unused_two, norm_pull = jax.vjp(layer_norm, middle, gain_two, shift_two)
    grad_mid_norm, grad_g2, grad_s2 = norm_pull(grad_two)
    grad_mid = grad_out + grad_mid_norm
    mid_low = grad_mid.astype(low)
    grad_bproj = jnp.sum(grad_mid, 0)
    grad_att = contract(mid_low, w_proj, 1, 0).astype(low).reshape(tok, H, head_dim)
    grad_probs = jnp.einsum(
        "thd,uhd->htu", grad_att, qkv_low[:, 2], preferred_element_type=jnp.float32
    )
    grad_vals = jnp.einsum("htu,thd->uhd", probs_low, grad_att, preferred_element_type=jnp.float32)
    grad_scores = attn_probs * (grad_probs - jnp.sum(attn_probs * grad_probs, -1, keepdims=True))
    score_low = (grad_scores * head_dim ** (-0.5)).astype(low)
    grad_q = jnp.einsum(
        "htu,uhd->thd", score_low, qkv_low[:, 1], preferred_element_type=jnp.float32
    )
    grad_k = jnp.einsum(
        "htu,thd->uhd", score_low, qkv_low[:, 0], preferred_element_type=jnp.float32
    )
    grad_qkv = jnp.stack([grad_q, grad_k, grad_vals], 1).reshape(tok, 3 * width)
    qkv_grad_low = grad_qkv.astype(low)
    grad_normed = contract(qkv_grad_low, w_qkv, 1, 0)
    unused_one, first_pull = jax.vjp(layer_norm, hidden, gain_one, shift_one)
    grad_in_norm, grad_g1, grad_s1 = first_pull(grad_normed)
    grad_in = grad_mid + grad_in_norm
    grad_mats = weight_grads(
        qkv_grad_low, mid_low, up_low, activ_low, normed_low, attended, two_low, out_low
    )
    grad_vecs = jnp.concatenate(
        [
            grad_g1,
            grad_s1,
            jnp.sum(grad_q, 0).reshape(width),
            jnp.sum(grad_vals, 0).reshape(width),
            grad_bproj,
            grad_g2,
            grad_s2,
            grad_bfc,
            grad_bout,
        ]
    )
    return (grad_in, grad_mats, grad_vecs)


def renew(weight, moment, average, grad, factor):
    clipped = factor * grad
    moment_next = momentum_coef * moment + clipped
    weight_next = weight - learn_rate * (clipped + momentum_coef * moment_next)
    average_next = ema_decay * average + (1.0 - ema_decay) * weight_next
    return (moment_next, weight_next, average_next, weight_next.astype(jnp.bfloat16))


SMALL_ROWS, LANES = 16, 128


def pack_small(values):
    room = SMALL_ROWS * LANES - values.shape[-1]
    pads = [(0, 0)] * (values.ndim - 1) + [(0, room)]
    return jnp.pad(values, pads).reshape(values.shape[:-1] + (SMALL_ROWS, LANES))


def per_device(
    token_ids,
    targets,
    lengths,
    embed_table,
    embed_moment,
    embed_average,
    blocks,
    block_moment,
    block_average,
    pos_table,
    pos_moment,
    pos_average,
    vectors,
    vector_moment,
    vector_average,
):
    devices = lax.axis_size(("dp", "vocab"))
    vocab_count = lax.axis_size("vocab")
    dp_count = lax.axis_size("dp")
    vocab_at = lax.axis_index("vocab")
    data_at = lax.axis_index("dp")
    tok = token_ids.shape[0]
    own_rows, width = embed_table.shape
    layers = blocks.shape[0]
    capacity = max(2, 2 * tok // devices)
    low = jnp.bfloat16
    blocks, block_moment, block_average = (
        jnp.transpose(item, (0, 2, 1)) for item in (blocks, block_moment, block_average)
    )
    pos_rows, pos_cols = pos_table.shape
    vec_own = vectors.shape[0]
    table_low = embed_table.astype(low)
    pad_rows = -own_rows % 16
    table_padded = jnp.pad(table_low, ((0, pad_rows), (0, 0)))
    slot_rows = own_rows + pad_rows

    owners = token_ids // own_rows
    tokens = jnp.arange(tok, dtype=jnp.int32)
    earlier = jnp.sum((owners[:, None] == owners[None, :]) & (tokens[None, :] < tokens[:, None]), 1)
    slot_hot = (owners * capacity + earlier)[:, None] == jnp.arange(
        devices * capacity, dtype=jnp.int32
    )[None, :]
    send_rows = jnp.sum(jnp.where(slot_hot, (token_ids % own_rows)[:, None], 0), 0)
    slot_hot = slot_hot.astype(low)
    local_rows = lax.all_to_all(send_rows, ("dp", "vocab"), split_axis=0, concat_axis=0, tiled=True)
    asked = (local_rows[:, None] == jnp.arange(own_rows, dtype=jnp.int32)[None, :]).astype(low)
    fetched = jnp.dot(asked, table_low, preferred_element_type=jnp.float32).astype(low)
    blocks, fetched = lax.optimization_barrier((blocks, fetched))
    returned_rows = lax.all_to_all(
        fetched.reshape(devices, capacity, width),
        ("dp", "vocab"),
        split_axis=0,
        concat_axis=0,
        tiled=True,
    ).reshape(devices * capacity, width)
    table_slice = lax.all_gather(table_padded, "dp", axis=0, tiled=True)
    target_owners = targets // own_rows
    codes = (
        (target_owners % vocab_count) * (dp_count * slot_rows)
        + (target_owners // vocab_count) * slot_rows
        + targets % own_rows
    )

    small = pack_small(
        jnp.concatenate([jnp.transpose(pos_table).reshape(-1), vectors]).astype(low)
    )
    mats_all, small_all = gather_weights(blocks, small)
    small_all = small_all.reshape(devices, -1)
    pos_low_t = small_all[:, : pos_rows * pos_cols].reshape(width, pos_rows)
    vecs_all = (
        small_all[:, pos_rows * pos_cols : pos_rows * pos_cols + vec_own]
        .reshape(-1)
        .astype(jnp.float32)
    )
    vec_width = (vecs_all.shape[0] - 2 * width) // layers

    lens_group = lengths[0]
    seg_group, pos_group, weight_group = jax.vmap(
        partial(doc_info, tok_count=tok, total_docs=devices * lens_group.shape[1])
    )(lens_group)
    weight_group = weight_group * device_rise(data_at * vocab_count, vocab_count, devices)[:, None]
    seg_ids = lax.dynamic_index_in_dim(seg_group, vocab_at, 0, keepdims=False)
    pos_ids = lax.dynamic_index_in_dim(pos_group, vocab_at, 0, keepdims=False)
    places = jnp.arange(tok, dtype=jnp.int32)
    attn_mask = (seg_ids[:, None] == seg_ids[None, :]) & (places[None, :] <= places[:, None])

    gotten = jnp.dot(slot_hot, returned_rows, preferred_element_type=jnp.float32)
    pos_hot = (pos_ids[:, None] == jnp.arange(pos_rows, dtype=jnp.int32)[None, :]).astype(low)
    hidden = gotten + contract(pos_hot, pos_low_t, 1, 1)
    kept = []
    for layer in range(layers):
        hidden, saved = layer_forward(
            hidden,
            mats_all[layer],
            vecs_all[layer * vec_width : (layer + 1) * vec_width],
            attn_mask,
        )
        kept.append(saved)
    tail = vecs_all[layers * vec_width :]
    final_low = layer_norm(hidden, tail[:width], tail[width:]).astype(low)
    grad_final, table_part, token_losses = head(
        final_low, jnp.broadcast_to(codes[None, :], (8, tok)), weight_group, table_slice
    )
    loss_part = jnp.sum(token_losses)
    table_grad = lax.psum_scatter(table_part, "dp", scatter_dimension=0, tiled=True)[
        :own_rows
    ].astype(jnp.float32)
    unused_final, final_pull = jax.vjp(layer_norm, hidden, tail[:width], tail[width:])
    grad_hidden, grad_gf, grad_sf = final_pull(grad_final)
    mats_parts = [None] * layers
    vec_parts = [None] * layers
    for layer in reversed(range(layers)):
        grad_hidden, mats_parts[layer], vec_parts[layer] = layer_backward(
            kept[layer],
            mats_all[layer],
            vecs_all[layer * vec_width : (layer + 1) * vec_width],
            grad_hidden,
        )
    grad_vec_all = jnp.concatenate(vec_parts + [grad_gf, grad_sf])
    grad_pos = lax.dot_general(
        grad_hidden,
        pos_hot.astype(jnp.float32),
        (((0,), (0,)), ((), ())),
        precision=lax.Precision.HIGHEST,
    )
    send_grads = contract(slot_hot, grad_hidden.astype(low), 0, 0).astype(low)
    mats_parts[0], send_grads = lax.optimization_barrier((mats_parts[0], send_grads))
    back_grads = lax.all_to_all(
        send_grads.reshape(devices, capacity, width),
        ("dp", "vocab"),
        split_axis=0,
        concat_axis=0,
        tiled=True,
    ).reshape(-1, width)
    small_grads = pack_small(
        jnp.concatenate(
            [grad_pos.reshape(devices, -1), grad_vec_all.reshape(devices, -1)], 1
        )
    )
    mats_shard, small_shard = reduce_weights(mats_parts[0], mats_parts[1], small_grads)
    small_shard = small_shard.reshape(-1)
    pos_shard = small_shard[: pos_rows * pos_cols].reshape(pos_cols, pos_rows)
    vec_shard = small_shard[pos_rows * pos_cols : pos_rows * pos_cols + vec_own]
    table_grad = table_grad + contract(asked, back_grads, 0, 0)
    local_squares = (
        jnp.sum(table_grad * table_grad)
        + jnp.sum(mats_shard * mats_shard)
        + jnp.sum(pos_shard * pos_shard)
        + jnp.sum(vec_shard * vec_shard)
    )
    both_sums = sum_all(
        jnp.broadcast_to(jnp.pad(jnp.stack([loss_part, local_squares]), (0, 6))[:, None], (8, LANES))
    )
    loss_sum, squares = both_sums[0, 0], both_sums[1, 0]
    grad_norm = jnp.sqrt(squares)
    factor = clip_bound / jnp.maximum(grad_norm, clip_bound)
    embed_out = renew(embed_table, embed_moment, embed_average, table_grad, factor)
    block_out = renew(blocks, block_moment, block_average, mats_shard, factor)
    block_out = tuple(jnp.transpose(item, (0, 2, 1)) for item in block_out)
    pos_out = renew(
        jnp.transpose(pos_table),
        jnp.transpose(pos_moment),
        jnp.transpose(pos_average),
        pos_shard,
        factor,
    )
    pos_out = tuple(jnp.transpose(item) for item in pos_out)
    vector_out = renew(vectors, vector_moment, vector_average, vec_shard, factor)
    return (loss_sum, grad_norm) + embed_out + block_out + pos_out + vector_out


def solution(mesh):
    table = P(("dp", "vocab"), None)
    cols = P(None, None, ("dp", "vocab"))
    pos = P(None, ("dp", "vocab"))
    vec = P(("dp", "vocab"))
    return jax.shard_map(
        per_device,
        mesh=mesh,
        in_specs=(vec, vec, P("dp", None, None))
        + (table,) * 3
        + (cols,) * 3
        + (pos,) * 3
        + (vec,) * 3,
        out_specs=(P(), P()) + (table,) * 4 + (cols,) * 4 + (pos,) * 4 + (vec,) * 4,
        check_vma=False,
    )
```

```python
from functools import partial

import jax
import jax.numpy as jnp
from jax import lax
from jax.experimental import pallas as pl
from jax.experimental.pallas import tpu as pltpu
from jax.sharding import PartitionSpec as P

H = 12
RING = 4
ORDERS = ((2, 1, 0), (1, 0, 2), (0, 2, 1))

norm_eps = 1e-05
clip_bound = 0.01
learn_rate = 10000.0
momentum_coef = 0.5
ema_decay = 0.5


def place():
    dp = lax.axis_index("dp")
    vocab = lax.axis_index("vocab")
    return (lax.div(dp, RING), lax.rem(dp, RING), lax.div(vocab, 2)), lax.rem(vocab, 2)


def device_at(at, core):
    return (at[0] * RING + at[1], at[2] * 2 + core)


def moved(at, axis, by):
    out = list(at)
    out[axis] = lax.rem(at[axis] + by, RING)
    return tuple(out)


class Wires:
    def __init__(self, send, recv):
        self.send, self.recv, self.count, self.live = send, recv, 0, []

    def copy(self, src, dst, device):
        number = self.count
        self.count += 1
        op = pltpu.make_async_remote_copy(
            src_ref=src,
            dst_ref=dst,
            send_sem=self.send.at[number],
            recv_sem=self.recv.at[number],
            device_id=device,
            device_id_type=pl.DeviceIdType.MESH,
        )
        op.start()
        self.live.append(op)
        return op

    def drain(self):
        for op in self.live:
            op.wait_send()


def greet(devices):
    barrier = pltpu.get_barrier_semaphore()
    for device in devices:
        pl.semaphore_signal(
            barrier, inc=1, device_id=device, device_id_type=pl.DeviceIdType.MESH
        )
    pl.semaphore_wait(barrier, len(devices))


def neighbours(at, core):
    near = [device_at(moved(at, axis, by), core) for axis in range(3) for by in (1, RING - 1)]
    return near + [device_at(at, 1 - core)]


def gather_kernel(
    mine_ref, small_ref, out_ref, small_out, peer, block, send, recv, local
):
    at, core = place()
    rows, half = mine_ref.shape[1], mine_ref.shape[2] // 2
    part = 2 * rows // 3
    sibling = device_at(at, 1 - core)
    greet(neighbours(at, core))
    wires = Wires(send, recv)
    cols = pl.ds(pl.multiple_of(core * half, half), half)
    other = pl.ds(pl.multiple_of((1 - core) * half, half), half)

    swap = wires.copy(mine_ref.at[:, :, other], peer, sibling)
    small_local = pltpu.make_async_copy(small_ref, small_out.at[at[0], at[1], at[2], core], local.at[0])
    small_local.start()
    swap.wait_recv()
    for layer in range(2):
        own = jnp.where(core == 0, mine_ref[layer, :, :half], mine_ref[layer, :, half:])
        got = peer[layer]
        both = jnp.concatenate(
            [jnp.where(core == 0, own, got), jnp.where(core == 0, got, own)], 0
        )
        block[layer] = both.astype(jnp.bfloat16)
    block_local = []
    for layer in range(2):
        op = pltpu.make_async_copy(
            block.at[layer],
            out_ref.at[layer, at[0], at[1], at[2], :, cols],
            local.at[1 + layer],
        )
        op.start()
        block_local.append(op)

    def bundle(layer, p, phase, c, piece=None):
        order = ORDERS[p]
        index = list(at)
        index[order[phase]] = c
        for axis in order[:phase]:
            index[axis] = pl.ds(0, RING)
        first, count = p * part, part
        if piece is not None:
            if phase == 0:
                first, count = (first, 32) if piece == 0 else (first + 32, part - 32)
            else:
                index[order[0]] = pl.ds(2 * piece, 2)
        return out_ref.at[layer, index[0], index[1], index[2], pl.ds(first, count), cols]

    def small_bundle(phase, c):
        order = ORDERS[0]
        index = list(at)
        index[order[phase]] = c
        for axis in order[:phase]:
            index[axis] = pl.ds(0, RING)
        return small_out.at[index[0], index[1], index[2], core]

    def right(axis):
        return device_at(moved(at, axis, 1), core)

    def left(axis):
        return device_at(moved(at, axis, RING - 1), core)

    chains = [(layer, p) for layer in range(2) for p in range(3)]
    pending = []
    small_local.wait()
    for op in block_local:
        op.wait()
    for phase in range(3):
        steps = {}
        for key in chains:
            layer, p = key
            axis = ORDERS[p][phase]
            src = bundle(layer, p, phase, at[axis])
            if phase == 2:
                pending.append(wires.copy(src, src, sibling))
            steps[key] = (wires.copy(src, src, right(axis)), wires.copy(src, src, left(axis)))
        axis = ORDERS[0][phase]
        src = small_bundle(phase, at[axis])
        small_steps = (wires.copy(src, src, right(axis)), wires.copy(src, src, left(axis)))
        forwards = {}
        for key in chains:
            layer, p = key
            axis = ORDERS[p][phase]
            before, after = lax.rem(at[axis] + 3, RING), lax.rem(at[axis] + 1, RING)
            steps[key][0].wait_recv()
            src = bundle(layer, p, phase, before, 0)
            one = wires.copy(src, src, right(axis))
            steps[key][1].wait_recv()
            src = bundle(layer, p, phase, after, 1)
            two = wires.copy(src, src, left(axis))
            forwards[key] = (one, two)
            if phase == 2:
                for c in (before, after):
                    src = bundle(layer, p, phase, c)
                    pending.append(wires.copy(src, src, sibling))
        axis = ORDERS[0][phase]
        for op in small_steps:
            op.wait_recv()
        src = small_bundle(phase, lax.rem(at[axis] + 3, RING))
        small_forward = wires.copy(src, src, right(axis))
        for key in chains:
            layer, p = key
            axis = ORDERS[p][phase]
            across = lax.rem(at[axis] + 2, RING)
            for piece in range(2):
                forwards[key][piece].wait_recv()
                if phase == 2:
                    src = bundle(layer, p, phase, across, piece)
                    pending.append(wires.copy(src, src, sibling))
        small_forward.wait_recv()
    src = small_out.at[:, :, :, core]
    pending.append(wires.copy(src, src, sibling))
    for op in pending:
        op.wait_recv()
    wires.drain()


GATHER_COPIES = 1 + 3 * (6 * 4 + 3) + 6 * 5 + 1


def gather_weights(mine, small):
    layers, rows, width = mine.shape
    whole = jax.ShapeDtypeStruct((layers, RING, RING, RING, 2 * rows, width), jnp.bfloat16)
    hbm = pl.BlockSpec(memory_space=pltpu.HBM)
    vmem = pl.BlockSpec(memory_space=pltpu.VMEM)
    mats, small_all = pl.pallas_call(
        gather_kernel,
        out_shape=(
            whole,
            jax.ShapeDtypeStruct((RING, RING, RING, 2) + small.shape, jnp.bfloat16),
        ),
        in_specs=[vmem, vmem],
        out_specs=(hbm, hbm),
        scratch_shapes=[
            pltpu.VMEM((layers, rows, width // 2), jnp.float32),
            pltpu.VMEM((layers, 2 * rows, width // 2), jnp.bfloat16),
            pltpu.SemaphoreType.DMA((GATHER_COPIES,)),
            pltpu.SemaphoreType.DMA((GATHER_COPIES,)),
            pltpu.SemaphoreType.DMA((3,)),
        ],
        compiler_params=pltpu.CompilerParams(
            collective_id=0, has_side_effects=True, vmem_limit_bytes=58 * 2**20
        ),
        cost_estimate=pl.CostEstimate(flops=0, bytes_accessed=250 * 10**6, transcendentals=0),
        name="gather_weights",
    )(mine, small)
    return (
        mats.reshape(layers * RING**3 * 2 * rows, width),
        small_all.reshape((2 * RING**3,) + small.shape),
    )


class Reduction:
    def __init__(self, at, core, send, recv):
        self.at, self.core, self.send, self.recv = at, core, send, recv
        self.number, self.level, self.halves, self.fulls = {}, {}, {}, {}
        self.final = None

    def copy(self, key, src, dst, device):
        number = self.number.setdefault(key, len(self.number))
        return pltpu.make_async_remote_copy(
            src_ref=src,
            dst_ref=dst,
            send_sem=self.send.at[number],
            recv_sem=self.recv.at[number],
            device_id=device,
            device_id_type=pl.DeviceIdType.MESH,
        )

    def axes(self, p):
        order = ORDERS[p]
        free = sorted(order[:2])
        return free, free.index(order[1])

    def ring(self, p, step):
        axis = ORDERS[p][2 - step]
        c = self.at[axis]
        right = device_at(moved(self.at, axis, 1), self.core)
        left = device_at(moved(self.at, axis, RING - 1), self.core)
        return c, lax.rem(c + 1, RING), lax.rem(c + 2, RING), lax.rem(c + 3, RING), right, left

    def index(self, layer, p, step, c, piece=None):
        part = 48
        cut, whole = (0, RING) if piece is None else (2 * piece, 2), (0, RING)
        if step == 0:
            free, unused = self.axes(p)
            spot = [c, c, c]
            spot[free[0]], spot[free[1]] = cut, whole
            return spot + [pl.ds(p * part, part)]
        if step == 1:
            unused, first = self.axes(p)
            spot = [cut, cut]
            spot[first] = c
            return [layer % self.level[1].shape[0], p] + spot
        if piece is None:
            return [layer, p, c]
        return [layer, p, c, pl.ds(0, 32) if piece == 0 else pl.ds(32, part - 32)]

    def view(self, layer, p, step, c, piece=None):
        index = self.index(layer, p, step, c, piece)
        held = self.level[0, layer] if step == 0 else self.level[step]
        return held.at[tuple(pl.ds(*item) if isinstance(item, tuple) else item for item in index)]

    def slot(self, layer, p, step, side, whole):
        store = (self.fulls if whole else self.halves)[step]
        if step == 2 and not whole:
            return store.at[layer, p, side, pl.ds(0, 32 if side == 0 else 16)]
        return store.at[layer % store.shape[0], p, side]

    def half_copies(self, layer, p, step):
        unused, after, across, before, right, left = self.ring(p, step)
        out = []
        for side, device in ((0, right), (1, left)):
            out.append(
                self.copy(
                    (layer, p, step, side),
                    self.view(layer, p, step, across, side),
                    self.slot(layer, p, step, side, False),
                    device,
                )
            )
        return out

    def full_copies(self, layer, p, step):
        unused, after, across, before, right, left = self.ring(p, step)
        out = []
        for side, c, device in ((0, after, right), (1, before, left)):
            out.append(
                self.copy(
                    (layer, p, step, 2 + side),
                    self.view(layer, p, step, c),
                    self.slot(layer, p, step, side, True),
                    device,
                )
            )
        return out

    def add(self, layer, p, step, c, piece, terms, into):
        held = self.level[0, layer] if step == 0 else self.level[step]
        index = self.index(layer, p, step, c, piece)
        sizes = [item[1] for item in index if isinstance(item, tuple)]
        total = 1
        for size in sizes:
            total *= size

        def body(n, unused):
            inner = [lax.div(n, sizes[1]), lax.rem(n, sizes[1])] if len(sizes) == 2 else [n] * len(sizes)
            places = iter(inner)
            spot = tuple(
                item[0] + next(places) if isinstance(item, tuple) else item for item in index
            )
            value = held[spot].astype(jnp.float32)
            for term in terms:
                value = value + term[tuple(inner) + (slice(None), slice(None))].astype(jnp.float32)
            into(held, spot, inner, value)
            return unused

        if total == 1:
            body(0, 0)
        else:
            lax.fori_loop(0, total, body, 0)

    def start(self, layer, step):
        for p in range(3):
            for op in self.half_copies(layer, p, step):
                op.start()

    def turn(self, layer, step):
        def back(held, spot, inner, value):
            held[spot] = value.astype(held.dtype)

        for p in range(3):
            unused, after, across, before, right, left = self.ring(p, step)
            halves, fulls = self.half_copies(layer, p, step), self.full_copies(layer, p, step)
            for side, c in ((0, after), (1, before)):
                halves[side].wait_recv()
                self.add(
                    layer, p, step, c, side, [self.slot(layer, p, step, side, False)], back
                )
                fulls[side].start()

    def finish(self, layer, step):
        for p in range(3):
            c = self.ring(p, step)[0]
            for op in self.full_copies(layer, p, step):
                op.wait_recv()
            terms = [self.slot(layer, p, step, side, True) for side in range(2)]

            def up(held, spot, inner, value, p=p):
                if step == 2:
                    self.final[layer, p * 48 : (p + 1) * 48] = value
                else:
                    target = self.level[step + 1]
                    spot = (layer % target.shape[0], p) + tuple(inner)
                    target[spot] = value.astype(target.dtype)

            self.add(layer, p, step, c, None, terms, up)

    def drain(self, layer, step):
        for p in range(3):
            for op in self.half_copies(layer, p, step) + self.full_copies(layer, p, step):
                op.wait_send()


def reduce_kernel(
    acc_ref,
    mid_ref,
    small_ref,
    out_ref,
    small_out,
    acc,
    mid,
    thin,
    half_0,
    half_1,
    half_2,
    full_0,
    full_1,
    full_2,
    small_acc,
    small_sib,
    small_wide,
    small_mid,
    small_thin,
    final,
    final_peer,
    send,
    recv,
    send_small,
    recv_small,
    local,
):
    at, core = place()
    own_rows, half = final_peer.shape[1], final_peer.shape[2]
    sibling = device_at(at, 1 - core)
    sums = Reduction(at, core, send, recv)
    sums.level = {(0, 0): acc, 1: mid, 2: thin}
    sums.halves = {0: half_0, 1: half_1, 2: half_2}
    sums.fulls = {0: full_0, 1: full_1, 2: full_2}
    sums.final = final

    mid_load = pltpu.make_async_copy(mid_ref, mid.at[1], local.at[0])
    mid_load.start()
    acc_load = pltpu.make_async_copy(acc_ref, acc, local.at[1])
    acc_load.start()
    small_load = pltpu.make_async_copy(small_ref.at[:, :, :, core], small_acc, local.at[2])
    small_load.start()
    greet(neighbours(at, core))
    wires = Wires(send_small, recv_small)
    small_swap = wires.copy(small_ref.at[:, :, :, 1 - core], small_sib, sibling)

    order = ORDERS[0]
    slots = (small_wide, small_mid, small_thin)

    def right(axis):
        return device_at(moved(at, axis, 1), core)

    def left(axis):
        return device_at(moved(at, axis, RING - 1), core)

    def small_view(step, c):
        index = list(at)
        index[order[2 - step]] = c
        for axis in order[: 2 - step]:
            index[axis] = slice(None)
        return tuple(index)

    def small_add(step, c, term):
        where = small_view(step, c)
        small_acc[where] = small_acc[where] + term

    def small_start(step):
        axis = order[2 - step]
        across = lax.rem(at[axis] + 2, RING)
        return wires.copy(small_acc.at[small_view(step, across)], slots[step].at[0], right(axis))

    def small_turn(step, op):
        axis = order[2 - step]
        after, before = lax.rem(at[axis] + 1, RING), lax.rem(at[axis] + 3, RING)
        op.wait_recv()
        small_add(step, after, slots[step][0])
        return (
            wires.copy(small_acc.at[small_view(step, after)], slots[step].at[1], right(axis)),
            wires.copy(small_acc.at[small_view(step, before)], slots[step].at[2], left(axis)),
        )

    def small_finish(step, ops):
        for op in ops:
            op.wait_recv()
        small_add(step, at[order[2 - step]], slots[step][1] + slots[step][2])

    mid_load.wait()
    sums.start(1, 1)
    acc_load.wait()
    sums.start(0, 0)
    small_load.wait()
    small_swap.wait_recv()
    small_acc[...] = small_acc[...] + small_sib[...]
    op = small_start(0)
    sums.turn(1, 1)
    sums.finish(1, 1)
    sums.start(1, 2)
    sums.turn(0, 0)
    ops = small_turn(0, op)
    sums.turn(1, 2)
    sums.finish(1, 2)
    small_finish(0, ops)
    op = small_start(1)
    ops = small_turn(1, op)
    small_finish(1, ops)
    op = small_start(2)
    ops = small_turn(2, op)
    sums.finish(0, 0)
    sums.start(0, 1)
    small_finish(2, ops)
    sums.turn(0, 1)
    sums.finish(0, 1)
    sums.start(0, 2)
    sums.turn(0, 2)
    sums.finish(0, 2)

    theirs = pl.ds(pl.multiple_of((1 - core) * own_rows, own_rows), own_rows)
    swap = wires.copy(final.at[:, theirs], final_peer, sibling)
    small_out[...] = small_acc[at]
    swap.wait_recv()
    for layer in range(2):
        own = jnp.where(core == 0, final[layer, :own_rows], final[layer, own_rows:])
        got = final_peer[layer]
        out_ref[layer, :, :half] = jnp.where(core == 0, own, got)
        out_ref[layer, :, half:] = jnp.where(core == 0, got, own)
    for layer, step in ((1, 1), (1, 2), (0, 0), (0, 1), (0, 2)):
        sums.drain(layer, step)
    wires.drain()


def reduce_weights(acc, mid, small):
    rows, half = acc.shape[3:]
    part = rows // 3
    torus = (RING, RING, RING)
    small_shape = small.shape[1:]
    hbm = pl.BlockSpec(memory_space=pltpu.HBM)
    vmem = pl.BlockSpec(memory_space=pltpu.VMEM)
    low = jnp.bfloat16
    return pl.pallas_call(
        reduce_kernel,
        out_shape=(
            jax.ShapeDtypeStruct((2, rows // 2, 2 * half), jnp.float32),
            jax.ShapeDtypeStruct(small_shape, jnp.float32),
        ),
        in_specs=[hbm, hbm, hbm],
        out_specs=(vmem, vmem),
        scratch_shapes=[
            pltpu.VMEM(torus + (rows, half), low),
            pltpu.VMEM((2, 3, RING, RING, part, half), low),
            pltpu.VMEM((2, 3, RING, part, half), low),
            pltpu.VMEM((1, 3, 2, 2, RING, part, half), low),
            pltpu.VMEM((2, 3, 2, 2, part, half), low),
            pltpu.VMEM((2, 3, 2, 32, half), low),
            pltpu.VMEM((1, 3, 2, RING, RING, part, half), low),
            pltpu.VMEM((2, 3, 2, RING, part, half), low),
            pltpu.VMEM((2, 3, 2, part, half), low),
            pltpu.VMEM(torus + small_shape, jnp.float32),
            pltpu.VMEM(torus + small_shape, jnp.float32),
            pltpu.VMEM((3, RING, RING) + small_shape, jnp.float32),
            pltpu.VMEM((3, RING) + small_shape, jnp.float32),
            pltpu.VMEM((3,) + small_shape, jnp.float32),
            pltpu.VMEM((2, rows, half), jnp.float32),
            pltpu.VMEM((2, rows // 2, half), jnp.float32),
            pltpu.SemaphoreType.DMA((60,)),
            pltpu.SemaphoreType.DMA((60,)),
            pltpu.SemaphoreType.DMA((11,)),
            pltpu.SemaphoreType.DMA((11,)),
            pltpu.SemaphoreType.DMA((3,)),
        ],
        compiler_params=pltpu.CompilerParams(
            collective_id=1, has_side_effects=True, vmem_limit_bytes=58 * 2**20
        ),
        cost_estimate=pl.CostEstimate(flops=0, bytes_accessed=180 * 10**6, transcendentals=0),
        name="reduce_weights",
    )(acc, mid, small.reshape(torus + (2,) + small_shape))


def sum_kernel(in_ref, out_ref, slots, send, recv):
    at, core = place()
    sibling = device_at(at, 1 - core)
    partners = [sibling] + [
        device_at(moved(at, axis, by), core) for axis in range(3) for by in range(1, RING)
    ]
    greet(partners)
    wires = Wires(send, recv)
    slots[0, core] = in_ref[...]
    swap = wires.copy(in_ref, slots.at[0, core], sibling)
    swap.wait_recv()
    value = slots[0, 0] + slots[0, 1]
    for axis in range(3):
        slots[1 + axis, at[axis]] = value
        ops = []
        for by in range(1, RING):
            ops.append(
                wires.copy(
                    slots.at[1 + axis, at[axis]],
                    slots.at[1 + axis, at[axis]],
                    device_at(moved(at, axis, by), core),
                )
            )
        for op in ops:
            op.wait_recv()
        value = slots[1 + axis, 0]
        for c in range(1, RING):
            value = value + slots[1 + axis, c]
    out_ref[...] = value
    wires.drain()


def sum_all(value):
    vmem = pl.BlockSpec(memory_space=pltpu.VMEM)
    return pl.pallas_call(
        sum_kernel,
        out_shape=jax.ShapeDtypeStruct(value.shape, jnp.float32),
        in_specs=[vmem],
        out_specs=vmem,
        scratch_shapes=[
            pltpu.VMEM((4, RING) + value.shape, jnp.float32),
            pltpu.SemaphoreType.DMA((10,)),
            pltpu.SemaphoreType.DMA((10,)),
        ],
        compiler_params=pltpu.CompilerParams(collective_id=2, has_side_effects=True),
        name="sum_all",
    )(value)


TILE = 800


def head_kernel(
    f_ref,
    code_ref,
    weight_ref,
    table_ref,
    grad_out,
    dtable_ref,
    loss_ref,
    f_all,
    codes,
    table,
    logits,
    probs,
    tops,
    stats,
    df,
    df_send,
    df_sib,
    ring,
    ring_half,
    ring_full,
    staged,
    send,
    recv,
    load,
    store,
):
    at, core = place()
    x = at[2]
    dp, vocab = lax.axis_index("dp"), lax.axis_index("vocab")
    tok, width = f_ref.shape
    group = f_all.shape[0]
    members = group // tok
    tiles = table.shape[0] // TILE
    low, f32 = jnp.bfloat16, jnp.float32

    def tile_rows(t):
        return pl.ds(pl.multiple_of(t * TILE, TILE), TILE)

    loads = []
    for t in range(tiles):
        op = pltpu.make_async_copy(
            table_ref.at[pl.ds(t * TILE, TILE)], table.at[pl.ds(t * TILE, TILE)], load.at[t]
        )
        op.start()
        loads.append(op)

    peers = [(dp, lax.rem(vocab + by, members)) for by in range(1, members)]
    greet(peers)
    wires = Wires(send, recv)
    sibling = device_at(at, 1 - core)
    right, left = device_at(moved(at, 2, 1), core), device_at(moved(at, 2, 3), core)
    before, after, across = lax.rem(x + 3, RING), lax.rem(x + 1, RING), lax.rem(x + 2, RING)

    def rows_of(at_x, piece=None):
        first = (at_x * 2 + core) * tok
        if piece is None:
            return f_all.at[pl.ds(pl.multiple_of(first, tok), tok)]
        half = tok // 2
        return f_all.at[pl.ds(pl.multiple_of(first + piece * half, half), half)]

    f_all[pl.ds(pl.multiple_of(vocab * tok, tok), tok), :] = f_ref[...]
    own = rows_of(x)
    one, two = wires.copy(own, own, right), wires.copy(own, own, left)
    pending = [wires.copy(own, own, sibling)]
    codes[vocab] = code_ref[...]
    for peer in peers:
        pending.append(wires.copy(codes.at[vocab], codes.at[vocab], peer))
    one.wait_recv()
    one_on = wires.copy(rows_of(before, 0), rows_of(before, 0), right)
    pending.append(wires.copy(rows_of(before), rows_of(before), sibling))
    two.wait_recv()
    two_on = wires.copy(rows_of(after, 1), rows_of(after, 1), left)
    pending.append(wires.copy(rows_of(after), rows_of(after), sibling))
    one_on.wait_recv()
    pending.append(wires.copy(rows_of(across, 0), rows_of(across, 0), sibling))
    two_on.wait_recv()
    pending.append(wires.copy(rows_of(across, 1), rows_of(across, 1), sibling))
    for op in pending:
        op.wait_recv()

    code_row = jnp.concatenate([codes[m, 0:1, :] for m in range(members)], 1) - vocab * table.shape[0]
    code8 = jnp.broadcast_to(code_row, (8, group))
    code16 = jnp.broadcast_to(code_row, (16, group))
    rows8 = lax.broadcasted_iota(jnp.int32, (8, group), 0)
    rows16 = lax.broadcasted_iota(jnp.int32, (16, group), 0)
    slot = TILE // 2
    real = slot - 7
    steps8, steps16 = 5, 5

    def first_pass(t, carry):
        top, total, target = carry
        here = tile_rows(t)
        logits[...] = lax.dot_general(
            table[here, :], f_all[...], (((1,), (1,)), ((), ())), preferred_element_type=f32
        )
        for part in range(2):
            last = pl.ds((part + 1) * slot - 8, 8)
            logits[last, :] = jnp.where(rows8 < 1, logits[last, :], -1e30)

        def look(i, state):
            high, hit = state
            for u in range(steps8):
                first = (i * steps8 + u) * 8
                value = logits[pl.ds(pl.multiple_of(first, 8), 8), :]
                high = jnp.maximum(high, value)
                hit = hit + jnp.where(rows8 + (first + t * TILE) == code8, value, 0.0)
            return high, hit

        high, hit = lax.fori_loop(
            0,
            TILE // (8 * steps8),
            look,
            (jnp.full((8, group), -1e30, f32), jnp.zeros((8, group), f32)),
        )
        top_next = jnp.maximum(top, jnp.max(high, 0, keepdims=True))
        target = target + jnp.sum(hit, 0, keepdims=True)

        def lift(i, acc):
            for u in range(steps16):
                first = (i * steps16 + u) * 16
                value = jnp.exp(logits[pl.ds(pl.multiple_of(first, 16), 16), :] - top_next)
                acc = acc + value
                probs[pl.ds(pl.multiple_of(t * TILE + first, 16), 16), :] = value.astype(low)
            return acc

        acc = lax.fori_loop(
            0, TILE // (16 * steps16), lift, jnp.zeros((16, group), f32)
        )
        total = total * jnp.exp(top - top_next) + jnp.sum(acc, 0, keepdims=True)
        tops[t] = top_next
        return top_next, total, target

    for op in loads:
        op.wait()
    start = (jnp.full((1, group), -1e30, f32), jnp.zeros((1, group), f32), jnp.zeros((1, group), f32))
    found = lax.fori_loop(0, tiles, first_pass, start)
    for k in range(3):
        for m in range(members):
            stats[vocab, k, m : m + 1, :] = found[k][:, m * tok : (m + 1) * tok]
    pending = [wires.copy(stats.at[vocab], stats.at[vocab], peer) for peer in peers]
    for op in pending:
        op.wait_recv()
    peak = stats[0, 0]
    for m in range(1, members):
        peak = jnp.maximum(peak, stats[m, 0])
    total, target = jnp.zeros_like(peak), jnp.zeros_like(peak)
    for m in range(members):
        total = total + stats[m, 1] * jnp.exp(stats[m, 0] - peak)
        target = target + stats[m, 2]
    lse = peak + jnp.log(total)
    weight = weight_ref[...]
    mine = lax.broadcasted_iota(jnp.int32, (members, tok), 0) == vocab
    loss_ref[...] = jnp.where(mine, weight * (lse - target), 0.0)
    lse_row = jnp.concatenate([lse[m : m + 1, :] for m in range(members)], 1)
    weight_row = jnp.concatenate([weight[m : m + 1, :] for m in range(members)], 1)

    df[...] = jnp.zeros_like(df)

    def second_pass(t, unused):
        scale = weight_row * jnp.exp(tops[t] - lse_row)

        def turn(i, unused):
            for u in range(steps16):
                first = t * TILE + (i * steps16 + u) * 16
                here = pl.ds(pl.multiple_of(first, 16), 16)
                value = probs[here, :].astype(f32) * scale
                value = value - jnp.where(rows16 + first == code16, weight_row, 0.0)
                probs[here, :] = value.astype(low)
            return unused

        lax.fori_loop(0, TILE // (16 * steps16), turn, 0)
        here = tile_rows(t)
        df[...] += lax.dot_general(
            probs[here, :], table[here, :], (((0,), (0,)), ((), ())), preferred_element_type=f32
        )
        return unused

    lax.fori_loop(0, tiles, second_pass, 0)

    def third_pass(t):
        if t >= 2:
            stores[t - 2].wait()
        staged[t % 2] = jnp.dot(
            probs[t * TILE : (t + 1) * TILE, :], f_all[...], preferred_element_type=f32
        ).astype(low)
        op = pltpu.make_async_copy(
            staged.at[t % 2], dtable_ref.at[pl.ds(t * TILE, TILE)], store.at[t]
        )
        op.start()
        stores.append(op)

    stores = []
    for m in range(members):
        df_send[m % 2, m // 2] = df[m * tok : (m + 1) * tok, :].astype(low)
    swap = wires.copy(df_send.at[1 - core], df_sib, sibling)
    third_pass(0)
    third_pass(1)
    swap.wait_recv()
    for k in range(RING):
        first = pl.multiple_of((2 * k + core) * tok, tok)
        ring[k] = (df[pl.ds(first, tok), :] + df_sib[k].astype(f32)).astype(low)
    half = tok // 2
    one = wires.copy(ring.at[across, pl.ds(0, half)], ring_half.at[0], right)
    two = wires.copy(ring.at[across, pl.ds(half, half)], ring_half.at[1], left)
    third_pass(2)
    third_pass(3)
    one.wait_recv()
    ring[after, :half] = (ring[after, :half].astype(f32) + ring_half[0].astype(f32)).astype(low)
    one = wires.copy(ring.at[after], ring_full.at[0], right)
    two.wait_recv()
    ring[before, half:] = (ring[before, half:].astype(f32) + ring_half[1].astype(f32)).astype(low)
    two = wires.copy(ring.at[before], ring_full.at[1], left)
    for t in range(4, tiles):
        third_pass(t)
    one.wait_recv()
    two.wait_recv()
    grad_out[...] = ring[x].astype(f32) + ring_full[0].astype(f32) + ring_full[1].astype(f32)
    for op in stores[-2:]:
        op.wait()
    wires.drain()


HEAD_COPIES = 9 + 7 + 7 + 5


def head(final_low, codes, weights, table):
    tok, width = final_low.shape
    rows = table.shape[0]
    members = weights.shape[0]
    group = members * tok
    tiles = rows // TILE
    hbm = pl.BlockSpec(memory_space=pltpu.HBM)
    vmem = pl.BlockSpec(memory_space=pltpu.VMEM)
    low, f32 = jnp.bfloat16, jnp.float32
    return pl.pallas_call(
        head_kernel,
        out_shape=(
            jax.ShapeDtypeStruct((tok, width), f32),
            jax.ShapeDtypeStruct((rows, width), low),
            jax.ShapeDtypeStruct((members, tok), f32),
        ),
        in_specs=[vmem, vmem, vmem, hbm],
        out_specs=(vmem, hbm, vmem),
        scratch_shapes=[
            pltpu.VMEM((group, width), low),
            pltpu.VMEM((members, 8, tok), jnp.int32),
            pltpu.VMEM((rows, width), low),
            pltpu.VMEM((TILE, group), f32),
            pltpu.VMEM((rows, group), low),
            pltpu.VMEM((tiles, 1, group), f32),
            pltpu.VMEM((members, 3, members, tok), f32),
            pltpu.VMEM((group, width), f32),
            pltpu.VMEM((2, RING, tok, width), low),
            pltpu.VMEM((RING, tok, width), low),
            pltpu.VMEM((RING, tok, width), low),
            pltpu.VMEM((2, tok // 2, width), low),
            pltpu.VMEM((2, tok, width), low),
            pltpu.VMEM((2, TILE, width), low),
            pltpu.SemaphoreType.DMA((HEAD_COPIES,)),
            pltpu.SemaphoreType.DMA((HEAD_COPIES,)),
            pltpu.SemaphoreType.DMA((tiles,)),
            pltpu.SemaphoreType.DMA((tiles,)),
        ],
        compiler_params=pltpu.CompilerParams(
            collective_id=3, has_side_effects=True, vmem_limit_bytes=58 * 2**20
        ),
        cost_estimate=pl.CostEstimate(
            flops=6 * group * rows * width, bytes_accessed=4 * rows * width, transcendentals=group * rows
        ),
        name="head",
    )(final_low, codes, weights, table)


G1, S1, BQ, BV, BPROJ, G2, S2, BFC, BOUT = 0, 1, 2, 3, 4, 5, 6, 7, 11
STEPS = 12
GELU_A, GELU_B = 0.7978845608028654, 0.044715


def across_k(left, right):
    return lax.dot_general(left, right, (((1,), (1,)), ((), ())), preferred_element_type=jnp.float32)


def along_k(left, right):
    return jnp.dot(left, right, preferred_element_type=jnp.float32)


def over_rows(left, right):
    return lax.dot_general(left, right, (((0,), (0,)), ((), ())), preferred_element_type=jnp.float32)


def normed(value):
    centered = value - jnp.mean(value, -1, keepdims=True)
    scale = lax.rsqrt(jnp.mean(centered * centered, -1, keepdims=True) + norm_eps)
    return centered * scale, scale


def norm_back(grad, value, gain):
    unit, scale = normed(value)
    inner = grad * gain
    mean = jnp.mean(inner, -1, keepdims=True)
    slope = jnp.mean(inner * unit, -1, keepdims=True)
    return (
        scale * (inner - mean - unit * slope),
        jnp.sum(grad * unit, 0, keepdims=True),
        jnp.sum(grad, 0, keepdims=True),
    )


def forward_kernel(
    hot_ref,
    rows_ref,
    pos_hot_ref,
    pos_ref,
    mask_ref,
    vec_ref,
    w_ref,
    x_out,
    a_out,
    qkv_out,
    probs_out,
    o_out,
    mid_out,
    m_out,
    u_out,
    g_out,
    hidden_out,
    final_out,
    cur,
):
    step = pl.program_id(0)
    layer, s = lax.div(step, STEPS), lax.rem(step, STEPS)
    low, f32 = jnp.bfloat16, jnp.float32
    width = cur.shape[1]
    head_dim = width // H

    def vec(row):
        return vec_ref[layer * STEPS + row]

    @pl.when(step == 0)
    def embed():
        cur[...] = along_k(hot_ref[...], rows_ref[...]) + across_k(pos_hot_ref[...], pos_ref[...])

    @pl.when(s == 0)
    def first_norm():
        x_out[layer] = cur[...]
        a_out[layer] = (normed(cur[...])[0] * vec(G1) + vec(S1)).astype(low)

    @pl.when(s < 3)
    def project():
        bias = jnp.where(s == 0, vec(BQ), jnp.where(s == 2, vec(BV), 0.0))
        qkv_out[layer, s] = (across_k(a_out[layer], w_ref[...]) + bias).astype(low)

    @pl.when(s == 2)
    def attend():
        lanes = lax.broadcasted_iota(jnp.int32, (1, 2 * head_dim), 1)
        for pair in range(H // 2):
            cols = slice(2 * head_dim * pair, 2 * head_dim * (pair + 1))
            q, k, v = (qkv_out[layer, part, :, cols] for part in range(3))
            total = None
            for side in range(2):
                own = (lanes < head_dim) if side == 0 else (lanes >= head_dim)
                scores = across_k(jnp.where(own, q, jnp.zeros_like(q)), k) * head_dim ** (-0.5)
                scores = jnp.where(mask_ref[...] > 0.0, scores, -1000000000.0)
                shifted = jnp.exp(scores - jnp.max(scores, -1, keepdims=True))
                probs = shifted / jnp.sum(shifted, -1, keepdims=True)
                probs_out[layer, 2 * pair + side] = probs
                term = along_k(probs.astype(low), jnp.where(own, v, jnp.zeros_like(v)))
                total = term if total is None else total + term
            o_out[layer, :, cols] = total.astype(low)

    @pl.when(s == 3)
    def second_norm():
        mid = cur[...] + across_k(o_out[layer], w_ref[...]) + vec(BPROJ)
        mid_out[layer] = mid
        m_out[layer] = (normed(mid)[0] * vec(G2) + vec(S2)).astype(low)
        cur[...] = mid + vec(BOUT)

    @pl.when((s >= 4) & (s < 8))
    def widen():
        u = across_k(m_out[layer], w_ref[...]) + vec(BFC + s - 4)
        u_out[layer, s - 4] = u
        g = 0.5 * u * (1.0 + jnp.tanh(GELU_A * (u + GELU_B * (u * u * u))))
        g_out[layer, s - 4] = g.astype(low)

    @pl.when(s >= 8)
    def narrow():
        cur[...] += along_k(g_out[layer, s - 8], w_ref[...])

    @pl.when(step == 2 * STEPS - 1)
    def last_norm():
        hidden_out[...] = cur[...]
        final_out[...] = (normed(cur[...])[0] * vec_ref[2 * STEPS] + vec_ref[2 * STEPS + 1]).astype(low)


def forward_layers(hot, rows, pos_hot, pos, mask, vecs, mats):
    tok, width = hot.shape[0], rows.shape[1]
    low, f32 = jnp.bfloat16, jnp.float32
    shape = jax.ShapeDtypeStruct
    vmem = pl.BlockSpec(memory_space=pltpu.VMEM)
    return pl.pallas_call(
        forward_kernel,
        grid=(2 * STEPS,),
        out_shape=(
            shape((2, tok, width), f32),
            shape((2, tok, width), low),
            shape((2, 3, tok, width), low),
            shape((2, H, tok, tok), f32),
            shape((2, tok, width), low),
            shape((2, tok, width), f32),
            shape((2, tok, width), low),
            shape((2, 4, tok, width), f32),
            shape((2, 4, tok, width), low),
            shape((tok, width), f32),
            shape((tok, width), low),
        ),
        in_specs=[vmem] * 6 + [pl.BlockSpec((width, width), lambda i: (i, 0))],
        out_specs=(vmem,) * 11,
        scratch_shapes=[pltpu.VMEM((tok, width), f32)],
        compiler_params=pltpu.CompilerParams(vmem_limit_bytes=58 * 2**20),
        cost_estimate=pl.CostEstimate(
            flops=2 * tok * mats.size, bytes_accessed=2 * mats.size, transcendentals=0
        ),
        name="forward_layers",
    )(hot, rows, pos_hot, pos, mask, vecs, mats)


def backward_kernel(
    grad_ref,
    hidden_ref,
    vec_ref,
    x_ref,
    a_ref,
    qkv_ref,
    probs_ref,
    o_ref,
    mid_ref,
    m_ref,
    u_ref,
    g_ref,
    w_ref,
    dx_out,
    vec_out,
    acc_out,
    sums_out,
    cur,
    wide,
    du_s,
    dqkv_s,
    left_s,
    right_s,
    own_s,
    send_s,
    recv_s,
    acc_0,
    acc_1,
    level_1,
    half_0,
    full_0,
    send,
    recv,
    send_pair,
    recv_pair,
    local,
):
    step = pl.program_id(0)
    layer, s = 1 - lax.div(step, STEPS), lax.rem(step, STEPS)
    low, f32 = jnp.bfloat16, jnp.float32
    tok, width = cur.shape
    half = width // 2
    head_dim = width // H
    at, core = place()
    sibling = device_at(at, 1 - core)
    sums = Reduction(at, core, send, recv)
    sums.level = {(0, 1): acc_1, 1: level_1}
    sums.halves, sums.fulls = {0: half_0}, {0: full_0}
    last = 2 * STEPS

    def vec(row):
        return vec_ref[layer * STEPS + row]

    def put(row, value):
        vec_out[layer * STEPS + row] = value

    def pair_copy(slot):
        return pltpu.make_async_remote_copy(
            src_ref=send_s.at[slot],
            dst_ref=recv_s.at[slot],
            send_sem=send_pair.at[slot],
            recv_sem=recv_pair.at[slot],
            device_id=sibling,
            device_id_type=pl.DeviceIdType.MESH,
        )

    def set_right(value):
        right_s[:, :half] = jnp.where(core == 0, value[:, :half], value[:, half:])
        right_s[:, half:] = jnp.where(core == 0, value[:, half:], value[:, :half])

    @pl.when(step == 0)
    def enter():
        greet(neighbours(at, core))
        dx, dg, ds = norm_back(grad_ref[...], hidden_ref[...], vec_ref[last])
        cur[...] = dx
        vec_out[last] = dg
        vec_out[last + 1] = ds

    def collect(acc, before):
        slot, b = lax.rem(before, 2), lax.rem(before, STEPS)
        tile = jnp.where(b < 4, 8 + b, jnp.where(b < 8, b, jnp.where(b == 8, 3, b - 9)))
        pair_copy(slot).wait_recv()
        rows, chunk = acc.shape[3], 16

        def body(n, unused):
            for u in range(4):
                first = (n * 4 + u) * chunk
                place_at = tile * width + first
                block = lax.div(place_at, rows)
                where = pl.ds(pl.multiple_of(lax.rem(place_at, rows), chunk), chunk)
                here = pl.ds(pl.multiple_of(first, chunk), chunk)
                value = own_s[here, :].astype(f32) + recv_s[slot, here, :].astype(f32)
                acc[
                    lax.div(block, RING * RING),
                    lax.rem(lax.div(block, RING), RING),
                    lax.rem(block, RING),
                    where,
                ] = value.astype(low)
            return unused

        lax.fori_loop(0, width // (4 * chunk), body, 0)

    pl.when((step >= 1) & (step <= STEPS))(lambda: collect(acc_1, step - 1))
    pl.when(step > STEPS)(lambda: collect(acc_0, step - 1))

    pl.when(step == STEPS)(lambda: sums.start(1, 0))
    pl.when(step == STEPS + 4)(lambda: sums.turn(1, 0))

    @pl.when((s == 0) & (step < last))
    def begin():
        put(BOUT, jnp.sum(cur[...], 0, keepdims=True))
        set_right(cur[...].astype(low))
        wide[...] = cur[...].astype(low)

    @pl.when((s < 4) & (step < last))
    def through_gelu():
        dg = across_k(wide[...], w_ref[...])
        u = u_ref[layer, s]
        square = u * u
        t = jnp.tanh(GELU_A * (u + GELU_B * (square * u)))
        slope = 0.5 * (1.0 + t) + (0.5 * GELU_A) * u * (1.0 - t * t) * (1.0 + (3.0 * GELU_B) * square)
        du = dg * slope
        put(BFC + s, jnp.sum(du, 0, keepdims=True))
        du_s[s] = du.astype(low)
        left_s[...] = g_ref[layer, s]

    @pl.when(s == 4)
    def begin_fc():
        set_right(m_ref[layer])
        dx_out[...] = jnp.zeros_like(dx_out)

    @pl.when((s >= 4) & (s < 8))
    def through_fc():
        left = du_s[s - 4]
        dx_out[...] += along_k(left, w_ref[...])
        left_s[...] = left

    @pl.when(s == 8)
    def through_attention():
        dx, dg, ds = norm_back(dx_out[...], mid_ref[layer], vec(G2))
        put(G2, dg)
        put(S2, ds)
        cur[...] = cur[...] + dx
        put(BPROJ, jnp.sum(cur[...], 0, keepdims=True))
        mid_low = cur[...].astype(low)
        left_s[...] = mid_low
        set_right(o_ref[layer])
        wide[...] = along_k(mid_low, w_ref[...]).astype(low)
        lanes = lax.broadcasted_iota(jnp.int32, (1, 2 * head_dim), 1)
        scale = head_dim ** (-0.5)
        for pair in range(H // 2):
            cols = slice(2 * head_dim * pair, 2 * head_dim * (pair + 1))
            q, k, v = (qkv_ref[layer, part, :, cols] for part in range(3))
            do = wide[:, cols]
            parts = [None] * 3
            for side in range(2):
                own = (lanes < head_dim) if side == 0 else (lanes >= head_dim)
                keep = lambda item, own=own: jnp.where(own, item, jnp.zeros_like(item))
                probs = probs_ref[layer, 2 * pair + side]
                do_own = keep(do)
                dprobs = across_k(do_own, v)
                dscores = probs * (dprobs - jnp.sum(probs * dprobs, -1, keepdims=True))
                dlow = (dscores * scale).astype(low)
                terms = (
                    along_k(dlow, keep(k)),
                    over_rows(dlow, keep(q)),
                    over_rows(probs.astype(low), do_own),
                )
                parts = [
                    term if held is None else held + term for held, term in zip(parts, terms)
                ]
            for part in range(3):
                dqkv_s[part, :, cols] = parts[part].astype(low)
            vec_out[layer * STEPS + BQ, :, cols] = jnp.sum(parts[0], 0, keepdims=True)
            vec_out[layer * STEPS + BV, :, cols] = jnp.sum(parts[2], 0, keepdims=True)

    @pl.when(s == 9)
    def begin_qkv():
        set_right(a_ref[layer])
        dx_out[...] = jnp.zeros_like(dx_out)

    @pl.when(s >= 9)
    def through_qkv():
        left = dqkv_s[s - 9]
        dx_out[...] += along_k(left, w_ref[...])
        left_s[...] = left

    @pl.when(step < last)
    def gradient():
        slot = lax.rem(step, 2)
        grad = over_rows(left_s[...], right_s[...])
        pl.when(step >= 2)(lambda: pair_copy(slot).wait_send())
        own_s[...] = grad[:, :half].astype(low)
        send_s[slot] = grad[:, half:].astype(low)
        pair_copy(slot).start()

    @pl.when(s == STEPS - 1)
    def end_layer():
        dx, dg, ds = norm_back(dx_out[...], x_ref[layer], vec(G1))
        put(G1, dg)
        put(S1, ds)
        cur[...] = cur[...] + dx

    @pl.when(step == last)
    def leave():
        copy_acc = pltpu.make_async_copy(acc_0, acc_out, local.at[0])
        copy_acc.start()
        dx_out[...] = cur[...]
        sums.finish(1, 0)
        copy_sums = pltpu.make_async_copy(level_1.at[0], sums_out, local.at[1])
        copy_sums.start()
        for slot in range(2):
            pair_copy(slot).wait_send()
        sums.drain(1, 0)
        copy_acc.wait()
        copy_sums.wait()


def backward_layers(grad, hidden, vecs, saved, mats):
    tok, width = grad.shape
    low, f32 = jnp.bfloat16, jnp.float32
    shape = jax.ShapeDtypeStruct
    vmem = pl.BlockSpec(memory_space=pltpu.VMEM)
    hbm = pl.BlockSpec(memory_space=pltpu.HBM)
    torus, half, rows = (RING, RING, RING), width // 2, 144
    part = rows // 3

    def tile(i):
        i = jnp.minimum(i, 2 * STEPS - 1)
        layer, s = 1 - i // STEPS, i % STEPS
        return (
            layer * STEPS
            + jnp.where(s < 4, 8 + s, jnp.where(s < 8, s, jnp.where(s == 8, 3, s - 9))),
            0,
        )

    return pl.pallas_call(
        backward_kernel,
        grid=(2 * STEPS + 1,),
        out_shape=(
            shape((tok, width), f32),
            shape((2 * STEPS + 2, 1, width), f32),
            shape(torus + (rows, half), low),
            shape((3, RING, RING, part, half), low),
        ),
        in_specs=[vmem] * 12 + [pl.BlockSpec((width, width), tile)],
        out_specs=(vmem, vmem, hbm, hbm),
        scratch_shapes=[
            pltpu.VMEM((tok, width), f32),
            pltpu.VMEM((tok, width), low),
            pltpu.VMEM((4, tok, width), low),
            pltpu.VMEM((3, tok, width), low),
            pltpu.VMEM((tok, width), low),
            pltpu.VMEM((tok, width), low),
            pltpu.VMEM((width, half), low),
            pltpu.VMEM((2, width, half), low),
            pltpu.VMEM((2, width, half), low),
            pltpu.VMEM(torus + (rows, half), low),
            pltpu.VMEM(torus + (rows, half), low),
            pltpu.VMEM((1, 3, RING, RING, part, half), low),
            pltpu.VMEM((1, 3, 2, 2, RING, part, half), low),
            pltpu.VMEM((1, 3, 2, RING, RING, part, half), low),
            pltpu.SemaphoreType.DMA((12,)),
            pltpu.SemaphoreType.DMA((12,)),
            pltpu.SemaphoreType.DMA((2,)),
            pltpu.SemaphoreType.DMA((2,)),
            pltpu.SemaphoreType.DMA((2,)),
        ],
        compiler_params=pltpu.CompilerParams(
            collective_id=4, has_side_effects=True, vmem_limit_bytes=60 * 2**20
        ),
        cost_estimate=pl.CostEstimate(
            flops=4 * tok * mats.size, bytes_accessed=2 * mats.size, transcendentals=0
        ),
        name="backward_layers",
    )(grad, hidden, vecs, *saved, mats)


def doc_info(doc_lens, tok_count, total_docs):
    doc_ends = jnp.cumsum(doc_lens)
    places = jnp.arange(tok_count, dtype=jnp.int32)
    seg_ids = jnp.sum((places[:, None] >= doc_ends[None, :]).astype(jnp.int32), 1)
    one_hot = seg_ids[:, None] == jnp.arange(doc_lens.shape[0], dtype=jnp.int32)[None, :]
    starts = doc_ends - doc_lens
    pos_ids = places - jnp.sum(jnp.where(one_hot, starts[None, :], 0), 1)
    doc_len = jnp.sum(jnp.where(one_hot, doc_lens[None, :], 0), 1)
    weights = 1.0 / (doc_len.astype(jnp.float32) * total_docs)
    return (seg_ids, pos_ids, weights)


def device_rise(first, count, devices):
    places = first + jnp.arange(count, dtype=jnp.int32)
    return 1.0 + 2.0 * places.astype(jnp.float32) / (devices - 1)


def contract(left, right, left_dim, right_dim):
    return lax.dot_general(
        left, right, (((left_dim,), (right_dim,)), ((), ())), preferred_element_type=jnp.float32
    )


def renew(weight, moment, average, grad, factor):
    clipped = factor * grad
    moment_next = momentum_coef * moment + clipped
    weight_next = weight - learn_rate * (clipped + momentum_coef * moment_next)
    average_next = ema_decay * average + (1.0 - ema_decay) * weight_next
    return (moment_next, weight_next, average_next, weight_next.astype(jnp.bfloat16))


SMALL_ROWS, LANES = 16, 128


def pack_small(values):
    room = SMALL_ROWS * LANES - values.shape[-1]
    pads = [(0, 0)] * (values.ndim - 1) + [(0, room)]
    return jnp.pad(values, pads).reshape(values.shape[:-1] + (SMALL_ROWS, LANES))


def per_device(
    token_ids,
    targets,
    lengths,
    embed_table,
    embed_moment,
    embed_average,
    blocks,
    block_moment,
    block_average,
    pos_table,
    pos_moment,
    pos_average,
    vectors,
    vector_moment,
    vector_average,
):
    devices = lax.axis_size(("dp", "vocab"))
    vocab_count = lax.axis_size("vocab")
    dp_count = lax.axis_size("dp")
    vocab_at = lax.axis_index("vocab")
    data_at = lax.axis_index("dp")
    tok = token_ids.shape[0]
    own_rows, width = embed_table.shape
    capacity = max(2, 2 * tok // devices)
    low = jnp.bfloat16
    blocks, block_moment, block_average = (
        jnp.transpose(item, (0, 2, 1)) for item in (blocks, block_moment, block_average)
    )
    pos_rows, pos_cols = pos_table.shape
    vec_own = vectors.shape[0]
    table_low = embed_table.astype(low)
    pad_rows = -own_rows % 16
    table_padded = jnp.pad(table_low, ((0, pad_rows), (0, 0)))
    slot_rows = own_rows + pad_rows

    owners = token_ids // own_rows
    tokens = jnp.arange(tok, dtype=jnp.int32)
    earlier = jnp.sum((owners[:, None] == owners[None, :]) & (tokens[None, :] < tokens[:, None]), 1)
    slot_hot = (owners * capacity + earlier)[:, None] == jnp.arange(
        devices * capacity, dtype=jnp.int32
    )[None, :]
    send_rows = jnp.sum(jnp.where(slot_hot, (token_ids % own_rows)[:, None], 0), 0)
    slot_hot = slot_hot.astype(low)
    local_rows = lax.all_to_all(send_rows, ("dp", "vocab"), split_axis=0, concat_axis=0, tiled=True)
    asked = (local_rows[:, None] == jnp.arange(own_rows, dtype=jnp.int32)[None, :]).astype(low)
    fetched = jnp.dot(asked, table_low, preferred_element_type=jnp.float32).astype(low)
    returned_rows = lax.all_to_all(
        fetched.reshape(devices, capacity, width),
        ("dp", "vocab"),
        split_axis=0,
        concat_axis=0,
        tiled=True,
    ).reshape(devices * capacity, width)
    blocks, returned_rows = lax.optimization_barrier((blocks, returned_rows))
    table_slice = lax.all_gather(table_padded, "dp", axis=0, tiled=True)
    target_owners = targets // own_rows
    codes = (
        (target_owners % vocab_count) * (dp_count * slot_rows)
        + (target_owners // vocab_count) * slot_rows
        + targets % own_rows
    )

    small = pack_small(
        jnp.concatenate([jnp.transpose(pos_table).reshape(-1), vectors]).astype(low)
    )
    mats_all, small_all = gather_weights(blocks, small)
    small_all = small_all.reshape(devices, -1)
    pos_low_t = small_all[:, : pos_rows * pos_cols].reshape(width, pos_rows)
    vecs_all = (
        small_all[:, pos_rows * pos_cols : pos_rows * pos_cols + vec_own]
        .reshape(-1)
        .astype(jnp.float32)
    )
    lens_group = lengths[0]
    seg_group, pos_group, weight_group = jax.vmap(
        partial(doc_info, tok_count=tok, total_docs=devices * lens_group.shape[1])
    )(lens_group)
    weight_group = weight_group * device_rise(data_at * vocab_count, vocab_count, devices)[:, None]
    seg_ids = lax.dynamic_index_in_dim(seg_group, vocab_at, 0, keepdims=False)
    pos_ids = lax.dynamic_index_in_dim(pos_group, vocab_at, 0, keepdims=False)
    places = jnp.arange(tok, dtype=jnp.int32)
    attn_mask = (seg_ids[:, None] == seg_ids[None, :]) & (places[None, :] <= places[:, None])

    pos_hot = (pos_ids[:, None] == jnp.arange(pos_rows, dtype=jnp.int32)[None, :]).astype(low)
    vec_rows = vecs_all.reshape(-1, 1, width)
    *saved, hidden, final_low = forward_layers(
        slot_hot,
        returned_rows,
        pos_hot,
        pos_low_t,
        attn_mask.astype(jnp.float32),
        vec_rows,
        mats_all,
    )
    grad_final, table_part, token_losses = head(
        final_low, jnp.broadcast_to(codes[None, :], (8, tok)), weight_group, table_slice
    )
    loss_part = jnp.sum(token_losses)
    table_grad = lax.psum_scatter(table_part, "dp", scatter_dimension=0, tiled=True)[
        :own_rows
    ].astype(jnp.float32)
    grad_hidden, grad_vecs, grad_acc, grad_sums = backward_layers(
        grad_final, hidden, vec_rows, saved, mats_all
    )
    grad_pos = lax.dot_general(
        grad_hidden,
        pos_hot.astype(jnp.float32),
        (((0,), (0,)), ((), ())),
        precision=lax.Precision.HIGHEST,
    )
    send_grads = contract(slot_hot, grad_hidden.astype(low), 0, 0).astype(low)
    grad_acc, send_grads = lax.optimization_barrier((grad_acc, send_grads))
    back_grads = lax.all_to_all(
        send_grads.reshape(devices, capacity, width),
        ("dp", "vocab"),
        split_axis=0,
        concat_axis=0,
        tiled=True,
    ).reshape(-1, width)
    small_grads = pack_small(
        jnp.concatenate(
            [grad_pos.reshape(devices, -1), grad_vecs.reshape(devices, -1)], 1
        )
    )
    mats_shard, small_shard = reduce_weights(grad_acc, grad_sums, small_grads)
    small_shard = small_shard.reshape(-1)
    pos_shard = small_shard[: pos_rows * pos_cols].reshape(pos_cols, pos_rows)
    vec_shard = small_shard[pos_rows * pos_cols : pos_rows * pos_cols + vec_own]
    table_grad = table_grad + contract(asked, back_grads, 0, 0)
    local_squares = (
        jnp.sum(table_grad * table_grad)
        + jnp.sum(mats_shard * mats_shard)
        + jnp.sum(pos_shard * pos_shard)
        + jnp.sum(vec_shard * vec_shard)
    )
    both_sums = sum_all(
        jnp.broadcast_to(jnp.pad(jnp.stack([loss_part, local_squares]), (0, 6))[:, None], (8, LANES))
    )
    loss_sum, squares = both_sums[0, 0], both_sums[1, 0]
    grad_norm = jnp.sqrt(squares)
    factor = clip_bound / jnp.maximum(grad_norm, clip_bound)
    embed_out = renew(embed_table, embed_moment, embed_average, table_grad, factor)
    block_out = renew(blocks, block_moment, block_average, mats_shard, factor)
    block_out = tuple(jnp.transpose(item, (0, 2, 1)) for item in block_out)
    pos_out = renew(
        jnp.transpose(pos_table),
        jnp.transpose(pos_moment),
        jnp.transpose(pos_average),
        pos_shard,
        factor,
    )
    pos_out = tuple(jnp.transpose(item) for item in pos_out)
    vector_out = renew(vectors, vector_moment, vector_average, vec_shard, factor)
    return (loss_sum, grad_norm) + embed_out + block_out + pos_out + vector_out


def solution(mesh):
    table = P(("dp", "vocab"), None)
    cols = P(None, None, ("dp", "vocab"))
    pos = P(None, ("dp", "vocab"))
    vec = P(("dp", "vocab"))
    return jax.shard_map(
        per_device,
        mesh=mesh,
        in_specs=(vec, vec, P("dp", None, None))
        + (table,) * 3
        + (cols,) * 3
        + (pos,) * 3
        + (vec,) * 3,
        out_specs=(P(), P()) + (table,) * 4 + (cols,) * 4 + (pos,) * 4 + (vec,) * 4,
        check_vma=False,
    )
```

```python
from functools import partial

import jax
import jax.numpy as jnp
from jax import lax
from jax.experimental import pallas as pl
from jax.experimental.pallas import tpu as pltpu
from jax.sharding import PartitionSpec as P

H = 12
RING = 4
ORDERS = ((2, 1, 0), (1, 0, 2), (0, 2, 1))
PARTS = ((0, 16), (16, 96), (112, 32))

norm_eps = 1e-05
clip_bound = 0.01
learn_rate = 10000.0
momentum_coef = 0.5
ema_decay = 0.5


def place():
    dp = lax.axis_index("dp")
    vocab = lax.axis_index("vocab")
    return (lax.div(dp, RING), lax.rem(dp, RING), lax.div(vocab, 2)), lax.rem(vocab, 2)


def device_at(at, core):
    return (at[0] * RING + at[1], at[2] * 2 + core)


def moved(at, axis, by):
    out = list(at)
    out[axis] = lax.rem(at[axis] + by, RING)
    return tuple(out)


class Wires:
    def __init__(self, send, recv):
        self.send, self.recv, self.count, self.live = send, recv, 0, []

    def copy(self, src, dst, device):
        number = self.count
        self.count += 1
        op = pltpu.make_async_remote_copy(
            src_ref=src,
            dst_ref=dst,
            send_sem=self.send.at[number],
            recv_sem=self.recv.at[number],
            device_id=device,
            device_id_type=pl.DeviceIdType.MESH,
        )
        op.start()
        self.live.append(op)
        return op

    def drain(self):
        for op in self.live:
            op.wait_send()


def greet(devices):
    barrier = pltpu.get_barrier_semaphore()
    for device in devices:
        pl.semaphore_signal(
            barrier, inc=1, device_id=device, device_id_type=pl.DeviceIdType.MESH
        )
    pl.semaphore_wait(barrier, len(devices))


def neighbours(at, core):
    near = [device_at(moved(at, axis, by), core) for axis in range(3) for by in (1, RING - 1)]
    return near + [device_at(at, 1 - core)]


def gather_kernel(
    mine_ref, small_ref, out_ref, small_out, peer, block, send, recv, local
):
    at, core = place()
    rows, half = mine_ref.shape[1], mine_ref.shape[2] // 2
    sibling = device_at(at, 1 - core)
    greet(neighbours(at, core))
    wires = Wires(send, recv)
    cols = pl.ds(pl.multiple_of(core * half, half), half)
    other = pl.ds(pl.multiple_of((1 - core) * half, half), half)

    swap = wires.copy(mine_ref.at[:, :, other], peer, sibling)
    small_local = pltpu.make_async_copy(small_ref, small_out.at[at[0], at[1], at[2], core], local.at[0])
    small_local.start()
    swap.wait_recv()
    for layer in range(2):
        own = jnp.where(core == 0, mine_ref[layer, :, :half], mine_ref[layer, :, half:])
        got = peer[layer]
        both = jnp.concatenate(
            [jnp.where(core == 0, own, got), jnp.where(core == 0, got, own)], 0
        )
        block[layer] = both.astype(jnp.bfloat16)
    block_local = []
    for layer in range(2):
        op = pltpu.make_async_copy(
            block.at[layer],
            out_ref.at[layer, at[0], at[1], at[2], :, cols],
            local.at[1 + layer],
        )
        op.start()
        block_local.append(op)

    def bundle(layer, p, phase, c, piece=None):
        order = ORDERS[p]
        index = list(at)
        index[order[phase]] = c
        for axis in order[:phase]:
            index[axis] = pl.ds(0, RING)
        first, count = PARTS[p]
        where = cols
        if piece is not None:
            if phase == 0:
                cut, size = (0, half - 128) if piece == 0 else (half - 128, 128)
                where = pl.ds(pl.multiple_of(core * half + cut, 128), size)
            else:
                index[order[0]] = pl.ds(2 * piece, 2)
        return out_ref.at[layer, index[0], index[1], index[2], pl.ds(first, count), where]

    def small_bundle(phase, c):
        order = ORDERS[0]
        index = list(at)
        index[order[phase]] = c
        for axis in order[:phase]:
            index[axis] = pl.ds(0, RING)
        return small_out.at[index[0], index[1], index[2], core]

    def right(axis):
        return device_at(moved(at, axis, 1), core)

    def left(axis):
        return device_at(moved(at, axis, RING - 1), core)

    chains = [(layer, p) for layer in range(2) for p in range(3)]
    pending = []
    small_local.wait()
    for op in block_local:
        op.wait()
    for phase in range(3):
        steps = {}
        for key in chains:
            layer, p = key
            axis = ORDERS[p][phase]
            src = bundle(layer, p, phase, at[axis])
            if phase == 2:
                pending.append(wires.copy(src, src, sibling))
            steps[key] = (wires.copy(src, src, right(axis)), wires.copy(src, src, left(axis)))
        axis = ORDERS[0][phase]
        src = small_bundle(phase, at[axis])
        small_steps = (wires.copy(src, src, right(axis)), wires.copy(src, src, left(axis)))
        forwards = {}
        for key in chains:
            layer, p = key
            axis = ORDERS[p][phase]
            before, after = lax.rem(at[axis] + 3, RING), lax.rem(at[axis] + 1, RING)
            steps[key][0].wait_recv()
            src = bundle(layer, p, phase, before, 0)
            one = wires.copy(src, src, right(axis))
            steps[key][1].wait_recv()
            src = bundle(layer, p, phase, after, 1)
            two = wires.copy(src, src, left(axis))
            forwards[key] = (one, two)
            if phase == 2:
                for c in (before, after):
                    src = bundle(layer, p, phase, c)
                    pending.append(wires.copy(src, src, sibling))
        axis = ORDERS[0][phase]
        for op in small_steps:
            op.wait_recv()
        src = small_bundle(phase, lax.rem(at[axis] + 3, RING))
        small_forward = wires.copy(src, src, right(axis))
        for key in chains:
            layer, p = key
            axis = ORDERS[p][phase]
            across = lax.rem(at[axis] + 2, RING)
            for piece in range(2):
                forwards[key][piece].wait_recv()
                if phase == 2:
                    src = bundle(layer, p, phase, across, piece)
                    pending.append(wires.copy(src, src, sibling))
        small_forward.wait_recv()
    src = small_out.at[:, :, :, core]
    pending.append(wires.copy(src, src, sibling))
    for op in pending:
        op.wait_recv()
    wires.drain()


GATHER_COPIES = 1 + 3 * (6 * 4 + 3) + 6 * 5 + 1


def gather_weights(mine, small):
    layers, rows, width = mine.shape
    whole = jax.ShapeDtypeStruct((layers, RING, RING, RING, 2 * rows, width), jnp.bfloat16)
    hbm = pl.BlockSpec(memory_space=pltpu.HBM)
    vmem = pl.BlockSpec(memory_space=pltpu.VMEM)
    mats, small_all = pl.pallas_call(
        gather_kernel,
        out_shape=(
            whole,
            jax.ShapeDtypeStruct((RING, RING, RING, 2) + small.shape, jnp.bfloat16),
        ),
        in_specs=[vmem, vmem],
        out_specs=(hbm, hbm),
        scratch_shapes=[
            pltpu.VMEM((layers, rows, width // 2), jnp.float32),
            pltpu.VMEM((layers, 2 * rows, width // 2), jnp.bfloat16),
            pltpu.SemaphoreType.DMA((GATHER_COPIES,)),
            pltpu.SemaphoreType.DMA((GATHER_COPIES,)),
            pltpu.SemaphoreType.DMA((3,)),
        ],
        compiler_params=pltpu.CompilerParams(
            collective_id=0, has_side_effects=True, vmem_limit_bytes=58 * 2**20
        ),
        cost_estimate=pl.CostEstimate(flops=0, bytes_accessed=250 * 10**6, transcendentals=0),
        name="gather_weights",
    )(mine, small)
    return (
        mats.reshape(layers * RING**3 * 2 * rows, width),
        small_all.reshape((2 * RING**3,) + small.shape),
    )


class Reduction:
    def __init__(self, at, core, send, recv):
        self.at, self.core, self.send, self.recv = at, core, send, recv
        self.number, self.level, self.halves, self.fulls = {}, {}, {}, {}
        self.final = None

    def copy(self, key, src, dst, device):
        number = self.number.setdefault(key, len(self.number))
        return pltpu.make_async_remote_copy(
            src_ref=src,
            dst_ref=dst,
            send_sem=self.send.at[number],
            recv_sem=self.recv.at[number],
            device_id=device,
            device_id_type=pl.DeviceIdType.MESH,
        )

    def axes(self, p):
        order = ORDERS[p]
        free = sorted(order[:2])
        return free, free.index(order[1])

    def ring(self, p, step):
        axis = ORDERS[p][2 - step]
        c = self.at[axis]
        right = device_at(moved(self.at, axis, 1), self.core)
        left = device_at(moved(self.at, axis, RING - 1), self.core)
        return c, lax.rem(c + 1, RING), lax.rem(c + 2, RING), lax.rem(c + 3, RING), right, left

    def index(self, layer, p, step, c, piece=None):
        part = 48
        cut, whole = (0, RING) if piece is None else (2 * piece, 2), (0, RING)
        if step == 0:
            free, unused = self.axes(p)
            spot = [c, c, c]
            spot[free[0]], spot[free[1]] = cut, whole
            return spot + [p]
        if step == 1:
            unused, first = self.axes(p)
            spot = [cut, cut]
            spot[first] = c
            return [layer % self.level[1].shape[0], p] + spot
        if piece is None:
            return [layer, p, c]
        return [layer, p, c, pl.ds(0, 32) if piece == 0 else pl.ds(32, part - 32)]

    def view(self, layer, p, step, c, piece=None):
        index = self.index(layer, p, step, c, piece)
        held = self.level[0, layer] if step == 0 else self.level[step]
        return held.at[tuple(pl.ds(*item) if isinstance(item, tuple) else item for item in index)]

    def slot(self, layer, p, step, side, whole):
        store = (self.fulls if whole else self.halves)[step]
        if step == 2 and not whole:
            return store.at[layer, p, side, pl.ds(0, 32 if side == 0 else 16)]
        return store.at[layer % store.shape[0], p, side]

    def half_copies(self, layer, p, step):
        unused, after, across, before, right, left = self.ring(p, step)
        out = []
        for side, device in ((0, right), (1, left)):
            out.append(
                self.copy(
                    (layer, p, step, side),
                    self.view(layer, p, step, across, side),
                    self.slot(layer, p, step, side, False),
                    device,
                )
            )
        return out

    def full_copies(self, layer, p, step):
        unused, after, across, before, right, left = self.ring(p, step)
        out = []
        for side, c, device in ((0, after, right), (1, before, left)):
            out.append(
                self.copy(
                    (layer, p, step, 2 + side),
                    self.view(layer, p, step, c),
                    self.slot(layer, p, step, side, True),
                    device,
                )
            )
        return out

    def add(self, layer, p, step, c, piece, terms, into):
        held = self.level[0, layer] if step == 0 else self.level[step]
        index = self.index(layer, p, step, c, piece)
        sizes = [item[1] for item in index if isinstance(item, tuple)]

        def one(inner):
            places = iter(inner)
            spot = tuple(
                item[0] + next(places) if isinstance(item, tuple) else item for item in index
            )
            value = held[spot].astype(jnp.float32)
            for term in terms:
                value = value + term[tuple(inner) + (slice(None), slice(None))].astype(jnp.float32)
            into(held, spot, inner, value)

        def body(n, unused):
            if len(sizes) == 2:
                for k in range(sizes[1]):
                    one([n, k])
            else:
                one([n])
            return unused

        if sizes:
            lax.fori_loop(0, sizes[0], body, 0)
        else:
            one([])

    def start(self, layer, step):
        for p in range(3):
            for op in self.half_copies(layer, p, step):
                op.start()

    def turn(self, layer, step):
        def back(held, spot, inner, value):
            held[spot] = value.astype(held.dtype)

        for p in range(3):
            unused, after, across, before, right, left = self.ring(p, step)
            halves, fulls = self.half_copies(layer, p, step), self.full_copies(layer, p, step)
            for side, c in ((0, after), (1, before)):
                halves[side].wait_recv()
                self.add(
                    layer, p, step, c, side, [self.slot(layer, p, step, side, False)], back
                )
                fulls[side].start()

    def finish(self, layer, step):
        for p in range(3):
            c = self.ring(p, step)[0]
            for op in self.full_copies(layer, p, step):
                op.wait_recv()
            terms = [self.slot(layer, p, step, side, True) for side in range(2)]

            def up(held, spot, inner, value, p=p):
                if step == 2:
                    self.final[layer, p * 48 : (p + 1) * 48] = value
                else:
                    target = self.level[step + 1]
                    spot = (layer % target.shape[0], p) + tuple(inner)
                    target[spot] = value.astype(target.dtype)

            self.add(layer, p, step, c, None, terms, up)

    def drain(self, layer, step):
        for p in range(3):
            for op in self.half_copies(layer, p, step) + self.full_copies(layer, p, step):
                op.wait_send()


def reduce_kernel(
    acc_ref,
    mid_ref,
    small_ref,
    out_ref,
    small_out,
    acc,
    mid,
    thin,
    half_0,
    half_1,
    half_2,
    full_0,
    full_1,
    full_2,
    small_acc,
    small_sib,
    small_wide,
    small_mid,
    small_thin,
    final,
    final_peer,
    send,
    recv,
    send_small,
    recv_small,
    local,
):
    at, core = place()
    own_rows, half = final_peer.shape[1], final_peer.shape[2]
    sibling = device_at(at, 1 - core)
    sums = Reduction(at, core, send, recv)
    sums.level = {(0, 0): acc, 1: mid, 2: thin}
    sums.halves = {0: half_0, 1: half_1, 2: half_2}
    sums.fulls = {0: full_0, 1: full_1, 2: full_2}
    sums.final = final

    mid_load = pltpu.make_async_copy(mid_ref, mid.at[1], local.at[0])
    mid_load.start()
    acc_loads = []
    for n in range(RING * RING):
        spot = (n // RING, n % RING)
        op = pltpu.make_async_copy(acc_ref.at[spot], acc.at[spot], local.at[2 + n])
        op.start()
        acc_loads.append(op)
    small_load = pltpu.make_async_copy(small_ref.at[:, :, :, core], small_acc, local.at[1])
    small_load.start()
    greet(neighbours(at, core))
    wires = Wires(send_small, recv_small)
    small_swap = wires.copy(small_ref.at[:, :, :, 1 - core], small_sib, sibling)

    order = ORDERS[0]
    slots = (small_wide, small_mid, small_thin)

    def right(axis):
        return device_at(moved(at, axis, 1), core)

    def left(axis):
        return device_at(moved(at, axis, RING - 1), core)

    def small_view(step, c):
        index = list(at)
        index[order[2 - step]] = c
        for axis in order[: 2 - step]:
            index[axis] = slice(None)
        return tuple(index)

    def small_add(step, c, term):
        where = small_view(step, c)
        small_acc[where] = small_acc[where] + term

    def small_start(step):
        axis = order[2 - step]
        across = lax.rem(at[axis] + 2, RING)
        return wires.copy(small_acc.at[small_view(step, across)], slots[step].at[0], right(axis))

    def small_turn(step, op):
        axis = order[2 - step]
        after, before = lax.rem(at[axis] + 1, RING), lax.rem(at[axis] + 3, RING)
        op.wait_recv()
        small_add(step, after, slots[step][0])
        return (
            wires.copy(small_acc.at[small_view(step, after)], slots[step].at[1], right(axis)),
            wires.copy(small_acc.at[small_view(step, before)], slots[step].at[2], left(axis)),
        )

    def small_finish(step, ops):
        for op in ops:
            op.wait_recv()
        small_add(step, at[order[2 - step]], slots[step][1] + slots[step][2])

    for op in acc_loads:
        op.wait()
    sums.start(0, 0)
    mid_load.wait()
    sums.start(1, 1)
    small_load.wait()
    small_swap.wait_recv()
    small_acc[...] = small_acc[...] + small_sib[...]
    op = small_start(0)
    sums.turn(0, 0)
    sums.turn(1, 1)
    ops = small_turn(0, op)
    sums.finish(1, 1)
    sums.start(1, 2)
    small_finish(0, ops)
    op = small_start(1)
    sums.turn(1, 2)
    ops = small_turn(1, op)
    sums.finish(1, 2)
    small_finish(1, ops)
    op = small_start(2)
    ops = small_turn(2, op)
    sums.finish(0, 0)
    sums.start(0, 1)
    small_finish(2, ops)
    sums.turn(0, 1)
    sums.finish(0, 1)
    sums.start(0, 2)
    sums.turn(0, 2)
    sums.finish(0, 2)

    theirs = pl.ds(pl.multiple_of((1 - core) * own_rows, own_rows), own_rows)
    swap = wires.copy(final.at[:, theirs], final_peer, sibling)
    small_out[...] = small_acc[at]
    swap.wait_recv()
    for layer in range(2):
        own = jnp.where(core == 0, final[layer, :own_rows], final[layer, own_rows:])
        got = final_peer[layer]
        out_ref[layer, :, :half] = jnp.where(core == 0, own, got)
        out_ref[layer, :, half:] = jnp.where(core == 0, got, own)
    for layer, step in ((1, 1), (1, 2), (0, 0), (0, 1), (0, 2)):
        sums.drain(layer, step)
    wires.drain()


def reduce_weights(acc, mid, small):
    part, half = acc.shape[4:]
    rows = 3 * part
    torus = (RING, RING, RING)
    small_shape = small.shape[1:]
    hbm = pl.BlockSpec(memory_space=pltpu.HBM)
    vmem = pl.BlockSpec(memory_space=pltpu.VMEM)
    low = jnp.bfloat16
    return pl.pallas_call(
        reduce_kernel,
        out_shape=(
            jax.ShapeDtypeStruct((2, rows // 2, 2 * half), jnp.float32),
            jax.ShapeDtypeStruct(small_shape, jnp.float32),
        ),
        in_specs=[hbm, hbm, hbm],
        out_specs=(vmem, vmem),
        scratch_shapes=[
            pltpu.VMEM(torus + (3, part, half), low),
            pltpu.VMEM((2, 3, RING, RING, part, half), low),
            pltpu.VMEM((2, 3, RING, part, half), low),
            pltpu.VMEM((1, 3, 2, 2, RING, part, half), low),
            pltpu.VMEM((2, 3, 2, 2, part, half), low),
            pltpu.VMEM((2, 3, 2, 32, half), low),
            pltpu.VMEM((1, 3, 2, RING, RING, part, half), low),
            pltpu.VMEM((2, 3, 2, RING, part, half), low),
            pltpu.VMEM((2, 3, 2, part, half), low),
            pltpu.VMEM(torus + small_shape, jnp.float32),
            pltpu.VMEM(torus + small_shape, jnp.float32),
            pltpu.VMEM((3, RING, RING) + small_shape, jnp.float32),
            pltpu.VMEM((3, RING) + small_shape, jnp.float32),
            pltpu.VMEM((3,) + small_shape, jnp.float32),
            pltpu.VMEM((2, rows, half), jnp.float32),
            pltpu.VMEM((2, rows // 2, half), jnp.float32),
            pltpu.SemaphoreType.DMA((60,)),
            pltpu.SemaphoreType.DMA((60,)),
            pltpu.SemaphoreType.DMA((11,)),
            pltpu.SemaphoreType.DMA((11,)),
            pltpu.SemaphoreType.DMA((2 + RING * RING,)),
        ],
        compiler_params=pltpu.CompilerParams(
            collective_id=1, has_side_effects=True, vmem_limit_bytes=58 * 2**20
        ),
        cost_estimate=pl.CostEstimate(flops=0, bytes_accessed=180 * 10**6, transcendentals=0),
        name="reduce_weights",
    )(acc, mid, small.reshape(torus + (2,) + small_shape))


def sum_kernel(in_ref, out_ref, slots, send, recv):
    at, core = place()
    sibling = device_at(at, 1 - core)
    partners = [sibling] + [
        device_at(moved(at, axis, by), core) for axis in range(3) for by in range(1, RING)
    ]
    greet(partners)
    wires = Wires(send, recv)
    slots[0, core] = in_ref[...]
    swap = wires.copy(in_ref, slots.at[0, core], sibling)
    swap.wait_recv()
    value = slots[0, 0] + slots[0, 1]
    for axis in range(3):
        slots[1 + axis, at[axis]] = value
        ops = []
        for by in range(1, RING):
            ops.append(
                wires.copy(
                    slots.at[1 + axis, at[axis]],
                    slots.at[1 + axis, at[axis]],
                    device_at(moved(at, axis, by), core),
                )
            )
        for op in ops:
            op.wait_recv()
        value = slots[1 + axis, 0]
        for c in range(1, RING):
            value = value + slots[1 + axis, c]
    out_ref[...] = value
    wires.drain()


def sum_all(value):
    vmem = pl.BlockSpec(memory_space=pltpu.VMEM)
    return pl.pallas_call(
        sum_kernel,
        out_shape=jax.ShapeDtypeStruct(value.shape, jnp.float32),
        in_specs=[vmem],
        out_specs=vmem,
        scratch_shapes=[
            pltpu.VMEM((4, RING) + value.shape, jnp.float32),
            pltpu.SemaphoreType.DMA((10,)),
            pltpu.SemaphoreType.DMA((10,)),
        ],
        compiler_params=pltpu.CompilerParams(collective_id=2, has_side_effects=True),
        name="sum_all",
    )(value)


TILE = 800


def head_kernel(
    f_ref,
    code_ref,
    weight_ref,
    table_ref,
    grad_out,
    dtable_ref,
    loss_ref,
    f_all,
    codes,
    table,
    logits,
    probs,
    tops,
    stats,
    df,
    df_send,
    df_sib,
    ring,
    ring_half,
    ring_full,
    staged,
    send,
    recv,
    load,
    store,
):
    at, core = place()
    x = at[2]
    dp, vocab = lax.axis_index("dp"), lax.axis_index("vocab")
    tok, width = f_ref.shape
    group = f_all.shape[0]
    members = group // tok
    tiles = table.shape[0] // TILE
    low, f32 = jnp.bfloat16, jnp.float32

    def tile_rows(t):
        return pl.ds(pl.multiple_of(t * TILE, TILE), TILE)

    loads = []
    for t in range(tiles):
        op = pltpu.make_async_copy(
            table_ref.at[pl.ds(t * TILE, TILE)], table.at[pl.ds(t * TILE, TILE)], load.at[t]
        )
        op.start()
        loads.append(op)

    peers = [(dp, lax.rem(vocab + by, members)) for by in range(1, members)]
    greet(peers)
    wires = Wires(send, recv)
    sibling = device_at(at, 1 - core)
    right, left = device_at(moved(at, 2, 1), core), device_at(moved(at, 2, 3), core)
    before, after, across = lax.rem(x + 3, RING), lax.rem(x + 1, RING), lax.rem(x + 2, RING)

    def rows_of(at_x, piece=None):
        first = (at_x * 2 + core) * tok
        if piece is None:
            return f_all.at[pl.ds(pl.multiple_of(first, tok), tok)]
        half = tok // 2
        return f_all.at[pl.ds(pl.multiple_of(first + piece * half, half), half)]

    f_all[pl.ds(pl.multiple_of(vocab * tok, tok), tok), :] = f_ref[...]
    own = rows_of(x)
    one, two = wires.copy(own, own, right), wires.copy(own, own, left)
    pending = [wires.copy(own, own, sibling)]
    codes[vocab] = code_ref[...]
    for peer in peers:
        pending.append(wires.copy(codes.at[vocab], codes.at[vocab], peer))
    one.wait_recv()
    one_on = wires.copy(rows_of(before, 0), rows_of(before, 0), right)
    pending.append(wires.copy(rows_of(before), rows_of(before), sibling))
    two.wait_recv()
    two_on = wires.copy(rows_of(after, 1), rows_of(after, 1), left)
    pending.append(wires.copy(rows_of(after), rows_of(after), sibling))
    one_on.wait_recv()
    pending.append(wires.copy(rows_of(across, 0), rows_of(across, 0), sibling))
    two_on.wait_recv()
    pending.append(wires.copy(rows_of(across, 1), rows_of(across, 1), sibling))
    for op in pending:
        op.wait_recv()

    code_row = jnp.concatenate([codes[m, 0:1, :] for m in range(members)], 1) - vocab * table.shape[0]
    code8 = jnp.broadcast_to(code_row, (8, group))
    code16 = jnp.broadcast_to(code_row, (16, group))
    rows8 = lax.broadcasted_iota(jnp.int32, (8, group), 0)
    rows16 = lax.broadcasted_iota(jnp.int32, (16, group), 0)
    slot = TILE // 2
    real = slot - 7
    steps8, steps16 = 5, 5

    def first_pass(t, carry):
        top, total, target = carry
        here = tile_rows(t)
        logits[...] = lax.dot_general(
            table[here, :], f_all[...], (((1,), (1,)), ((), ())), preferred_element_type=f32
        )
        for part in range(2):
            last = pl.ds((part + 1) * slot - 8, 8)
            logits[last, :] = jnp.where(rows8 < 1, logits[last, :], -1e30)

        def look(i, state):
            high, hit = state
            for u in range(steps8):
                first = (i * steps8 + u) * 8
                value = logits[pl.ds(pl.multiple_of(first, 8), 8), :]
                high = jnp.maximum(high, value)
                hit = hit + jnp.where(rows8 + (first + t * TILE) == code8, value, 0.0)
            return high, hit

        high, hit = lax.fori_loop(
            0,
            TILE // (8 * steps8),
            look,
            (jnp.full((8, group), -1e30, f32), jnp.zeros((8, group), f32)),
        )
        top_next = jnp.maximum(top, jnp.max(high, 0, keepdims=True))
        target = target + jnp.sum(hit, 0, keepdims=True)

        def lift(i, acc):
            for u in range(steps16):
                first = (i * steps16 + u) * 16
                value = jnp.exp(logits[pl.ds(pl.multiple_of(first, 16), 16), :] - top_next)
                acc = acc + value
                probs[pl.ds(pl.multiple_of(t * TILE + first, 16), 16), :] = value.astype(low)
            return acc

        acc = lax.fori_loop(
            0, TILE // (16 * steps16), lift, jnp.zeros((16, group), f32)
        )
        total = total * jnp.exp(top - top_next) + jnp.sum(acc, 0, keepdims=True)
        tops[t] = top_next
        return top_next, total, target

    for op in loads:
        op.wait()
    start = (jnp.full((1, group), -1e30, f32), jnp.zeros((1, group), f32), jnp.zeros((1, group), f32))
    found = lax.fori_loop(0, tiles, first_pass, start)
    for k in range(3):
        for m in range(members):
            stats[vocab, k, m : m + 1, :] = found[k][:, m * tok : (m + 1) * tok]
    pending = [wires.copy(stats.at[vocab], stats.at[vocab], peer) for peer in peers]
    for op in pending:
        op.wait_recv()
    peak = stats[0, 0]
    for m in range(1, members):
        peak = jnp.maximum(peak, stats[m, 0])
    total, target = jnp.zeros_like(peak), jnp.zeros_like(peak)
    for m in range(members):
        total = total + stats[m, 1] * jnp.exp(stats[m, 0] - peak)
        target = target + stats[m, 2]
    lse = peak + jnp.log(total)
    weight = weight_ref[...]
    mine = lax.broadcasted_iota(jnp.int32, (members, tok), 0) == vocab
    loss_ref[...] = jnp.where(mine, weight * (lse - target), 0.0)
    lse_row = jnp.concatenate([lse[m : m + 1, :] for m in range(members)], 1)
    weight_row = jnp.concatenate([weight[m : m + 1, :] for m in range(members)], 1)

    df[...] = jnp.zeros_like(df)

    def second_pass(t, unused):
        scale = weight_row * jnp.exp(tops[t] - lse_row)

        def turn(i, unused):
            for u in range(steps16):
                first = t * TILE + (i * steps16 + u) * 16
                here = pl.ds(pl.multiple_of(first, 16), 16)
                value = probs[here, :].astype(f32) * scale
                value = value - jnp.where(rows16 + first == code16, weight_row, 0.0)
                probs[here, :] = value.astype(low)
            return unused

        lax.fori_loop(0, TILE // (16 * steps16), turn, 0)
        here = tile_rows(t)
        df[...] += lax.dot_general(
            probs[here, :], table[here, :], (((0,), (0,)), ((), ())), preferred_element_type=f32
        )
        return unused

    lax.fori_loop(0, tiles, second_pass, 0)

    def third_pass(t):
        if t >= 2:
            stores[t - 2].wait()
        staged[t % 2] = jnp.dot(
            probs[t * TILE : (t + 1) * TILE, :], f_all[...], preferred_element_type=f32
        ).astype(low)
        op = pltpu.make_async_copy(
            staged.at[t % 2], dtable_ref.at[pl.ds(t * TILE, TILE)], store.at[t]
        )
        op.start()
        stores.append(op)

    stores = []
    for m in range(members):
        df_send[m % 2, m // 2] = df[m * tok : (m + 1) * tok, :].astype(low)
    swap = wires.copy(df_send.at[1 - core], df_sib, sibling)
    third_pass(0)
    third_pass(1)
    swap.wait_recv()
    for k in range(RING):
        first = pl.multiple_of((2 * k + core) * tok, tok)
        ring[k] = (df[pl.ds(first, tok), :] + df_sib[k].astype(f32)).astype(low)
    half = tok // 2
    one = wires.copy(ring.at[across, pl.ds(0, half)], ring_half.at[0], right)
    two = wires.copy(ring.at[across, pl.ds(half, half)], ring_half.at[1], left)
    third_pass(2)
    third_pass(3)
    one.wait_recv()
    ring[after, :half] = (ring[after, :half].astype(f32) + ring_half[0].astype(f32)).astype(low)
    one = wires.copy(ring.at[after], ring_full.at[0], right)
    two.wait_recv()
    ring[before, half:] = (ring[before, half:].astype(f32) + ring_half[1].astype(f32)).astype(low)
    two = wires.copy(ring.at[before], ring_full.at[1], left)
    for t in range(4, tiles):
        third_pass(t)
    one.wait_recv()
    two.wait_recv()
    grad_out[...] = ring[x].astype(f32) + ring_full[0].astype(f32) + ring_full[1].astype(f32)
    for op in stores[-2:]:
        op.wait()
    wires.drain()


HEAD_COPIES = 9 + 7 + 7 + 5


def head(final_low, codes, weights, table):
    tok, width = final_low.shape
    rows = table.shape[0]
    members = weights.shape[0]
    group = members * tok
    tiles = rows // TILE
    hbm = pl.BlockSpec(memory_space=pltpu.HBM)
    vmem = pl.BlockSpec(memory_space=pltpu.VMEM)
    low, f32 = jnp.bfloat16, jnp.float32
    return pl.pallas_call(
        head_kernel,
        out_shape=(
            jax.ShapeDtypeStruct((tok, width), f32),
            jax.ShapeDtypeStruct((rows, width), low),
            jax.ShapeDtypeStruct((members, tok), f32),
        ),
        in_specs=[vmem, vmem, vmem, hbm],
        out_specs=(vmem, hbm, vmem),
        scratch_shapes=[
            pltpu.VMEM((group, width), low),
            pltpu.VMEM((members, 8, tok), jnp.int32),
            pltpu.VMEM((rows, width), low),
            pltpu.VMEM((TILE, group), f32),
            pltpu.VMEM((rows, group), low),
            pltpu.VMEM((tiles, 1, group), f32),
            pltpu.VMEM((members, 3, members, tok), f32),
            pltpu.VMEM((group, width), f32),
            pltpu.VMEM((2, RING, tok, width), low),
            pltpu.VMEM((RING, tok, width), low),
            pltpu.VMEM((RING, tok, width), low),
            pltpu.VMEM((2, tok // 2, width), low),
            pltpu.VMEM((2, tok, width), low),
            pltpu.VMEM((2, TILE, width), low),
            pltpu.SemaphoreType.DMA((HEAD_COPIES,)),
            pltpu.SemaphoreType.DMA((HEAD_COPIES,)),
            pltpu.SemaphoreType.DMA((tiles,)),
            pltpu.SemaphoreType.DMA((tiles,)),
        ],
        compiler_params=pltpu.CompilerParams(
            collective_id=3, has_side_effects=True, vmem_limit_bytes=58 * 2**20
        ),
        cost_estimate=pl.CostEstimate(
            flops=6 * group * rows * width, bytes_accessed=4 * rows * width, transcendentals=group * rows
        ),
        name="head",
    )(final_low, codes, weights, table)


TILE_ORDER = (8, 9, 10, 11, 4, 5, 6, 7, 3, 0, 1, 2)
G1, S1, BQ, BV, BPROJ, G2, S2, BFC, BOUT = 0, 1, 2, 3, 4, 5, 6, 7, 11
STEPS = 12
GELU_A, GELU_B = 0.7978845608028654, 0.044715


def across_k(left, right):
    return lax.dot_general(left, right, (((1,), (1,)), ((), ())), preferred_element_type=jnp.float32)


def along_k(left, right):
    return jnp.dot(left, right, preferred_element_type=jnp.float32)


def over_rows(left, right):
    return lax.dot_general(left, right, (((0,), (0,)), ((), ())), preferred_element_type=jnp.float32)


def tile_across(left, tile):
    return jnp.concatenate([across_k(left, block[...]) for block in tile], 1)


def tile_along(left, tile):
    total = None
    for n, block in enumerate(tile):
        rows = block.shape[0]
        term = along_k(left[:, n * rows : (n + 1) * rows], block[...])
        total = term if total is None else total + term
    return total


def tile_specs(width, tile):
    return [
        pl.BlockSpec((width // 3, width), lambda i, n=n: (3 * tile(i) + n, 0))
        for n in range(3)
    ]


def normed(value):
    centered = value - jnp.mean(value, -1, keepdims=True)
    scale = lax.rsqrt(jnp.mean(centered * centered, -1, keepdims=True) + norm_eps)
    return centered * scale, scale


def norm_back(grad, value, gain):
    unit, scale = normed(value)
    inner = grad * gain
    mean = jnp.mean(inner, -1, keepdims=True)
    slope = jnp.mean(inner * unit, -1, keepdims=True)
    return (
        scale * (inner - mean - unit * slope),
        jnp.sum(grad * unit, 0, keepdims=True),
        jnp.sum(grad, 0, keepdims=True),
    )


def forward_kernel(
    hot_ref,
    rows_ref,
    pos_hot_ref,
    pos_ref,
    mask_ref,
    vec_ref,
    w_0,
    w_1,
    w_2,
    x_out,
    a_out,
    qkv_out,
    probs_out,
    o_out,
    mid_out,
    m_out,
    u_out,
    g_out,
    hidden_out,
    final_out,
    cur,
):
    step = pl.program_id(0)
    layer, s = lax.div(step, STEPS), lax.rem(step, STEPS)
    low, f32 = jnp.bfloat16, jnp.float32
    width = cur.shape[1]
    head_dim = width // H

    tile = (w_0, w_1, w_2)

    def vec(row):
        return vec_ref[layer * STEPS + row]

    @pl.when(step == 0)
    def embed():
        cur[...] = along_k(hot_ref[...], rows_ref[...]) + across_k(pos_hot_ref[...], pos_ref[...])

    @pl.when(s == 0)
    def first_norm():
        x_out[layer] = cur[...]
        a_out[layer] = (normed(cur[...])[0] * vec(G1) + vec(S1)).astype(low)

    @pl.when(s < 3)
    def project():
        bias = jnp.where(s == 0, vec(BQ), jnp.where(s == 2, vec(BV), 0.0))
        qkv_out[layer, s] = (tile_across(a_out[layer], tile) + bias).astype(low)

    @pl.when(s == 2)
    def attend():
        lanes = lax.broadcasted_iota(jnp.int32, (1, 2 * head_dim), 1)
        for pair in range(H // 2):
            cols = slice(2 * head_dim * pair, 2 * head_dim * (pair + 1))
            q, k, v = (qkv_out[layer, part, :, cols] for part in range(3))
            total = None
            for side in range(2):
                own = (lanes < head_dim) if side == 0 else (lanes >= head_dim)
                scores = across_k(jnp.where(own, q, jnp.zeros_like(q)), k) * head_dim ** (-0.5)
                scores = jnp.where(mask_ref[...] > 0.0, scores, -1000000000.0)
                shifted = jnp.exp(scores - jnp.max(scores, -1, keepdims=True))
                probs = shifted / jnp.sum(shifted, -1, keepdims=True)
                probs_out[layer, 2 * pair + side] = probs
                term = along_k(probs.astype(low), jnp.where(own, v, jnp.zeros_like(v)))
                total = term if total is None else total + term
            o_out[layer, :, cols] = total.astype(low)

    @pl.when(s == 3)
    def second_norm():
        mid = cur[...] + tile_across(o_out[layer], tile) + vec(BPROJ)
        mid_out[layer] = mid
        m_out[layer] = (normed(mid)[0] * vec(G2) + vec(S2)).astype(low)
        cur[...] = mid + vec(BOUT)

    @pl.when((s >= 4) & (s < 8))
    def widen():
        u = tile_across(m_out[layer], tile) + vec(BFC + s - 4)
        u_out[layer, s - 4] = u
        g = 0.5 * u * (1.0 + jnp.tanh(GELU_A * (u + GELU_B * (u * u * u))))
        g_out[layer, s - 4] = g.astype(low)

    @pl.when(s >= 8)
    def narrow():
        cur[...] += tile_along(g_out[layer, s - 8], tile)

    @pl.when(step == 2 * STEPS - 1)
    def last_norm():
        hidden_out[...] = cur[...]
        final_out[...] = (normed(cur[...])[0] * vec_ref[2 * STEPS] + vec_ref[2 * STEPS + 1]).astype(low)


def forward_layers(hot, rows, pos_hot, pos, mask, vecs, mats):
    tok, width = hot.shape[0], rows.shape[1]
    low, f32 = jnp.bfloat16, jnp.float32
    shape = jax.ShapeDtypeStruct
    vmem = pl.BlockSpec(memory_space=pltpu.VMEM)
    return pl.pallas_call(
        forward_kernel,
        grid=(2 * STEPS,),
        out_shape=(
            shape((2, tok, width), f32),
            shape((2, tok, width), low),
            shape((2, 3, tok, width), low),
            shape((2, H, tok, tok), f32),
            shape((2, tok, width), low),
            shape((2, tok, width), f32),
            shape((2, tok, width), low),
            shape((2, 4, tok, width), f32),
            shape((2, 4, tok, width), low),
            shape((tok, width), f32),
            shape((tok, width), low),
        ),
        in_specs=[vmem] * 6 + tile_specs(width, lambda i: i),
        out_specs=(vmem,) * 11,
        scratch_shapes=[pltpu.VMEM((tok, width), f32)],
        compiler_params=pltpu.CompilerParams(vmem_limit_bytes=58 * 2**20),
        cost_estimate=pl.CostEstimate(
            flops=2 * tok * mats.size, bytes_accessed=2 * mats.size, transcendentals=0
        ),
        name="forward_layers",
    )(hot, rows, pos_hot, pos, mask, vecs, mats, mats, mats)


def backward_kernel(
    grad_ref,
    hidden_ref,
    vec_ref,
    x_ref,
    a_ref,
    qkv_ref,
    probs_ref,
    o_ref,
    mid_ref,
    m_ref,
    u_ref,
    g_ref,
    w_0,
    w_1,
    w_2,
    dx_out,
    vec_out,
    acc_out,
    sums_out,
    cur,
    wide,
    du_s,
    dqkv_s,
    left_s,
    right_s,
    own_s,
    send_s,
    recv_s,
    acc_0,
    acc_1,
    level_1,
    half_0,
    full_0,
    send,
    recv,
    send_pair,
    recv_pair,
    local,
):
    step = pl.program_id(0)
    layer, s = 1 - lax.div(step, STEPS), lax.rem(step, STEPS)
    low, f32 = jnp.bfloat16, jnp.float32
    tok, width = cur.shape
    half = width // 2
    head_dim = width // H
    at, core = place()
    sibling = device_at(at, 1 - core)
    sums = Reduction(at, core, send, recv)
    sums.level = {(0, 1): acc_1, 1: level_1}
    sums.halves, sums.fulls = {0: half_0}, {0: full_0}
    last = 2 * STEPS
    tile = (w_0, w_1, w_2)

    def vec(row):
        return vec_ref[layer * STEPS + row]

    def put(row, value):
        vec_out[layer * STEPS + row] = value

    def pair_copy(slot):
        return pltpu.make_async_remote_copy(
            src_ref=send_s.at[slot],
            dst_ref=recv_s.at[slot],
            send_sem=send_pair.at[slot],
            recv_sem=recv_pair.at[slot],
            device_id=sibling,
            device_id_type=pl.DeviceIdType.MESH,
        )

    def set_right(value):
        right_s[:, :half] = jnp.where(core == 0, value[:, :half], value[:, half:])
        right_s[:, half:] = jnp.where(core == 0, value[:, half:], value[:, :half])

    @pl.when(step == 0)
    def enter():
        greet(neighbours(at, core))
        dx, dg, ds = norm_back(grad_ref[...], hidden_ref[...], vec_ref[last])
        cur[...] = dx
        vec_out[last] = dg
        vec_out[last + 1] = ds

    def collect(before):
        slot, b = before % 2, before % STEPS
        acc = acc_1 if before < STEPS else acc_0
        tile_at = TILE_ORDER[b]
        pair_copy(slot).wait_recv()
        granule = acc.shape[4]
        count = width // granule
        for g in range(count):
            block, p = divmod(tile_at * count + g, 3)
            here = slice(g * granule, (g + 1) * granule)
            value = own_s[here, :].astype(f32) + recv_s[slot, here, :].astype(f32)
            acc[block // (RING * RING), block // RING % RING, block % RING, p] = value.astype(low)

    for n in range(1, last + 1):
        pl.when(step == n)(lambda n=n: collect(n - 1))

    pl.when(step == STEPS)(lambda: sums.start(1, 0))
    pl.when(step == STEPS + 4)(lambda: sums.turn(1, 0))

    @pl.when((s == 0) & (step < last))
    def begin():
        put(BOUT, jnp.sum(cur[...], 0, keepdims=True))
        set_right(cur[...].astype(low))
        wide[...] = cur[...].astype(low)

    @pl.when((s < 4) & (step < last))
    def through_gelu():
        dg = tile_across(wide[...], tile)
        u = u_ref[layer, s]
        square = u * u
        t = jnp.tanh(GELU_A * (u + GELU_B * (square * u)))
        slope = 0.5 * (1.0 + t) + (0.5 * GELU_A) * u * (1.0 - t * t) * (1.0 + (3.0 * GELU_B) * square)
        du = dg * slope
        put(BFC + s, jnp.sum(du, 0, keepdims=True))
        du_s[s] = du.astype(low)
        left_s[...] = g_ref[layer, s]

    @pl.when(s == 4)
    def begin_fc():
        set_right(m_ref[layer])
        dx_out[...] = jnp.zeros_like(dx_out)

    @pl.when((s >= 4) & (s < 8))
    def through_fc():
        left = du_s[s - 4]
        dx_out[...] += tile_along(left, tile)
        left_s[...] = left

    @pl.when(s == 8)
    def through_attention():
        dx, dg, ds = norm_back(dx_out[...], mid_ref[layer], vec(G2))
        put(G2, dg)
        put(S2, ds)
        cur[...] = cur[...] + dx
        put(BPROJ, jnp.sum(cur[...], 0, keepdims=True))
        mid_low = cur[...].astype(low)
        left_s[...] = mid_low
        set_right(o_ref[layer])
        wide[...] = tile_along(mid_low, tile).astype(low)
        lanes = lax.broadcasted_iota(jnp.int32, (1, 2 * head_dim), 1)
        scale = head_dim ** (-0.5)
        for pair in range(H // 2):
            cols = slice(2 * head_dim * pair, 2 * head_dim * (pair + 1))
            q, k, v = (qkv_ref[layer, part, :, cols] for part in range(3))
            do = wide[:, cols]
            parts = [None] * 3
            for side in range(2):
                own = (lanes < head_dim) if side == 0 else (lanes >= head_dim)
                keep = lambda item, own=own: jnp.where(own, item, jnp.zeros_like(item))
                probs = probs_ref[layer, 2 * pair + side]
                do_own = keep(do)
                dprobs = across_k(do_own, v)
                dscores = probs * (dprobs - jnp.sum(probs * dprobs, -1, keepdims=True))
                dlow = (dscores * scale).astype(low)
                terms = (
                    along_k(dlow, keep(k)),
                    over_rows(dlow, keep(q)),
                    over_rows(probs.astype(low), do_own),
                )
                parts = [
                    term if held is None else held + term for held, term in zip(parts, terms)
                ]
            for part in range(3):
                dqkv_s[part, :, cols] = parts[part].astype(low)
            vec_out[layer * STEPS + BQ, :, cols] = jnp.sum(parts[0], 0, keepdims=True)
            vec_out[layer * STEPS + BV, :, cols] = jnp.sum(parts[2], 0, keepdims=True)

    @pl.when(s == 9)
    def begin_qkv():
        set_right(a_ref[layer])
        dx_out[...] = jnp.zeros_like(dx_out)

    @pl.when(s >= 9)
    def through_qkv():
        left = dqkv_s[s - 9]
        dx_out[...] += tile_along(left, tile)
        left_s[...] = left

    @pl.when(step < last)
    def gradient():
        slot = lax.rem(step, 2)
        grad = over_rows(left_s[...], right_s[...])
        pl.when(step >= 2)(lambda: pair_copy(slot).wait_send())
        own_s[...] = grad[:, :half].astype(low)
        send_s[slot] = grad[:, half:].astype(low)
        pair_copy(slot).start()

    @pl.when(s == STEPS - 1)
    def end_layer():
        dx, dg, ds = norm_back(dx_out[...], x_ref[layer], vec(G1))
        put(G1, dg)
        put(S1, ds)
        cur[...] = cur[...] + dx

    @pl.when(step == last)
    def leave():
        copies = []
        for n in range(RING * RING):
            spot = (n // RING, n % RING)
            op = pltpu.make_async_copy(acc_0.at[spot], acc_out.at[spot], local.at[n])
            op.start()
            copies.append(op)
        dx_out[...] = cur[...]
        sums.finish(1, 0)
        copies.append(pltpu.make_async_copy(level_1.at[0], sums_out, local.at[RING * RING]))
        copies[-1].start()
        for slot in range(2):
            pair_copy(slot).wait_send()
        sums.drain(1, 0)
        for op in copies:
            op.wait()


def backward_layers(grad, hidden, vecs, saved, mats):
    tok, width = grad.shape
    low, f32 = jnp.bfloat16, jnp.float32
    shape = jax.ShapeDtypeStruct
    vmem = pl.BlockSpec(memory_space=pltpu.VMEM)
    hbm = pl.BlockSpec(memory_space=pltpu.HBM)
    torus, half, part = (RING, RING, RING), width // 2, 48

    def tile(i):
        i = jnp.minimum(i, 2 * STEPS - 1)
        layer, s = 1 - i // STEPS, i % STEPS
        return layer * STEPS + jnp.where(
            s < 4, 8 + s, jnp.where(s < 8, s, jnp.where(s == 8, 3, s - 9))
        )

    return pl.pallas_call(
        backward_kernel,
        grid=(2 * STEPS + 1,),
        out_shape=(
            shape((tok, width), f32),
            shape((2 * STEPS + 2, 1, width), f32),
            shape(torus + (3, part, half), low),
            shape((3, RING, RING, part, half), low),
        ),
        in_specs=[vmem] * 12 + tile_specs(width, tile),
        out_specs=(vmem, vmem, hbm, hbm),
        scratch_shapes=[
            pltpu.VMEM((tok, width), f32),
            pltpu.VMEM((tok, width), low),
            pltpu.VMEM((4, tok, width), low),
            pltpu.VMEM((3, tok, width), low),
            pltpu.VMEM((tok, width), low),
            pltpu.VMEM((tok, width), low),
            pltpu.VMEM((width, half), low),
            pltpu.VMEM((2, width, half), low),
            pltpu.VMEM((2, width, half), low),
            pltpu.VMEM(torus + (3, part, half), low),
            pltpu.VMEM(torus + (3, part, half), low),
            pltpu.VMEM((1, 3, RING, RING, part, half), low),
            pltpu.VMEM((1, 3, 2, 2, RING, part, half), low),
            pltpu.VMEM((1, 3, 2, RING, RING, part, half), low),
            pltpu.SemaphoreType.DMA((12,)),
            pltpu.SemaphoreType.DMA((12,)),
            pltpu.SemaphoreType.DMA((2,)),
            pltpu.SemaphoreType.DMA((2,)),
            pltpu.SemaphoreType.DMA((RING * RING + 1,)),
        ],
        compiler_params=pltpu.CompilerParams(
            collective_id=4, has_side_effects=True, vmem_limit_bytes=60 * 2**20
        ),
        cost_estimate=pl.CostEstimate(
            flops=4 * tok * mats.size, bytes_accessed=2 * mats.size, transcendentals=0
        ),
        name="backward_layers",
    )(grad, hidden, vecs, *saved, mats, mats, mats)


def doc_info(doc_lens, tok_count, total_docs):
    doc_ends = jnp.cumsum(doc_lens)
    places = jnp.arange(tok_count, dtype=jnp.int32)
    seg_ids = jnp.sum((places[:, None] >= doc_ends[None, :]).astype(jnp.int32), 1)
    one_hot = seg_ids[:, None] == jnp.arange(doc_lens.shape[0], dtype=jnp.int32)[None, :]
    starts = doc_ends - doc_lens
    pos_ids = places - jnp.sum(jnp.where(one_hot, starts[None, :], 0), 1)
    doc_len = jnp.sum(jnp.where(one_hot, doc_lens[None, :], 0), 1)
    weights = 1.0 / (doc_len.astype(jnp.float32) * total_docs)
    return (seg_ids, pos_ids, weights)


def device_rise(first, count, devices):
    places = first + jnp.arange(count, dtype=jnp.int32)
    return 1.0 + 2.0 * places.astype(jnp.float32) / (devices - 1)


def contract(left, right, left_dim, right_dim):
    return lax.dot_general(
        left, right, (((left_dim,), (right_dim,)), ((), ())), preferred_element_type=jnp.float32
    )


def renew(weight, moment, average, grad, factor):
    clipped = factor * grad
    moment_next = momentum_coef * moment + clipped
    weight_next = weight - learn_rate * (clipped + momentum_coef * moment_next)
    average_next = ema_decay * average + (1.0 - ema_decay) * weight_next
    return (moment_next, weight_next, average_next, weight_next.astype(jnp.bfloat16))


SMALL_ROWS, LANES = 16, 128


def pack_small(values):
    room = SMALL_ROWS * LANES - values.shape[-1]
    pads = [(0, 0)] * (values.ndim - 1) + [(0, room)]
    return jnp.pad(values, pads).reshape(values.shape[:-1] + (SMALL_ROWS, LANES))


def per_device(
    token_ids,
    targets,
    lengths,
    embed_table,
    embed_moment,
    embed_average,
    blocks,
    block_moment,
    block_average,
    pos_table,
    pos_moment,
    pos_average,
    vectors,
    vector_moment,
    vector_average,
):
    devices = lax.axis_size(("dp", "vocab"))
    vocab_count = lax.axis_size("vocab")
    dp_count = lax.axis_size("dp")
    vocab_at = lax.axis_index("vocab")
    data_at = lax.axis_index("dp")
    tok = token_ids.shape[0]
    own_rows, width = embed_table.shape
    capacity = max(2, 2 * tok // devices)
    low = jnp.bfloat16
    blocks, block_moment, block_average = (
        jnp.transpose(item, (0, 2, 1)) for item in (blocks, block_moment, block_average)
    )
    pos_rows, pos_cols = pos_table.shape
    vec_own = vectors.shape[0]
    table_low = embed_table.astype(low)
    pad_rows = -own_rows % 16
    table_padded = jnp.pad(table_low, ((0, pad_rows), (0, 0)))
    slot_rows = own_rows + pad_rows

    owners = token_ids // own_rows
    tokens = jnp.arange(tok, dtype=jnp.int32)
    earlier = jnp.sum((owners[:, None] == owners[None, :]) & (tokens[None, :] < tokens[:, None]), 1)
    slot_hot = (owners * capacity + earlier)[:, None] == jnp.arange(
        devices * capacity, dtype=jnp.int32
    )[None, :]
    send_rows = jnp.sum(jnp.where(slot_hot, (token_ids % own_rows)[:, None], 0), 0)
    slot_hot = slot_hot.astype(low)
    local_rows = lax.all_to_all(send_rows, ("dp", "vocab"), split_axis=0, concat_axis=0, tiled=True)
    asked = (local_rows[:, None] == jnp.arange(own_rows, dtype=jnp.int32)[None, :]).astype(low)
    fetched = jnp.dot(asked, table_low, preferred_element_type=jnp.float32).astype(low)
    returned_rows = lax.all_to_all(
        fetched.reshape(devices, capacity, width),
        ("dp", "vocab"),
        split_axis=0,
        concat_axis=0,
        tiled=True,
    ).reshape(devices * capacity, width)
    blocks, returned_rows = lax.optimization_barrier((blocks, returned_rows))
    table_slice = lax.all_gather(table_padded, "dp", axis=0, tiled=True)
    target_owners = targets // own_rows
    codes = (
        (target_owners % vocab_count) * (dp_count * slot_rows)
        + (target_owners // vocab_count) * slot_rows
        + targets % own_rows
    )

    small = pack_small(
        jnp.concatenate([jnp.transpose(pos_table).reshape(-1), vectors]).astype(low)
    )
    mats_all, small_all = gather_weights(blocks, small)
    small_all = small_all.reshape(devices, -1)
    pos_low_t = small_all[:, : pos_rows * pos_cols].reshape(width, pos_rows)
    vecs_all = (
        small_all[:, pos_rows * pos_cols : pos_rows * pos_cols + vec_own]
        .reshape(-1)
        .astype(jnp.float32)
    )
    lens_group = lengths[0]
    seg_group, pos_group, weight_group = jax.vmap(
        partial(doc_info, tok_count=tok, total_docs=devices * lens_group.shape[1])
    )(lens_group)
    weight_group = weight_group * device_rise(data_at * vocab_count, vocab_count, devices)[:, None]
    seg_ids = lax.dynamic_index_in_dim(seg_group, vocab_at, 0, keepdims=False)
    pos_ids = lax.dynamic_index_in_dim(pos_group, vocab_at, 0, keepdims=False)
    places = jnp.arange(tok, dtype=jnp.int32)
    attn_mask = (seg_ids[:, None] == seg_ids[None, :]) & (places[None, :] <= places[:, None])

    pos_hot = (pos_ids[:, None] == jnp.arange(pos_rows, dtype=jnp.int32)[None, :]).astype(low)
    vec_rows = vecs_all.reshape(-1, 1, width)
    *saved, hidden, final_low = forward_layers(
        slot_hot,
        returned_rows,
        pos_hot,
        pos_low_t,
        attn_mask.astype(jnp.float32),
        vec_rows,
        mats_all,
    )
    grad_final, table_part, token_losses = head(
        final_low, jnp.broadcast_to(codes[None, :], (8, tok)), weight_group, table_slice
    )
    loss_part = jnp.sum(token_losses)
    table_grad = lax.psum_scatter(table_part, "dp", scatter_dimension=0, tiled=True)[
        :own_rows
    ].astype(jnp.float32)
    grad_hidden, grad_vecs, grad_acc, grad_sums = backward_layers(
        grad_final, hidden, vec_rows, saved, mats_all
    )
    grad_pos = lax.dot_general(
        grad_hidden,
        pos_hot.astype(jnp.float32),
        (((0,), (0,)), ((), ())),
        precision=lax.Precision.HIGHEST,
    )
    send_grads = contract(slot_hot, grad_hidden.astype(low), 0, 0).astype(low)
    grad_acc, send_grads = lax.optimization_barrier((grad_acc, send_grads))
    back_grads = lax.all_to_all(
        send_grads.reshape(devices, capacity, width),
        ("dp", "vocab"),
        split_axis=0,
        concat_axis=0,
        tiled=True,
    ).reshape(-1, width)
    small_grads = pack_small(
        jnp.concatenate(
            [grad_pos.reshape(devices, -1), grad_vecs.reshape(devices, -1)], 1
        )
    )
    mats_shard, small_shard = reduce_weights(grad_acc, grad_sums, small_grads)
    small_shard = small_shard.reshape(-1)
    pos_shard = small_shard[: pos_rows * pos_cols].reshape(pos_cols, pos_rows)
    vec_shard = small_shard[pos_rows * pos_cols : pos_rows * pos_cols + vec_own]
    table_grad = table_grad + contract(asked, back_grads, 0, 0)
    local_squares = (
        jnp.sum(table_grad * table_grad)
        + jnp.sum(mats_shard * mats_shard)
        + jnp.sum(pos_shard * pos_shard)
        + jnp.sum(vec_shard * vec_shard)
    )
    both_sums = sum_all(
        jnp.broadcast_to(jnp.pad(jnp.stack([loss_part, local_squares]), (0, 6))[:, None], (8, LANES))
    )
    loss_sum, squares = both_sums[0, 0], both_sums[1, 0]
    grad_norm = jnp.sqrt(squares)
    factor = clip_bound / jnp.maximum(grad_norm, clip_bound)
    embed_out = renew(embed_table, embed_moment, embed_average, table_grad, factor)
    block_out = renew(blocks, block_moment, block_average, mats_shard, factor)
    block_out = tuple(jnp.transpose(item, (0, 2, 1)) for item in block_out)
    pos_out = renew(
        jnp.transpose(pos_table),
        jnp.transpose(pos_moment),
        jnp.transpose(pos_average),
        pos_shard,
        factor,
    )
    pos_out = tuple(jnp.transpose(item) for item in pos_out)
    vector_out = renew(vectors, vector_moment, vector_average, vec_shard, factor)
    return (loss_sum, grad_norm) + embed_out + block_out + pos_out + vector_out


def solution(mesh):
    table = P(("dp", "vocab"), None)
    cols = P(None, None, ("dp", "vocab"))
    pos = P(None, ("dp", "vocab"))
    vec = P(("dp", "vocab"))
    return jax.shard_map(
        per_device,
        mesh=mesh,
        in_specs=(vec, vec, P("dp", None, None))
        + (table,) * 3
        + (cols,) * 3
        + (pos,) * 3
        + (vec,) * 3,
        out_specs=(P(), P()) + (table,) * 4 + (cols,) * 4 + (pos,) * 4 + (vec,) * 4,
        check_vma=False,
    )
```

```python
from functools import partial

import jax
import jax.numpy as jnp
from jax import lax
from jax.experimental import pallas as pl
from jax.experimental.pallas import tpu as pltpu
from jax.sharding import PartitionSpec as P

H = 12
RING = 4
ORDERS = ((2, 1, 0), (1, 0, 2), (0, 2, 1))

norm_eps = 1e-05
clip_bound = 0.01
learn_rate = 10000.0
momentum_coef = 0.5
ema_decay = 0.5


def place():
    dp = lax.axis_index("dp")
    vocab = lax.axis_index("vocab")
    return (lax.div(dp, RING), lax.rem(dp, RING), lax.div(vocab, 2)), lax.rem(vocab, 2)


def device_at(at, core):
    return (at[0] * RING + at[1], at[2] * 2 + core)


def moved(at, axis, by):
    out = list(at)
    out[axis] = lax.rem(at[axis] + by, RING)
    return tuple(out)


class Wires:
    def __init__(self, send, recv):
        self.send, self.recv, self.count, self.live = send, recv, 0, []

    def copy(self, src, dst, device):
        number = self.count
        self.count += 1
        op = pltpu.make_async_remote_copy(
            src_ref=src,
            dst_ref=dst,
            send_sem=self.send.at[number],
            recv_sem=self.recv.at[number],
            device_id=device,
            device_id_type=pl.DeviceIdType.MESH,
        )
        op.start()
        self.live.append(op)
        return op

    def drain(self):
        for op in self.live:
            op.wait_send()


def greet(devices):
    barrier = pltpu.get_barrier_semaphore()
    for device in devices:
        pl.semaphore_signal(
            barrier, inc=1, device_id=device, device_id_type=pl.DeviceIdType.MESH
        )
    pl.semaphore_wait(barrier, len(devices))


def ring_peers(at, core):
    near = [device_at(moved(at, axis, by), core) for axis in range(3) for by in range(1, RING)]
    return near + [device_at(at, 1 - core)]


def neighbours(at, core):
    near = [device_at(moved(at, axis, by), core) for axis in range(3) for by in (1, RING - 1)]
    return near + [device_at(at, 1 - core)]


def gather_kernel(
    mine_ref,
    small_ref,
    table_ref,
    spread_ref,
    earlier_ref,
    slot_ref,
    swap_ref,
    out_ref,
    small_out,
    rows_out,
    asked_out,
    peer,
    block,
    asked_rows,
    over_z,
    over_y,
    sorted_rows,
    over_x,
    send,
    recv,
    local,
):
    at, core = place()
    z, y, x = at
    rows, half = mine_ref.shape[1], mine_ref.shape[2] // 2
    part = 2 * rows // 3
    low, f32 = jnp.bfloat16, jnp.float32
    sibling = device_at(at, 1 - core)
    greet(ring_peers(at, core))
    wires = Wires(send, recv)
    cols = pl.ds(pl.multiple_of(core * half, half), half)
    other = pl.ds(pl.multiple_of((1 - core) * half, half), half)

    swap = wires.copy(mine_ref.at[:, :, other], peer, sibling)
    small_out[z, y, x, core] = small_ref[...]

    def right(axis):
        return device_at(moved(at, axis, 1), core)

    def left(axis):
        return device_at(moved(at, axis, RING - 1), core)

    def all_around(axis, src_of, dst):
        out = []
        for by in range(1, RING):
            there = moved(at, axis, by)
            out.append(wires.copy(src_of(there[axis]), dst, device_at(there, core)))
        return out

    def small_start(phase):
        index = [z, y, x]
        for axis in ORDERS[0][:phase]:
            index[axis] = pl.ds(0, RING)
        own = small_out.at[index[0], index[1], index[2], core]
        return all_around(ORDERS[0][phase], lambda c: own, own)

    def arrive(ops):
        for op in ops:
            op.wait_recv()

    small_ops = small_start(0)
    swap.wait_recv()
    for layer in range(2):
        own = jnp.where(core == 0, mine_ref[layer, :, :half], mine_ref[layer, :, half:])
        got = peer[layer]
        both = jnp.concatenate(
            [jnp.where(core == 0, own, got), jnp.where(core == 0, got, own)], 0
        )
        block[layer] = both.astype(low)
    block_local = []
    for layer in range(2):
        op = pltpu.make_async_copy(
            block.at[layer], out_ref.at[layer, z, y, x, :, cols], local.at[layer]
        )
        op.start()
        block_local.append(op)

    def bundle(layer, p, phase, c, piece=None):
        order = ORDERS[p]
        index = list(at)
        index[order[phase]] = c
        for axis in order[:phase]:
            index[axis] = pl.ds(0, RING)
        first, count = p * part, part
        if piece is not None:
            if phase == 0:
                first, count = (first, 32) if piece == 0 else (first + 32, part - 32)
            else:
                index[order[0]] = pl.ds(2 * piece, 2)
        return out_ref.at[layer, index[0], index[1], index[2], pl.ds(first, count), cols]

    chains = [(layer, p) for layer in range(2) for p in range(3)]
    pending = []
    steps, forwards = {}, {}

    def start(phase):
        for key in chains:
            layer, p = key
            axis = ORDERS[p][phase]
            src = bundle(layer, p, phase, at[axis])
            if phase == 2:
                pending.append(wires.copy(src, src, sibling))
            steps[key] = (wires.copy(src, src, right(axis)), wires.copy(src, src, left(axis)))

    def forward(phase):
        for key in chains:
            layer, p = key
            axis = ORDERS[p][phase]
            before, after = lax.rem(at[axis] + 3, RING), lax.rem(at[axis] + 1, RING)
            steps[key][0].wait_recv()
            src = bundle(layer, p, phase, before, 0)
            one = wires.copy(src, src, right(axis))
            steps[key][1].wait_recv()
            src = bundle(layer, p, phase, after, 1)
            two = wires.copy(src, src, left(axis))
            forwards[key] = (one, two)
            if phase == 2:
                for c in (before, after):
                    src = bundle(layer, p, phase, c)
                    pending.append(wires.copy(src, src, sibling))

    def finish(phase):
        for key in chains:
            layer, p = key
            axis = ORDERS[p][phase]
            across = lax.rem(at[axis] + 2, RING)
            for piece in range(2):
                forwards[key][piece].wait_recv()
                if phase == 2:
                    src = bundle(layer, p, phase, across, piece)
                    pending.append(wires.copy(src, src, sibling))

    arrive(block_local_wait(block_local))
    start(0)
    arrive(small_ops)
    small_ops = small_start(1)
    forward(0)
    arrive(small_ops)
    small_ops = small_start(2)
    finish(0)
    start(1)
    arrive(small_ops)
    own = small_out.at[:, :, :, core]
    small_ops = [wires.copy(own, own, sibling)]
    forward(1)
    arrive(small_ops)

    count = 2 * RING**3
    smalls = small_out[...].reshape((count,) + small_ref.shape)
    high, rest = (
        jnp.dot(spread_ref[...], smalls[:, IDS_ROW + n, :], preferred_element_type=f32)
        for n in range(2)
    )
    own_rows = TABLE_ROWS
    me = ((z * RING + y) * RING + x) * 2 + core
    local_id = high * 256.0 + rest - (me * own_rows).astype(f32)
    mine = (local_id >= 0.0) & (local_id < float(own_rows))
    rank = jnp.dot(
        jnp.where(mine, 1.0, 0.0).astype(low), earlier_ref[...], preferred_element_type=f32
    )
    picked = jnp.where(mine & (rank == slot_ref[...]), local_id, 0.0)
    row = jnp.sum(picked, 1, keepdims=True).astype(jnp.int32)
    places = lax.broadcasted_iota(jnp.int32, asked_out.shape, 1)
    asked = jnp.where(places == row, 1.0, 0.0).astype(low)
    asked_out[...] = asked
    found = jnp.dot(asked, table_ref[...], preferred_element_type=f32).astype(low)
    asked_rows[...] = found.reshape(asked_rows.shape)
    over_z[z] = asked_rows[z]
    row_ops = all_around(0, lambda c: asked_rows.at[c], over_z.at[z])

    finish(1)
    start(2)
    arrive(row_ops)
    over_y[y] = over_z[:, y]
    row_ops = all_around(1, lambda c: over_z.at[:, c], over_y.at[y])
    forward(2)
    arrive(row_ops)
    sorted_rows[...] = (
        jnp.dot(
            swap_ref[...], over_y[...].reshape(2 * count, table_ref.shape[1]), preferred_element_type=f32
        )
        .astype(low)
        .reshape(sorted_rows.shape)
    )
    over_x[x] = sorted_rows[x]
    row_ops = all_around(2, lambda c: sorted_rows.at[c], over_x.at[x])
    finish(2)
    arrive(row_ops)
    pending.append(wires.copy(over_x.at[:, 1 - core], rows_out.at[:, core], sibling))
    rows_out[:, core] = over_x[:, core]
    arrive(pending)
    wires.drain()


def block_local_wait(ops):
    for op in ops:
        op.wait()
    return []


IDS_ROW = 8
TABLE_ROWS = 393
GATHER_COPIES = 1 + 3 * (6 * 4 + 3) + 6 * 5 + 1 + 9 + 1


def gather_weights(mine, small, table, spread, earlier, slots, swap):
    layers, rows, width = mine.shape
    table_rows = table.shape[0]
    count = 2 * RING**3
    low = jnp.bfloat16
    hbm = pl.BlockSpec(memory_space=pltpu.HBM)
    vmem = pl.BlockSpec(memory_space=pltpu.VMEM)
    mats, small_all, fetched, asked = pl.pallas_call(
        gather_kernel,
        out_shape=(
            jax.ShapeDtypeStruct((layers, RING, RING, RING, 2 * rows, width), low),
            jax.ShapeDtypeStruct((RING, RING, RING, 2) + small.shape, low),
            jax.ShapeDtypeStruct((RING, 2, count // 4, width), low),
            jax.ShapeDtypeStruct((2 * count, table_rows), low),
        ),
        in_specs=[vmem] * 7,
        out_specs=(hbm, vmem, vmem, vmem),
        scratch_shapes=[
            pltpu.VMEM((layers, rows, width // 2), jnp.float32),
            pltpu.VMEM((layers, 2 * rows, width // 2), low),
            pltpu.VMEM((RING, RING, 16, width), low),
            pltpu.VMEM((RING, RING, 16, width), low),
            pltpu.VMEM((RING, RING, 16, width), low),
            pltpu.VMEM((RING, 2, count // 4, width), low),
            pltpu.VMEM((RING, 2, count // 4, width), low),
            pltpu.SemaphoreType.DMA((GATHER_COPIES,)),
            pltpu.SemaphoreType.DMA((GATHER_COPIES,)),
            pltpu.SemaphoreType.DMA((2,)),
        ],
        compiler_params=pltpu.CompilerParams(
            collective_id=0, has_side_effects=True, vmem_limit_bytes=58 * 2**20
        ),
        cost_estimate=pl.CostEstimate(flops=0, bytes_accessed=250 * 10**6, transcendentals=0),
        name="gather_weights",
    )(mine, small, table, spread, earlier, slots, swap)
    return (
        mats.reshape(layers * RING**3 * 2 * rows, width),
        small_all.reshape((count,) + small.shape),
        fetched.reshape(2 * count, width),
        asked,
    )


class Reduction:
    def __init__(self, at, core, send, recv):
        self.at, self.core, self.send, self.recv = at, core, send, recv
        self.number, self.level, self.halves, self.fulls = {}, {}, {}, {}
        self.final = None

    def copy(self, key, src, dst, device):
        number = self.number.setdefault(key, len(self.number))
        return pltpu.make_async_remote_copy(
            src_ref=src,
            dst_ref=dst,
            send_sem=self.send.at[number],
            recv_sem=self.recv.at[number],
            device_id=device,
            device_id_type=pl.DeviceIdType.MESH,
        )

    def axes(self, p):
        order = ORDERS[p]
        free = sorted(order[:2])
        return free, free.index(order[1])

    def ring(self, p, step):
        axis = ORDERS[p][2 - step]
        c = self.at[axis]
        right = device_at(moved(self.at, axis, 1), self.core)
        left = device_at(moved(self.at, axis, RING - 1), self.core)
        return c, lax.rem(c + 1, RING), lax.rem(c + 2, RING), lax.rem(c + 3, RING), right, left

    def index(self, layer, p, step, c, piece=None):
        part = 48
        cut, whole = (0, RING) if piece is None else (2 * piece, 2), (0, RING)
        if step == 0:
            free, unused = self.axes(p)
            spot = [c, c, c]
            spot[free[0]], spot[free[1]] = cut, whole
            return spot + [p]
        if step == 1:
            unused, first = self.axes(p)
            spot = [cut, cut]
            spot[first] = c
            return [layer % self.level[1].shape[0], p] + spot
        if piece is None:
            return [layer, p, c]
        return [layer, p, c, pl.ds(0, 32) if piece == 0 else pl.ds(32, part - 32)]

    def view(self, layer, p, step, c, piece=None):
        index = self.index(layer, p, step, c, piece)
        held = self.level[0, layer] if step == 0 else self.level[step]
        return held.at[tuple(pl.ds(*item) if isinstance(item, tuple) else item for item in index)]

    def slot(self, layer, p, step, side, whole):
        store = (self.fulls if whole else self.halves)[step]
        if step == 2 and not whole:
            return store.at[layer, p, side, pl.ds(0, 32 if side == 0 else 16)]
        return store.at[layer % store.shape[0], p, side]

    def half_copies(self, layer, p, step):
        unused, after, across, before, right, left = self.ring(p, step)
        out = []
        for side, device in ((0, right), (1, left)):
            out.append(
                self.copy(
                    (layer, p, step, side),
                    self.view(layer, p, step, across, side),
                    self.slot(layer, p, step, side, False),
                    device,
                )
            )
        return out

    def full_copies(self, layer, p, step):
        unused, after, across, before, right, left = self.ring(p, step)
        out = []
        for side, c, device in ((0, after, right), (1, before, left)):
            out.append(
                self.copy(
                    (layer, p, step, 2 + side),
                    self.view(layer, p, step, c),
                    self.slot(layer, p, step, side, True),
                    device,
                )
            )
        return out

    def add(self, layer, p, step, c, piece, terms, into):
        held = self.level[0, layer] if step == 0 else self.level[step]
        index = self.index(layer, p, step, c, piece)
        sizes = [item[1] for item in index if isinstance(item, tuple)]

        def one(inner):
            places = iter(inner)
            spot = tuple(
                item[0] + next(places) if isinstance(item, tuple) else item for item in index
            )
            value = held[spot].astype(jnp.float32)
            for term in terms:
                value = value + term[tuple(inner) + (slice(None), slice(None))].astype(jnp.float32)
            into(held, spot, inner, value)

        def body(n, unused):
            if len(sizes) == 2:
                for k in range(sizes[1]):
                    one([n, k])
            else:
                one([n])
            return unused

        if sizes:
            lax.fori_loop(0, sizes[0], body, 0)
        else:
            one([])

    def start(self, layer, step):
        for p in range(3):
            for op in self.half_copies(layer, p, step):
                op.start()

    def turn(self, layer, step):
        def back(held, spot, inner, value):
            held[spot] = value.astype(held.dtype)

        for p in range(3):
            unused, after, across, before, right, left = self.ring(p, step)
            halves, fulls = self.half_copies(layer, p, step), self.full_copies(layer, p, step)
            for side, c in ((0, after), (1, before)):
                halves[side].wait_recv()
                self.add(
                    layer, p, step, c, side, [self.slot(layer, p, step, side, False)], back
                )
                fulls[side].start()

    def finish(self, layer, step):
        for p in range(3):
            c = self.ring(p, step)[0]
            for op in self.full_copies(layer, p, step):
                op.wait_recv()
            terms = [self.slot(layer, p, step, side, True) for side in range(2)]

            def up(held, spot, inner, value, p=p):
                if step == 2:
                    self.final[layer, p * 48 : (p + 1) * 48] = value
                else:
                    target = self.level[step + 1]
                    spot = (layer % target.shape[0], p) + tuple(inner)
                    target[spot] = value.astype(target.dtype)

            self.add(layer, p, step, c, None, terms, up)

    def drain(self, layer, step):
        for p in range(3):
            for op in self.half_copies(layer, p, step) + self.full_copies(layer, p, step):
                op.wait_send()


def reduce_kernel(
    acc_ref,
    small_ref,
    rows_ref,
    swap_ref,
    out_ref,
    small_out,
    rows_out,
    acc_0,
    acc_1,
    mid,
    thin,
    half_0,
    half_1,
    half_2,
    full_0,
    full_1,
    full_2,
    small_acc,
    small_sib,
    small_wide,
    small_mid,
    small_thin,
    final,
    final_peer,
    over_core,
    over_x,
    sorted_rows,
    over_y,
    send,
    recv,
    send_small,
    recv_small,
    local,
):
    at, core = place()
    own_rows, half = final_peer.shape[1], final_peer.shape[2]
    sibling = device_at(at, 1 - core)
    sums = Reduction(at, core, send, recv)
    sums.level = {(0, 0): acc_0, (0, 1): acc_1, 1: mid, 2: thin}
    sums.halves = {0: half_0, 1: half_1, 2: half_2}
    sums.fulls = {0: full_0, 1: full_1, 2: full_2}
    sums.final = final

    accs = (acc_0, acc_1)
    loads = {}
    for layer in (1, 0):
        for n in range(RING * RING):
            spot = (n // RING, n % RING)
            op = pltpu.make_async_copy(
                acc_ref.at[(layer,) + spot], accs[layer].at[spot], local.at[1 + 16 * layer + n]
            )
            op.start()
            loads[layer, n] = op
    small_load = pltpu.make_async_copy(small_ref.at[:, :, :, core], small_acc, local.at[0])
    small_load.start()
    greet(ring_peers(at, core))
    wires = Wires(send_small, recv_small)
    small_swap = wires.copy(small_ref.at[:, :, :, 1 - core], small_sib, sibling)

    order = ORDERS[0]
    slots = (small_wide, small_mid, small_thin)

    def right(axis):
        return device_at(moved(at, axis, 1), core)

    def left(axis):
        return device_at(moved(at, axis, RING - 1), core)

    def small_view(step, c):
        index = list(at)
        index[order[2 - step]] = c
        for axis in order[: 2 - step]:
            index[axis] = slice(None)
        return tuple(index)

    def small_add(step, c, term):
        where = small_view(step, c)
        small_acc[where] = small_acc[where] + term

    def small_start(step):
        axis = order[2 - step]
        across = lax.rem(at[axis] + 2, RING)
        return wires.copy(small_acc.at[small_view(step, across)], slots[step].at[0], right(axis))

    def small_turn(step, op):
        axis = order[2 - step]
        after, before = lax.rem(at[axis] + 1, RING), lax.rem(at[axis] + 3, RING)
        op.wait_recv()
        small_add(step, after, slots[step][0])
        return (
            wires.copy(small_acc.at[small_view(step, after)], slots[step].at[1], right(axis)),
            wires.copy(small_acc.at[small_view(step, before)], slots[step].at[2], left(axis)),
        )

    def small_finish(step, ops):
        for op in ops:
            op.wait_recv()
        small_add(step, at[order[2 - step]], slots[step][1] + slots[step][2])

    z, y, x = at

    def all_around(axis, src_of, dst):
        out = []
        for by in range(1, RING):
            there = moved(at, axis, by)
            out.append(wires.copy(src_of(there[axis]), dst, device_at(there, core)))
        return out

    def arrive(ops):
        for op in ops:
            op.wait_recv()

    for layer in (1, 0):
        for n in range(RING * RING):
            loads[layer, n].wait()
        sums.start(layer, 0)
    row_ops = [wires.copy(rows_ref.at[:, 1 - core], over_core.at[:, core], sibling)]
    over_core[:, core] = rows_ref[:, core]
    small_load.wait()
    small_swap.wait_recv()
    small_acc[...] = small_acc[...] + small_sib[...]
    op = small_start(0)
    arrive(row_ops)
    over_x[x] = over_core[x]
    row_ops = all_around(2, lambda c: over_core.at[c], over_x.at[x])
    sums.turn(1, 0)
    sums.turn(0, 0)
    ops = small_turn(0, op)
    arrive(row_ops)
    count, width = swap_ref.shape[0], rows_ref.shape[3]
    sorted_rows[...] = (
        jnp.dot(
            swap_ref[...], over_x[...].reshape(count, width), preferred_element_type=jnp.float32
        )
        .astype(jnp.bfloat16)
        .reshape(sorted_rows.shape)
    )
    over_y[y] = sorted_rows[y]
    row_ops = all_around(1, lambda c: sorted_rows.at[c], over_y.at[y])
    small_finish(0, ops)
    op = small_start(1)
    sums.finish(1, 0)
    sums.start(1, 1)
    arrive(row_ops)
    rows_out[z] = over_y[:, z]
    row_ops = all_around(0, lambda c: over_y.at[:, c], rows_out.at[z])
    ops = small_turn(1, op)
    sums.finish(0, 0)
    sums.start(0, 1)
    small_finish(1, ops)
    op = small_start(2)
    sums.turn(1, 1)
    ops = small_turn(2, op)
    sums.turn(0, 1)
    sums.finish(1, 1)
    sums.start(1, 2)
    sums.finish(0, 1)
    sums.start(0, 2)
    small_finish(2, ops)
    sums.turn(1, 2)
    sums.turn(0, 2)
    sums.finish(1, 2)
    sums.finish(0, 2)
    arrive(row_ops)

    theirs = pl.ds(pl.multiple_of((1 - core) * own_rows, own_rows), own_rows)
    swap = wires.copy(final.at[:, theirs], final_peer, sibling)
    small_out[...] = small_acc[at]
    swap.wait_recv()
    for layer in range(2):
        own = jnp.where(core == 0, final[layer, :own_rows], final[layer, own_rows:])
        got = final_peer[layer]
        out_ref[layer, :, :half] = jnp.where(core == 0, own, got)
        out_ref[layer, :, half:] = jnp.where(core == 0, got, own)
    for layer in range(2):
        for step in range(3):
            sums.drain(layer, step)
    wires.drain()


def reduce_weights(acc, small, rows_back, swap):
    part, half = acc.shape[5:]
    rows = 3 * part
    torus = (RING, RING, RING)
    small_shape = small.shape[1:]
    hbm = pl.BlockSpec(memory_space=pltpu.HBM)
    vmem = pl.BlockSpec(memory_space=pltpu.VMEM)
    low = jnp.bfloat16
    return pl.pallas_call(
        reduce_kernel,
        out_shape=(
            jax.ShapeDtypeStruct((2, rows // 2, 2 * half), jnp.float32),
            jax.ShapeDtypeStruct(small_shape, jnp.float32),
            jax.ShapeDtypeStruct((RING, RING, 16, 2 * half), low),
        ),
        in_specs=[hbm, hbm, vmem, vmem],
        out_specs=(vmem, vmem, vmem),
        scratch_shapes=[
            pltpu.VMEM(torus + (3, part, half), low),
            pltpu.VMEM(torus + (3, part, half), low),
            pltpu.VMEM((2, 3, RING, RING, part, half), low),
            pltpu.VMEM((2, 3, RING, part, half), low),
            pltpu.VMEM((2, 3, 2, 2, RING, part, half), low),
            pltpu.VMEM((2, 3, 2, 2, part, half), low),
            pltpu.VMEM((2, 3, 2, 32, half), low),
            pltpu.VMEM((2, 3, 2, RING, RING, part, half), low),
            pltpu.VMEM((2, 3, 2, RING, part, half), low),
            pltpu.VMEM((2, 3, 2, part, half), low),
            pltpu.VMEM(torus + small_shape, jnp.float32),
            pltpu.VMEM(torus + small_shape, jnp.float32),
            pltpu.VMEM((3, RING, RING) + small_shape, jnp.float32),
            pltpu.VMEM((3, RING) + small_shape, jnp.float32),
            pltpu.VMEM((3,) + small_shape, jnp.float32),
            pltpu.VMEM((2, rows, half), jnp.float32),
            pltpu.VMEM((2, rows // 2, half), jnp.float32),
            pltpu.VMEM((RING, 2, 32, 2 * half), low),
            pltpu.VMEM((RING, 2, 32, 2 * half), low),
            pltpu.VMEM((RING, RING, 16, 2 * half), low),
            pltpu.VMEM((RING, RING, 16, 2 * half), low),
            pltpu.SemaphoreType.DMA((72,)),
            pltpu.SemaphoreType.DMA((72,)),
            pltpu.SemaphoreType.DMA((21,)),
            pltpu.SemaphoreType.DMA((21,)),
            pltpu.SemaphoreType.DMA((33,)),
        ],
        compiler_params=pltpu.CompilerParams(
            collective_id=1, has_side_effects=True, vmem_limit_bytes=58 * 2**20
        ),
        cost_estimate=pl.CostEstimate(flops=0, bytes_accessed=280 * 10**6, transcendentals=0),
        name="reduce_weights",
    )(acc, small.reshape(torus + (2,) + small_shape), rows_back, swap)


def sum_kernel(in_ref, out_ref, slots, send, recv):
    at, core = place()
    sibling = device_at(at, 1 - core)
    partners = [sibling] + [
        device_at(moved(at, axis, by), core) for axis in range(3) for by in range(1, RING)
    ]
    greet(partners)
    wires = Wires(send, recv)
    slots[0, core] = in_ref[...]
    swap = wires.copy(in_ref, slots.at[0, core], sibling)
    swap.wait_recv()
    value = slots[0, 0] + slots[0, 1]
    for axis in range(3):
        slots[1 + axis, at[axis]] = value
        ops = []
        for by in range(1, RING):
            ops.append(
                wires.copy(
                    slots.at[1 + axis, at[axis]],
                    slots.at[1 + axis, at[axis]],
                    device_at(moved(at, axis, by), core),
                )
            )
        for op in ops:
            op.wait_recv()
        value = slots[1 + axis, 0]
        for c in range(1, RING):
            value = value + slots[1 + axis, c]
    out_ref[...] = value
    wires.drain()


def sum_all(value):
    vmem = pl.BlockSpec(memory_space=pltpu.VMEM)
    return pl.pallas_call(
        sum_kernel,
        out_shape=jax.ShapeDtypeStruct(value.shape, jnp.float32),
        in_specs=[vmem],
        out_specs=vmem,
        scratch_shapes=[
            pltpu.VMEM((4, RING) + value.shape, jnp.float32),
            pltpu.SemaphoreType.DMA((10,)),
            pltpu.SemaphoreType.DMA((10,)),
        ],
        compiler_params=pltpu.CompilerParams(collective_id=2, has_side_effects=True),
        name="sum_all",
    )(value)


TILE = 800


def head_kernel(
    f_ref,
    code_ref,
    weight_ref,
    table_ref,
    grad_out,
    dtable_ref,
    loss_ref,
    f_all,
    codes,
    table,
    logits,
    probs,
    tops,
    stats,
    df,
    df_send,
    df_sib,
    ring,
    ring_half,
    ring_full,
    staged,
    send,
    recv,
    load,
    store,
):
    at, core = place()
    x = at[2]
    dp, vocab = lax.axis_index("dp"), lax.axis_index("vocab")
    tok, width = f_ref.shape
    group = f_all.shape[0]
    members = group // tok
    tiles = table.shape[0] // TILE
    low, f32 = jnp.bfloat16, jnp.float32

    def tile_rows(t):
        return pl.ds(pl.multiple_of(t * TILE, TILE), TILE)

    loads = []
    for t in range(tiles):
        op = pltpu.make_async_copy(
            table_ref.at[pl.ds(t * TILE, TILE)], table.at[pl.ds(t * TILE, TILE)], load.at[t]
        )
        op.start()
        loads.append(op)

    peers = [(dp, lax.rem(vocab + by, members)) for by in range(1, members)]
    greet(peers)
    wires = Wires(send, recv)
    sibling = device_at(at, 1 - core)
    right, left = device_at(moved(at, 2, 1), core), device_at(moved(at, 2, 3), core)
    before, after, across = lax.rem(x + 3, RING), lax.rem(x + 1, RING), lax.rem(x + 2, RING)

    def rows_of(at_x, piece=None):
        first = (at_x * 2 + core) * tok
        if piece is None:
            return f_all.at[pl.ds(pl.multiple_of(first, tok), tok)]
        half = tok // 2
        return f_all.at[pl.ds(pl.multiple_of(first + piece * half, half), half)]

    f_all[pl.ds(pl.multiple_of(vocab * tok, tok), tok), :] = f_ref[...]
    own = rows_of(x)
    one, two = wires.copy(own, own, right), wires.copy(own, own, left)
    pending = [wires.copy(own, own, sibling)]
    codes[vocab] = code_ref[...]
    for peer in peers:
        pending.append(wires.copy(codes.at[vocab], codes.at[vocab], peer))
    one.wait_recv()
    one_on = wires.copy(rows_of(before, 0), rows_of(before, 0), right)
    pending.append(wires.copy(rows_of(before), rows_of(before), sibling))
    two.wait_recv()
    two_on = wires.copy(rows_of(after, 1), rows_of(after, 1), left)
    pending.append(wires.copy(rows_of(after), rows_of(after), sibling))
    one_on.wait_recv()
    pending.append(wires.copy(rows_of(across, 0), rows_of(across, 0), sibling))
    two_on.wait_recv()
    pending.append(wires.copy(rows_of(across, 1), rows_of(across, 1), sibling))
    for op in pending:
        op.wait_recv()

    code_row = jnp.concatenate([codes[m, 0:1, :] for m in range(members)], 1) - vocab * table.shape[0]
    code8 = jnp.broadcast_to(code_row, (8, group))
    code16 = jnp.broadcast_to(code_row, (16, group))
    rows8 = lax.broadcasted_iota(jnp.int32, (8, group), 0)
    rows16 = lax.broadcasted_iota(jnp.int32, (16, group), 0)
    slot = TILE // 2
    real = slot - 7
    steps8, steps16 = 5, 5

    def first_pass(t, carry):
        top, total, target = carry
        here = tile_rows(t)
        logits[...] = lax.dot_general(
            table[here, :], f_all[...], (((1,), (1,)), ((), ())), preferred_element_type=f32
        )
        for part in range(2):
            last = pl.ds((part + 1) * slot - 8, 8)
            logits[last, :] = jnp.where(rows8 < 1, logits[last, :], -1e30)

        def look(i, state):
            high, hit = state
            for u in range(steps8):
                first = (i * steps8 + u) * 8
                value = logits[pl.ds(pl.multiple_of(first, 8), 8), :]
                high = jnp.maximum(high, value)
                hit = hit + jnp.where(rows8 + (first + t * TILE) == code8, value, 0.0)
            return high, hit

        high, hit = lax.fori_loop(
            0,
            TILE // (8 * steps8),
            look,
            (jnp.full((8, group), -1e30, f32), jnp.zeros((8, group), f32)),
        )
        top_next = jnp.maximum(top, jnp.max(high, 0, keepdims=True))
        target = target + jnp.sum(hit, 0, keepdims=True)

        def lift(i, acc):
            for u in range(steps16):
                first = (i * steps16 + u) * 16
                value = jnp.exp(logits[pl.ds(pl.multiple_of(first, 16), 16), :] - top_next)
                acc = acc + value
                probs[pl.ds(pl.multiple_of(t * TILE + first, 16), 16), :] = value.astype(low)
            return acc

        acc = lax.fori_loop(
            0, TILE // (16 * steps16), lift, jnp.zeros((16, group), f32)
        )
        total = total * jnp.exp(top - top_next) + jnp.sum(acc, 0, keepdims=True)
        tops[t] = top_next
        return top_next, total, target

    for op in loads:
        op.wait()
    start = (jnp.full((1, group), -1e30, f32), jnp.zeros((1, group), f32), jnp.zeros((1, group), f32))
    found = lax.fori_loop(0, tiles, first_pass, start)
    for k in range(3):
        for m in range(members):
            stats[vocab, k, m : m + 1, :] = found[k][:, m * tok : (m + 1) * tok]
    pending = [wires.copy(stats.at[vocab], stats.at[vocab], peer) for peer in peers]
    for op in pending:
        op.wait_recv()
    peak = stats[0, 0]
    for m in range(1, members):
        peak = jnp.maximum(peak, stats[m, 0])
    total, target = jnp.zeros_like(peak), jnp.zeros_like(peak)
    for m in range(members):
        total = total + stats[m, 1] * jnp.exp(stats[m, 0] - peak)
        target = target + stats[m, 2]
    lse = peak + jnp.log(total)
    weight = weight_ref[...]
    mine = lax.broadcasted_iota(jnp.int32, (members, tok), 0) == vocab
    loss_ref[...] = jnp.where(mine, weight * (lse - target), 0.0)
    lse_row = jnp.concatenate([lse[m : m + 1, :] for m in range(members)], 1)
    weight_row = jnp.concatenate([weight[m : m + 1, :] for m in range(members)], 1)

    df[...] = jnp.zeros_like(df)

    def second_pass(t, unused):
        scale = weight_row * jnp.exp(tops[t] - lse_row)

        def turn(i, unused):
            for u in range(steps16):
                first = t * TILE + (i * steps16 + u) * 16
                here = pl.ds(pl.multiple_of(first, 16), 16)
                value = probs[here, :].astype(f32) * scale
                value = value - jnp.where(rows16 + first == code16, weight_row, 0.0)
                probs[here, :] = value.astype(low)
            return unused

        lax.fori_loop(0, TILE // (16 * steps16), turn, 0)
        here = tile_rows(t)
        df[...] += lax.dot_general(
            probs[here, :], table[here, :], (((0,), (0,)), ((), ())), preferred_element_type=f32
        )
        return unused

    lax.fori_loop(0, tiles, second_pass, 0)

    def third_pass(t):
        if t >= 2:
            stores[t - 2].wait()
        staged[t % 2] = jnp.dot(
            probs[t * TILE : (t + 1) * TILE, :], f_all[...], preferred_element_type=f32
        ).astype(low)
        op = pltpu.make_async_copy(
            staged.at[t % 2], dtable_ref.at[pl.ds(t * TILE, TILE)], store.at[t]
        )
        op.start()
        stores.append(op)

    stores = []
    for m in range(members):
        df_send[m % 2, m // 2] = df[m * tok : (m + 1) * tok, :].astype(low)
    swap = wires.copy(df_send.at[1 - core], df_sib, sibling)
    third_pass(0)
    third_pass(1)
    swap.wait_recv()
    for k in range(RING):
        first = pl.multiple_of((2 * k + core) * tok, tok)
        ring[k] = (df[pl.ds(first, tok), :] + df_sib[k].astype(f32)).astype(low)
    half = tok // 2
    one = wires.copy(ring.at[across, pl.ds(0, half)], ring_half.at[0], right)
    two = wires.copy(ring.at[across, pl.ds(half, half)], ring_half.at[1], left)
    third_pass(2)
    third_pass(3)
    one.wait_recv()
    ring[after, :half] = (ring[after, :half].astype(f32) + ring_half[0].astype(f32)).astype(low)
    one = wires.copy(ring.at[after], ring_full.at[0], right)
    two.wait_recv()
    ring[before, half:] = (ring[before, half:].astype(f32) + ring_half[1].astype(f32)).astype(low)
    two = wires.copy(ring.at[before], ring_full.at[1], left)
    for t in range(4, tiles):
        third_pass(t)
    one.wait_recv()
    two.wait_recv()
    grad_out[...] = ring[x].astype(f32) + ring_full[0].astype(f32) + ring_full[1].astype(f32)
    for op in stores[-2:]:
        op.wait()
    wires.drain()


HEAD_COPIES = 9 + 7 + 7 + 5


def head(final_low, codes, weights, table):
    tok, width = final_low.shape
    rows = table.shape[0]
    members = weights.shape[0]
    group = members * tok
    tiles = rows // TILE
    hbm = pl.BlockSpec(memory_space=pltpu.HBM)
    vmem = pl.BlockSpec(memory_space=pltpu.VMEM)
    low, f32 = jnp.bfloat16, jnp.float32
    return pl.pallas_call(
        head_kernel,
        out_shape=(
            jax.ShapeDtypeStruct((tok, width), f32),
            jax.ShapeDtypeStruct((rows, width), low),
            jax.ShapeDtypeStruct((members, tok), f32),
        ),
        in_specs=[vmem, vmem, vmem, hbm],
        out_specs=(vmem, hbm, vmem),
        scratch_shapes=[
            pltpu.VMEM((group, width), low),
            pltpu.VMEM((members, 8, tok), jnp.int32),
            pltpu.VMEM((rows, width), low),
            pltpu.VMEM((TILE, group), f32),
            pltpu.VMEM((rows, group), low),
            pltpu.VMEM((tiles, 1, group), f32),
            pltpu.VMEM((members, 3, members, tok), f32),
            pltpu.VMEM((group, width), f32),
            pltpu.VMEM((2, RING, tok, width), low),
            pltpu.VMEM((RING, tok, width), low),
            pltpu.VMEM((RING, tok, width), low),
            pltpu.VMEM((2, tok // 2, width), low),
            pltpu.VMEM((2, tok, width), low),
            pltpu.VMEM((2, TILE, width), low),
            pltpu.SemaphoreType.DMA((HEAD_COPIES,)),
            pltpu.SemaphoreType.DMA((HEAD_COPIES,)),
            pltpu.SemaphoreType.DMA((tiles,)),
            pltpu.SemaphoreType.DMA((tiles,)),
        ],
        compiler_params=pltpu.CompilerParams(
            collective_id=3, has_side_effects=True, vmem_limit_bytes=58 * 2**20
        ),
        cost_estimate=pl.CostEstimate(
            flops=6 * group * rows * width, bytes_accessed=4 * rows * width, transcendentals=group * rows
        ),
        name="head",
    )(final_low, codes, weights, table)


TILE_ORDER = (8, 9, 10, 11, 4, 5, 6, 7, 3, 0, 1, 2)
G1, S1, BQ, BV, BPROJ, G2, S2, BFC, BOUT = 0, 1, 2, 3, 4, 5, 6, 7, 11
STEPS = 12
GELU_A, GELU_B = 0.7978845608028654, 0.044715


def across_k(left, right):
    return lax.dot_general(left, right, (((1,), (1,)), ((), ())), preferred_element_type=jnp.float32)


def along_k(left, right):
    return jnp.dot(left, right, preferred_element_type=jnp.float32)


def over_rows(left, right):
    return lax.dot_general(left, right, (((0,), (0,)), ((), ())), preferred_element_type=jnp.float32)


def tile_across(left, tile):
    return jnp.concatenate([across_k(left, block[...]) for block in tile], 1)


def tile_along(left, tile):
    total = None
    for n, block in enumerate(tile):
        rows = block.shape[0]
        term = along_k(left[:, n * rows : (n + 1) * rows], block[...])
        total = term if total is None else total + term
    return total


def tile_specs(width, tile):
    return [
        pl.BlockSpec((width // 3, width), lambda i, n=n: (3 * tile(i) + n, 0))
        for n in range(3)
    ]


def normed(value):
    centered = value - jnp.mean(value, -1, keepdims=True)
    scale = lax.rsqrt(jnp.mean(centered * centered, -1, keepdims=True) + norm_eps)
    return centered * scale, scale


def norm_back(grad, value, gain):
    unit, scale = normed(value)
    inner = grad * gain
    mean = jnp.mean(inner, -1, keepdims=True)
    slope = jnp.mean(inner * unit, -1, keepdims=True)
    return (
        scale * (inner - mean - unit * slope),
        jnp.sum(grad * unit, 0, keepdims=True),
        jnp.sum(grad, 0, keepdims=True),
    )


def forward_kernel(
    hot_ref,
    rows_ref,
    pos_hot_ref,
    pos_ref,
    mask_ref,
    vec_ref,
    w_0,
    w_1,
    w_2,
    x_out,
    a_out,
    qkv_out,
    probs_out,
    o_out,
    mid_out,
    m_out,
    u_out,
    g_out,
    hidden_out,
    final_out,
    cur,
):
    step = pl.program_id(0)
    layer, s = lax.div(step, STEPS), lax.rem(step, STEPS)
    low, f32 = jnp.bfloat16, jnp.float32
    width = cur.shape[1]
    head_dim = width // H

    tile = (w_0, w_1, w_2)

    def vec(row):
        return vec_ref[layer * STEPS + row]

    @pl.when(step == 0)
    def embed():
        cur[...] = along_k(hot_ref[...], rows_ref[...]) + across_k(pos_hot_ref[...], pos_ref[...])

    @pl.when(s == 0)
    def first_norm():
        x_out[layer] = cur[...]
        a_out[layer] = (normed(cur[...])[0] * vec(G1) + vec(S1)).astype(low)

    @pl.when(s < 3)
    def project():
        bias = jnp.where(s == 0, vec(BQ), jnp.where(s == 2, vec(BV), 0.0))
        qkv_out[layer, s] = (tile_across(a_out[layer], tile) + bias).astype(low)

    @pl.when(s == 2)
    def attend():
        lanes = lax.broadcasted_iota(jnp.int32, (1, 2 * head_dim), 1)
        for pair in range(H // 2):
            cols = slice(2 * head_dim * pair, 2 * head_dim * (pair + 1))
            q, k, v = (qkv_out[layer, part, :, cols] for part in range(3))
            total = None
            for side in range(2):
                own = (lanes < head_dim) if side == 0 else (lanes >= head_dim)
                scores = across_k(jnp.where(own, q, jnp.zeros_like(q)), k) * head_dim ** (-0.5)
                scores = jnp.where(mask_ref[...] > 0.0, scores, -1000000000.0)
                shifted = jnp.exp(scores - jnp.max(scores, -1, keepdims=True))
                probs = shifted / jnp.sum(shifted, -1, keepdims=True)
                probs_out[layer, 2 * pair + side] = probs
                term = along_k(probs.astype(low), jnp.where(own, v, jnp.zeros_like(v)))
                total = term if total is None else total + term
            o_out[layer, :, cols] = total.astype(low)

    @pl.when(s == 3)
    def second_norm():
        mid = cur[...] + tile_across(o_out[layer], tile) + vec(BPROJ)
        mid_out[layer] = mid
        m_out[layer] = (normed(mid)[0] * vec(G2) + vec(S2)).astype(low)
        cur[...] = mid + vec(BOUT)

    @pl.when((s >= 4) & (s < 8))
    def widen():
        u = tile_across(m_out[layer], tile) + vec(BFC + s - 4)
        u_out[layer, s - 4] = u
        g = 0.5 * u * (1.0 + jnp.tanh(GELU_A * (u + GELU_B * (u * u * u))))
        g_out[layer, s - 4] = g.astype(low)

    @pl.when(s >= 8)
    def narrow():
        cur[...] += tile_along(g_out[layer, s - 8], tile)

    @pl.when(step == 2 * STEPS - 1)
    def last_norm():
        hidden_out[...] = cur[...]
        final_out[...] = (normed(cur[...])[0] * vec_ref[2 * STEPS] + vec_ref[2 * STEPS + 1]).astype(low)


def forward_layers(hot, rows, pos_hot, pos, mask, vecs, mats):
    tok, width = hot.shape[0], rows.shape[1]
    low, f32 = jnp.bfloat16, jnp.float32
    shape = jax.ShapeDtypeStruct
    vmem = pl.BlockSpec(memory_space=pltpu.VMEM)
    return pl.pallas_call(
        forward_kernel,
        grid=(2 * STEPS,),
        out_shape=(
            shape((2, tok, width), f32),
            shape((2, tok, width), low),
            shape((2, 3, tok, width), low),
            shape((2, H, tok, tok), f32),
            shape((2, tok, width), low),
            shape((2, tok, width), f32),
            shape((2, tok, width), low),
            shape((2, 4, tok, width), f32),
            shape((2, 4, tok, width), low),
            shape((tok, width), f32),
            shape((tok, width), low),
        ),
        in_specs=[vmem] * 6 + tile_specs(width, lambda i: i),
        out_specs=(vmem,) * 11,
        scratch_shapes=[pltpu.VMEM((tok, width), f32)],
        compiler_params=pltpu.CompilerParams(vmem_limit_bytes=58 * 2**20),
        cost_estimate=pl.CostEstimate(
            flops=2 * tok * mats.size, bytes_accessed=2 * mats.size, transcendentals=0
        ),
        name="forward_layers",
    )(hot, rows, pos_hot, pos, mask, vecs, mats, mats, mats)


def backward_kernel(
    grad_ref,
    hidden_ref,
    vec_ref,
    x_ref,
    a_ref,
    qkv_ref,
    probs_ref,
    o_ref,
    mid_ref,
    m_ref,
    u_ref,
    g_ref,
    hot_ref,
    w_0,
    w_1,
    w_2,
    dx_out,
    vec_out,
    rows_out,
    acc_out,
    cur,
    wide,
    du_s,
    dqkv_s,
    left_s,
    right_s,
    own_s,
    send_s,
    recv_s,
    acc_0,
    acc_1,
    send_pair,
    recv_pair,
    local,
):
    step = pl.program_id(0)
    layer, s = 1 - lax.div(step, STEPS), lax.rem(step, STEPS)
    low, f32 = jnp.bfloat16, jnp.float32
    tok, width = cur.shape
    half = width // 2
    head_dim = width // H
    at, core = place()
    sibling = device_at(at, 1 - core)
    last = 2 * STEPS
    tile = (w_0, w_1, w_2)

    def vec(row):
        return vec_ref[layer * STEPS + row]

    def put(row, value):
        vec_out[layer * STEPS + row] = value

    def pair_copy(slot):
        return pltpu.make_async_remote_copy(
            src_ref=send_s.at[slot],
            dst_ref=recv_s.at[slot],
            send_sem=send_pair.at[slot],
            recv_sem=recv_pair.at[slot],
            device_id=sibling,
            device_id_type=pl.DeviceIdType.MESH,
        )

    def set_right(value):
        right_s[:, :half] = jnp.where(core == 0, value[:, :half], value[:, half:])
        right_s[:, half:] = jnp.where(core == 0, value[:, half:], value[:, :half])

    @pl.when(step == 0)
    def enter():
        greet([sibling])
        dx, dg, ds = norm_back(grad_ref[...], hidden_ref[...], vec_ref[last])
        cur[...] = dx
        vec_out[last] = dg
        vec_out[last + 1] = ds

    def collect(before):
        slot, b = before % 2, before % STEPS
        acc = acc_1 if before < STEPS else acc_0
        tile_at = TILE_ORDER[b]
        pair_copy(slot).wait_recv()
        granule = acc.shape[4]
        count = width // granule
        for g in range(count):
            block, p = divmod(tile_at * count + g, 3)
            here = slice(g * granule, (g + 1) * granule)
            value = own_s[here, :].astype(f32) + recv_s[slot, here, :].astype(f32)
            acc[block // (RING * RING), block // RING % RING, block % RING, p] = value.astype(low)

    for n in range(1, last + 1):
        pl.when(step == n)(lambda n=n: collect(n - 1))

    def leave_copies(layer, acc):
        return [
            pltpu.make_async_copy(
                acc.at[n // RING, n % RING],
                acc_out.at[layer, n // RING, n % RING],
                local.at[layer * RING * RING + n],
            )
            for n in range(RING * RING)
        ]

    @pl.when(step == STEPS)
    def leave_second():
        for op in leave_copies(1, acc_1):
            op.start()

    @pl.when((s == 0) & (step < last))
    def begin():
        put(BOUT, jnp.sum(cur[...], 0, keepdims=True))
        set_right(cur[...].astype(low))
        wide[...] = cur[...].astype(low)

    @pl.when((s < 4) & (step < last))
    def through_gelu():
        dg = tile_across(wide[...], tile)
        u = u_ref[layer, s]
        square = u * u
        t = jnp.tanh(GELU_A * (u + GELU_B * (square * u)))
        slope = 0.5 * (1.0 + t) + (0.5 * GELU_A) * u * (1.0 - t * t) * (1.0 + (3.0 * GELU_B) * square)
        du = dg * slope
        put(BFC + s, jnp.sum(du, 0, keepdims=True))
        du_s[s] = du.astype(low)
        left_s[...] = g_ref[layer, s]

    @pl.when(s == 4)
    def begin_fc():
        set_right(m_ref[layer])
        dx_out[...] = jnp.zeros_like(dx_out)

    @pl.when((s >= 4) & (s < 8))
    def through_fc():
        left = du_s[s - 4]
        dx_out[...] += tile_along(left, tile)
        left_s[...] = left

    @pl.when(s == 8)
    def through_attention():
        dx, dg, ds = norm_back(dx_out[...], mid_ref[layer], vec(G2))
        put(G2, dg)
        put(S2, ds)
        cur[...] = cur[...] + dx
        put(BPROJ, jnp.sum(cur[...], 0, keepdims=True))
        mid_low = cur[...].astype(low)
        left_s[...] = mid_low
        set_right(o_ref[layer])
        wide[...] = tile_along(mid_low, tile).astype(low)
        lanes = lax.broadcasted_iota(jnp.int32, (1, 2 * head_dim), 1)
        scale = head_dim ** (-0.5)
        for pair in range(H // 2):
            cols = slice(2 * head_dim * pair, 2 * head_dim * (pair + 1))
            q, k, v = (qkv_ref[layer, part, :, cols] for part in range(3))
            do = wide[:, cols]
            parts = [None] * 3
            for side in range(2):
                own = (lanes < head_dim) if side == 0 else (lanes >= head_dim)
                keep = lambda item, own=own: jnp.where(own, item, jnp.zeros_like(item))
                probs = probs_ref[layer, 2 * pair + side]
                do_own = keep(do)
                dprobs = across_k(do_own, v)
                dscores = probs * (dprobs - jnp.sum(probs * dprobs, -1, keepdims=True))
                dlow = (dscores * scale).astype(low)
                terms = (
                    along_k(dlow, keep(k)),
                    over_rows(dlow, keep(q)),
                    over_rows(probs.astype(low), do_own),
                )
                parts = [
                    term if held is None else held + term for held, term in zip(parts, terms)
                ]
            for part in range(3):
                dqkv_s[part, :, cols] = parts[part].astype(low)
            vec_out[layer * STEPS + BQ, :, cols] = jnp.sum(parts[0], 0, keepdims=True)
            vec_out[layer * STEPS + BV, :, cols] = jnp.sum(parts[2], 0, keepdims=True)

    @pl.when(s == 9)
    def begin_qkv():
        set_right(a_ref[layer])
        dx_out[...] = jnp.zeros_like(dx_out)

    @pl.when(s >= 9)
    def through_qkv():
        left = dqkv_s[s - 9]
        dx_out[...] += tile_along(left, tile)
        left_s[...] = left

    @pl.when(step < last)
    def gradient():
        slot = lax.rem(step, 2)
        grad = over_rows(left_s[...], right_s[...])
        pl.when(step >= 2)(lambda: pair_copy(slot).wait_send())
        own_s[...] = grad[:, :half].astype(low)
        send_s[slot] = grad[:, half:].astype(low)
        pair_copy(slot).start()

    @pl.when(s == STEPS - 1)
    def end_layer():
        dx, dg, ds = norm_back(dx_out[...], x_ref[layer], vec(G1))
        put(G1, dg)
        put(S1, ds)
        cur[...] = cur[...] + dx

    @pl.when(step == last)
    def leave():
        for op in leave_copies(0, acc_0):
            op.start()
        dx_out[...] = cur[...]
        rows = over_rows(hot_ref[...], cur[...].astype(low)).astype(low)
        rows_out[...] = rows.reshape(rows_out.shape)
        for slot in range(2):
            pair_copy(slot).wait_send()
        for layer_at, acc in ((1, acc_1), (0, acc_0)):
            for op in leave_copies(layer_at, acc):
                op.wait()


def backward_layers(grad, hidden, vecs, saved, hot, mats):
    tok, width = grad.shape
    low, f32 = jnp.bfloat16, jnp.float32
    shape = jax.ShapeDtypeStruct
    vmem = pl.BlockSpec(memory_space=pltpu.VMEM)
    hbm = pl.BlockSpec(memory_space=pltpu.HBM)
    torus, half, part = (RING, RING, RING), width // 2, 48

    def tile(i):
        i = jnp.minimum(i, 2 * STEPS - 1)
        layer, s = 1 - i // STEPS, i % STEPS
        return layer * STEPS + jnp.where(
            s < 4, 8 + s, jnp.where(s < 8, s, jnp.where(s == 8, 3, s - 9))
        )

    return pl.pallas_call(
        backward_kernel,
        grid=(2 * STEPS + 1,),
        out_shape=(
            shape((tok, width), f32),
            shape((2 * STEPS + 2, 1, width), f32),
            shape((RING, 2, 32, width), low),
            shape((2,) + torus + (3, part, half), low),
        ),
        in_specs=[vmem] * 13 + tile_specs(width, tile),
        out_specs=(vmem, vmem, vmem, hbm),
        scratch_shapes=[
            pltpu.VMEM((tok, width), f32),
            pltpu.VMEM((tok, width), low),
            pltpu.VMEM((4, tok, width), low),
            pltpu.VMEM((3, tok, width), low),
            pltpu.VMEM((tok, width), low),
            pltpu.VMEM((tok, width), low),
            pltpu.VMEM((width, half), low),
            pltpu.VMEM((2, width, half), low),
            pltpu.VMEM((2, width, half), low),
            pltpu.VMEM(torus + (3, part, half), low),
            pltpu.VMEM(torus + (3, part, half), low),
            pltpu.SemaphoreType.DMA((2,)),
            pltpu.SemaphoreType.DMA((2,)),
            pltpu.SemaphoreType.DMA((2 * RING * RING,)),
        ],
        compiler_params=pltpu.CompilerParams(
            collective_id=4, has_side_effects=True, vmem_limit_bytes=60 * 2**20
        ),
        cost_estimate=pl.CostEstimate(
            flops=4 * tok * mats.size, bytes_accessed=2 * mats.size, transcendentals=0
        ),
        name="backward_layers",
    )(grad, hidden, vecs, *saved, hot, mats, mats, mats)


def doc_info(doc_lens, tok_count, total_docs):
    doc_ends = jnp.cumsum(doc_lens)
    places = jnp.arange(tok_count, dtype=jnp.int32)
    seg_ids = jnp.sum((places[:, None] >= doc_ends[None, :]).astype(jnp.int32), 1)
    one_hot = seg_ids[:, None] == jnp.arange(doc_lens.shape[0], dtype=jnp.int32)[None, :]
    starts = doc_ends - doc_lens
    pos_ids = places - jnp.sum(jnp.where(one_hot, starts[None, :], 0), 1)
    doc_len = jnp.sum(jnp.where(one_hot, doc_lens[None, :], 0), 1)
    weights = 1.0 / (doc_len.astype(jnp.float32) * total_docs)
    return (seg_ids, pos_ids, weights)


def device_rise(first, count, devices):
    places = first + jnp.arange(count, dtype=jnp.int32)
    return 1.0 + 2.0 * places.astype(jnp.float32) / (devices - 1)


def contract(left, right, left_dim, right_dim):
    return lax.dot_general(
        left, right, (((left_dim,), (right_dim,)), ((), ())), preferred_element_type=jnp.float32
    )


def renew(weight, moment, average, grad, factor):
    clipped = factor * grad
    moment_next = momentum_coef * moment + clipped
    weight_next = weight - learn_rate * (clipped + momentum_coef * moment_next)
    average_next = ema_decay * average + (1.0 - ema_decay) * weight_next
    return (moment_next, weight_next, average_next, weight_next.astype(jnp.bfloat16))


SMALL_ROWS, LANES = 16, 128


def pack_small(values):
    room = SMALL_ROWS * LANES - values.shape[-1]
    pads = [(0, 0)] * (values.ndim - 1) + [(0, room)]
    return jnp.pad(values, pads).reshape(values.shape[:-1] + (SMALL_ROWS, LANES))


def per_device(
    token_ids,
    targets,
    lengths,
    embed_table,
    embed_moment,
    embed_average,
    blocks,
    block_moment,
    block_average,
    pos_table,
    pos_moment,
    pos_average,
    vectors,
    vector_moment,
    vector_average,
):
    devices = lax.axis_size(("dp", "vocab"))
    vocab_count = lax.axis_size("vocab")
    dp_count = lax.axis_size("dp")
    vocab_at = lax.axis_index("vocab")
    data_at = lax.axis_index("dp")
    tok = token_ids.shape[0]
    own_rows, width = embed_table.shape
    capacity = max(2, 2 * tok // devices)
    low = jnp.bfloat16
    blocks, block_moment, block_average = (
        jnp.transpose(item, (0, 2, 1)) for item in (blocks, block_moment, block_average)
    )
    pos_rows, pos_cols = pos_table.shape
    vec_own = vectors.shape[0]
    table_low = embed_table.astype(low)
    pad_rows = -own_rows % 16
    table_padded = jnp.pad(table_low, ((0, pad_rows), (0, 0)))
    slot_rows = own_rows + pad_rows

    table_slice = lax.all_gather(table_padded, "dp", axis=0, tiled=True)
    target_owners = targets // own_rows
    codes = (
        (target_owners % vocab_count) * (dp_count * slot_rows)
        + (target_owners // vocab_count) * slot_rows
        + targets % own_rows
    )

    owners = token_ids // own_rows
    tokens = jnp.arange(tok, dtype=jnp.int32)
    rank = jnp.sum((owners[:, None] == owners[None, :]) & (tokens[None, :] < tokens[:, None]), 1)
    slot_count = devices * capacity
    slots = jnp.arange(slot_count, dtype=jnp.int32)
    arrival = (
        (owners % 8) * 32 + (owners // 8 % RING) * 8 + (owners // 32) * capacity + rank
    )
    slot_hot = (arrival[:, None] == slots[None, :]).astype(low)
    spread = (slots[:, None] // capacity == jnp.arange(devices)[None, :]).astype(low)
    earlier = (tokens[:, None] < tokens[None, :]).astype(low)
    slot_number = jnp.broadcast_to((slots % capacity).astype(jnp.float32)[:, None], (slot_count, tok))
    by_owner = (
        (slots % 64 // 16) * 2 + slots // 64 * 8 + slots % 16 // 2 * 32 + slots % capacity
    )
    swap = (by_owner[:, None] == slots[None, :]).astype(low)
    values = jnp.concatenate([jnp.transpose(pos_table).reshape(-1), vectors]).astype(low)
    small = jnp.concatenate(
        [
            jnp.pad(values, (0, IDS_ROW * LANES - values.shape[0])).reshape(IDS_ROW, LANES),
            jnp.stack([token_ids // 256, token_ids % 256]).astype(low),
            jnp.zeros((SMALL_ROWS - IDS_ROW - 2, LANES), low),
        ]
    )
    mats_all, small_all, returned_rows, asked = gather_weights(
        blocks, small, table_padded, spread, earlier, slot_number, jnp.transpose(swap)
    )
    small_all = small_all.reshape(devices, -1)
    pos_low_t = small_all[:, : pos_rows * pos_cols].reshape(width, pos_rows)
    vecs_all = (
        small_all[:, pos_rows * pos_cols : pos_rows * pos_cols + vec_own]
        .reshape(-1)
        .astype(jnp.float32)
    )
    lens_group = lengths[0]
    seg_group, pos_group, weight_group = jax.vmap(
        partial(doc_info, tok_count=tok, total_docs=devices * lens_group.shape[1])
    )(lens_group)
    weight_group = weight_group * device_rise(data_at * vocab_count, vocab_count, devices)[:, None]
    seg_ids = lax.dynamic_index_in_dim(seg_group, vocab_at, 0, keepdims=False)
    pos_ids = lax.dynamic_index_in_dim(pos_group, vocab_at, 0, keepdims=False)
    places = jnp.arange(tok, dtype=jnp.int32)
    attn_mask = (seg_ids[:, None] == seg_ids[None, :]) & (places[None, :] <= places[:, None])

    pos_hot = (pos_ids[:, None] == jnp.arange(pos_rows, dtype=jnp.int32)[None, :]).astype(low)
    vec_rows = vecs_all.reshape(-1, 1, width)
    *saved, hidden, final_low = forward_layers(
        slot_hot,
        returned_rows,
        pos_hot,
        pos_low_t,
        attn_mask.astype(jnp.float32),
        vec_rows,
        mats_all,
    )
    grad_final, table_part, token_losses = head(
        final_low, jnp.broadcast_to(codes[None, :], (8, tok)), weight_group, table_slice
    )
    loss_part = jnp.sum(token_losses)
    table_grad = lax.psum_scatter(table_part, "dp", scatter_dimension=0, tiled=True)[
        :own_rows
    ].astype(jnp.float32)
    grad_hidden, grad_vecs, rows_back, grad_acc = backward_layers(
        grad_final, hidden, vec_rows, saved, slot_hot, mats_all
    )
    grad_pos = lax.dot_general(
        grad_hidden,
        pos_hot.astype(jnp.float32),
        (((0,), (0,)), ((), ())),
        precision=lax.Precision.HIGHEST,
    )
    small_grads = pack_small(
        jnp.concatenate(
            [grad_pos.reshape(devices, -1), grad_vecs.reshape(devices, -1)], 1
        )
    )
    mats_shard, small_shard, back_grads = reduce_weights(grad_acc, small_grads, rows_back, swap)
    small_shard = small_shard.reshape(-1)
    pos_shard = small_shard[: pos_rows * pos_cols].reshape(pos_cols, pos_rows)
    vec_shard = small_shard[pos_rows * pos_cols : pos_rows * pos_cols + vec_own]
    table_grad = table_grad + contract(asked, back_grads.reshape(slot_count, width), 0, 0)[:own_rows]
    local_squares = (
        jnp.sum(table_grad * table_grad)
        + jnp.sum(mats_shard * mats_shard)
        + jnp.sum(pos_shard * pos_shard)
        + jnp.sum(vec_shard * vec_shard)
    )
    both_sums = sum_all(
        jnp.broadcast_to(jnp.pad(jnp.stack([loss_part, local_squares]), (0, 6))[:, None], (8, LANES))
    )
    loss_sum, squares = both_sums[0, 0], both_sums[1, 0]
    grad_norm = jnp.sqrt(squares)
    factor = clip_bound / jnp.maximum(grad_norm, clip_bound)
    embed_out = renew(embed_table, embed_moment, embed_average, table_grad, factor)
    block_out = renew(blocks, block_moment, block_average, mats_shard, factor)
    block_out = tuple(jnp.transpose(item, (0, 2, 1)) for item in block_out)
    pos_out = renew(
        jnp.transpose(pos_table),
        jnp.transpose(pos_moment),
        jnp.transpose(pos_average),
        pos_shard,
        factor,
    )
    pos_out = tuple(jnp.transpose(item) for item in pos_out)
    vector_out = renew(vectors, vector_moment, vector_average, vec_shard, factor)
    return (loss_sum, grad_norm) + embed_out + block_out + pos_out + vector_out


def solution(mesh):
    table = P(("dp", "vocab"), None)
    cols = P(None, None, ("dp", "vocab"))
    pos = P(None, ("dp", "vocab"))
    vec = P(("dp", "vocab"))
    return jax.shard_map(
        per_device,
        mesh=mesh,
        in_specs=(vec, vec, P("dp", None, None))
        + (table,) * 3
        + (cols,) * 3
        + (pos,) * 3
        + (vec,) * 3,
        out_specs=(P(), P()) + (table,) * 4 + (cols,) * 4 + (pos,) * 4 + (vec,) * 4,
        check_vma=False,
    )
```

```python
from functools import partial

import jax
import jax.numpy as jnp
from jax import lax
from jax.experimental import pallas as pl
from jax.experimental.pallas import tpu as pltpu
from jax.sharding import PartitionSpec as P

H = 12
RING = 4
ORDERS = ((2, 1, 0), (1, 0, 2), (0, 2, 1))

norm_eps = 1e-05
clip_bound = 0.01
learn_rate = 10000.0
momentum_coef = 0.5
ema_decay = 0.5


def place():
    dp = lax.axis_index("dp")
    vocab = lax.axis_index("vocab")
    return (lax.div(dp, RING), lax.rem(dp, RING), lax.div(vocab, 2)), lax.rem(vocab, 2)


def device_at(at, core):
    return (at[0] * RING + at[1], at[2] * 2 + core)


def moved(at, axis, by):
    out = list(at)
    out[axis] = lax.rem(at[axis] + by, RING)
    return tuple(out)


class Wires:
    def __init__(self, send, recv):
        self.send, self.recv, self.count, self.live = send, recv, 0, []

    def copy(self, src, dst, device):
        number = self.count
        self.count += 1
        op = pltpu.make_async_remote_copy(
            src_ref=src,
            dst_ref=dst,
            send_sem=self.send.at[number],
            recv_sem=self.recv.at[number],
            device_id=device,
            device_id_type=pl.DeviceIdType.MESH,
        )
        op.start()
        self.live.append(op)
        return op

    def drain(self):
        for op in self.live:
            op.wait_send()


def greet(devices):
    barrier = pltpu.get_barrier_semaphore()
    for device in devices:
        pl.semaphore_signal(
            barrier, inc=1, device_id=device, device_id_type=pl.DeviceIdType.MESH
        )
    pl.semaphore_wait(barrier, len(devices))


def ring_peers(at, core):
    near = [device_at(moved(at, axis, by), core) for axis in range(3) for by in range(1, RING)]
    return near + [device_at(at, 1 - core)]


def neighbours(at, core):
    near = [device_at(moved(at, axis, by), core) for axis in range(3) for by in (1, RING - 1)]
    return near + [device_at(at, 1 - core)]


def gather_kernel(
    mine_ref,
    small_ref,
    table_ref,
    spread_ref,
    earlier_ref,
    slot_ref,
    swap_ref,
    out_ref,
    small_out,
    rows_out,
    asked_out,
    peer,
    block,
    asked_rows,
    over_z,
    over_y,
    sorted_rows,
    over_x,
    send,
    recv,
    local,
):
    at, core = place()
    z, y, x = at
    rows, half = mine_ref.shape[1], mine_ref.shape[2] // 2
    part = 2 * rows // 3
    low, f32 = jnp.bfloat16, jnp.float32
    sibling = device_at(at, 1 - core)
    greet(ring_peers(at, core))
    wires = Wires(send, recv)
    cols = pl.ds(pl.multiple_of(core * half, half), half)
    other = pl.ds(pl.multiple_of((1 - core) * half, half), half)

    swap = wires.copy(mine_ref.at[:, :, other], peer, sibling)
    small_out[z, y, x, core] = small_ref[...]

    def right(axis):
        return device_at(moved(at, axis, 1), core)

    def left(axis):
        return device_at(moved(at, axis, RING - 1), core)

    def all_around(axis, src_of, dst):
        out = []
        for by in range(1, RING):
            there = moved(at, axis, by)
            out.append(wires.copy(src_of(there[axis]), dst, device_at(there, core)))
        return out

    def small_start(phase):
        index = [z, y, x]
        for axis in ORDERS[0][:phase]:
            index[axis] = pl.ds(0, RING)
        own = small_out.at[index[0], index[1], index[2], core]
        return all_around(ORDERS[0][phase], lambda c: own, own)

    def arrive(ops):
        for op in ops:
            op.wait_recv()

    small_ops = small_start(0)
    swap.wait_recv()
    for layer in range(2):
        own = jnp.where(core == 0, mine_ref[layer, :, :half], mine_ref[layer, :, half:])
        got = peer[layer]
        both = jnp.concatenate(
            [jnp.where(core == 0, own, got), jnp.where(core == 0, got, own)], 0
        )
        block[layer] = both.astype(low)
    block_local = []
    for layer in range(2):
        op = pltpu.make_async_copy(
            block.at[layer], out_ref.at[layer, z, y, x, :, cols], local.at[layer]
        )
        op.start()
        block_local.append(op)

    def bundle(layer, p, phase, c, piece=None):
        order = ORDERS[p]
        index = list(at)
        index[order[phase]] = c
        for axis in order[:phase]:
            index[axis] = pl.ds(0, RING)
        first, count = p * part, part
        if piece is not None:
            if phase == 0:
                first, count = (first, 32) if piece == 0 else (first + 32, part - 32)
            else:
                index[order[0]] = pl.ds(2 * piece, 2)
        return out_ref.at[layer, index[0], index[1], index[2], pl.ds(first, count), cols]

    chains = [(layer, p) for layer in range(2) for p in range(3)]
    pending = []
    steps, forwards = {}, {}

    def start(phase):
        for key in chains:
            layer, p = key
            axis = ORDERS[p][phase]
            src = bundle(layer, p, phase, at[axis])
            if phase == 2:
                pending.append(wires.copy(src, src, sibling))
            steps[key] = (wires.copy(src, src, right(axis)), wires.copy(src, src, left(axis)))

    def forward(phase):
        for key in chains:
            layer, p = key
            axis = ORDERS[p][phase]
            before, after = lax.rem(at[axis] + 3, RING), lax.rem(at[axis] + 1, RING)
            steps[key][0].wait_recv()
            src = bundle(layer, p, phase, before, 0)
            one = wires.copy(src, src, right(axis))
            steps[key][1].wait_recv()
            src = bundle(layer, p, phase, after, 1)
            two = wires.copy(src, src, left(axis))
            forwards[key] = (one, two)
            if phase == 2:
                for c in (before, after):
                    src = bundle(layer, p, phase, c)
                    pending.append(wires.copy(src, src, sibling))

    def finish(phase):
        for key in chains:
            layer, p = key
            axis = ORDERS[p][phase]
            across = lax.rem(at[axis] + 2, RING)
            for piece in range(2):
                forwards[key][piece].wait_recv()
                if phase == 2:
                    src = bundle(layer, p, phase, across, piece)
                    pending.append(wires.copy(src, src, sibling))

    arrive(block_local_wait(block_local))
    start(0)
    arrive(small_ops)
    small_ops = small_start(1)
    forward(0)
    arrive(small_ops)
    small_ops = small_start(2)
    finish(0)
    start(1)
    arrive(small_ops)
    own = small_out.at[:, :, :, core]
    small_ops = [wires.copy(own, own, sibling)]
    forward(1)
    arrive(small_ops)

    count = 2 * RING**3
    smalls = small_out[...].reshape((count,) + small_ref.shape)
    high, rest = (
        jnp.dot(spread_ref[...], smalls[:, IDS_ROW + n, :], preferred_element_type=f32)
        for n in range(2)
    )
    own_rows = TABLE_ROWS
    me = ((z * RING + y) * RING + x) * 2 + core
    local_id = high * 256.0 + rest - (me * own_rows).astype(f32)
    mine = (local_id >= 0.0) & (local_id < float(own_rows))
    rank = jnp.dot(
        jnp.where(mine, 1.0, 0.0).astype(low), earlier_ref[...], preferred_element_type=f32
    )
    picked = jnp.where(mine & (rank == slot_ref[...]), local_id, 0.0)
    row = jnp.sum(picked, 1, keepdims=True).astype(jnp.int32)
    places = lax.broadcasted_iota(jnp.int32, asked_out.shape, 1)
    asked = jnp.where(places == row, 1.0, 0.0).astype(low)
    asked_out[...] = asked
    found = jnp.dot(asked, table_ref[...], preferred_element_type=f32).astype(low)
    asked_rows[...] = found.reshape(asked_rows.shape)
    over_z[z] = asked_rows[z]
    row_ops = all_around(0, lambda c: asked_rows.at[c], over_z.at[z])

    finish(1)
    start(2)
    arrive(row_ops)
    over_y[y] = over_z[:, y]
    row_ops = all_around(1, lambda c: over_z.at[:, c], over_y.at[y])
    forward(2)
    arrive(row_ops)
    sorted_rows[...] = (
        jnp.dot(
            swap_ref[...], over_y[...].reshape(2 * count, table_ref.shape[1]), preferred_element_type=f32
        )
        .astype(low)
        .reshape(sorted_rows.shape)
    )
    over_x[x] = sorted_rows[x]
    row_ops = all_around(2, lambda c: sorted_rows.at[c], over_x.at[x])
    finish(2)
    arrive(row_ops)
    pending.append(wires.copy(over_x.at[:, 1 - core], rows_out.at[:, core], sibling))
    rows_out[:, core] = over_x[:, core]
    arrive(pending)
    wires.drain()


def block_local_wait(ops):
    for op in ops:
        op.wait()
    return []


IDS_ROW = 8
TABLE_ROWS = 393
GATHER_COPIES = 1 + 3 * (6 * 4 + 3) + 6 * 5 + 1 + 9 + 1


def gather_weights(mine, small, table, spread, earlier, slots, swap):
    layers, rows, width = mine.shape
    table_rows = table.shape[0]
    count = 2 * RING**3
    low = jnp.bfloat16
    hbm = pl.BlockSpec(memory_space=pltpu.HBM)
    vmem = pl.BlockSpec(memory_space=pltpu.VMEM)
    mats, small_all, fetched, asked = pl.pallas_call(
        gather_kernel,
        out_shape=(
            jax.ShapeDtypeStruct((layers, RING, RING, RING, 2 * rows, width), low),
            jax.ShapeDtypeStruct((RING, RING, RING, 2) + small.shape, low),
            jax.ShapeDtypeStruct((RING, 2, count // 4, width), low),
            jax.ShapeDtypeStruct((2 * count, table_rows), low),
        ),
        in_specs=[vmem] * 7,
        out_specs=(hbm, vmem, vmem, vmem),
        scratch_shapes=[
            pltpu.VMEM((layers, rows, width // 2), jnp.float32),
            pltpu.VMEM((layers, 2 * rows, width // 2), low),
            pltpu.VMEM((RING, RING, 16, width), low),
            pltpu.VMEM((RING, RING, 16, width), low),
            pltpu.VMEM((RING, RING, 16, width), low),
            pltpu.VMEM((RING, 2, count // 4, width), low),
            pltpu.VMEM((RING, 2, count // 4, width), low),
            pltpu.SemaphoreType.DMA((GATHER_COPIES,)),
            pltpu.SemaphoreType.DMA((GATHER_COPIES,)),
            pltpu.SemaphoreType.DMA((2,)),
        ],
        compiler_params=pltpu.CompilerParams(
            collective_id=0, has_side_effects=True, vmem_limit_bytes=58 * 2**20
        ),
        cost_estimate=pl.CostEstimate(flops=0, bytes_accessed=250 * 10**6, transcendentals=0),
        name="gather_weights",
    )(mine, small, table, spread, earlier, slots, swap)
    return (
        mats.reshape(layers * RING**3 * 2 * rows, width),
        small_all.reshape((count,) + small.shape),
        fetched.reshape(2 * count, width),
        asked,
    )


class Reduction:
    def __init__(self, at, core, send, recv):
        self.at, self.core, self.send, self.recv = at, core, send, recv
        self.number, self.level, self.halves, self.fulls = {}, {}, {}, {}
        self.final = None

    def copy(self, key, src, dst, device):
        number = self.number.setdefault(key, len(self.number))
        return pltpu.make_async_remote_copy(
            src_ref=src,
            dst_ref=dst,
            send_sem=self.send.at[number],
            recv_sem=self.recv.at[number],
            device_id=device,
            device_id_type=pl.DeviceIdType.MESH,
        )

    def axes(self, p):
        order = ORDERS[p]
        free = sorted(order[:2])
        return free, free.index(order[1])

    def ring(self, p, step):
        axis = ORDERS[p][2 - step]
        c = self.at[axis]
        right = device_at(moved(self.at, axis, 1), self.core)
        left = device_at(moved(self.at, axis, RING - 1), self.core)
        return c, lax.rem(c + 1, RING), lax.rem(c + 2, RING), lax.rem(c + 3, RING), right, left

    def index(self, layer, p, step, c, piece=None):
        part = 48
        cut, whole = (0, RING) if piece is None else (2 * piece, 2), (0, RING)
        if step == 0:
            free, unused = self.axes(p)
            spot = [c, c, c]
            spot[free[0]], spot[free[1]] = cut, whole
            return spot + [p]
        if step == 1:
            unused, first = self.axes(p)
            spot = [cut, cut]
            spot[first] = c
            return [layer % self.level[1].shape[0], p] + spot
        if piece is None:
            return [layer, p, c]
        return [layer, p, c, pl.ds(0, 32) if piece == 0 else pl.ds(32, part - 32)]

    def view(self, layer, p, step, c, piece=None):
        index = self.index(layer, p, step, c, piece)
        held = self.level[0, layer] if step == 0 else self.level[step]
        return held.at[tuple(pl.ds(*item) if isinstance(item, tuple) else item for item in index)]

    def slot(self, layer, p, step, side, whole):
        store = (self.fulls if whole else self.halves)[step]
        if step == 2 and not whole:
            return store.at[layer, p, side, pl.ds(0, 32 if side == 0 else 16)]
        return store.at[layer % store.shape[0], p, side]

    def half_copies(self, layer, p, step):
        unused, after, across, before, right, left = self.ring(p, step)
        out = []
        for side, device in ((0, right), (1, left)):
            out.append(
                self.copy(
                    (layer, p, step, side),
                    self.view(layer, p, step, across, side),
                    self.slot(layer, p, step, side, False),
                    device,
                )
            )
        return out

    def full_copies(self, layer, p, step):
        unused, after, across, before, right, left = self.ring(p, step)
        out = []
        for side, c, device in ((0, after, right), (1, before, left)):
            out.append(
                self.copy(
                    (layer, p, step, 2 + side),
                    self.view(layer, p, step, c),
                    self.slot(layer, p, step, side, True),
                    device,
                )
            )
        return out

    def add(self, layer, p, step, c, piece, terms, into):
        held = self.level[0, layer] if step == 0 else self.level[step]
        index = self.index(layer, p, step, c, piece)
        sizes = [item[1] for item in index if isinstance(item, tuple)]

        def one(inner):
            places = iter(inner)
            spot = tuple(
                item[0] + next(places) if isinstance(item, tuple) else item for item in index
            )
            value = held[spot].astype(jnp.float32)
            for term in terms:
                value = value + term[tuple(inner) + (slice(None), slice(None))].astype(jnp.float32)
            into(held, spot, inner, value)

        def body(n, unused):
            if len(sizes) == 2:
                for k in range(sizes[1]):
                    one([n, k])
            else:
                one([n])
            return unused

        if sizes:
            lax.fori_loop(0, sizes[0], body, 0)
        else:
            one([])

    def start(self, layer, step):
        for p in range(3):
            for op in self.half_copies(layer, p, step):
                op.start()

    def turn(self, layer, step):
        def back(held, spot, inner, value):
            held[spot] = value.astype(held.dtype)

        for p in range(3):
            unused, after, across, before, right, left = self.ring(p, step)
            halves, fulls = self.half_copies(layer, p, step), self.full_copies(layer, p, step)
            for side, c in ((0, after), (1, before)):
                halves[side].wait_recv()
                self.add(
                    layer, p, step, c, side, [self.slot(layer, p, step, side, False)], back
                )
                fulls[side].start()

    def finish(self, layer, step):
        for p in range(3):
            c = self.ring(p, step)[0]
            for op in self.full_copies(layer, p, step):
                op.wait_recv()
            terms = [self.slot(layer, p, step, side, True) for side in range(2)]

            def up(held, spot, inner, value, p=p):
                if step == 2:
                    self.final[layer, p * 48 : (p + 1) * 48] = value
                else:
                    target = self.level[step + 1]
                    spot = (layer % target.shape[0], p) + tuple(inner)
                    target[spot] = value.astype(target.dtype)

            self.add(layer, p, step, c, None, terms, up)

    def drain(self, layer, step):
        for p in range(3):
            for op in self.half_copies(layer, p, step) + self.full_copies(layer, p, step):
                op.wait_send()


def reduce_kernel(
    acc_ref,
    small_ref,
    rows_ref,
    swap_ref,
    out_ref,
    small_out,
    rows_out,
    acc_0,
    acc_1,
    mid,
    thin,
    half_0,
    half_1,
    half_2,
    full_0,
    full_1,
    full_2,
    small_acc,
    small_sib,
    small_wide,
    small_mid,
    small_thin,
    final,
    final_peer,
    over_core,
    over_x,
    sorted_rows,
    over_y,
    send,
    recv,
    send_small,
    recv_small,
    local,
):
    at, core = place()
    own_rows, half = final_peer.shape[1], final_peer.shape[2]
    sibling = device_at(at, 1 - core)
    sums = Reduction(at, core, send, recv)
    sums.level = {(0, 0): acc_0, (0, 1): acc_1, 1: mid, 2: thin}
    sums.halves = {0: half_0, 1: half_1, 2: half_2}
    sums.fulls = {0: full_0, 1: full_1, 2: full_2}
    sums.final = final

    accs = (acc_0, acc_1)
    loads = {}
    for layer in (1, 0):
        for n in range(RING * RING):
            spot = (n // RING, n % RING)
            op = pltpu.make_async_copy(
                acc_ref.at[(layer,) + spot], accs[layer].at[spot], local.at[1 + 16 * layer + n]
            )
            op.start()
            loads[layer, n] = op
    small_load = pltpu.make_async_copy(small_ref.at[:, :, :, core], small_acc, local.at[0])
    small_load.start()
    greet(ring_peers(at, core))
    wires = Wires(send_small, recv_small)
    small_swap = wires.copy(small_ref.at[:, :, :, 1 - core], small_sib, sibling)

    order = ORDERS[0]
    slots = (small_wide, small_mid, small_thin)

    def right(axis):
        return device_at(moved(at, axis, 1), core)

    def left(axis):
        return device_at(moved(at, axis, RING - 1), core)

    def small_view(step, c):
        index = list(at)
        index[order[2 - step]] = c
        for axis in order[: 2 - step]:
            index[axis] = slice(None)
        return tuple(index)

    def small_add(step, c, term):
        where = small_view(step, c)
        small_acc[where] = small_acc[where] + term

    def small_start(step):
        axis = order[2 - step]
        across = lax.rem(at[axis] + 2, RING)
        return wires.copy(small_acc.at[small_view(step, across)], slots[step].at[0], right(axis))

    def small_turn(step, op):
        axis = order[2 - step]
        after, before = lax.rem(at[axis] + 1, RING), lax.rem(at[axis] + 3, RING)
        op.wait_recv()
        small_add(step, after, slots[step][0])
        return (
            wires.copy(small_acc.at[small_view(step, after)], slots[step].at[1], right(axis)),
            wires.copy(small_acc.at[small_view(step, before)], slots[step].at[2], left(axis)),
        )

    def small_finish(step, ops):
        for op in ops:
            op.wait_recv()
        small_add(step, at[order[2 - step]], slots[step][1] + slots[step][2])

    z, y, x = at

    def all_around(axis, src_of, dst):
        out = []
        for by in range(1, RING):
            there = moved(at, axis, by)
            out.append(wires.copy(src_of(there[axis]), dst, device_at(there, core)))
        return out

    def arrive(ops):
        for op in ops:
            op.wait_recv()

    for layer in (1, 0):
        for n in range(RING * RING):
            loads[layer, n].wait()
        sums.start(layer, 0)
    row_ops = [wires.copy(rows_ref.at[:, 1 - core], over_core.at[:, core], sibling)]
    over_core[:, core] = rows_ref[:, core]
    small_load.wait()
    small_swap.wait_recv()
    small_acc[...] = small_acc[...] + small_sib[...]
    op = small_start(0)
    arrive(row_ops)
    over_x[x] = over_core[x]
    row_ops = all_around(2, lambda c: over_core.at[c], over_x.at[x])
    sums.turn(1, 0)
    sums.turn(0, 0)
    ops = small_turn(0, op)
    arrive(row_ops)
    count, width = swap_ref.shape[0], rows_ref.shape[3]
    sorted_rows[...] = (
        jnp.dot(
            swap_ref[...], over_x[...].reshape(count, width), preferred_element_type=jnp.float32
        )
        .astype(jnp.bfloat16)
        .reshape(sorted_rows.shape)
    )
    over_y[y] = sorted_rows[y]
    row_ops = all_around(1, lambda c: sorted_rows.at[c], over_y.at[y])
    small_finish(0, ops)
    op = small_start(1)
    sums.finish(1, 0)
    sums.start(1, 1)
    arrive(row_ops)
    rows_out[z] = over_y[:, z]
    row_ops = all_around(0, lambda c: over_y.at[:, c], rows_out.at[z])
    ops = small_turn(1, op)
    sums.finish(0, 0)
    sums.start(0, 1)
    small_finish(1, ops)
    op = small_start(2)
    sums.turn(1, 1)
    ops = small_turn(2, op)
    sums.turn(0, 1)
    sums.finish(1, 1)
    sums.start(1, 2)
    sums.finish(0, 1)
    sums.start(0, 2)
    small_finish(2, ops)
    sums.turn(1, 2)
    sums.turn(0, 2)
    sums.finish(1, 2)
    sums.finish(0, 2)
    arrive(row_ops)

    theirs = pl.ds(pl.multiple_of((1 - core) * own_rows, own_rows), own_rows)
    swap = wires.copy(final.at[:, theirs], final_peer, sibling)
    small_out[...] = small_acc[at]
    swap.wait_recv()
    for layer in range(2):
        own = jnp.where(core == 0, final[layer, :own_rows], final[layer, own_rows:])
        got = final_peer[layer]
        out_ref[layer, :, :half] = jnp.where(core == 0, own, got)
        out_ref[layer, :, half:] = jnp.where(core == 0, got, own)
    for layer in range(2):
        for step in range(3):
            sums.drain(layer, step)
    wires.drain()


def reduce_weights(acc, small, rows_back, swap):
    part, half = acc.shape[5:]
    rows = 3 * part
    torus = (RING, RING, RING)
    small_shape = small.shape[1:]
    hbm = pl.BlockSpec(memory_space=pltpu.HBM)
    vmem = pl.BlockSpec(memory_space=pltpu.VMEM)
    low = jnp.bfloat16
    return pl.pallas_call(
        reduce_kernel,
        out_shape=(
            jax.ShapeDtypeStruct((2, rows // 2, 2 * half), jnp.float32),
            jax.ShapeDtypeStruct(small_shape, jnp.float32),
            jax.ShapeDtypeStruct((RING, RING, 16, 2 * half), low),
        ),
        in_specs=[hbm, hbm, vmem, vmem],
        out_specs=(vmem, vmem, vmem),
        scratch_shapes=[
            pltpu.VMEM(torus + (3, part, half), low),
            pltpu.VMEM(torus + (3, part, half), low),
            pltpu.VMEM((2, 3, RING, RING, part, half), low),
            pltpu.VMEM((2, 3, RING, part, half), low),
            pltpu.VMEM((2, 3, 2, 2, RING, part, half), low),
            pltpu.VMEM((2, 3, 2, 2, part, half), low),
            pltpu.VMEM((2, 3, 2, 32, half), low),
            pltpu.VMEM((2, 3, 2, RING, RING, part, half), low),
            pltpu.VMEM((2, 3, 2, RING, part, half), low),
            pltpu.VMEM((2, 3, 2, part, half), low),
            pltpu.VMEM(torus + small_shape, jnp.float32),
            pltpu.VMEM(torus + small_shape, jnp.float32),
            pltpu.VMEM((3, RING, RING) + small_shape, jnp.float32),
            pltpu.VMEM((3, RING) + small_shape, jnp.float32),
            pltpu.VMEM((3,) + small_shape, jnp.float32),
            pltpu.VMEM((2, rows, half), jnp.float32),
            pltpu.VMEM((2, rows // 2, half), jnp.float32),
            pltpu.VMEM((RING, 2, 32, 2 * half), low),
            pltpu.VMEM((RING, 2, 32, 2 * half), low),
            pltpu.VMEM((RING, RING, 16, 2 * half), low),
            pltpu.VMEM((RING, RING, 16, 2 * half), low),
            pltpu.SemaphoreType.DMA((72,)),
            pltpu.SemaphoreType.DMA((72,)),
            pltpu.SemaphoreType.DMA((21,)),
            pltpu.SemaphoreType.DMA((21,)),
            pltpu.SemaphoreType.DMA((33,)),
        ],
        compiler_params=pltpu.CompilerParams(
            collective_id=1, has_side_effects=True, vmem_limit_bytes=58 * 2**20
        ),
        cost_estimate=pl.CostEstimate(flops=0, bytes_accessed=280 * 10**6, transcendentals=0),
        name="reduce_weights",
    )(acc, small.reshape(torus + (2,) + small_shape), rows_back, swap)


def sum_kernel(
    part_ref, asked_ref, back_ref, mats_ref, small_ref, loss_ref, out_ref, table_ref, slots, send, recv
):
    at, core = place()
    sibling = device_at(at, 1 - core)
    greet(ring_peers(at, core))
    wires = Wires(send, recv)
    table = part_ref[...].astype(jnp.float32) + lax.dot_general(
        asked_ref[...],
        back_ref[...],
        (((0,), (0,)), ((), ())),
        preferred_element_type=jnp.float32,
    )
    table_ref[...] = table

    def total(value):
        while value.ndim > 2:
            value = jnp.sum(value, 0)
        return jnp.sum(jnp.sum(value, 0, keepdims=True), 1, keepdims=True)

    mats, small = mats_ref[...], small_ref[...]
    squares = total(table * table) + total(mats * mats) + total(small * small)
    rows = lax.broadcasted_iota(jnp.int32, out_ref.shape, 0)
    slots[0, core] = jnp.where(rows == 0, total(loss_ref[...]), squares)
    swap = wires.copy(slots.at[0, core], slots.at[0, core], sibling)
    swap.wait_recv()
    value = slots[0, 0] + slots[0, 1]
    for axis in range(3):
        slots[1 + axis, at[axis]] = value
        ops = []
        for by in range(1, RING):
            ops.append(
                wires.copy(
                    slots.at[1 + axis, at[axis]],
                    slots.at[1 + axis, at[axis]],
                    device_at(moved(at, axis, by), core),
                )
            )
        for op in ops:
            op.wait_recv()
        value = slots[1 + axis, 0]
        for c in range(1, RING):
            value = value + slots[1 + axis, c]
    out_ref[...] = value
    wires.drain()


def sum_all(part, asked, back, mats, small, losses):
    vmem = pl.BlockSpec(memory_space=pltpu.VMEM)
    value = (8, 128)
    return pl.pallas_call(
        sum_kernel,
        out_shape=(
            jax.ShapeDtypeStruct(value, jnp.float32),
            jax.ShapeDtypeStruct(part.shape, jnp.float32),
        ),
        in_specs=[vmem] * 6,
        out_specs=(vmem, vmem),
        scratch_shapes=[
            pltpu.VMEM((4, RING) + value, jnp.float32),
            pltpu.SemaphoreType.DMA((10,)),
            pltpu.SemaphoreType.DMA((10,)),
        ],
        compiler_params=pltpu.CompilerParams(
            collective_id=2, has_side_effects=True, vmem_limit_bytes=32 * 2**20
        ),
        cost_estimate=pl.CostEstimate(flops=0, bytes_accessed=40 * 10**6, transcendentals=0),
        name="sum_all",
    )(part, asked, back, mats, small, losses)


def update_kernel(sums_ref, *refs):
    norm = jnp.sqrt(sums_ref[1:2, 0:1])
    factor = clip_bound / jnp.maximum(norm, clip_bound)
    for n in range(2):
        weight, moment, average, grad = refs[4 * n : 4 * n + 4]
        outs = refs[8 + 4 * n : 12 + 4 * n]
        rows = weight.shape[0]
        results = renew(weight[...], moment[...], average[...], grad[:rows, :], factor)
        for out, value in zip(outs, results):
            out[...] = value


def update(sums, table, mats):
    vmem = pl.BlockSpec(memory_space=pltpu.VMEM)
    shapes = []
    for item in (table[0], mats[0]):
        shapes += [jax.ShapeDtypeStruct(item.shape, jnp.float32)] * 3
        shapes += [jax.ShapeDtypeStruct(item.shape, jnp.bfloat16)]
    outs = pl.pallas_call(
        update_kernel,
        out_shape=tuple(shapes),
        in_specs=[vmem] * 9,
        out_specs=(vmem,) * 8,
        compiler_params=pltpu.CompilerParams(vmem_limit_bytes=40 * 2**20),
        name="update",
    )(sums, *table, *mats)
    return outs[:4], outs[4:]


TILE = 800


def head_kernel(
    f_ref,
    code_ref,
    weight_ref,
    table_ref,
    grad_out,
    dtable_ref,
    loss_ref,
    f_all,
    codes,
    table,
    logits,
    probs,
    tops,
    stats,
    df,
    df_send,
    df_sib,
    ring,
    ring_half,
    ring_full,
    staged,
    send,
    recv,
    load,
    store,
):
    at, core = place()
    x = at[2]
    dp, vocab = lax.axis_index("dp"), lax.axis_index("vocab")
    tok, width = f_ref.shape
    group = f_all.shape[0]
    members = group // tok
    tiles = table.shape[0] // TILE
    low, f32 = jnp.bfloat16, jnp.float32

    def tile_rows(t):
        return pl.ds(pl.multiple_of(t * TILE, TILE), TILE)

    loads = []
    for t in range(tiles):
        op = pltpu.make_async_copy(
            table_ref.at[pl.ds(t * TILE, TILE)], table.at[pl.ds(t * TILE, TILE)], load.at[t]
        )
        op.start()
        loads.append(op)

    peers = [(dp, lax.rem(vocab + by, members)) for by in range(1, members)]
    greet(peers)
    wires = Wires(send, recv)
    sibling = device_at(at, 1 - core)
    right, left = device_at(moved(at, 2, 1), core), device_at(moved(at, 2, 3), core)
    before, after, across = lax.rem(x + 3, RING), lax.rem(x + 1, RING), lax.rem(x + 2, RING)

    def rows_of(at_x, piece=None):
        first = (at_x * 2 + core) * tok
        if piece is None:
            return f_all.at[pl.ds(pl.multiple_of(first, tok), tok)]
        half = tok // 2
        return f_all.at[pl.ds(pl.multiple_of(first + piece * half, half), half)]

    f_all[pl.ds(pl.multiple_of(vocab * tok, tok), tok), :] = f_ref[...]
    own = rows_of(x)
    one, two = wires.copy(own, own, right), wires.copy(own, own, left)
    pending = [wires.copy(own, own, sibling)]
    codes[vocab] = code_ref[...]
    for peer in peers:
        pending.append(wires.copy(codes.at[vocab], codes.at[vocab], peer))
    one.wait_recv()
    one_on = wires.copy(rows_of(before, 0), rows_of(before, 0), right)
    pending.append(wires.copy(rows_of(before), rows_of(before), sibling))
    two.wait_recv()
    two_on = wires.copy(rows_of(after, 1), rows_of(after, 1), left)
    pending.append(wires.copy(rows_of(after), rows_of(after), sibling))
    one_on.wait_recv()
    pending.append(wires.copy(rows_of(across, 0), rows_of(across, 0), sibling))
    two_on.wait_recv()
    pending.append(wires.copy(rows_of(across, 1), rows_of(across, 1), sibling))
    for op in pending:
        op.wait_recv()

    code_row = jnp.concatenate([codes[m, 0:1, :] for m in range(members)], 1) - vocab * table.shape[0]
    code8 = jnp.broadcast_to(code_row, (8, group))
    code16 = jnp.broadcast_to(code_row, (16, group))
    rows8 = lax.broadcasted_iota(jnp.int32, (8, group), 0)
    rows16 = lax.broadcasted_iota(jnp.int32, (16, group), 0)
    slot = TILE // 2
    real = slot - 7
    steps8, steps16 = 5, 5

    def first_pass(t, carry):
        top, total, target = carry
        here = tile_rows(t)
        logits[...] = lax.dot_general(
            table[here, :], f_all[...], (((1,), (1,)), ((), ())), preferred_element_type=f32
        )
        for part in range(2):
            last = pl.ds((part + 1) * slot - 8, 8)
            logits[last, :] = jnp.where(rows8 < 1, logits[last, :], -1e30)

        def look(i, state):
            high, hit = state
            for u in range(steps8):
                first = (i * steps8 + u) * 8
                value = logits[pl.ds(pl.multiple_of(first, 8), 8), :]
                high = jnp.maximum(high, value)
                hit = hit + jnp.where(rows8 + (first + t * TILE) == code8, value, 0.0)
            return high, hit

        high, hit = lax.fori_loop(
            0,
            TILE // (8 * steps8),
            look,
            (jnp.full((8, group), -1e30, f32), jnp.zeros((8, group), f32)),
        )
        top_next = jnp.maximum(top, jnp.max(high, 0, keepdims=True))
        target = target + jnp.sum(hit, 0, keepdims=True)

        def lift(i, acc):
            for u in range(steps16):
                first = (i * steps16 + u) * 16
                value = jnp.exp(logits[pl.ds(pl.multiple_of(first, 16), 16), :] - top_next)
                acc = acc + value
                probs[pl.ds(pl.multiple_of(t * TILE + first, 16), 16), :] = value.astype(low)
            return acc

        acc = lax.fori_loop(
            0, TILE // (16 * steps16), lift, jnp.zeros((16, group), f32)
        )
        total = total * jnp.exp(top - top_next) + jnp.sum(acc, 0, keepdims=True)
        tops[t] = top_next
        return top_next, total, target

    for op in loads:
        op.wait()
    start = (jnp.full((1, group), -1e30, f32), jnp.zeros((1, group), f32), jnp.zeros((1, group), f32))
    found = lax.fori_loop(0, tiles, first_pass, start)
    for k in range(3):
        for m in range(members):
            stats[vocab, k, m : m + 1, :] = found[k][:, m * tok : (m + 1) * tok]
    pending = [wires.copy(stats.at[vocab], stats.at[vocab], peer) for peer in peers]
    for op in pending:
        op.wait_recv()
    peak = stats[0, 0]
    for m in range(1, members):
        peak = jnp.maximum(peak, stats[m, 0])
    total, target = jnp.zeros_like(peak), jnp.zeros_like(peak)
    for m in range(members):
        total = total + stats[m, 1] * jnp.exp(stats[m, 0] - peak)
        target = target + stats[m, 2]
    lse = peak + jnp.log(total)
    weight = weight_ref[...]
    mine = lax.broadcasted_iota(jnp.int32, (members, tok), 0) == vocab
    loss_ref[...] = jnp.where(mine, weight * (lse - target), 0.0)
    lse_row = jnp.concatenate([lse[m : m + 1, :] for m in range(members)], 1)
    weight_row = jnp.concatenate([weight[m : m + 1, :] for m in range(members)], 1)

    df[...] = jnp.zeros_like(df)

    def second_pass(t, unused):
        scale = weight_row * jnp.exp(tops[t] - lse_row)

        def turn(i, unused):
            for u in range(steps16):
                first = t * TILE + (i * steps16 + u) * 16
                here = pl.ds(pl.multiple_of(first, 16), 16)
                value = probs[here, :].astype(f32) * scale
                value = value - jnp.where(rows16 + first == code16, weight_row, 0.0)
                probs[here, :] = value.astype(low)
            return unused

        lax.fori_loop(0, TILE // (16 * steps16), turn, 0)
        here = tile_rows(t)
        df[...] += lax.dot_general(
            probs[here, :], table[here, :], (((0,), (0,)), ((), ())), preferred_element_type=f32
        )
        return unused

    lax.fori_loop(0, tiles, second_pass, 0)

    def third_pass(t):
        if t >= 2:
            stores[t - 2].wait()
        staged[t % 2] = jnp.dot(
            probs[t * TILE : (t + 1) * TILE, :], f_all[...], preferred_element_type=f32
        ).astype(low)
        op = pltpu.make_async_copy(
            staged.at[t % 2], dtable_ref.at[pl.ds(t * TILE, TILE)], store.at[t]
        )
        op.start()
        stores.append(op)

    stores = []
    for m in range(members):
        df_send[m % 2, m // 2] = df[m * tok : (m + 1) * tok, :].astype(low)
    swap = wires.copy(df_send.at[1 - core], df_sib, sibling)
    third_pass(0)
    third_pass(1)
    swap.wait_recv()
    for k in range(RING):
        first = pl.multiple_of((2 * k + core) * tok, tok)
        ring[k] = (df[pl.ds(first, tok), :] + df_sib[k].astype(f32)).astype(low)
    half = tok // 2
    one = wires.copy(ring.at[across, pl.ds(0, half)], ring_half.at[0], right)
    two = wires.copy(ring.at[across, pl.ds(half, half)], ring_half.at[1], left)
    third_pass(2)
    third_pass(3)
    one.wait_recv()
    ring[after, :half] = (ring[after, :half].astype(f32) + ring_half[0].astype(f32)).astype(low)
    one = wires.copy(ring.at[after], ring_full.at[0], right)
    two.wait_recv()
    ring[before, half:] = (ring[before, half:].astype(f32) + ring_half[1].astype(f32)).astype(low)
    two = wires.copy(ring.at[before], ring_full.at[1], left)
    for t in range(4, tiles):
        third_pass(t)
    one.wait_recv()
    two.wait_recv()
    grad_out[...] = ring[x].astype(f32) + ring_full[0].astype(f32) + ring_full[1].astype(f32)
    for op in stores[-2:]:
        op.wait()
    wires.drain()


HEAD_COPIES = 9 + 7 + 7 + 5


def head(final_low, codes, weights, table):
    tok, width = final_low.shape
    rows = table.shape[0]
    members = weights.shape[0]
    group = members * tok
    tiles = rows // TILE
    hbm = pl.BlockSpec(memory_space=pltpu.HBM)
    vmem = pl.BlockSpec(memory_space=pltpu.VMEM)
    low, f32 = jnp.bfloat16, jnp.float32
    return pl.pallas_call(
        head_kernel,
        out_shape=(
            jax.ShapeDtypeStruct((tok, width), f32),
            jax.ShapeDtypeStruct((rows, width), low),
            jax.ShapeDtypeStruct((members, tok), f32),
        ),
        in_specs=[vmem, vmem, vmem, hbm],
        out_specs=(vmem, hbm, vmem),
        scratch_shapes=[
            pltpu.VMEM((group, width), low),
            pltpu.VMEM((members, 8, tok), jnp.int32),
            pltpu.VMEM((rows, width), low),
            pltpu.VMEM((TILE, group), f32),
            pltpu.VMEM((rows, group), low),
            pltpu.VMEM((tiles, 1, group), f32),
            pltpu.VMEM((members, 3, members, tok), f32),
            pltpu.VMEM((group, width), f32),
            pltpu.VMEM((2, RING, tok, width), low),
            pltpu.VMEM((RING, tok, width), low),
            pltpu.VMEM((RING, tok, width), low),
            pltpu.VMEM((2, tok // 2, width), low),
            pltpu.VMEM((2, tok, width), low),
            pltpu.VMEM((2, TILE, width), low),
            pltpu.SemaphoreType.DMA((HEAD_COPIES,)),
            pltpu.SemaphoreType.DMA((HEAD_COPIES,)),
            pltpu.SemaphoreType.DMA((tiles,)),
            pltpu.SemaphoreType.DMA((tiles,)),
        ],
        compiler_params=pltpu.CompilerParams(
            collective_id=3, has_side_effects=True, vmem_limit_bytes=58 * 2**20
        ),
        cost_estimate=pl.CostEstimate(
            flops=6 * group * rows * width, bytes_accessed=4 * rows * width, transcendentals=group * rows
        ),
        name="head",
    )(final_low, codes, weights, table)


TILE_ORDER = (8, 9, 10, 11, 4, 5, 6, 7, 3, 0, 1, 2)
G1, S1, BQ, BV, BPROJ, G2, S2, BFC, BOUT = 0, 1, 2, 3, 4, 5, 6, 7, 11
STEPS = 12
GELU_A, GELU_B = 0.7978845608028654, 0.044715


def across_k(left, right):
    return lax.dot_general(left, right, (((1,), (1,)), ((), ())), preferred_element_type=jnp.float32)


def along_k(left, right):
    return jnp.dot(left, right, preferred_element_type=jnp.float32)


def over_rows(left, right):
    return lax.dot_general(left, right, (((0,), (0,)), ((), ())), preferred_element_type=jnp.float32)


def tile_copy(mats_ref, weights, ready, tile, step):
    rows = weights.shape[1]
    return pltpu.make_async_copy(
        mats_ref.at[pl.ds(tile * rows, rows)], weights.at[step], ready.at[step]
    )


def normed(value):
    centered = value - jnp.mean(value, -1, keepdims=True)
    scale = lax.rsqrt(jnp.mean(centered * centered, -1, keepdims=True) + norm_eps)
    return centered * scale, scale


def norm_back(grad, value, gain):
    unit, scale = normed(value)
    inner = grad * gain
    mean = jnp.mean(inner, -1, keepdims=True)
    slope = jnp.mean(inner * unit, -1, keepdims=True)
    return (
        scale * (inner - mean - unit * slope),
        jnp.sum(grad * unit, 0, keepdims=True),
        jnp.sum(grad, 0, keepdims=True),
    )


def forward_kernel(
    hot_ref,
    rows_ref,
    pos_hot_ref,
    pos_ref,
    mask_ref,
    vec_ref,
    mats_ref,
    x_out,
    a_out,
    qkv_out,
    probs_out,
    o_out,
    mid_out,
    m_out,
    u_out,
    g_out,
    hidden_out,
    final_out,
    cur,
    weights,
    ready,
):
    step = pl.program_id(0)
    layer, s = lax.div(step, STEPS), lax.rem(step, STEPS)
    low, f32 = jnp.bfloat16, jnp.float32
    width = cur.shape[1]
    head_dim = width // H


    def vec(row):
        return vec_ref[layer * STEPS + row]

    @pl.when(step == 0)
    def fetch():
        for n in range(2 * STEPS):
            tile_copy(mats_ref, weights, ready, n, n).start()

    @pl.when(step == 0)
    def embed():
        cur[...] = along_k(hot_ref[...], rows_ref[...]) + across_k(pos_hot_ref[...], pos_ref[...])

    @pl.when(s == 0)
    def first_norm():
        x_out[layer] = cur[...]
        a_out[layer] = (normed(cur[...])[0] * vec(G1) + vec(S1)).astype(low)

    tile_copy(mats_ref, weights, ready, 0, step).wait()

    @pl.when(s < 3)
    def project():
        bias = jnp.where(s == 0, vec(BQ), jnp.where(s == 2, vec(BV), 0.0))
        qkv_out[layer, s] = (across_k(a_out[layer], weights[step]) + bias).astype(low)

    @pl.when(s == 2)
    def attend():
        lanes = lax.broadcasted_iota(jnp.int32, (1, 2 * head_dim), 1)
        for pair in range(H // 2):
            cols = slice(2 * head_dim * pair, 2 * head_dim * (pair + 1))
            q, k, v = (qkv_out[layer, part, :, cols] for part in range(3))
            total = None
            for side in range(2):
                own = (lanes < head_dim) if side == 0 else (lanes >= head_dim)
                scores = across_k(jnp.where(own, q, jnp.zeros_like(q)), k) * head_dim ** (-0.5)
                scores = jnp.where(mask_ref[...] > 0.0, scores, -1000000000.0)
                shifted = jnp.exp(scores - jnp.max(scores, -1, keepdims=True))
                probs = shifted / jnp.sum(shifted, -1, keepdims=True)
                probs_out[layer, 2 * pair + side] = probs
                term = along_k(probs.astype(low), jnp.where(own, v, jnp.zeros_like(v)))
                total = term if total is None else total + term
            o_out[layer, :, cols] = total.astype(low)

    @pl.when(s == 3)
    def second_norm():
        mid = cur[...] + across_k(o_out[layer], weights[step]) + vec(BPROJ)
        mid_out[layer] = mid
        m_out[layer] = (normed(mid)[0] * vec(G2) + vec(S2)).astype(low)
        cur[...] = mid + vec(BOUT)

    @pl.when((s >= 4) & (s < 8))
    def widen():
        u = across_k(m_out[layer], weights[step]) + vec(BFC + s - 4)
        u_out[layer, s - 4] = u
        g = 0.5 * u * (1.0 + jnp.tanh(GELU_A * (u + GELU_B * (u * u * u))))
        g_out[layer, s - 4] = g.astype(low)

    @pl.when(s >= 8)
    def narrow():
        cur[...] += along_k(g_out[layer, s - 8], weights[step])

    @pl.when(step == 2 * STEPS - 1)
    def last_norm():
        hidden_out[...] = cur[...]
        final_out[...] = (normed(cur[...])[0] * vec_ref[2 * STEPS] + vec_ref[2 * STEPS + 1]).astype(low)


def forward_layers(hot, rows, pos_hot, pos, mask, vecs, mats):
    tok, width = hot.shape[0], rows.shape[1]
    low, f32 = jnp.bfloat16, jnp.float32
    shape = jax.ShapeDtypeStruct
    vmem = pl.BlockSpec(memory_space=pltpu.VMEM)
    return pl.pallas_call(
        forward_kernel,
        grid=(2 * STEPS,),
        out_shape=(
            shape((2, tok, width), f32),
            shape((2, tok, width), low),
            shape((2, 3, tok, width), low),
            shape((2, H, tok, tok), f32),
            shape((2, tok, width), low),
            shape((2, tok, width), f32),
            shape((2, tok, width), low),
            shape((2, 4, tok, width), f32),
            shape((2, 4, tok, width), low),
            shape((tok, width), f32),
            shape((tok, width), low),
        ),
        in_specs=[vmem] * 6 + [pl.BlockSpec(memory_space=pltpu.HBM)],
        out_specs=(vmem,) * 11,
        scratch_shapes=[
            pltpu.VMEM((tok, width), f32),
            pltpu.VMEM((2 * STEPS, width, width), low),
            pltpu.SemaphoreType.DMA((2 * STEPS,)),
        ],
        compiler_params=pltpu.CompilerParams(vmem_limit_bytes=58 * 2**20),
        cost_estimate=pl.CostEstimate(
            flops=2 * tok * mats.size, bytes_accessed=2 * mats.size, transcendentals=0
        ),
        name="forward_layers",
    )(hot, rows, pos_hot, pos, mask, vecs, mats)


def backward_kernel(
    grad_ref,
    hidden_ref,
    vec_ref,
    x_ref,
    a_ref,
    qkv_ref,
    probs_ref,
    o_ref,
    mid_ref,
    m_ref,
    u_ref,
    g_ref,
    hot_ref,
    mats_ref,
    dx_out,
    vec_out,
    rows_out,
    acc_out,
    cur,
    wide,
    du_s,
    dqkv_s,
    lefts,
    rights,
    right_send,
    weights,
    ready,
    send_left,
    recv_left,
    send_right,
    recv_right,
):
    step = pl.program_id(0)
    layer, s = 1 - lax.div(step, STEPS), lax.rem(step, STEPS)
    low, f32 = jnp.bfloat16, jnp.float32
    tok, width = cur.shape
    half = width // 2
    head_dim = width // H
    at, core = place()
    sibling = device_at(at, 1 - core)
    last = 2 * STEPS
    slot = lax.rem(step, 4)

    def vec(row):
        return vec_ref[layer * STEPS + row]

    def put(row, value):
        vec_out[layer * STEPS + row] = value

    def to_sibling(src, dst, send, recv):
        return pltpu.make_async_remote_copy(
            src_ref=src,
            dst_ref=dst,
            send_sem=send,
            recv_sem=recv,
            device_id=sibling,
            device_id_type=pl.DeviceIdType.MESH,
        )

    def left_copy(n):
        return to_sibling(
            lefts.at[n, pl.ds(0, tok)],
            lefts.at[n, pl.ds(tok, tok)],
            send_left.at[n],
            recv_left.at[n],
        )

    def right_copy(n):
        return to_sibling(
            right_send.at[n], rights.at[n, pl.ds(tok, tok)], send_right.at[n], recv_right.at[n]
        )

    def set_left(value):
        lefts[slot, :tok, :] = value

    def set_right(n, value):
        pl.when(step >= STEPS)(lambda: right_copy(n).wait_send())
        rights[n, :tok, :] = jnp.where(core == 0, value[:, :half], value[:, half:])
        right_send[n] = jnp.where(core == 0, value[:, half:], value[:, :half])

    @pl.when(step == 0)
    def enter():
        for n in range(last):
            tile = STEPS * (1 - n // STEPS) + TILE_ORDER[n % STEPS]
            tile_copy(mats_ref, weights, ready, tile, n).start()
        greet([sibling])
        dx, dg, ds = norm_back(grad_ref[...], hidden_ref[...], vec_ref[last])
        cur[...] = dx
        vec_out[last] = dg
        vec_out[last + 1] = ds

    @pl.when(step < last)
    def arrived():
        tile_copy(mats_ref, weights, ready, 0, step).wait()

    pl.when((step >= 4) & (step < last))(lambda: left_copy(slot).wait_send())

    @pl.when((s == 0) & (step < last))
    def begin():
        put(BOUT, jnp.sum(cur[...], 0, keepdims=True))
        set_right(0, cur[...].astype(low))
        wide[...] = cur[...].astype(low)

    @pl.when((s < 4) & (step < last))
    def through_gelu():
        dg = across_k(wide[...], weights[step])
        u = u_ref[layer, s]
        square = u * u
        t = jnp.tanh(GELU_A * (u + GELU_B * (square * u)))
        slope = 0.5 * (1.0 + t) + (0.5 * GELU_A) * u * (1.0 - t * t) * (1.0 + (3.0 * GELU_B) * square)
        du = dg * slope
        put(BFC + s, jnp.sum(du, 0, keepdims=True))
        du_s[s] = du.astype(low)
        set_left(g_ref[layer, s])

    @pl.when(s == 4)
    def begin_fc():
        set_right(1, m_ref[layer])
        dx_out[...] = jnp.zeros_like(dx_out)

    @pl.when((s >= 4) & (s < 8))
    def through_fc():
        left = du_s[s - 4]
        dx_out[...] += along_k(left, weights[step])
        set_left(left)

    @pl.when(s == 8)
    def through_attention():
        dx, dg, ds = norm_back(dx_out[...], mid_ref[layer], vec(G2))
        put(G2, dg)
        put(S2, ds)
        cur[...] = cur[...] + dx
        put(BPROJ, jnp.sum(cur[...], 0, keepdims=True))
        mid_low = cur[...].astype(low)
        set_left(mid_low)
        set_right(2, o_ref[layer])
        wide[...] = along_k(mid_low, weights[step]).astype(low)
        lanes = lax.broadcasted_iota(jnp.int32, (1, 2 * head_dim), 1)
        scale = head_dim ** (-0.5)
        for pair in range(H // 2):
            cols = slice(2 * head_dim * pair, 2 * head_dim * (pair + 1))
            q, k, v = (qkv_ref[layer, part, :, cols] for part in range(3))
            do = wide[:, cols]
            parts = [None] * 3
            for side in range(2):
                own = (lanes < head_dim) if side == 0 else (lanes >= head_dim)
                keep = lambda item, own=own: jnp.where(own, item, jnp.zeros_like(item))
                probs = probs_ref[layer, 2 * pair + side]
                do_own = keep(do)
                dprobs = across_k(do_own, v)
                dscores = probs * (dprobs - jnp.sum(probs * dprobs, -1, keepdims=True))
                dlow = (dscores * scale).astype(low)
                terms = (
                    along_k(dlow, keep(k)),
                    over_rows(dlow, keep(q)),
                    over_rows(probs.astype(low), do_own),
                )
                parts = [
                    term if held is None else held + term for held, term in zip(parts, terms)
                ]
            for part in range(3):
                dqkv_s[part, :, cols] = parts[part].astype(low)
            vec_out[layer * STEPS + BQ, :, cols] = jnp.sum(parts[0], 0, keepdims=True)
            vec_out[layer * STEPS + BV, :, cols] = jnp.sum(parts[2], 0, keepdims=True)

    @pl.when(s == 9)
    def begin_qkv():
        set_right(3, a_ref[layer])
        dx_out[...] = jnp.zeros_like(dx_out)

    @pl.when(s >= 9)
    def through_qkv():
        left = dqkv_s[s - 9]
        dx_out[...] += along_k(left, weights[step])
        set_left(left)

    def kind_of(at_s):
        return jnp.where(at_s < 4, 0, jnp.where(at_s < 8, 1, jnp.where(at_s == 8, 2, 3)))

    def fresh(at_s):
        return (at_s == 0) | (at_s == 4) | (at_s == 8) | (at_s == 9)

    @pl.when(step >= 2)
    def gradient():
        slot_then, s_then = lax.rem(step - 2, 4), lax.rem(step - 2, STEPS)
        kind = kind_of(s_then)
        left_copy(slot_then).wait_recv()
        pl.when(fresh(s_then))(lambda: right_copy(kind).wait_recv())
        grad = over_rows(lefts[slot_then], rights[kind])
        acc_out[0] = grad.astype(low).reshape(acc_out.shape[1:])

    @pl.when(step < last)
    def share():
        left_copy(slot).start()
        pl.when(fresh(s))(lambda: right_copy(kind_of(s)).start())

    @pl.when(s == STEPS - 1)
    def end_layer():
        dx, dg, ds = norm_back(dx_out[...], x_ref[layer], vec(G1))
        put(G1, dg)
        put(S1, ds)
        cur[...] = cur[...] + dx

    @pl.when(step == last + 1)
    def leave():
        dx_out[...] = cur[...]
        rows = over_rows(hot_ref[...], cur[...].astype(low)).astype(low)
        rows_out[...] = rows.reshape(rows_out.shape)
        for n in range(4):
            left_copy(n).wait_send()
            right_copy(n).wait_send()


def backward_layers(grad, hidden, vecs, saved, hot, mats):
    tok, width = grad.shape
    low, f32 = jnp.bfloat16, jnp.float32
    shape = jax.ShapeDtypeStruct
    vmem = pl.BlockSpec(memory_space=pltpu.VMEM)
    hbm = pl.BlockSpec(memory_space=pltpu.HBM)
    half, part = width // 2, 48
    granules = width // part

    def tile(i):
        i = jnp.clip(i - 2, 0, 2 * STEPS - 1)
        layer, s = 1 - i // STEPS, i % STEPS
        return (
            layer,
            jnp.where(s < 4, 8 + s, jnp.where(s < 8, s, jnp.where(s == 8, 3, s - 9))),
            0,
            0,
        )

    return pl.pallas_call(
        backward_kernel,
        grid=(2 * STEPS + 2,),
        out_shape=(
            shape((tok, width), f32),
            shape((2 * STEPS + 2, 1, width), f32),
            shape((RING, 2, 32, width), low),
            shape((2, STEPS * granules, part, half), low),
        ),
        in_specs=[vmem] * 13 + [hbm],
        out_specs=(vmem, vmem, vmem, pl.BlockSpec((1, granules, part, half), tile)),
        scratch_shapes=[
            pltpu.VMEM((tok, width), f32),
            pltpu.VMEM((tok, width), low),
            pltpu.VMEM((4, tok, width), low),
            pltpu.VMEM((3, tok, width), low),
            pltpu.VMEM((4, 2 * tok, width), low),
            pltpu.VMEM((4, 2 * tok, half), low),
            pltpu.VMEM((4, tok, half), low),
            pltpu.VMEM((2 * STEPS, width, width), low),
            pltpu.SemaphoreType.DMA((2 * STEPS,)),
            pltpu.SemaphoreType.DMA((4,)),
            pltpu.SemaphoreType.DMA((4,)),
            pltpu.SemaphoreType.DMA((4,)),
            pltpu.SemaphoreType.DMA((4,)),
        ],
        compiler_params=pltpu.CompilerParams(
            collective_id=4, has_side_effects=True, vmem_limit_bytes=60 * 2**20
        ),
        cost_estimate=pl.CostEstimate(
            flops=4 * tok * mats.size, bytes_accessed=2 * mats.size, transcendentals=0
        ),
        name="backward_layers",
    )(grad, hidden, vecs, *saved, hot, mats)


def doc_info(doc_lens, tok_count, total_docs):
    doc_ends = jnp.cumsum(doc_lens)
    places = jnp.arange(tok_count, dtype=jnp.int32)
    seg_ids = jnp.sum((places[:, None] >= doc_ends[None, :]).astype(jnp.int32), 1)
    one_hot = seg_ids[:, None] == jnp.arange(doc_lens.shape[0], dtype=jnp.int32)[None, :]
    starts = doc_ends - doc_lens
    pos_ids = places - jnp.sum(jnp.where(one_hot, starts[None, :], 0), 1)
    doc_len = jnp.sum(jnp.where(one_hot, doc_lens[None, :], 0), 1)
    weights = 1.0 / (doc_len.astype(jnp.float32) * total_docs)
    return (seg_ids, pos_ids, weights)


def device_rise(first, count, devices):
    places = first + jnp.arange(count, dtype=jnp.int32)
    return 1.0 + 2.0 * places.astype(jnp.float32) / (devices - 1)


def contract(left, right, left_dim, right_dim):
    return lax.dot_general(
        left, right, (((left_dim,), (right_dim,)), ((), ())), preferred_element_type=jnp.float32
    )


def renew(weight, moment, average, grad, factor):
    clipped = factor * grad
    moment_next = momentum_coef * moment + clipped
    weight_next = weight - learn_rate * (clipped + momentum_coef * moment_next)
    average_next = ema_decay * average + (1.0 - ema_decay) * weight_next
    return (moment_next, weight_next, average_next, weight_next.astype(jnp.bfloat16))


SMALL_ROWS, LANES = 16, 128


def pack_small(values):
    room = SMALL_ROWS * LANES - values.shape[-1]
    pads = [(0, 0)] * (values.ndim - 1) + [(0, room)]
    return jnp.pad(values, pads).reshape(values.shape[:-1] + (SMALL_ROWS, LANES))


def per_device(
    token_ids,
    targets,
    lengths,
    embed_table,
    embed_moment,
    embed_average,
    blocks,
    block_moment,
    block_average,
    pos_table,
    pos_moment,
    pos_average,
    vectors,
    vector_moment,
    vector_average,
):
    devices = lax.axis_size(("dp", "vocab"))
    vocab_count = lax.axis_size("vocab")
    dp_count = lax.axis_size("dp")
    vocab_at = lax.axis_index("vocab")
    data_at = lax.axis_index("dp")
    tok = token_ids.shape[0]
    own_rows, width = embed_table.shape
    capacity = max(2, 2 * tok // devices)
    low = jnp.bfloat16
    blocks, block_moment, block_average = (
        jnp.transpose(item, (0, 2, 1)) for item in (blocks, block_moment, block_average)
    )
    pos_rows, pos_cols = pos_table.shape
    vec_own = vectors.shape[0]
    table_low = embed_table.astype(low)
    pad_rows = -own_rows % 16
    table_padded = jnp.pad(table_low, ((0, pad_rows), (0, 0)))
    slot_rows = own_rows + pad_rows

    table_slice = lax.all_gather(table_padded, "dp", axis=0, tiled=True)
    target_owners = targets // own_rows
    codes = (
        (target_owners % vocab_count) * (dp_count * slot_rows)
        + (target_owners // vocab_count) * slot_rows
        + targets % own_rows
    )

    owners = token_ids // own_rows
    tokens = jnp.arange(tok, dtype=jnp.int32)
    rank = jnp.sum((owners[:, None] == owners[None, :]) & (tokens[None, :] < tokens[:, None]), 1)
    slot_count = devices * capacity
    slots = jnp.arange(slot_count, dtype=jnp.int32)
    arrival = (
        (owners % 8) * 32 + (owners // 8 % RING) * 8 + (owners // 32) * capacity + rank
    )
    slot_hot = (arrival[:, None] == slots[None, :]).astype(low)
    spread = (slots[:, None] // capacity == jnp.arange(devices)[None, :]).astype(low)
    earlier = (tokens[:, None] < tokens[None, :]).astype(low)
    slot_number = jnp.broadcast_to((slots % capacity).astype(jnp.float32)[:, None], (slot_count, tok))
    by_owner = (
        (slots % 64 // 16) * 2 + slots // 64 * 8 + slots % 16 // 2 * 32 + slots % capacity
    )
    swap = (by_owner[:, None] == slots[None, :]).astype(low)
    values = jnp.concatenate([jnp.transpose(pos_table).reshape(-1), vectors]).astype(low)
    small = jnp.concatenate(
        [
            jnp.pad(values, (0, IDS_ROW * LANES - values.shape[0])).reshape(IDS_ROW, LANES),
            jnp.stack([token_ids // 256, token_ids % 256]).astype(low),
            jnp.zeros((SMALL_ROWS - IDS_ROW - 2, LANES), low),
        ]
    )
    mats_all, small_all, returned_rows, asked = gather_weights(
        blocks, small, table_padded, spread, earlier, slot_number, jnp.transpose(swap)
    )
    small_all = small_all.reshape(devices, -1)
    pos_low_t = small_all[:, : pos_rows * pos_cols].reshape(width, pos_rows)
    vecs_all = (
        small_all[:, pos_rows * pos_cols : pos_rows * pos_cols + vec_own]
        .reshape(-1)
        .astype(jnp.float32)
    )
    lens_group = lengths[0]
    seg_group, pos_group, weight_group = jax.vmap(
        partial(doc_info, tok_count=tok, total_docs=devices * lens_group.shape[1])
    )(lens_group)
    weight_group = weight_group * device_rise(data_at * vocab_count, vocab_count, devices)[:, None]
    seg_ids = lax.dynamic_index_in_dim(seg_group, vocab_at, 0, keepdims=False)
    pos_ids = lax.dynamic_index_in_dim(pos_group, vocab_at, 0, keepdims=False)
    places = jnp.arange(tok, dtype=jnp.int32)
    attn_mask = (seg_ids[:, None] == seg_ids[None, :]) & (places[None, :] <= places[:, None])

    pos_hot = (pos_ids[:, None] == jnp.arange(pos_rows, dtype=jnp.int32)[None, :]).astype(low)
    vec_rows = vecs_all.reshape(-1, 1, width)
    *saved, hidden, final_low = forward_layers(
        slot_hot,
        returned_rows,
        pos_hot,
        pos_low_t,
        attn_mask.astype(jnp.float32),
        vec_rows,
        mats_all,
    )
    grad_final, table_part, token_losses = head(
        final_low, jnp.broadcast_to(codes[None, :], (8, tok)), weight_group, table_slice
    )
    table_part = lax.psum_scatter(table_part, "dp", scatter_dimension=0, tiled=True)
    grad_hidden, grad_vecs, rows_back, grad_acc = backward_layers(
        grad_final, hidden, vec_rows, saved, slot_hot, mats_all
    )
    grad_pos = lax.dot_general(
        grad_hidden,
        pos_hot.astype(jnp.float32),
        (((0,), (0,)), ((), ())),
        precision=lax.Precision.HIGHEST,
    )
    small_grads = pack_small(
        jnp.concatenate(
            [grad_pos.reshape(devices, -1), grad_vecs.reshape(devices, -1)], 1
        )
    )
    mats_shard, small_shard, back_grads = reduce_weights(grad_acc.reshape(2, RING, RING, RING, 3, 48, width // 2), small_grads, rows_back, swap)
    both_sums, table_grad = sum_all(
        table_part,
        asked,
        back_grads.reshape(slot_count, width),
        mats_shard,
        small_shard,
        token_losses,
    )
    small_shard = small_shard.reshape(-1)
    pos_shard = small_shard[: pos_rows * pos_cols].reshape(pos_cols, pos_rows)
    vec_shard = small_shard[pos_rows * pos_cols : pos_rows * pos_cols + vec_own]
    loss_sum, squares = both_sums[0, 0], both_sums[1, 0]
    grad_norm = jnp.sqrt(squares)
    factor = clip_bound / jnp.maximum(grad_norm, clip_bound)
    own_shape = blocks.shape
    flat = lambda item: item.reshape(-1, width)
    embed_out, block_out = update(
        both_sums,
        (embed_table, embed_moment, embed_average, table_grad),
        (flat(blocks), flat(block_moment), flat(block_average), flat(mats_shard)),
    )
    block_out = tuple(
        jnp.transpose(item.reshape(own_shape), (0, 2, 1)) for item in block_out
    )
    pos_out = renew(
        jnp.transpose(pos_table),
        jnp.transpose(pos_moment),
        jnp.transpose(pos_average),
        pos_shard,
        factor,
    )
    pos_out = tuple(jnp.transpose(item) for item in pos_out)
    vector_out = renew(vectors, vector_moment, vector_average, vec_shard, factor)
    return (loss_sum, grad_norm) + tuple(embed_out) + block_out + pos_out + vector_out


def solution(mesh):
    table = P(("dp", "vocab"), None)
    cols = P(None, None, ("dp", "vocab"))
    pos = P(None, ("dp", "vocab"))
    vec = P(("dp", "vocab"))
    return jax.shard_map(
        per_device,
        mesh=mesh,
        in_specs=(vec, vec, P("dp", None, None))
        + (table,) * 3
        + (cols,) * 3
        + (pos,) * 3
        + (vec,) * 3,
        out_specs=(P(), P()) + (table,) * 4 + (cols,) * 4 + (pos,) * 4 + (vec,) * 4,
        check_vma=False,
    )
```

```python
from functools import partial

import jax
import jax.numpy as jnp
import ml_dtypes
import numpy as np
from jax import lax
from jax.experimental import pallas as pl
from jax.experimental.pallas import tpu as pltpu
from jax.sharding import PartitionSpec as P

H = 12
RING = 4
ORDERS = ((2, 1, 0), (1, 0, 2), (0, 2, 1))

norm_eps = 1e-05
clip_bound = 0.01
learn_rate = 10000.0
momentum_coef = 0.5
ema_decay = 0.5


def place():
    dp = lax.axis_index("dp")
    vocab = lax.axis_index("vocab")
    return (lax.div(dp, RING), lax.rem(dp, RING), lax.div(vocab, 2)), lax.rem(vocab, 2)


def device_at(at, core):
    return (at[0] * RING + at[1], at[2] * 2 + core)


def moved(at, axis, by):
    out = list(at)
    out[axis] = lax.rem(at[axis] + by, RING)
    return tuple(out)


class Wires:
    def __init__(self, send, recv):
        self.send, self.recv, self.count, self.live = send, recv, 0, []

    def copy(self, src, dst, device):
        number = self.count
        self.count += 1
        op = pltpu.make_async_remote_copy(
            src_ref=src,
            dst_ref=dst,
            send_sem=self.send.at[number],
            recv_sem=self.recv.at[number],
            device_id=device,
            device_id_type=pl.DeviceIdType.MESH,
        )
        op.start()
        self.live.append(op)
        return op

    def drain(self):
        for op in self.live:
            op.wait_send()


def greet(devices):
    barrier = pltpu.get_barrier_semaphore()
    for device in devices:
        pl.semaphore_signal(
            barrier, inc=1, device_id=device, device_id_type=pl.DeviceIdType.MESH
        )
    pl.semaphore_wait(barrier, len(devices))


def ring_peers(at, core):
    near = [device_at(moved(at, axis, by), core) for axis in range(3) for by in range(1, RING)]
    return near + [device_at(at, 1 - core)]


def neighbours(at, core):
    near = [device_at(moved(at, axis, by), core) for axis in range(3) for by in (1, RING - 1)]
    return near + [device_at(at, 1 - core)]


def gather_kernel(
    mine_ref,
    small_ref,
    table_ref,
    spread_ref,
    earlier_ref,
    slot_ref,
    swap_ref,
    out_ref,
    small_out,
    rows_out,
    asked_out,
    peer,
    block,
    asked_rows,
    over_z,
    over_y,
    sorted_rows,
    over_x,
    send,
    recv,
    local,
):
    at, core = place()
    z, y, x = at
    rows, half = mine_ref.shape[1], mine_ref.shape[2] // 2
    part = 2 * rows // 3
    low, f32 = jnp.bfloat16, jnp.float32
    sibling = device_at(at, 1 - core)
    greet(ring_peers(at, core))
    wires = Wires(send, recv)
    cols = pl.ds(pl.multiple_of(core * half, half), half)
    other = pl.ds(pl.multiple_of((1 - core) * half, half), half)

    swap = wires.copy(mine_ref.at[:, :, other], peer, sibling)
    small_out[z, y, x, core] = small_ref[...]

    def right(axis):
        return device_at(moved(at, axis, 1), core)

    def left(axis):
        return device_at(moved(at, axis, RING - 1), core)

    def all_around(axis, src_of, dst):
        out = []
        for by in range(1, RING):
            there = moved(at, axis, by)
            out.append(wires.copy(src_of(there[axis]), dst, device_at(there, core)))
        return out

    def small_start(phase):
        index = [z, y, x]
        for axis in ORDERS[0][:phase]:
            index[axis] = pl.ds(0, RING)
        own = small_out.at[index[0], index[1], index[2], core]
        return all_around(ORDERS[0][phase], lambda c: own, own)

    def arrive(ops):
        for op in ops:
            op.wait_recv()

    small_ops = small_start(0)
    swap.wait_recv()
    for layer in range(2):
        own = jnp.where(core == 0, mine_ref[layer, :, :half], mine_ref[layer, :, half:])
        got = peer[layer]
        both = jnp.concatenate(
            [jnp.where(core == 0, own, got), jnp.where(core == 0, got, own)], 0
        )
        block[layer] = both.astype(low)
    block_local = []
    for layer in range(2):
        op = pltpu.make_async_copy(
            block.at[layer], out_ref.at[layer, z, y, x, :, cols], local.at[layer]
        )
        op.start()
        block_local.append(op)

    def bundle(layer, p, phase, c, piece=None):
        order = ORDERS[p]
        index = list(at)
        index[order[phase]] = c
        for axis in order[:phase]:
            index[axis] = pl.ds(0, RING)
        first, count = p * part, part
        if piece is not None:
            if phase == 0:
                first, count = (first, 32) if piece == 0 else (first + 32, part - 32)
            else:
                index[order[0]] = pl.ds(2 * piece, 2)
        return out_ref.at[layer, index[0], index[1], index[2], pl.ds(first, count), cols]

    chains = [(layer, p) for layer in range(2) for p in range(3)]
    pending = []
    steps, forwards = {}, {}

    def start(phase):
        for key in chains:
            layer, p = key
            axis = ORDERS[p][phase]
            src = bundle(layer, p, phase, at[axis])
            if phase == 2:
                pending.append(wires.copy(src, src, sibling))
            steps[key] = (wires.copy(src, src, right(axis)), wires.copy(src, src, left(axis)))

    def forward(phase):
        for key in chains:
            layer, p = key
            axis = ORDERS[p][phase]
            before, after = lax.rem(at[axis] + 3, RING), lax.rem(at[axis] + 1, RING)
            steps[key][0].wait_recv()
            src = bundle(layer, p, phase, before, 0)
            one = wires.copy(src, src, right(axis))
            steps[key][1].wait_recv()
            src = bundle(layer, p, phase, after, 1)
            two = wires.copy(src, src, left(axis))
            forwards[key] = (one, two)
            if phase == 2:
                for c in (before, after):
                    src = bundle(layer, p, phase, c)
                    pending.append(wires.copy(src, src, sibling))

    def finish(phase):
        for key in chains:
            layer, p = key
            axis = ORDERS[p][phase]
            across = lax.rem(at[axis] + 2, RING)
            for piece in range(2):
                forwards[key][piece].wait_recv()
                if phase == 2:
                    src = bundle(layer, p, phase, across, piece)
                    pending.append(wires.copy(src, src, sibling))

    arrive(block_local_wait(block_local))
    start(0)
    arrive(small_ops)
    small_ops = small_start(1)
    forward(0)
    arrive(small_ops)
    small_ops = small_start(2)
    finish(0)
    start(1)
    arrive(small_ops)
    own = small_out.at[:, :, :, core]
    small_ops = [wires.copy(own, own, sibling)]
    forward(1)
    arrive(small_ops)

    count = 2 * RING**3
    smalls = small_out[...].reshape((count,) + small_ref.shape)
    high, rest = (
        jnp.dot(spread_ref[...], smalls[:, IDS_ROW + n, :], preferred_element_type=f32)
        for n in range(2)
    )
    own_rows = TABLE_ROWS
    me = ((z * RING + y) * RING + x) * 2 + core
    local_id = high * 256.0 + rest - (me * own_rows).astype(f32)
    mine = (local_id >= 0.0) & (local_id < float(own_rows))
    rank = jnp.dot(
        jnp.where(mine, 1.0, 0.0).astype(low), earlier_ref[...], preferred_element_type=f32
    )
    picked = jnp.where(mine & (rank == slot_ref[...]), local_id, 0.0)
    row = jnp.sum(picked, 1, keepdims=True).astype(jnp.int32)
    places = lax.broadcasted_iota(jnp.int32, asked_out.shape, 1)
    asked = jnp.where(places == row, 1.0, 0.0).astype(low)
    asked_out[...] = asked
    found = jnp.dot(asked, table_ref[...], preferred_element_type=f32).astype(low)
    asked_rows[...] = found.reshape(asked_rows.shape)
    over_z[z] = asked_rows[z]
    row_ops = all_around(0, lambda c: asked_rows.at[c], over_z.at[z])

    finish(1)
    start(2)
    arrive(row_ops)
    over_y[y] = over_z[:, y]
    row_ops = all_around(1, lambda c: over_z.at[:, c], over_y.at[y])
    forward(2)
    arrive(row_ops)
    sorted_rows[...] = (
        jnp.dot(
            swap_ref[...], over_y[...].reshape(2 * count, table_ref.shape[1]), preferred_element_type=f32
        )
        .astype(low)
        .reshape(sorted_rows.shape)
    )
    over_x[x] = sorted_rows[x]
    row_ops = all_around(2, lambda c: sorted_rows.at[c], over_x.at[x])
    finish(2)
    arrive(row_ops)
    pending.append(wires.copy(over_x.at[:, 1 - core], rows_out.at[:, core], sibling))
    rows_out[:, core] = over_x[:, core]
    arrive(pending)
    wires.drain()


def block_local_wait(ops):
    for op in ops:
        op.wait()
    return []


IDS_ROW = 8
TABLE_ROWS = 393
GATHER_COPIES = 1 + 3 * (6 * 4 + 3) + 6 * 5 + 1 + 9 + 1


def gather_weights(mine, small, table, spread, earlier, slots, swap):
    layers, rows, width = mine.shape
    table_rows = table.shape[0]
    count = 2 * RING**3
    low = jnp.bfloat16
    hbm = pl.BlockSpec(memory_space=pltpu.HBM)
    vmem = pl.BlockSpec(memory_space=pltpu.VMEM)
    mats, small_all, fetched, asked = pl.pallas_call(
        gather_kernel,
        out_shape=(
            jax.ShapeDtypeStruct((layers, RING, RING, RING, 2 * rows, width), low),
            jax.ShapeDtypeStruct((RING, RING, RING, 2) + small.shape, low),
            jax.ShapeDtypeStruct((RING, 2, count // 4, width), low),
            jax.ShapeDtypeStruct((2 * count, table_rows), low),
        ),
        in_specs=[vmem] * 7,
        out_specs=(hbm, vmem, vmem, vmem),
        scratch_shapes=[
            pltpu.VMEM((layers, rows, width // 2), jnp.float32),
            pltpu.VMEM((layers, 2 * rows, width // 2), low),
            pltpu.VMEM((RING, RING, 16, width), low),
            pltpu.VMEM((RING, RING, 16, width), low),
            pltpu.VMEM((RING, RING, 16, width), low),
            pltpu.VMEM((RING, 2, count // 4, width), low),
            pltpu.VMEM((RING, 2, count // 4, width), low),
            pltpu.SemaphoreType.DMA((GATHER_COPIES,)),
            pltpu.SemaphoreType.DMA((GATHER_COPIES,)),
            pltpu.SemaphoreType.DMA((2,)),
        ],
        compiler_params=pltpu.CompilerParams(
            collective_id=0, has_side_effects=True, vmem_limit_bytes=58 * 2**20
        ),
        cost_estimate=pl.CostEstimate(flops=0, bytes_accessed=250 * 10**6, transcendentals=0),
        name="gather_weights",
    )(mine, small, table, spread, earlier, slots, swap)
    return (
        mats.reshape(layers * RING**3 * 2 * rows, width),
        small_all.reshape((count,) + small.shape),
        fetched.reshape(2 * count, width),
        asked,
    )


SUM_PARTS = ((0, 2), (2, 5), (7, 2))


class Reduction:
    def __init__(self, at, core, send, recv):
        self.at, self.core, self.send, self.recv = at, core, send, recv
        self.number, self.level, self.halves, self.fulls = {}, {}, {}, {}
        self.final = None

    def copy(self, key, src, dst, device):
        number = self.number.setdefault(key, len(self.number))
        return pltpu.make_async_remote_copy(
            src_ref=src,
            dst_ref=dst,
            send_sem=self.send.at[number],
            recv_sem=self.recv.at[number],
            device_id=device,
            device_id_type=pl.DeviceIdType.MESH,
        )

    def axes(self, p):
        order = ORDERS[p]
        free = sorted(order[:2])
        return free, free.index(order[1])

    def ring(self, p, step):
        axis = ORDERS[p][2 - step]
        c = self.at[axis]
        right = device_at(moved(self.at, axis, 1), self.core)
        left = device_at(moved(self.at, axis, RING - 1), self.core)
        return c, lax.rem(c + 1, RING), lax.rem(c + 2, RING), lax.rem(c + 3, RING), right, left

    def index(self, layer, p, step, c, piece=None):
        cut, whole = (0, RING) if piece is None else (2 * piece, 2), (0, RING)
        if step == 0:
            free, unused = self.axes(p)
            spot = [c, c, c]
            spot[free[0]], spot[free[1]] = cut, whole
            return spot + [pl.ds(*SUM_PARTS[p])]
        if step == 1:
            unused, first = self.axes(p)
            spot = [cut, cut]
            spot[first] = c
            return [layer] + spot
        if piece is None:
            return [layer, c]
        return [layer, c, pl.ds(*self.cut(p, piece))]

    def cut(self, p, piece):
        count = SUM_PARTS[p][1]
        first = (count + 1) // 2
        return (0, first) if piece == 0 else (first, count - first)

    def view(self, layer, p, step, c, piece=None):
        index = self.index(layer, p, step, c, piece)
        held = self.held(layer, p, step)
        return held.at[tuple(pl.ds(*item) if isinstance(item, tuple) else item for item in index)]

    def held(self, layer, p, step):
        return self.level[0, layer] if step == 0 else self.level[step][p]

    def slot(self, layer, p, step, side, whole):
        store = (self.fulls if whole else self.halves)[step][p]
        if step == 2 and not whole:
            return store.at[layer, side, pl.ds(0, self.cut(p, side)[1])]
        return store.at[layer, side]

    def half_copies(self, layer, p, step):
        unused, after, across, before, right, left = self.ring(p, step)
        out = []
        for side, device in ((0, right), (1, left)):
            out.append(
                self.copy(
                    (layer, p, step, side),
                    self.view(layer, p, step, across, side),
                    self.slot(layer, p, step, side, False),
                    device,
                )
            )
        return out

    def full_copies(self, layer, p, step):
        unused, after, across, before, right, left = self.ring(p, step)
        out = []
        for side, c, device in ((0, after, right), (1, before, left)):
            out.append(
                self.copy(
                    (layer, p, step, 2 + side),
                    self.view(layer, p, step, c),
                    self.slot(layer, p, step, side, True),
                    device,
                )
            )
        return out

    def add(self, layer, p, step, c, piece, terms, into):
        held = self.held(layer, p, step)
        index = self.index(layer, p, step, c, piece)
        sizes = [item[1] for item in index if isinstance(item, tuple)]

        def one(inner):
            places = iter(inner)
            spot = tuple(
                item[0] + next(places) if isinstance(item, tuple) else item for item in index
            )
            value = held[spot].astype(jnp.float32)
            for term in terms:
                value = value + term[tuple(inner) + (slice(None),) * 3].astype(jnp.float32)
            into(held, spot, inner, value)

        def body(n, unused):
            if len(sizes) == 2:
                for k in range(sizes[1]):
                    one([n, k])
            else:
                one([n])
            return unused

        if sizes:
            lax.fori_loop(0, sizes[0], body, 0)
        else:
            one([])

    def start(self, layer, step):
        for p in range(3):
            for op in self.half_copies(layer, p, step):
                op.start()

    def turn(self, layer, step):
        def back(held, spot, inner, value):
            held[spot] = value.astype(held.dtype)

        for p in range(3):
            unused, after, across, before, right, left = self.ring(p, step)
            halves, fulls = self.half_copies(layer, p, step), self.full_copies(layer, p, step)
            for side, c in ((0, after), (1, before)):
                halves[side].wait_recv()
                self.add(
                    layer, p, step, c, side, [self.slot(layer, p, step, side, False)], back
                )
                fulls[side].start()

    def finish(self, layer, step):
        for p in range(3):
            c = self.ring(p, step)[0]
            for op in self.full_copies(layer, p, step):
                op.wait_recv()
            terms = [self.slot(layer, p, step, side, True) for side in range(2)]

            def up(held, spot, inner, value, p=p):
                if step == 2:
                    first, count = SUM_PARTS[p]
                    rows = value.reshape(count * value.shape[1], value.shape[2])
                    self.final[layer, 16 * first : 16 * (first + count)] = rows
                else:
                    target = self.level[step + 1][p]
                    target[(layer,) + tuple(inner)] = value.astype(target.dtype)

            self.add(layer, p, step, c, None, terms, up)

    def drain(self, layer, step):
        for p in range(3):
            for op in self.half_copies(layer, p, step) + self.full_copies(layer, p, step):
                op.wait_send()


def reduce_kernel(
    acc_ref,
    small_ref,
    rows_ref,
    swap_ref,
    out_ref,
    small_out,
    rows_out,
    acc_0,
    acc_1,
    by_part,
    small_acc,
    small_sib,
    small_wide,
    small_mid,
    small_thin,
    final,
    final_peer,
    over_core,
    over_x,
    sorted_rows,
    over_y,
    send,
    recv,
    send_small,
    recv_small,
    local,
):
    at, core = place()
    own_rows, half = final_peer.shape[1], final_peer.shape[2]
    sibling = device_at(at, 1 - core)
    sums = Reduction(at, core, send, recv)
    sums.level = {(0, 0): acc_0, (0, 1): acc_1, 1: by_part[0], 2: by_part[1]}
    sums.halves = dict(enumerate(by_part[2:5]))
    sums.fulls = dict(enumerate(by_part[5:8]))
    sums.final = final

    accs = (acc_0, acc_1)
    loads = {}
    for layer in (1, 0):
        for n in range(RING * RING):
            spot = (n // RING, n % RING)
            op = pltpu.make_async_copy(
                acc_ref.at[(layer,) + spot], accs[layer].at[spot], local.at[1 + 16 * layer + n]
            )
            op.start()
            loads[layer, n] = op
    small_load = pltpu.make_async_copy(small_ref.at[:, :, :, core], small_acc, local.at[0])
    small_load.start()
    greet(ring_peers(at, core))
    wires = Wires(send_small, recv_small)
    small_swap = wires.copy(small_ref.at[:, :, :, 1 - core], small_sib, sibling)

    order = ORDERS[0]
    slots = (small_wide, small_mid, small_thin)

    def right(axis):
        return device_at(moved(at, axis, 1), core)

    def left(axis):
        return device_at(moved(at, axis, RING - 1), core)

    def small_view(step, c):
        index = list(at)
        index[order[2 - step]] = c
        for axis in order[: 2 - step]:
            index[axis] = slice(None)
        return tuple(index)

    def small_add(step, c, term):
        where = small_view(step, c)
        small_acc[where] = small_acc[where] + term

    def small_start(step):
        axis = order[2 - step]
        across = lax.rem(at[axis] + 2, RING)
        return wires.copy(small_acc.at[small_view(step, across)], slots[step].at[0], right(axis))

    def small_turn(step, op):
        axis = order[2 - step]
        after, before = lax.rem(at[axis] + 1, RING), lax.rem(at[axis] + 3, RING)
        op.wait_recv()
        small_add(step, after, slots[step][0])
        return (
            wires.copy(small_acc.at[small_view(step, after)], slots[step].at[1], right(axis)),
            wires.copy(small_acc.at[small_view(step, before)], slots[step].at[2], left(axis)),
        )

    def small_finish(step, ops):
        for op in ops:
            op.wait_recv()
        small_add(step, at[order[2 - step]], slots[step][1] + slots[step][2])

    z, y, x = at

    def all_around(axis, src_of, dst):
        out = []
        for by in range(1, RING):
            there = moved(at, axis, by)
            out.append(wires.copy(src_of(there[axis]), dst, device_at(there, core)))
        return out

    def arrive(ops):
        for op in ops:
            op.wait_recv()

    for layer in (1, 0):
        for n in range(RING * RING):
            loads[layer, n].wait()
        sums.start(layer, 0)
    row_ops = [wires.copy(rows_ref.at[:, 1 - core], over_core.at[:, core], sibling)]
    over_core[:, core] = rows_ref[:, core]
    small_load.wait()
    small_swap.wait_recv()
    small_acc[...] = small_acc[...] + small_sib[...]
    op = small_start(0)
    arrive(row_ops)
    over_x[x] = over_core[x]
    row_ops = all_around(2, lambda c: over_core.at[c], over_x.at[x])
    sums.turn(1, 0)
    sums.turn(0, 0)
    ops = small_turn(0, op)
    arrive(row_ops)
    count, width = swap_ref.shape[0], rows_ref.shape[3]
    sorted_rows[...] = (
        jnp.dot(
            swap_ref[...], over_x[...].reshape(count, width), preferred_element_type=jnp.float32
        )
        .astype(jnp.bfloat16)
        .reshape(sorted_rows.shape)
    )
    over_y[y] = sorted_rows[y]
    row_ops = all_around(1, lambda c: sorted_rows.at[c], over_y.at[y])
    small_finish(0, ops)
    op = small_start(1)
    sums.finish(1, 0)
    sums.start(1, 1)
    arrive(row_ops)
    rows_out[z] = over_y[:, z]
    row_ops = all_around(0, lambda c: over_y.at[:, c], rows_out.at[z])
    ops = small_turn(1, op)
    sums.finish(0, 0)
    sums.start(0, 1)
    small_finish(1, ops)
    op = small_start(2)
    sums.turn(1, 1)
    ops = small_turn(2, op)
    sums.turn(0, 1)
    sums.finish(1, 1)
    sums.start(1, 2)
    sums.finish(0, 1)
    sums.start(0, 2)
    small_finish(2, ops)
    sums.turn(1, 2)
    sums.turn(0, 2)
    sums.finish(1, 2)
    sums.finish(0, 2)
    arrive(row_ops)

    theirs = pl.ds(pl.multiple_of((1 - core) * own_rows, own_rows), own_rows)
    swap = wires.copy(final.at[:, theirs], final_peer, sibling)
    small_out[...] = small_acc[at]
    swap.wait_recv()
    for layer in range(2):
        own = jnp.where(core == 0, final[layer, :own_rows], final[layer, own_rows:])
        got = final_peer[layer]
        out_ref[layer, :, :half] = jnp.where(core == 0, own, got)
        out_ref[layer, :, half:] = jnp.where(core == 0, got, own)
    for layer in range(2):
        for step in range(3):
            sums.drain(layer, step)
    wires.drain()


def reduce_weights(acc, small, rows_back, swap):
    granules, part, half = acc.shape[4:]
    rows = granules * part
    torus = (RING, RING, RING)
    small_shape = small.shape[1:]
    hbm = pl.BlockSpec(memory_space=pltpu.HBM)
    vmem = pl.BlockSpec(memory_space=pltpu.VMEM)
    low = jnp.bfloat16
    return pl.pallas_call(
        reduce_kernel,
        out_shape=(
            jax.ShapeDtypeStruct((2, rows // 2, 2 * half), jnp.float32),
            jax.ShapeDtypeStruct(small_shape, jnp.float32),
            jax.ShapeDtypeStruct((RING, RING, 16, 2 * half), low),
        ),
        in_specs=[hbm, hbm, vmem, vmem],
        out_specs=(vmem, vmem, vmem),
        scratch_shapes=[
            pltpu.VMEM(torus + (granules, part, half), low),
            pltpu.VMEM(torus + (granules, part, half), low),
            [
                [pltpu.VMEM(lead + (count(p), part, half), low) for p in range(3)]
                for lead, count in (
                    ((2, RING, RING), lambda p: SUM_PARTS[p][1]),
                    ((2, RING), lambda p: SUM_PARTS[p][1]),
                    ((2, 2, 2, RING), lambda p: SUM_PARTS[p][1]),
                    ((2, 2, 2), lambda p: SUM_PARTS[p][1]),
                    ((2, 2), lambda p: (SUM_PARTS[p][1] + 1) // 2),
                    ((2, 2, RING, RING), lambda p: SUM_PARTS[p][1]),
                    ((2, 2, RING), lambda p: SUM_PARTS[p][1]),
                    ((2, 2), lambda p: SUM_PARTS[p][1]),
                )
            ],
            pltpu.VMEM(torus + small_shape, jnp.float32),
            pltpu.VMEM(torus + small_shape, jnp.float32),
            pltpu.VMEM((3, RING, RING) + small_shape, jnp.float32),
            pltpu.VMEM((3, RING) + small_shape, jnp.float32),
            pltpu.VMEM((3,) + small_shape, jnp.float32),
            pltpu.VMEM((2, rows, half), jnp.float32),
            pltpu.VMEM((2, rows // 2, half), jnp.float32),
            pltpu.VMEM((RING, 2, 32, 2 * half), low),
            pltpu.VMEM((RING, 2, 32, 2 * half), low),
            pltpu.VMEM((RING, RING, 16, 2 * half), low),
            pltpu.VMEM((RING, RING, 16, 2 * half), low),
            pltpu.SemaphoreType.DMA((72,)),
            pltpu.SemaphoreType.DMA((72,)),
            pltpu.SemaphoreType.DMA((21,)),
            pltpu.SemaphoreType.DMA((21,)),
            pltpu.SemaphoreType.DMA((33,)),
        ],
        compiler_params=pltpu.CompilerParams(
            collective_id=1, has_side_effects=True, vmem_limit_bytes=44 * 2**20
        ),
        cost_estimate=pl.CostEstimate(flops=0, bytes_accessed=280 * 10**6, transcendentals=0),
        name="reduce_weights",
    )(acc, small.reshape(torus + (2,) + small_shape), rows_back, swap)


def sum_kernel(
    part_ref, asked_ref, back_ref, mats_ref, small_ref, loss_ref, out_ref, table_ref, group, slots, send, recv
):
    at, core = place()
    members = group.shape[0]
    peers = [
        (lax.axis_index("dp"), lax.rem(lax.axis_index("vocab") + by, members))
        for by in range(1, members)
    ]
    greet(
        peers
        + [device_at(moved(at, axis, by), core) for axis in range(2) for by in range(1, RING)]
    )
    wires = Wires(send, recv)
    table = part_ref[...].astype(jnp.float32) + lax.dot_general(
        asked_ref[...],
        back_ref[...],
        (((0,), (0,)), ((), ())),
        preferred_element_type=jnp.float32,
    )
    table_ref[...] = table

    def total(value):
        while value.ndim > 2:
            value = jnp.sum(value, 0)
        return jnp.sum(jnp.sum(value, 0, keepdims=True), 1, keepdims=True)

    mats, small = mats_ref[...], small_ref[...]
    squares = total(table * table) + total(mats * mats) + total(small * small)
    rows = lax.broadcasted_iota(jnp.int32, out_ref.shape, 0)
    vocab = lax.axis_index("vocab")
    group[vocab] = jnp.where(rows == 0, total(loss_ref[...]), squares)
    ops = [wires.copy(group.at[vocab], group.at[vocab], peer) for peer in peers]
    for op in ops:
        op.wait_recv()
    value = group[0]
    for m in range(1, members):
        value = value + group[m]
    for axis in range(2):
        slots[axis, at[axis]] = value
        ops = []
        for by in range(1, RING):
            ops.append(
                wires.copy(
                    slots.at[axis, at[axis]],
                    slots.at[axis, at[axis]],
                    device_at(moved(at, axis, by), core),
                )
            )
        for op in ops:
            op.wait_recv()
        value = slots[axis, 0]
        for c in range(1, RING):
            value = value + slots[axis, c]
    out_ref[...] = value
    wires.drain()


def sum_all(part, asked, back, mats, small, losses):
    vmem = pl.BlockSpec(memory_space=pltpu.VMEM)
    value = (8, 128)
    return pl.pallas_call(
        sum_kernel,
        out_shape=(
            jax.ShapeDtypeStruct(value, jnp.float32),
            jax.ShapeDtypeStruct(part.shape, jnp.float32),
        ),
        in_specs=[vmem] * 6,
        out_specs=(vmem, vmem),
        scratch_shapes=[
            pltpu.VMEM((8,) + value, jnp.float32),
            pltpu.VMEM((2, RING) + value, jnp.float32),
            pltpu.SemaphoreType.DMA((13,)),
            pltpu.SemaphoreType.DMA((13,)),
        ],
        compiler_params=pltpu.CompilerParams(
            collective_id=2, has_side_effects=True, vmem_limit_bytes=24 * 2**20
        ),
        cost_estimate=pl.CostEstimate(flops=0, bytes_accessed=40 * 10**6, transcendentals=0),
        name="sum_all",
    )(part, asked, back, mats, small, losses)


def update_kernel(sums_ref, *refs):
    norm = jnp.sqrt(sums_ref[1:2, 0:1])
    factor = clip_bound / jnp.maximum(norm, clip_bound)
    for n in range(2):
        weight, moment, average, grad = refs[4 * n : 4 * n + 4]
        outs = refs[8 + 4 * n : 12 + 4 * n]
        rows = weight.shape[0]
        results = renew(weight[...], moment[...], average[...], grad[:rows, :], factor)
        for out, value in zip(outs, results):
            out[...] = value


def update(sums, table, mats):
    vmem = pl.BlockSpec(memory_space=pltpu.VMEM)
    shapes = []
    for item in (table[0], mats[0]):
        shapes += [jax.ShapeDtypeStruct(item.shape, jnp.float32)] * 3
        shapes += [jax.ShapeDtypeStruct(item.shape, jnp.bfloat16)]
    outs = pl.pallas_call(
        update_kernel,
        out_shape=tuple(shapes),
        in_specs=[vmem] * 9,
        out_specs=(vmem,) * 8,
        compiler_params=pltpu.CompilerParams(vmem_limit_bytes=32 * 2**20),
        name="update",
    )(sums, *table, *mats)
    return outs[:4], outs[4:]


TILE = 800


def head_kernel(
    f_ref,
    code_ref,
    weight_ref,
    table_ref,
    grad_out,
    dtable_ref,
    loss_ref,
    f_all,
    codes,
    table,
    logits,
    probs,
    tops,
    stats,
    df,
    df_send,
    df_sib,
    ring,
    ring_half,
    ring_full,
    staged,
    send,
    recv,
    load,
    store,
):
    at, core = place()
    x = at[2]
    dp, vocab = lax.axis_index("dp"), lax.axis_index("vocab")
    tok, width = f_ref.shape
    group = f_all.shape[0]
    members = group // tok
    tiles = table.shape[0] // TILE
    low, f32 = jnp.bfloat16, jnp.float32

    def tile_rows(t):
        return pl.ds(pl.multiple_of(t * TILE, TILE), TILE)

    loads = []
    for t in range(tiles):
        op = pltpu.make_async_copy(
            table_ref.at[pl.ds(t * TILE, TILE)], table.at[pl.ds(t * TILE, TILE)], load.at[t]
        )
        op.start()
        loads.append(op)

    peers = [(dp, lax.rem(vocab + by, members)) for by in range(1, members)]
    greet(peers)
    wires = Wires(send, recv)
    sibling = device_at(at, 1 - core)
    right, left = device_at(moved(at, 2, 1), core), device_at(moved(at, 2, 3), core)
    before, after, across = lax.rem(x + 3, RING), lax.rem(x + 1, RING), lax.rem(x + 2, RING)

    def rows_of(at_x, piece=None):
        first = (at_x * 2 + core) * tok
        if piece is None:
            return f_all.at[pl.ds(pl.multiple_of(first, tok), tok)]
        half = tok // 2
        return f_all.at[pl.ds(pl.multiple_of(first + piece * half, half), half)]

    f_all[pl.ds(pl.multiple_of(vocab * tok, tok), tok), :] = f_ref[...]
    own = rows_of(x)
    one, two = wires.copy(own, own, right), wires.copy(own, own, left)
    pending = [wires.copy(own, own, sibling)]
    codes[vocab] = code_ref[...]
    for peer in peers:
        pending.append(wires.copy(codes.at[vocab], codes.at[vocab], peer))
    one.wait_recv()
    one_on = wires.copy(rows_of(before, 0), rows_of(before, 0), right)
    pending.append(wires.copy(rows_of(before), rows_of(before), sibling))
    two.wait_recv()
    two_on = wires.copy(rows_of(after, 1), rows_of(after, 1), left)
    pending.append(wires.copy(rows_of(after), rows_of(after), sibling))
    one_on.wait_recv()
    pending.append(wires.copy(rows_of(across, 0), rows_of(across, 0), sibling))
    two_on.wait_recv()
    pending.append(wires.copy(rows_of(across, 1), rows_of(across, 1), sibling))
    for op in pending:
        op.wait_recv()

    code_row = jnp.concatenate([codes[m, 0:1, :] for m in range(members)], 1) - vocab * table.shape[0]
    code8 = jnp.broadcast_to(code_row, (8, group))
    code16 = jnp.broadcast_to(code_row, (16, group))
    rows8 = lax.broadcasted_iota(jnp.int32, (8, group), 0)
    rows16 = lax.broadcasted_iota(jnp.int32, (16, group), 0)
    slot = TILE // 2
    real = slot - 7
    steps8, steps16 = 5, 5

    def first_pass(t, carry):
        top, total, target = carry
        here = tile_rows(t)
        logits[...] = lax.dot_general(
            table[here, :], f_all[...], (((1,), (1,)), ((), ())), preferred_element_type=f32
        )
        for part in range(2):
            last = pl.ds((part + 1) * slot - 8, 8)
            logits[last, :] = jnp.where(rows8 < 1, logits[last, :], -1e30)

        def look(i, state):
            high, hit = state
            for u in range(steps8):
                first = (i * steps8 + u) * 8
                value = logits[pl.ds(pl.multiple_of(first, 8), 8), :]
                high = jnp.maximum(high, value)
                hit = hit + jnp.where(rows8 + (first + t * TILE) == code8, value, 0.0)
            return high, hit

        high, hit = lax.fori_loop(
            0,
            TILE // (8 * steps8),
            look,
            (jnp.full((8, group), -1e30, f32), jnp.zeros((8, group), f32)),
        )
        top_next = jnp.maximum(top, jnp.max(high, 0, keepdims=True))
        target = target + jnp.sum(hit, 0, keepdims=True)

        def lift(i, acc):
            for u in range(steps16):
                first = (i * steps16 + u) * 16
                value = jnp.exp(logits[pl.ds(pl.multiple_of(first, 16), 16), :] - top_next)
                acc = acc + value
                probs[pl.ds(pl.multiple_of(t * TILE + first, 16), 16), :] = value.astype(low)
            return acc

        acc = lax.fori_loop(
            0, TILE // (16 * steps16), lift, jnp.zeros((16, group), f32)
        )
        total = total * jnp.exp(top - top_next) + jnp.sum(acc, 0, keepdims=True)
        tops[t] = top_next
        return top_next, total, target

    for op in loads:
        op.wait()
    start = (jnp.full((1, group), -1e30, f32), jnp.zeros((1, group), f32), jnp.zeros((1, group), f32))
    found = lax.fori_loop(0, tiles, first_pass, start)
    for k in range(3):
        for m in range(members):
            stats[vocab, k, m : m + 1, :] = found[k][:, m * tok : (m + 1) * tok]
    pending = [wires.copy(stats.at[vocab], stats.at[vocab], peer) for peer in peers]
    for op in pending:
        op.wait_recv()
    peak = stats[0, 0]
    for m in range(1, members):
        peak = jnp.maximum(peak, stats[m, 0])
    total, target = jnp.zeros_like(peak), jnp.zeros_like(peak)
    for m in range(members):
        total = total + stats[m, 1] * jnp.exp(stats[m, 0] - peak)
        target = target + stats[m, 2]
    lse = peak + jnp.log(total)
    weight = weight_ref[...]
    mine = lax.broadcasted_iota(jnp.int32, (members, tok), 0) == vocab
    loss_ref[...] = jnp.where(mine, weight * (lse - target), 0.0)
    lse_row = jnp.concatenate([lse[m : m + 1, :] for m in range(members)], 1)
    weight_row = jnp.concatenate([weight[m : m + 1, :] for m in range(members)], 1)

    df[...] = jnp.zeros_like(df)

    def second_pass(t, unused):
        scale = weight_row * jnp.exp(tops[t] - lse_row)

        def turn(i, unused):
            for u in range(steps16):
                first = t * TILE + (i * steps16 + u) * 16
                here = pl.ds(pl.multiple_of(first, 16), 16)
                value = probs[here, :].astype(f32) * scale
                value = value - jnp.where(rows16 + first == code16, weight_row, 0.0)
                probs[here, :] = value.astype(low)
            return unused

        lax.fori_loop(0, TILE // (16 * steps16), turn, 0)
        here = tile_rows(t)
        df[...] += lax.dot_general(
            probs[here, :], table[here, :], (((0,), (0,)), ((), ())), preferred_element_type=f32
        )
        return unused

    lax.fori_loop(0, tiles, second_pass, 0)

    def third_pass(t):
        if t >= 2:
            stores[t - 2].wait()
        staged[t % 2] = jnp.dot(
            probs[t * TILE : (t + 1) * TILE, :], f_all[...], preferred_element_type=f32
        ).astype(low)
        op = pltpu.make_async_copy(
            staged.at[t % 2], dtable_ref.at[pl.ds(t * TILE, TILE)], store.at[t]
        )
        op.start()
        stores.append(op)

    stores = []
    for m in range(members):
        df_send[m % 2, m // 2] = df[m * tok : (m + 1) * tok, :].astype(low)
    swap = wires.copy(df_send.at[1 - core], df_sib, sibling)
    third_pass(0)
    third_pass(1)
    swap.wait_recv()
    for k in range(RING):
        first = pl.multiple_of((2 * k + core) * tok, tok)
        ring[k] = (df[pl.ds(first, tok), :] + df_sib[k].astype(f32)).astype(low)
    half = tok // 2
    one = wires.copy(ring.at[across, pl.ds(0, half)], ring_half.at[0], right)
    two = wires.copy(ring.at[across, pl.ds(half, half)], ring_half.at[1], left)
    third_pass(2)
    third_pass(3)
    one.wait_recv()
    ring[after, :half] = (ring[after, :half].astype(f32) + ring_half[0].astype(f32)).astype(low)
    one = wires.copy(ring.at[after], ring_full.at[0], right)
    two.wait_recv()
    ring[before, half:] = (ring[before, half:].astype(f32) + ring_half[1].astype(f32)).astype(low)
    two = wires.copy(ring.at[before], ring_full.at[1], left)
    for t in range(4, tiles):
        third_pass(t)
    one.wait_recv()
    two.wait_recv()
    grad_out[...] = ring[x].astype(f32) + ring_full[0].astype(f32) + ring_full[1].astype(f32)
    for op in stores[-2:]:
        op.wait()
    wires.drain()


HEAD_COPIES = 9 + 7 + 7 + 5


def head(final_low, codes, weights, table):
    tok, width = final_low.shape
    rows = table.shape[0]
    members = weights.shape[0]
    group = members * tok
    tiles = rows // TILE
    hbm = pl.BlockSpec(memory_space=pltpu.HBM)
    vmem = pl.BlockSpec(memory_space=pltpu.VMEM)
    low, f32 = jnp.bfloat16, jnp.float32
    return pl.pallas_call(
        head_kernel,
        out_shape=(
            jax.ShapeDtypeStruct((tok, width), f32),
            jax.ShapeDtypeStruct((rows, width), low),
            jax.ShapeDtypeStruct((members, tok), f32),
        ),
        in_specs=[vmem, vmem, vmem, hbm],
        out_specs=(vmem, hbm, vmem),
        scratch_shapes=[
            pltpu.VMEM((group, width), low),
            pltpu.VMEM((members, 8, tok), jnp.int32),
            pltpu.VMEM((rows, width), low),
            pltpu.VMEM((TILE, group), f32),
            pltpu.VMEM((rows, group), low),
            pltpu.VMEM((tiles, 1, group), f32),
            pltpu.VMEM((members, 3, members, tok), f32),
            pltpu.VMEM((group, width), f32),
            pltpu.VMEM((2, RING, tok, width), low),
            pltpu.VMEM((RING, tok, width), low),
            pltpu.VMEM((RING, tok, width), low),
            pltpu.VMEM((2, tok // 2, width), low),
            pltpu.VMEM((2, tok, width), low),
            pltpu.VMEM((2, TILE, width), low),
            pltpu.SemaphoreType.DMA((HEAD_COPIES,)),
            pltpu.SemaphoreType.DMA((HEAD_COPIES,)),
            pltpu.SemaphoreType.DMA((tiles,)),
            pltpu.SemaphoreType.DMA((tiles,)),
        ],
        compiler_params=pltpu.CompilerParams(
            collective_id=3, has_side_effects=True, vmem_limit_bytes=58 * 2**20
        ),
        cost_estimate=pl.CostEstimate(
            flops=6 * group * rows * width, bytes_accessed=4 * rows * width, transcendentals=group * rows
        ),
        name="head",
    )(final_low, codes, weights, table)


TILE_ORDER = (8, 9, 10, 11, 4, 5, 6, 7, 3, 0, 1, 2)
G1, S1, BQ, BV, BPROJ, G2, S2, BFC, BOUT = 0, 1, 2, 3, 4, 5, 6, 7, 11
STEPS = 12
GELU_A, GELU_B = 0.7978845608028654, 0.044715


def across_k(left, right):
    return lax.dot_general(left, right, (((1,), (1,)), ((), ())), preferred_element_type=jnp.float32)


def along_k(left, right):
    return jnp.dot(left, right, preferred_element_type=jnp.float32)


def over_rows(left, right):
    return lax.dot_general(left, right, (((0,), (0,)), ((), ())), preferred_element_type=jnp.float32)


def tile_copy(mats_ref, weights, ready, tile, step):
    rows = weights.shape[1]
    return pltpu.make_async_copy(
        mats_ref.at[pl.ds(tile * rows, rows)], weights.at[step], ready.at[step]
    )


def normed(value):
    centered = value - jnp.mean(value, -1, keepdims=True)
    scale = lax.rsqrt(jnp.mean(centered * centered, -1, keepdims=True) + norm_eps)
    return centered * scale, scale


def norm_back(grad, value, gain):
    unit, scale = normed(value)
    inner = grad * gain
    mean = jnp.mean(inner, -1, keepdims=True)
    slope = jnp.mean(inner * unit, -1, keepdims=True)
    return (
        scale * (inner - mean - unit * slope),
        jnp.sum(grad * unit, 0, keepdims=True),
        jnp.sum(grad, 0, keepdims=True),
    )


def forward_kernel(
    hot_ref,
    rows_ref,
    pos_hot_ref,
    pos_ref,
    mask_ref,
    vec_ref,
    mats_ref,
    x_out,
    a_out,
    qkv_out,
    probs_out,
    o_out,
    mid_out,
    m_out,
    u_out,
    g_out,
    hidden_out,
    final_out,
    cur,
    weights,
    ready,
):
    step = pl.program_id(0)
    layer, s = lax.div(step, STEPS), lax.rem(step, STEPS)
    low, f32 = jnp.bfloat16, jnp.float32
    width = cur.shape[1]
    head_dim = width // H


    def vec(row):
        return vec_ref[layer * STEPS + row]

    @pl.when(step == 0)
    def fetch():
        for n in range(2 * STEPS):
            tile_copy(mats_ref, weights, ready, n, n).start()

    @pl.when(step == 0)
    def embed():
        cur[...] = along_k(hot_ref[...], rows_ref[...]) + across_k(pos_hot_ref[...], pos_ref[...])

    @pl.when(s == 0)
    def first_norm():
        x_out[layer] = cur[...]
        a_out[layer] = (normed(cur[...])[0] * vec(G1) + vec(S1)).astype(low)

    tile_copy(mats_ref, weights, ready, 0, step).wait()

    @pl.when(s < 3)
    def project():
        bias = jnp.where(s == 0, vec(BQ), jnp.where(s == 2, vec(BV), 0.0))
        qkv_out[layer, s] = (across_k(a_out[layer], weights[step]) + bias).astype(low)

    @pl.when(s == 2)
    def attend():
        lanes = lax.broadcasted_iota(jnp.int32, (1, 2 * head_dim), 1)
        for pair in range(H // 2):
            cols = slice(2 * head_dim * pair, 2 * head_dim * (pair + 1))
            q, k, v = (qkv_out[layer, part, :, cols] for part in range(3))
            total = None
            for side in range(2):
                own = (lanes < head_dim) if side == 0 else (lanes >= head_dim)
                scores = across_k(jnp.where(own, q, jnp.zeros_like(q)), k) * head_dim ** (-0.5)
                scores = jnp.where(mask_ref[...] > 0.0, scores, -1000000000.0)
                shifted = jnp.exp(scores - jnp.max(scores, -1, keepdims=True))
                probs = shifted / jnp.sum(shifted, -1, keepdims=True)
                probs_out[layer, 2 * pair + side] = probs
                term = along_k(probs.astype(low), jnp.where(own, v, jnp.zeros_like(v)))
                total = term if total is None else total + term
            o_out[layer, :, cols] = total.astype(low)

    @pl.when(s == 3)
    def second_norm():
        mid = cur[...] + across_k(o_out[layer], weights[step]) + vec(BPROJ)
        mid_out[layer] = mid
        m_out[layer] = (normed(mid)[0] * vec(G2) + vec(S2)).astype(low)
        cur[...] = mid + vec(BOUT)

    @pl.when((s >= 4) & (s < 8))
    def widen():
        u = across_k(m_out[layer], weights[step]) + vec(BFC + s - 4)
        u_out[layer, s - 4] = u
        g = 0.5 * u * (1.0 + jnp.tanh(GELU_A * (u + GELU_B * (u * u * u))))
        g_out[layer, s - 4] = g.astype(low)

    @pl.when(s >= 8)
    def narrow():
        cur[...] += along_k(g_out[layer, s - 8], weights[step])

    @pl.when(step == 2 * STEPS - 1)
    def last_norm():
        hidden_out[...] = cur[...]
        final_out[...] = (normed(cur[...])[0] * vec_ref[2 * STEPS] + vec_ref[2 * STEPS + 1]).astype(low)


def forward_layers(hot, rows, pos_hot, pos, mask, vecs, mats):
    tok, width = hot.shape[0], rows.shape[1]
    low, f32 = jnp.bfloat16, jnp.float32
    shape = jax.ShapeDtypeStruct
    vmem = pl.BlockSpec(memory_space=pltpu.VMEM)
    return pl.pallas_call(
        forward_kernel,
        grid=(2 * STEPS,),
        out_shape=(
            shape((2, tok, width), f32),
            shape((2, tok, width), low),
            shape((2, 3, tok, width), low),
            shape((2, H, tok, tok), f32),
            shape((2, tok, width), low),
            shape((2, tok, width), f32),
            shape((2, tok, width), low),
            shape((2, 4, tok, width), f32),
            shape((2, 4, tok, width), low),
            shape((tok, width), f32),
            shape((tok, width), low),
        ),
        in_specs=[vmem] * 6 + [pl.BlockSpec(memory_space=pltpu.HBM)],
        out_specs=(vmem,) * 11,
        scratch_shapes=[
            pltpu.VMEM((tok, width), f32),
            pltpu.VMEM((2 * STEPS, width, width), low),
            pltpu.SemaphoreType.DMA((2 * STEPS,)),
        ],
        compiler_params=pltpu.CompilerParams(vmem_limit_bytes=58 * 2**20),
        cost_estimate=pl.CostEstimate(
            flops=2 * tok * mats.size, bytes_accessed=2 * mats.size, transcendentals=0
        ),
        name="forward_layers",
    )(hot, rows, pos_hot, pos, mask, vecs, mats)


def backward_kernel(
    grad_ref,
    hidden_ref,
    vec_ref,
    x_ref,
    a_ref,
    qkv_ref,
    probs_ref,
    o_ref,
    mid_ref,
    m_ref,
    u_ref,
    g_ref,
    hot_ref,
    mats_ref,
    dx_out,
    vec_out,
    rows_out,
    acc_out,
    cur,
    wide,
    du_s,
    dqkv_s,
    lefts,
    rights,
    right_send,
    weights,
    ready,
    send_left,
    recv_left,
    send_right,
    recv_right,
):
    step = pl.program_id(0)
    layer, s = 1 - lax.div(step, STEPS), lax.rem(step, STEPS)
    low, f32 = jnp.bfloat16, jnp.float32
    tok, width = cur.shape
    half = width // 2
    head_dim = width // H
    at, core = place()
    sibling = device_at(at, 1 - core)
    last = 2 * STEPS
    slot = lax.rem(step, 4)

    def vec(row):
        return vec_ref[layer * STEPS + row]

    def put(row, value):
        vec_out[layer * STEPS + row] = value

    def to_sibling(src, dst, send, recv):
        return pltpu.make_async_remote_copy(
            src_ref=src,
            dst_ref=dst,
            send_sem=send,
            recv_sem=recv,
            device_id=sibling,
            device_id_type=pl.DeviceIdType.MESH,
        )

    def left_copy(n):
        return to_sibling(
            lefts.at[n, pl.ds(0, tok)],
            lefts.at[n, pl.ds(tok, tok)],
            send_left.at[n],
            recv_left.at[n],
        )

    def right_copy(n):
        return to_sibling(
            right_send.at[n], rights.at[n, pl.ds(tok, tok)], send_right.at[n], recv_right.at[n]
        )

    def set_left(value):
        lefts[slot, :tok, :] = value

    def set_right(n, value):
        pl.when(step >= STEPS)(lambda: right_copy(n).wait_send())
        rights[n, :tok, :] = jnp.where(core == 0, value[:, :half], value[:, half:])
        right_send[n] = jnp.where(core == 0, value[:, half:], value[:, :half])

    @pl.when(step == 0)
    def enter():
        for n in range(last):
            tile = STEPS * (1 - n // STEPS) + TILE_ORDER[n % STEPS]
            tile_copy(mats_ref, weights, ready, tile, n).start()
        greet([sibling])
        dx, dg, ds = norm_back(grad_ref[...], hidden_ref[...], vec_ref[last])
        cur[...] = dx
        vec_out[last] = dg
        vec_out[last + 1] = ds

    @pl.when(step < last)
    def arrived():
        tile_copy(mats_ref, weights, ready, 0, step).wait()

    pl.when((step >= 4) & (step < last))(lambda: left_copy(slot).wait_send())

    @pl.when((s == 0) & (step < last))
    def begin():
        put(BOUT, jnp.sum(cur[...], 0, keepdims=True))
        set_right(0, cur[...].astype(low))
        wide[...] = cur[...].astype(low)

    @pl.when((s < 4) & (step < last))
    def through_gelu():
        dg = across_k(wide[...], weights[step])
        u = u_ref[layer, s]
        square = u * u
        t = jnp.tanh(GELU_A * (u + GELU_B * (square * u)))
        slope = 0.5 * (1.0 + t) + (0.5 * GELU_A) * u * (1.0 - t * t) * (1.0 + (3.0 * GELU_B) * square)
        du = dg * slope
        put(BFC + s, jnp.sum(du, 0, keepdims=True))
        du_s[s] = du.astype(low)
        set_left(g_ref[layer, s])

    @pl.when(s == 4)
    def begin_fc():
        set_right(1, m_ref[layer])
        dx_out[...] = jnp.zeros_like(dx_out)

    @pl.when((s >= 4) & (s < 8))
    def through_fc():
        left = du_s[s - 4]
        dx_out[...] += along_k(left, weights[step])
        set_left(left)

    @pl.when(s == 8)
    def through_attention():
        dx, dg, ds = norm_back(dx_out[...], mid_ref[layer], vec(G2))
        put(G2, dg)
        put(S2, ds)
        cur[...] = cur[...] + dx
        put(BPROJ, jnp.sum(cur[...], 0, keepdims=True))
        mid_low = cur[...].astype(low)
        set_left(mid_low)
        set_right(2, o_ref[layer])
        wide[...] = along_k(mid_low, weights[step]).astype(low)
        lanes = lax.broadcasted_iota(jnp.int32, (1, 2 * head_dim), 1)
        scale = head_dim ** (-0.5)
        for pair in range(H // 2):
            cols = slice(2 * head_dim * pair, 2 * head_dim * (pair + 1))
            q, k, v = (qkv_ref[layer, part, :, cols] for part in range(3))
            do = wide[:, cols]
            parts = [None] * 3
            for side in range(2):
                own = (lanes < head_dim) if side == 0 else (lanes >= head_dim)
                keep = lambda item, own=own: jnp.where(own, item, jnp.zeros_like(item))
                probs = probs_ref[layer, 2 * pair + side]
                do_own = keep(do)
                dprobs = across_k(do_own, v)
                dscores = probs * (dprobs - jnp.sum(probs * dprobs, -1, keepdims=True))
                dlow = (dscores * scale).astype(low)
                terms = (
                    along_k(dlow, keep(k)),
                    over_rows(dlow, keep(q)),
                    over_rows(probs.astype(low), do_own),
                )
                parts = [
                    term if held is None else held + term for held, term in zip(parts, terms)
                ]
            for part in range(3):
                dqkv_s[part, :, cols] = parts[part].astype(low)
            vec_out[layer * STEPS + BQ, :, cols] = jnp.sum(parts[0], 0, keepdims=True)
            vec_out[layer * STEPS + BV, :, cols] = jnp.sum(parts[2], 0, keepdims=True)

    @pl.when(s == 9)
    def begin_qkv():
        set_right(3, a_ref[layer])
        dx_out[...] = jnp.zeros_like(dx_out)

    @pl.when(s >= 9)
    def through_qkv():
        left = dqkv_s[s - 9]
        dx_out[...] += along_k(left, weights[step])
        set_left(left)

    def kind_of(at_s):
        return jnp.where(at_s < 4, 0, jnp.where(at_s < 8, 1, jnp.where(at_s == 8, 2, 3)))

    def fresh(at_s):
        return (at_s == 0) | (at_s == 4) | (at_s == 8) | (at_s == 9)

    @pl.when(step >= 2)
    def gradient():
        slot_then, s_then = lax.rem(step - 2, 4), lax.rem(step - 2, STEPS)
        kind = kind_of(s_then)
        left_copy(slot_then).wait_recv()
        pl.when(fresh(s_then))(lambda: right_copy(kind).wait_recv())
        grad = over_rows(lefts[slot_then], rights[kind])
        acc_out[0] = grad.astype(low).reshape(acc_out.shape[1:])

    @pl.when(step < last)
    def share():
        left_copy(slot).start()
        pl.when(fresh(s))(lambda: right_copy(kind_of(s)).start())

    @pl.when(s == STEPS - 1)
    def end_layer():
        dx, dg, ds = norm_back(dx_out[...], x_ref[layer], vec(G1))
        put(G1, dg)
        put(S1, ds)
        cur[...] = cur[...] + dx

    @pl.when(step == last + 1)
    def leave():
        dx_out[...] = cur[...]
        rows = over_rows(hot_ref[...], cur[...].astype(low)).astype(low)
        rows_out[...] = rows.reshape(rows_out.shape)
        for n in range(4):
            left_copy(n).wait_send()
            right_copy(n).wait_send()


def backward_layers(grad, hidden, vecs, saved, hot, mats):
    tok, width = grad.shape
    low, f32 = jnp.bfloat16, jnp.float32
    shape = jax.ShapeDtypeStruct
    vmem = pl.BlockSpec(memory_space=pltpu.VMEM)
    hbm = pl.BlockSpec(memory_space=pltpu.HBM)
    half, part = width // 2, 16
    granules = width // part

    def tile(i):
        i = jnp.clip(i - 2, 0, 2 * STEPS - 1)
        layer, s = 1 - i // STEPS, i % STEPS
        return (
            layer,
            jnp.where(s < 4, 8 + s, jnp.where(s < 8, s, jnp.where(s == 8, 3, s - 9))),
            0,
            0,
        )

    return pl.pallas_call(
        backward_kernel,
        grid=(2 * STEPS + 2,),
        out_shape=(
            shape((tok, width), f32),
            shape((2 * STEPS + 2, 1, width), f32),
            shape((RING, 2, 32, width), low),
            shape((2, STEPS * granules, part, half), low),
        ),
        in_specs=[vmem] * 13 + [hbm],
        out_specs=(vmem, vmem, vmem, pl.BlockSpec((1, granules, part, half), tile)),
        scratch_shapes=[
            pltpu.VMEM((tok, width), f32),
            pltpu.VMEM((tok, width), low),
            pltpu.VMEM((4, tok, width), low),
            pltpu.VMEM((3, tok, width), low),
            pltpu.VMEM((4, 2 * tok, width), low),
            pltpu.VMEM((4, 2 * tok, half), low),
            pltpu.VMEM((4, tok, half), low),
            pltpu.VMEM((2 * STEPS, width, width), low),
            pltpu.SemaphoreType.DMA((2 * STEPS,)),
            pltpu.SemaphoreType.DMA((4,)),
            pltpu.SemaphoreType.DMA((4,)),
            pltpu.SemaphoreType.DMA((4,)),
            pltpu.SemaphoreType.DMA((4,)),
        ],
        compiler_params=pltpu.CompilerParams(
            collective_id=4, has_side_effects=True, vmem_limit_bytes=60 * 2**20
        ),
        cost_estimate=pl.CostEstimate(
            flops=4 * tok * mats.size, bytes_accessed=2 * mats.size, transcendentals=0
        ),
        name="backward_layers",
    )(grad, hidden, vecs, *saved, hot, mats)


def doc_info(doc_lens, tok_count, total_docs):
    doc_ends = jnp.cumsum(doc_lens)
    places = jnp.arange(tok_count, dtype=jnp.int32)
    seg_ids = jnp.sum((places[:, None] >= doc_ends[None, :]).astype(jnp.int32), 1)
    one_hot = seg_ids[:, None] == jnp.arange(doc_lens.shape[0], dtype=jnp.int32)[None, :]
    starts = doc_ends - doc_lens
    pos_ids = places - jnp.sum(jnp.where(one_hot, starts[None, :], 0), 1)
    doc_len = jnp.sum(jnp.where(one_hot, doc_lens[None, :], 0), 1)
    weights = 1.0 / (doc_len.astype(jnp.float32) * total_docs)
    return (seg_ids, pos_ids, weights)


def device_rise(first, count, devices):
    places = first + jnp.arange(count, dtype=jnp.int32)
    return 1.0 + 2.0 * places.astype(jnp.float32) / (devices - 1)


def contract(left, right, left_dim, right_dim):
    return lax.dot_general(
        left, right, (((left_dim,), (right_dim,)), ((), ())), preferred_element_type=jnp.float32
    )


def renew(weight, moment, average, grad, factor):
    clipped = factor * grad
    moment_next = momentum_coef * moment + clipped
    weight_next = weight - learn_rate * (clipped + momentum_coef * moment_next)
    average_next = ema_decay * average + (1.0 - ema_decay) * weight_next
    return (moment_next, weight_next, average_next, weight_next.astype(jnp.bfloat16))


SMALL_ROWS, LANES = 16, 128


def pack_small(values):
    room = SMALL_ROWS * LANES - values.shape[-1]
    pads = [(0, 0)] * (values.ndim - 1) + [(0, room)]
    return jnp.pad(values, pads).reshape(values.shape[:-1] + (SMALL_ROWS, LANES))


def per_device(
    token_ids,
    targets,
    lengths,
    embed_table,
    embed_moment,
    embed_average,
    blocks,
    block_moment,
    block_average,
    pos_table,
    pos_moment,
    pos_average,
    vectors,
    vector_moment,
    vector_average,
):
    devices = lax.axis_size(("dp", "vocab"))
    vocab_count = lax.axis_size("vocab")
    dp_count = lax.axis_size("dp")
    vocab_at = lax.axis_index("vocab")
    data_at = lax.axis_index("dp")
    tok = token_ids.shape[0]
    own_rows, width = embed_table.shape
    capacity = max(2, 2 * tok // devices)
    low = jnp.bfloat16
    blocks, block_moment, block_average = (
        jnp.transpose(item, (0, 2, 1)) for item in (blocks, block_moment, block_average)
    )
    pos_rows, pos_cols = pos_table.shape
    vec_own = vectors.shape[0]
    pad_rows = -own_rows % 16
    table_padded = jnp.pad(embed_table, ((0, pad_rows), (0, 0))).astype(low)
    slot_rows = own_rows + pad_rows

    table_slice = lax.all_gather(table_padded, "dp", axis=0, tiled=True)
    target_owners = targets // own_rows
    codes = (
        (target_owners % vocab_count) * (dp_count * slot_rows)
        + (target_owners // vocab_count) * slot_rows
        + targets % own_rows
    )

    owners = token_ids // own_rows
    tokens = jnp.arange(tok, dtype=jnp.int32)
    rank = jnp.sum((owners[:, None] == owners[None, :]) & (tokens[None, :] < tokens[:, None]), 1)
    slot_count = devices * capacity
    slots = jnp.arange(slot_count, dtype=jnp.int32)
    arrival = (
        (owners % 8) * 32 + (owners // 8 % RING) * 8 + (owners // 32) * capacity + rank
    )
    slot_hot = (arrival[:, None] == slots[None, :]).astype(low)
    hot = lambda condition: condition.astype(ml_dtypes.bfloat16)
    line, step = np.arange(slot_count), np.arange(tok)
    spread = hot(line[:, None] // capacity == np.arange(devices)[None, :])
    earlier = hot(step[:, None] < step[None, :])
    slot_number = np.broadcast_to((line % capacity).astype(np.float32)[:, None], (slot_count, tok)).copy()
    by_owner = line % 64 // 16 * 2 + line // 64 * 8 + line % 16 // 2 * 32 + line % capacity
    swap = hot(by_owner[:, None] == line[None, :])
    values = jnp.concatenate([jnp.transpose(pos_table).reshape(-1), vectors]).astype(low)
    small = jnp.concatenate(
        [
            jnp.pad(values, (0, IDS_ROW * LANES - values.shape[0])).reshape(IDS_ROW, LANES),
            jnp.stack([token_ids // 256, token_ids % 256]).astype(low),
            jnp.zeros((SMALL_ROWS - IDS_ROW - 2, LANES), low),
        ]
    )
    mats_all, small_all, returned_rows, asked = gather_weights(
        blocks, small, table_padded, spread, earlier, slot_number, swap.T.copy()
    )
    small_all = small_all.reshape(devices, -1)
    pos_low_t = small_all[:, : pos_rows * pos_cols].reshape(width, pos_rows)
    vecs_all = (
        small_all[:, pos_rows * pos_cols : pos_rows * pos_cols + vec_own]
        .reshape(-1)
        .astype(jnp.float32)
    )
    lens_group = lengths[0]
    seg_group, pos_group, weight_group = jax.vmap(
        partial(doc_info, tok_count=tok, total_docs=devices * lens_group.shape[1])
    )(lens_group)
    weight_group = weight_group * device_rise(data_at * vocab_count, vocab_count, devices)[:, None]
    seg_ids = lax.dynamic_index_in_dim(seg_group, vocab_at, 0, keepdims=False)
    pos_ids = lax.dynamic_index_in_dim(pos_group, vocab_at, 0, keepdims=False)
    places = jnp.arange(tok, dtype=jnp.int32)
    attn_mask = (seg_ids[:, None] == seg_ids[None, :]) & (places[None, :] <= places[:, None])

    pos_hot = (pos_ids[:, None] == jnp.arange(pos_rows, dtype=jnp.int32)[None, :]).astype(low)
    vec_rows = vecs_all.reshape(-1, 1, width)
    *saved, hidden, final_low = forward_layers(
        slot_hot,
        returned_rows,
        pos_hot,
        pos_low_t,
        attn_mask.astype(jnp.float32),
        vec_rows,
        mats_all,
    )
    grad_final, table_part, token_losses = head(
        final_low, jnp.broadcast_to(codes[None, :], (8, tok)), weight_group, table_slice
    )
    table_part = lax.psum_scatter(table_part, "dp", scatter_dimension=0, tiled=True)
    grad_hidden, grad_vecs, rows_back, grad_acc = backward_layers(
        grad_final, hidden, vec_rows, saved, slot_hot, mats_all
    )
    grad_pos = lax.dot_general(
        grad_hidden,
        pos_hot.astype(jnp.float32),
        (((0,), (0,)), ((), ())),
        precision=lax.Precision.HIGHEST,
    )
    small_grads = pack_small(
        jnp.concatenate(
            [grad_pos.reshape(devices, -1), grad_vecs.reshape(devices, -1)], 1
        )
    )
    mats_shard, small_shard, back_grads = reduce_weights(grad_acc.reshape(2, RING, RING, RING, 9, 16, width // 2), small_grads, rows_back, swap)
    both_sums, table_grad = sum_all(
        table_part,
        asked,
        back_grads.reshape(slot_count, width),
        mats_shard,
        small_shard,
        token_losses,
    )
    small_shard = small_shard.reshape(-1)
    pos_shard = small_shard[: pos_rows * pos_cols].reshape(pos_cols, pos_rows)
    vec_shard = small_shard[pos_rows * pos_cols : pos_rows * pos_cols + vec_own]
    loss_sum, squares = both_sums[0, 0], both_sums[1, 0]
    grad_norm = jnp.sqrt(squares)
    factor = clip_bound / jnp.maximum(grad_norm, clip_bound)
    own_shape = blocks.shape
    flat = lambda item: item.reshape(-1, width)
    embed_out, block_out = update(
        both_sums,
        (embed_table, embed_moment, embed_average, table_grad),
        (flat(blocks), flat(block_moment), flat(block_average), flat(mats_shard)),
    )
    block_out = tuple(
        jnp.transpose(item.reshape(own_shape), (0, 2, 1)) for item in block_out
    )
    pos_out = renew(
        jnp.transpose(pos_table),
        jnp.transpose(pos_moment),
        jnp.transpose(pos_average),
        pos_shard,
        factor,
    )
    pos_out = tuple(jnp.transpose(item) for item in pos_out)
    vector_out = renew(vectors, vector_moment, vector_average, vec_shard, factor)
    return (loss_sum, grad_norm) + tuple(embed_out) + block_out + pos_out + vector_out


def solution(mesh):
    table = P(("dp", "vocab"), None)
    cols = P(None, None, ("dp", "vocab"))
    pos = P(None, ("dp", "vocab"))
    vec = P(("dp", "vocab"))
    return jax.shard_map(
        per_device,
        mesh=mesh,
        in_specs=(vec, vec, P("dp", None, None))
        + (table,) * 3
        + (cols,) * 3
        + (pos,) * 3
        + (vec,) * 3,
        out_specs=(P(), P()) + (table,) * 4 + (cols,) * 4 + (pos,) * 4 + (vec,) * 4,
        check_vma=False,
    )
```

```python
from functools import partial

import jax
import jax.numpy as jnp
import ml_dtypes
import numpy as np
from jax import lax
from jax.experimental import pallas as pl
from jax.experimental.pallas import tpu as pltpu
from jax.sharding import PartitionSpec as P

H = 12
RING = 4
ORDERS = ((2, 1, 0), (1, 0, 2), (0, 2, 1))

norm_eps = 1e-05
clip_bound = 0.01
learn_rate = 10000.0
momentum_coef = 0.5
ema_decay = 0.5


def place():
    dp = lax.axis_index("dp")
    vocab = lax.axis_index("vocab")
    return (lax.div(dp, RING), lax.rem(dp, RING), lax.div(vocab, 2)), lax.rem(vocab, 2)


def device_at(at, core):
    return (at[0] * RING + at[1], at[2] * 2 + core)


def moved(at, axis, by):
    out = list(at)
    out[axis] = lax.rem(at[axis] + by, RING)
    return tuple(out)


class Wires:
    def __init__(self, send, recv):
        self.send, self.recv, self.count, self.live = send, recv, 0, []

    def copy(self, src, dst, device):
        number = self.count
        self.count += 1
        op = pltpu.make_async_remote_copy(
            src_ref=src,
            dst_ref=dst,
            send_sem=self.send.at[number],
            recv_sem=self.recv.at[number],
            device_id=device,
            device_id_type=pl.DeviceIdType.MESH,
        )
        op.start()
        self.live.append(op)
        return op

    def drain(self):
        for op in self.live:
            op.wait_send()


def greet(devices):
    barrier = pltpu.get_barrier_semaphore()
    for device in devices:
        pl.semaphore_signal(
            barrier, inc=1, device_id=device, device_id_type=pl.DeviceIdType.MESH
        )
    pl.semaphore_wait(barrier, len(devices))


def ring_peers(at, core):
    near = [device_at(moved(at, axis, by), core) for axis in range(3) for by in range(1, RING)]
    return near + [device_at(at, 1 - core)]


def neighbours(at, core):
    near = [device_at(moved(at, axis, by), core) for axis in range(3) for by in (1, RING - 1)]
    return near + [device_at(at, 1 - core)]


def gather_kernel(
    mine_ref,
    small_ref,
    table_ref,
    spread_ref,
    earlier_ref,
    slot_ref,
    swap_ref,
    out_ref,
    small_out,
    rows_out,
    asked_out,
    peer,
    block,
    asked_rows,
    over_z,
    over_y,
    sorted_rows,
    over_x,
    send,
    recv,
    local,
):
    at, core = place()
    z, y, x = at
    rows, half = mine_ref.shape[1], mine_ref.shape[2] // 2
    part = 2 * rows // 3
    low, f32 = jnp.bfloat16, jnp.float32
    sibling = device_at(at, 1 - core)
    greet(ring_peers(at, core))
    wires = Wires(send, recv)
    cols = pl.ds(pl.multiple_of(core * half, half), half)
    other = pl.ds(pl.multiple_of((1 - core) * half, half), half)

    swap = wires.copy(mine_ref.at[:, :, other], peer, sibling)
    small_out[z, y, x, core] = small_ref[...]

    def right(axis):
        return device_at(moved(at, axis, 1), core)

    def left(axis):
        return device_at(moved(at, axis, RING - 1), core)

    def all_around(axis, src_of, dst):
        out = []
        for by in range(1, RING):
            there = moved(at, axis, by)
            out.append(wires.copy(src_of(there[axis]), dst, device_at(there, core)))
        return out

    def small_start(phase):
        index = [z, y, x]
        for axis in ORDERS[0][:phase]:
            index[axis] = pl.ds(0, RING)
        own = small_out.at[index[0], index[1], index[2], core]
        return all_around(ORDERS[0][phase], lambda c: own, own)

    def arrive(ops):
        for op in ops:
            op.wait_recv()

    small_ops = small_start(0)
    swap.wait_recv()
    for layer in range(2):
        own = jnp.where(core == 0, mine_ref[layer, :, :half], mine_ref[layer, :, half:])
        got = peer[layer]
        both = jnp.concatenate(
            [jnp.where(core == 0, own, got), jnp.where(core == 0, got, own)], 0
        )
        block[layer] = both.astype(low)
    block_local = []
    for layer in range(2):
        op = pltpu.make_async_copy(
            block.at[layer], out_ref.at[layer, z, y, x, :, cols], local.at[layer]
        )
        op.start()
        block_local.append(op)

    def bundle(layer, p, phase, c, piece=None):
        order = ORDERS[p]
        index = list(at)
        index[order[phase]] = c
        for axis in order[:phase]:
            index[axis] = pl.ds(0, RING)
        first, count = p * part, part
        if piece is not None:
            if phase == 0:
                first, count = (first, 32) if piece == 0 else (first + 32, part - 32)
            else:
                index[order[0]] = pl.ds(2 * piece, 2)
        return out_ref.at[layer, index[0], index[1], index[2], pl.ds(first, count), cols]

    chains = [(layer, p) for layer in range(2) for p in range(3)]
    pending = []
    steps, forwards = {}, {}

    def start(phase):
        for key in chains:
            layer, p = key
            axis = ORDERS[p][phase]
            src = bundle(layer, p, phase, at[axis])
            if phase == 2:
                pending.append(wires.copy(src, src, sibling))
            steps[key] = (wires.copy(src, src, right(axis)), wires.copy(src, src, left(axis)))

    def forward(phase):
        for key in chains:
            layer, p = key
            axis = ORDERS[p][phase]
            before, after = lax.rem(at[axis] + 3, RING), lax.rem(at[axis] + 1, RING)
            steps[key][0].wait_recv()
            src = bundle(layer, p, phase, before, 0)
            one = wires.copy(src, src, right(axis))
            steps[key][1].wait_recv()
            src = bundle(layer, p, phase, after, 1)
            two = wires.copy(src, src, left(axis))
            forwards[key] = (one, two)
            if phase == 2:
                for c in (before, after):
                    src = bundle(layer, p, phase, c)
                    pending.append(wires.copy(src, src, sibling))

    def finish(phase):
        for key in chains:
            layer, p = key
            axis = ORDERS[p][phase]
            across = lax.rem(at[axis] + 2, RING)
            for piece in range(2):
                forwards[key][piece].wait_recv()
                if phase == 2:
                    src = bundle(layer, p, phase, across, piece)
                    pending.append(wires.copy(src, src, sibling))

    arrive(block_local_wait(block_local))
    start(0)
    arrive(small_ops)
    small_ops = small_start(1)
    forward(0)
    arrive(small_ops)
    small_ops = small_start(2)
    finish(0)
    start(1)
    arrive(small_ops)
    own = small_out.at[:, :, :, core]
    small_ops = [wires.copy(own, own, sibling)]
    forward(1)
    arrive(small_ops)

    count = 2 * RING**3
    smalls = small_out[...].reshape((count,) + small_ref.shape)
    high, rest = (
        jnp.dot(spread_ref[...], smalls[:, IDS_ROW + n, :], preferred_element_type=f32)
        for n in range(2)
    )
    own_rows = TABLE_ROWS
    me = ((z * RING + y) * RING + x) * 2 + core
    local_id = high * 256.0 + rest - (me * own_rows).astype(f32)
    mine = (local_id >= 0.0) & (local_id < float(own_rows))
    rank = jnp.dot(
        jnp.where(mine, 1.0, 0.0).astype(low), earlier_ref[...], preferred_element_type=f32
    )
    picked = jnp.where(mine & (rank == slot_ref[...]), local_id, 0.0)
    row = jnp.sum(picked, 1, keepdims=True).astype(jnp.int32)
    places = lax.broadcasted_iota(jnp.int32, asked_out.shape, 1)
    asked = jnp.where(places == row, 1.0, 0.0).astype(low)
    asked_out[...] = asked
    found = jnp.dot(asked, table_ref[...], preferred_element_type=f32).astype(low)
    asked_rows[...] = found.reshape(asked_rows.shape)
    over_z[z] = asked_rows[z]
    row_ops = all_around(0, lambda c: asked_rows.at[c], over_z.at[z])

    finish(1)
    start(2)
    arrive(row_ops)
    over_y[y] = over_z[:, y]
    row_ops = all_around(1, lambda c: over_z.at[:, c], over_y.at[y])
    forward(2)
    arrive(row_ops)
    sorted_rows[...] = (
        jnp.dot(
            swap_ref[...], over_y[...].reshape(2 * count, table_ref.shape[1]), preferred_element_type=f32
        )
        .astype(low)
        .reshape(sorted_rows.shape)
    )
    over_x[x] = sorted_rows[x]
    row_ops = all_around(2, lambda c: sorted_rows.at[c], over_x.at[x])
    finish(2)
    arrive(row_ops)
    pending.append(wires.copy(over_x.at[:, 1 - core], rows_out.at[:, core], sibling))
    rows_out[:, core] = over_x[:, core]
    arrive(pending)
    wires.drain()


def block_local_wait(ops):
    for op in ops:
        op.wait()
    return []


IDS_ROW = 8
TABLE_ROWS = 393
GATHER_COPIES = 1 + 3 * (6 * 4 + 3) + 6 * 5 + 1 + 9 + 1


def gather_weights(mine, small, table, spread, earlier, slots, swap):
    layers, rows, width = mine.shape
    table_rows = table.shape[0]
    count = 2 * RING**3
    low = jnp.bfloat16
    hbm = pl.BlockSpec(memory_space=pltpu.HBM)
    vmem = pl.BlockSpec(memory_space=pltpu.VMEM)
    mats, small_all, fetched, asked = pl.pallas_call(
        gather_kernel,
        out_shape=(
            jax.ShapeDtypeStruct((layers, RING, RING, RING, 2 * rows, width), low),
            jax.ShapeDtypeStruct((RING, RING, RING, 2) + small.shape, low),
            jax.ShapeDtypeStruct((RING, 2, count // 4, width), low),
            jax.ShapeDtypeStruct((2 * count, table_rows), low),
        ),
        in_specs=[vmem] * 7,
        out_specs=(hbm, vmem, vmem, vmem),
        scratch_shapes=[
            pltpu.VMEM((layers, rows, width // 2), jnp.float32),
            pltpu.VMEM((layers, 2 * rows, width // 2), low),
            pltpu.VMEM((RING, RING, 16, width), low),
            pltpu.VMEM((RING, RING, 16, width), low),
            pltpu.VMEM((RING, RING, 16, width), low),
            pltpu.VMEM((RING, 2, count // 4, width), low),
            pltpu.VMEM((RING, 2, count // 4, width), low),
            pltpu.SemaphoreType.DMA((GATHER_COPIES,)),
            pltpu.SemaphoreType.DMA((GATHER_COPIES,)),
            pltpu.SemaphoreType.DMA((2,)),
        ],
        compiler_params=pltpu.CompilerParams(
            collective_id=0, has_side_effects=True, vmem_limit_bytes=58 * 2**20
        ),
        cost_estimate=pl.CostEstimate(flops=0, bytes_accessed=250 * 10**6, transcendentals=0),
        name="gather_weights",
    )(mine, small, table, spread, earlier, slots, swap)
    return (
        mats.reshape(layers * RING**3 * 2 * rows, width),
        small_all.reshape((count,) + small.shape),
        fetched.reshape(2 * count, width),
        asked,
    )


class Reduction:
    def __init__(self, at, core, send, recv):
        self.at, self.core, self.send, self.recv = at, core, send, recv
        self.number, self.level, self.halves, self.fulls = {}, {}, {}, {}
        self.final = None

    def copy(self, key, src, dst, device):
        number = self.number.setdefault(key, len(self.number))
        return pltpu.make_async_remote_copy(
            src_ref=src,
            dst_ref=dst,
            send_sem=self.send.at[number],
            recv_sem=self.recv.at[number],
            device_id=device,
            device_id_type=pl.DeviceIdType.MESH,
        )

    def axes(self, p):
        order = ORDERS[p]
        free = sorted(order[:2])
        return free, free.index(order[1])

    def ring(self, p, step):
        axis = ORDERS[p][2 - step]
        c = self.at[axis]
        right = device_at(moved(self.at, axis, 1), self.core)
        left = device_at(moved(self.at, axis, RING - 1), self.core)
        return c, lax.rem(c + 1, RING), lax.rem(c + 2, RING), lax.rem(c + 3, RING), right, left

    def index(self, layer, p, step, c, piece=None):
        part = 48
        cut, whole = (0, RING) if piece is None else (2 * piece, 2), (0, RING)
        if step == 0:
            free, unused = self.axes(p)
            spot = [c, c, c]
            spot[free[0]], spot[free[1]] = cut, whole
            return spot + [p]
        if step == 1:
            unused, first = self.axes(p)
            spot = [cut, cut]
            spot[first] = c
            return [layer % self.level[1].shape[0], p] + spot
        if piece is None:
            return [layer, p, c]
        return [layer, p, c, pl.ds(0, 32) if piece == 0 else pl.ds(32, part - 32)]

    def view(self, layer, p, step, c, piece=None):
        index = self.index(layer, p, step, c, piece)
        held = self.level[0, layer] if step == 0 else self.level[step]
        return held.at[tuple(pl.ds(*item) if isinstance(item, tuple) else item for item in index)]

    def slot(self, layer, p, step, side, whole):
        store = (self.fulls if whole else self.halves)[step]
        if step == 2 and not whole:
            return store.at[layer, p, side, pl.ds(0, 32 if side == 0 else 16)]
        return store.at[layer % store.shape[0], p, side]

    def half_copies(self, layer, p, step):
        unused, after, across, before, right, left = self.ring(p, step)
        out = []
        for side, device in ((0, right), (1, left)):
            out.append(
                self.copy(
                    (layer, p, step, side),
                    self.view(layer, p, step, across, side),
                    self.slot(layer, p, step, side, False),
                    device,
                )
            )
        return out

    def full_copies(self, layer, p, step):
        unused, after, across, before, right, left = self.ring(p, step)
        out = []
        for side, c, device in ((0, after, right), (1, before, left)):
            out.append(
                self.copy(
                    (layer, p, step, 2 + side),
                    self.view(layer, p, step, c),
                    self.slot(layer, p, step, side, True),
                    device,
                )
            )
        return out

    def add(self, layer, p, step, c, piece, terms, into):
        held = self.level[0, layer] if step == 0 else self.level[step]
        index = self.index(layer, p, step, c, piece)
        sizes = [item[1] for item in index if isinstance(item, tuple)]

        def one(inner):
            places = iter(inner)
            spot = tuple(
                item[0] + next(places) if isinstance(item, tuple) else item for item in index
            )
            value = held[spot].astype(jnp.float32)
            for term in terms:
                value = value + term[tuple(inner) + (slice(None), slice(None))].astype(jnp.float32)
            into(held, spot, inner, value)

        def body(n, unused):
            if len(sizes) == 2:
                for k in range(sizes[1]):
                    one([n, k])
            else:
                one([n])
            return unused

        if sizes:
            lax.fori_loop(0, sizes[0], body, 0)
        else:
            one([])

    def start(self, layer, step):
        for p in range(3):
            for op in self.half_copies(layer, p, step):
                op.start()

    def turn(self, layer, step):
        def back(held, spot, inner, value):
            held[spot] = value.astype(held.dtype)

        for p in range(3):
            unused, after, across, before, right, left = self.ring(p, step)
            halves, fulls = self.half_copies(layer, p, step), self.full_copies(layer, p, step)
            for side, c in ((0, after), (1, before)):
                halves[side].wait_recv()
                self.add(
                    layer, p, step, c, side, [self.slot(layer, p, step, side, False)], back
                )
                fulls[side].start()

    def finish(self, layer, step):
        for p in range(3):
            c = self.ring(p, step)[0]
            for op in self.full_copies(layer, p, step):
                op.wait_recv()
            terms = [self.slot(layer, p, step, side, True) for side in range(2)]

            def up(held, spot, inner, value, p=p):
                if step == 2:
                    self.final[layer, p * 48 : (p + 1) * 48] = value
                else:
                    target = self.level[step + 1]
                    spot = (layer % target.shape[0], p) + tuple(inner)
                    target[spot] = value.astype(target.dtype)

            self.add(layer, p, step, c, None, terms, up)

    def drain(self, layer, step):
        for p in range(3):
            for op in self.half_copies(layer, p, step) + self.full_copies(layer, p, step):
                op.wait_send()


def reduce_kernel(
    acc_ref,
    small_ref,
    rows_ref,
    swap_ref,
    out_ref,
    small_out,
    rows_out,
    acc_0,
    acc_1,
    mid,
    thin,
    half_0,
    half_1,
    half_2,
    full_0,
    full_1,
    full_2,
    small_acc,
    small_sib,
    small_wide,
    small_mid,
    small_thin,
    final,
    final_peer,
    over_core,
    over_x,
    sorted_rows,
    over_y,
    send,
    recv,
    send_small,
    recv_small,
    local,
):
    at, core = place()
    own_rows, half = final_peer.shape[1], final_peer.shape[2]
    sibling = device_at(at, 1 - core)
    sums = Reduction(at, core, send, recv)
    sums.level = {(0, 0): acc_0, (0, 1): acc_1, 1: mid, 2: thin}
    sums.halves = {0: half_0, 1: half_1, 2: half_2}
    sums.fulls = {0: full_0, 1: full_1, 2: full_2}
    sums.final = final

    accs = (acc_0, acc_1)
    loads = {}
    for layer in (1, 0):
        for n in range(RING * RING):
            spot = (n // RING, n % RING)
            op = pltpu.make_async_copy(
                acc_ref.at[(layer,) + spot], accs[layer].at[spot], local.at[1 + 16 * layer + n]
            )
            op.start()
            loads[layer, n] = op
    small_load = pltpu.make_async_copy(small_ref.at[:, :, :, core], small_acc, local.at[0])
    small_load.start()
    greet(ring_peers(at, core))
    wires = Wires(send_small, recv_small)
    small_swap = wires.copy(small_ref.at[:, :, :, 1 - core], small_sib, sibling)

    order = ORDERS[0]
    slots = (small_wide, small_mid, small_thin)

    def right(axis):
        return device_at(moved(at, axis, 1), core)

    def left(axis):
        return device_at(moved(at, axis, RING - 1), core)

    def small_view(step, c):
        index = list(at)
        index[order[2 - step]] = c
        for axis in order[: 2 - step]:
            index[axis] = slice(None)
        return tuple(index)

    def small_add(step, c, term):
        where = small_view(step, c)
        small_acc[where] = small_acc[where] + term

    def small_start(step):
        axis = order[2 - step]
        across = lax.rem(at[axis] + 2, RING)
        return wires.copy(small_acc.at[small_view(step, across)], slots[step].at[0], right(axis))

    def small_turn(step, op):
        axis = order[2 - step]
        after, before = lax.rem(at[axis] + 1, RING), lax.rem(at[axis] + 3, RING)
        op.wait_recv()
        small_add(step, after, slots[step][0])
        return (
            wires.copy(small_acc.at[small_view(step, after)], slots[step].at[1], right(axis)),
            wires.copy(small_acc.at[small_view(step, before)], slots[step].at[2], left(axis)),
        )

    def small_finish(step, ops):
        for op in ops:
            op.wait_recv()
        small_add(step, at[order[2 - step]], slots[step][1] + slots[step][2])

    z, y, x = at

    def all_around(axis, src_of, dst):
        out = []
        for by in range(1, RING):
            there = moved(at, axis, by)
            out.append(wires.copy(src_of(there[axis]), dst, device_at(there, core)))
        return out

    def arrive(ops):
        for op in ops:
            op.wait_recv()

    for layer in (1, 0):
        for n in range(RING * RING):
            loads[layer, n].wait()
        sums.start(layer, 0)
    row_ops = [wires.copy(rows_ref.at[:, 1 - core], over_core.at[:, core], sibling)]
    over_core[:, core] = rows_ref[:, core]
    small_load.wait()
    small_swap.wait_recv()
    small_acc[...] = small_acc[...] + small_sib[...]
    op = small_start(0)
    arrive(row_ops)
    over_x[x] = over_core[x]
    row_ops = all_around(2, lambda c: over_core.at[c], over_x.at[x])
    sums.turn(1, 0)
    sums.turn(0, 0)
    ops = small_turn(0, op)
    arrive(row_ops)
    count, width = swap_ref.shape[0], rows_ref.shape[3]
    sorted_rows[...] = (
        jnp.dot(
            swap_ref[...], over_x[...].reshape(count, width), preferred_element_type=jnp.float32
        )
        .astype(jnp.bfloat16)
        .reshape(sorted_rows.shape)
    )
    over_y[y] = sorted_rows[y]
    row_ops = all_around(1, lambda c: sorted_rows.at[c], over_y.at[y])
    small_finish(0, ops)
    op = small_start(1)
    sums.finish(1, 0)
    sums.start(1, 1)
    arrive(row_ops)
    rows_out[z] = over_y[:, z]
    row_ops = all_around(0, lambda c: over_y.at[:, c], rows_out.at[z])
    ops = small_turn(1, op)
    sums.finish(0, 0)
    sums.start(0, 1)
    small_finish(1, ops)
    op = small_start(2)
    sums.turn(1, 1)
    ops = small_turn(2, op)
    sums.turn(0, 1)
    sums.finish(1, 1)
    sums.start(1, 2)
    sums.finish(0, 1)
    sums.start(0, 2)
    small_finish(2, ops)
    sums.turn(1, 2)
    sums.turn(0, 2)
    sums.finish(1, 2)
    sums.finish(0, 2)
    arrive(row_ops)

    theirs = pl.ds(pl.multiple_of((1 - core) * own_rows, own_rows), own_rows)
    swap = wires.copy(final.at[:, theirs], final_peer, sibling)
    small_out[...] = small_acc[at]
    swap.wait_recv()
    for layer in range(2):
        own = jnp.where(core == 0, final[layer, :own_rows], final[layer, own_rows:])
        got = final_peer[layer]
        out_ref[layer, :, :half] = jnp.where(core == 0, own, got)
        out_ref[layer, :, half:] = jnp.where(core == 0, got, own)
    for layer in range(2):
        for step in range(3):
            sums.drain(layer, step)
    wires.drain()


def reduce_weights(acc, small, rows_back, swap):
    part, half = acc.shape[5:]
    rows = 3 * part
    torus = (RING, RING, RING)
    small_shape = small.shape[1:]
    hbm = pl.BlockSpec(memory_space=pltpu.HBM)
    vmem = pl.BlockSpec(memory_space=pltpu.VMEM)
    low = jnp.bfloat16
    return pl.pallas_call(
        reduce_kernel,
        out_shape=(
            jax.ShapeDtypeStruct((2, rows // 2, 2 * half), jnp.float32),
            jax.ShapeDtypeStruct(small_shape, jnp.float32),
            jax.ShapeDtypeStruct((RING, RING, 16, 2 * half), low),
        ),
        in_specs=[hbm, hbm, vmem, vmem],
        out_specs=(vmem, vmem, vmem),
        scratch_shapes=[
            pltpu.VMEM(torus + (3, part, half), low),
            pltpu.VMEM(torus + (3, part, half), low),
            pltpu.VMEM((2, 3, RING, RING, part, half), low),
            pltpu.VMEM((2, 3, RING, part, half), low),
            pltpu.VMEM((2, 3, 2, 2, RING, part, half), low),
            pltpu.VMEM((2, 3, 2, 2, part, half), low),
            pltpu.VMEM((2, 3, 2, 32, half), low),
            pltpu.VMEM((2, 3, 2, RING, RING, part, half), low),
            pltpu.VMEM((2, 3, 2, RING, part, half), low),
            pltpu.VMEM((2, 3, 2, part, half), low),
            pltpu.VMEM(torus + small_shape, jnp.float32),
            pltpu.VMEM(torus + small_shape, jnp.float32),
            pltpu.VMEM((3, RING, RING) + small_shape, jnp.float32),
            pltpu.VMEM((3, RING) + small_shape, jnp.float32),
            pltpu.VMEM((3,) + small_shape, jnp.float32),
            pltpu.VMEM((2, rows, half), jnp.float32),
            pltpu.VMEM((2, rows // 2, half), jnp.float32),
            pltpu.VMEM((RING, 2, 32, 2 * half), low),
            pltpu.VMEM((RING, 2, 32, 2 * half), low),
            pltpu.VMEM((RING, RING, 16, 2 * half), low),
            pltpu.VMEM((RING, RING, 16, 2 * half), low),
            pltpu.SemaphoreType.DMA((72,)),
            pltpu.SemaphoreType.DMA((72,)),
            pltpu.SemaphoreType.DMA((21,)),
            pltpu.SemaphoreType.DMA((21,)),
            pltpu.SemaphoreType.DMA((33,)),
        ],
        compiler_params=pltpu.CompilerParams(
            collective_id=1, has_side_effects=True, vmem_limit_bytes=58 * 2**20
        ),
        cost_estimate=pl.CostEstimate(flops=0, bytes_accessed=280 * 10**6, transcendentals=0),
        name="reduce_weights",
    )(acc, small.reshape(torus + (2,) + small_shape), rows_back, swap)


def sum_kernel(
    part_ref, asked_ref, back_ref, mats_ref, small_ref, loss_ref, out_ref, table_ref, slots, send, recv
):
    at, core = place()
    sibling = device_at(at, 1 - core)
    greet(ring_peers(at, core))
    wires = Wires(send, recv)
    table = part_ref[...].astype(jnp.float32) + lax.dot_general(
        asked_ref[...],
        back_ref[...],
        (((0,), (0,)), ((), ())),
        preferred_element_type=jnp.float32,
    )
    table_ref[...] = table

    def total(value):
        while value.ndim > 2:
            value = jnp.sum(value, 0)
        return jnp.sum(jnp.sum(value, 0, keepdims=True), 1, keepdims=True)

    mats, small = mats_ref[...], small_ref[...]
    squares = total(table * table) + total(mats * mats) + total(small * small)
    rows = lax.broadcasted_iota(jnp.int32, out_ref.shape, 0)
    slots[0, core] = jnp.where(rows == 0, total(loss_ref[...]), squares)
    swap = wires.copy(slots.at[0, core], slots.at[0, core], sibling)
    swap.wait_recv()
    value = slots[0, 0] + slots[0, 1]
    for axis in range(3):
        slots[1 + axis, at[axis]] = value
        ops = []
        for by in range(1, RING):
            ops.append(
                wires.copy(
                    slots.at[1 + axis, at[axis]],
                    slots.at[1 + axis, at[axis]],
                    device_at(moved(at, axis, by), core),
                )
            )
        for op in ops:
            op.wait_recv()
        value = slots[1 + axis, 0]
        for c in range(1, RING):
            value = value + slots[1 + axis, c]
    out_ref[...] = value
    wires.drain()


def sum_all(part, asked, back, mats, small, losses):
    vmem = pl.BlockSpec(memory_space=pltpu.VMEM)
    value = (8, 128)
    return pl.pallas_call(
        sum_kernel,
        out_shape=(
            jax.ShapeDtypeStruct(value, jnp.float32),
            jax.ShapeDtypeStruct(part.shape, jnp.float32),
        ),
        in_specs=[vmem] * 6,
        out_specs=(vmem, vmem),
        scratch_shapes=[
            pltpu.VMEM((4, RING) + value, jnp.float32),
            pltpu.SemaphoreType.DMA((10,)),
            pltpu.SemaphoreType.DMA((10,)),
        ],
        compiler_params=pltpu.CompilerParams(
            collective_id=2, has_side_effects=True, vmem_limit_bytes=24 * 2**20
        ),
        cost_estimate=pl.CostEstimate(flops=0, bytes_accessed=40 * 10**6, transcendentals=0),
        name="sum_all",
    )(part, asked, back, mats, small, losses)


def update_kernel(sums_ref, *refs):
    norm = jnp.sqrt(sums_ref[1:2, 0:1])
    factor = clip_bound / jnp.maximum(norm, clip_bound)
    for n in range(2):
        weight, moment, average, grad = refs[4 * n : 4 * n + 4]
        outs = refs[8 + 4 * n : 12 + 4 * n]
        rows = weight.shape[0]
        results = renew(weight[...], moment[...], average[...], grad[:rows, :], factor)
        for out, value in zip(outs, results):
            out[...] = value


def update(sums, table, mats):
    shapes = []
    for item in (table[0], mats[0]):
        shapes += [jax.ShapeDtypeStruct(item.shape, jnp.float32)] * 3
        shapes += [jax.ShapeDtypeStruct(item.shape, jnp.bfloat16)]
    width = table[0].shape[1]
    block = pl.BlockSpec((144, width), lambda i: (i, 0))
    third = pl.BlockSpec((mats[0].shape[0] // 3, width), lambda i: (i, 0))
    whole = pl.BlockSpec(sums.shape, lambda i: (0, 0))
    outs = pl.pallas_call(
        update_kernel,
        grid=(3,),
        out_shape=tuple(shapes),
        in_specs=[whole] + [block] * 4 + [third] * 4,
        out_specs=(block,) * 4 + (third,) * 4,
        compiler_params=pltpu.CompilerParams(vmem_limit_bytes=32 * 2**20),
        name="update",
    )(sums, *table, *mats)
    return outs[:4], outs[4:]


TILE = 800


def head_kernel(
    f_ref,
    code_ref,
    weight_ref,
    table_ref,
    grad_out,
    dtable_ref,
    loss_ref,
    f_all,
    codes,
    table,
    logits,
    probs,
    tops,
    stats,
    df,
    df_send,
    df_sib,
    ring,
    ring_half,
    ring_full,
    staged,
    send,
    recv,
    load,
    store,
):
    at, core = place()
    x = at[2]
    dp, vocab = lax.axis_index("dp"), lax.axis_index("vocab")
    tok, width = f_ref.shape
    group = f_all.shape[0]
    members = group // tok
    tiles = table.shape[0] // TILE
    low, f32 = jnp.bfloat16, jnp.float32

    def tile_rows(t):
        return pl.ds(pl.multiple_of(t * TILE, TILE), TILE)

    loads = []
    for t in range(tiles):
        op = pltpu.make_async_copy(
            table_ref.at[pl.ds(t * TILE, TILE)], table.at[pl.ds(t * TILE, TILE)], load.at[t]
        )
        op.start()
        loads.append(op)

    peers = [(dp, lax.rem(vocab + by, members)) for by in range(1, members)]
    greet(peers)
    wires = Wires(send, recv)
    sibling = device_at(at, 1 - core)
    right, left = device_at(moved(at, 2, 1), core), device_at(moved(at, 2, 3), core)
    before, after, across = lax.rem(x + 3, RING), lax.rem(x + 1, RING), lax.rem(x + 2, RING)

    def rows_of(at_x, piece=None):
        first = (at_x * 2 + core) * tok
        if piece is None:
            return f_all.at[pl.ds(pl.multiple_of(first, tok), tok)]
        half = tok // 2
        return f_all.at[pl.ds(pl.multiple_of(first + piece * half, half), half)]

    f_all[pl.ds(pl.multiple_of(vocab * tok, tok), tok), :] = f_ref[...]
    own = rows_of(x)
    one, two = wires.copy(own, own, right), wires.copy(own, own, left)
    pending = [wires.copy(own, own, sibling)]
    codes[vocab] = code_ref[...]
    for peer in peers:
        pending.append(wires.copy(codes.at[vocab], codes.at[vocab], peer))
    one.wait_recv()
    one_on = wires.copy(rows_of(before, 0), rows_of(before, 0), right)
    pending.append(wires.copy(rows_of(before), rows_of(before), sibling))
    two.wait_recv()
    two_on = wires.copy(rows_of(after, 1), rows_of(after, 1), left)
    pending.append(wires.copy(rows_of(after), rows_of(after), sibling))
    one_on.wait_recv()
    pending.append(wires.copy(rows_of(across, 0), rows_of(across, 0), sibling))
    two_on.wait_recv()
    pending.append(wires.copy(rows_of(across, 1), rows_of(across, 1), sibling))
    for op in pending:
        op.wait_recv()

    code_row = jnp.concatenate([codes[m, 0:1, :] for m in range(members)], 1) - vocab * table.shape[0]
    code8 = jnp.broadcast_to(code_row, (8, group))
    code16 = jnp.broadcast_to(code_row, (16, group))
    rows8 = lax.broadcasted_iota(jnp.int32, (8, group), 0)
    rows16 = lax.broadcasted_iota(jnp.int32, (16, group), 0)
    slot = TILE // 2
    real = slot - 7
    steps8, steps16 = 5, 5

    def first_pass(t, carry):
        top, total, target = carry
        here = tile_rows(t)
        logits[...] = lax.dot_general(
            table[here, :], f_all[...], (((1,), (1,)), ((), ())), preferred_element_type=f32
        )
        for part in range(2):
            last = pl.ds((part + 1) * slot - 8, 8)
            logits[last, :] = jnp.where(rows8 < 1, logits[last, :], -1e30)

        def look(i, state):
            high, hit = state
            for u in range(steps8):
                first = (i * steps8 + u) * 8
                value = logits[pl.ds(pl.multiple_of(first, 8), 8), :]
                high = jnp.maximum(high, value)
                hit = hit + jnp.where(rows8 + (first + t * TILE) == code8, value, 0.0)
            return high, hit

        high, hit = lax.fori_loop(
            0,
            TILE // (8 * steps8),
            look,
            (jnp.full((8, group), -1e30, f32), jnp.zeros((8, group), f32)),
        )
        top_next = jnp.maximum(top, jnp.max(high, 0, keepdims=True))
        target = target + jnp.sum(hit, 0, keepdims=True)

        def lift(i, acc):
            for u in range(steps16):
                first = (i * steps16 + u) * 16
                value = jnp.exp(logits[pl.ds(pl.multiple_of(first, 16), 16), :] - top_next)
                acc = acc + value
                probs[pl.ds(pl.multiple_of(t * TILE + first, 16), 16), :] = value.astype(low)
            return acc

        acc = lax.fori_loop(
            0, TILE // (16 * steps16), lift, jnp.zeros((16, group), f32)
        )
        total = total * jnp.exp(top - top_next) + jnp.sum(acc, 0, keepdims=True)
        tops[t] = top_next
        return top_next, total, target

    for op in loads:
        op.wait()
    start = (jnp.full((1, group), -1e30, f32), jnp.zeros((1, group), f32), jnp.zeros((1, group), f32))
    found = lax.fori_loop(0, tiles, first_pass, start)
    for k in range(3):
        for m in range(members):
            stats[vocab, k, m : m + 1, :] = found[k][:, m * tok : (m + 1) * tok]
    pending = [wires.copy(stats.at[vocab], stats.at[vocab], peer) for peer in peers]
    for op in pending:
        op.wait_recv()
    peak = stats[0, 0]
    for m in range(1, members):
        peak = jnp.maximum(peak, stats[m, 0])
    total, target = jnp.zeros_like(peak), jnp.zeros_like(peak)
    for m in range(members):
        total = total + stats[m, 1] * jnp.exp(stats[m, 0] - peak)
        target = target + stats[m, 2]
    lse = peak + jnp.log(total)
    weight = weight_ref[...]
    mine = lax.broadcasted_iota(jnp.int32, (members, tok), 0) == vocab
    loss_ref[...] = jnp.where(mine, weight * (lse - target), 0.0)
    lse_row = jnp.concatenate([lse[m : m + 1, :] for m in range(members)], 1)
    weight_row = jnp.concatenate([weight[m : m + 1, :] for m in range(members)], 1)

    df[...] = jnp.zeros_like(df)

    def second_pass(t, unused):
        scale = weight_row * jnp.exp(tops[t] - lse_row)

        def turn(i, unused):
            for u in range(steps16):
                first = t * TILE + (i * steps16 + u) * 16
                here = pl.ds(pl.multiple_of(first, 16), 16)
                value = probs[here, :].astype(f32) * scale
                value = value - jnp.where(rows16 + first == code16, weight_row, 0.0)
                probs[here, :] = value.astype(low)
            return unused

        lax.fori_loop(0, TILE // (16 * steps16), turn, 0)
        here = tile_rows(t)
        df[...] += lax.dot_general(
            probs[here, :], table[here, :], (((0,), (0,)), ((), ())), preferred_element_type=f32
        )
        return unused

    lax.fori_loop(0, tiles, second_pass, 0)

    def third_pass(t):
        if t >= 2:
            stores[t - 2].wait()
        staged[t % 2] = jnp.dot(
            probs[t * TILE : (t + 1) * TILE, :], f_all[...], preferred_element_type=f32
        ).astype(low)
        op = pltpu.make_async_copy(
            staged.at[t % 2], dtable_ref.at[pl.ds(t * TILE, TILE)], store.at[t]
        )
        op.start()
        stores.append(op)

    stores = []
    for m in range(members):
        df_send[m % 2, m // 2] = df[m * tok : (m + 1) * tok, :].astype(low)
    swap = wires.copy(df_send.at[1 - core], df_sib, sibling)
    third_pass(0)
    third_pass(1)
    swap.wait_recv()
    for k in range(RING):
        first = pl.multiple_of((2 * k + core) * tok, tok)
        ring[k] = (df[pl.ds(first, tok), :] + df_sib[k].astype(f32)).astype(low)
    half = tok // 2
    one = wires.copy(ring.at[across, pl.ds(0, half)], ring_half.at[0], right)
    two = wires.copy(ring.at[across, pl.ds(half, half)], ring_half.at[1], left)
    third_pass(2)
    third_pass(3)
    one.wait_recv()
    ring[after, :half] = (ring[after, :half].astype(f32) + ring_half[0].astype(f32)).astype(low)
    one = wires.copy(ring.at[after], ring_full.at[0], right)
    two.wait_recv()
    ring[before, half:] = (ring[before, half:].astype(f32) + ring_half[1].astype(f32)).astype(low)
    two = wires.copy(ring.at[before], ring_full.at[1], left)
    for t in range(4, tiles):
        third_pass(t)
    one.wait_recv()
    two.wait_recv()
    grad_out[...] = ring[x].astype(f32) + ring_full[0].astype(f32) + ring_full[1].astype(f32)
    for op in stores[-2:]:
        op.wait()
    wires.drain()


HEAD_COPIES = 9 + 7 + 7 + 5


def head(final_low, codes, weights, table):
    tok, width = final_low.shape
    rows = table.shape[0]
    members = weights.shape[0]
    group = members * tok
    tiles = rows // TILE
    hbm = pl.BlockSpec(memory_space=pltpu.HBM)
    vmem = pl.BlockSpec(memory_space=pltpu.VMEM)
    low, f32 = jnp.bfloat16, jnp.float32
    return pl.pallas_call(
        head_kernel,
        out_shape=(
            jax.ShapeDtypeStruct((tok, width), f32),
            jax.ShapeDtypeStruct((rows, width), low),
            jax.ShapeDtypeStruct((members, tok), f32),
        ),
        in_specs=[vmem, vmem, vmem, hbm],
        out_specs=(vmem, hbm, vmem),
        scratch_shapes=[
            pltpu.VMEM((group, width), low),
            pltpu.VMEM((members, 8, tok), jnp.int32),
            pltpu.VMEM((rows, width), low),
            pltpu.VMEM((TILE, group), f32),
            pltpu.VMEM((rows, group), low),
            pltpu.VMEM((tiles, 1, group), f32),
            pltpu.VMEM((members, 3, members, tok), f32),
            pltpu.VMEM((group, width), f32),
            pltpu.VMEM((2, RING, tok, width), low),
            pltpu.VMEM((RING, tok, width), low),
            pltpu.VMEM((RING, tok, width), low),
            pltpu.VMEM((2, tok // 2, width), low),
            pltpu.VMEM((2, tok, width), low),
            pltpu.VMEM((2, TILE, width), low),
            pltpu.SemaphoreType.DMA((HEAD_COPIES,)),
            pltpu.SemaphoreType.DMA((HEAD_COPIES,)),
            pltpu.SemaphoreType.DMA((tiles,)),
            pltpu.SemaphoreType.DMA((tiles,)),
        ],
        compiler_params=pltpu.CompilerParams(
            collective_id=3, has_side_effects=True, vmem_limit_bytes=58 * 2**20
        ),
        cost_estimate=pl.CostEstimate(
            flops=6 * group * rows * width, bytes_accessed=4 * rows * width, transcendentals=group * rows
        ),
        name="head",
    )(final_low, codes, weights, table)


TILE_ORDER = (8, 9, 10, 11, 4, 5, 6, 7, 3, 0, 1, 2)
G1, S1, BQ, BV, BPROJ, G2, S2, BFC, BOUT = 0, 1, 2, 3, 4, 5, 6, 7, 11
STEPS = 12
GELU_A, GELU_B = 0.7978845608028654, 0.044715


def across_k(left, right):
    return lax.dot_general(left, right, (((1,), (1,)), ((), ())), preferred_element_type=jnp.float32)


def along_k(left, right):
    return jnp.dot(left, right, preferred_element_type=jnp.float32)


def over_rows(left, right):
    return lax.dot_general(left, right, (((0,), (0,)), ((), ())), preferred_element_type=jnp.float32)


def tile_copy(mats_ref, weights, ready, tile, step):
    rows = weights.shape[1]
    return pltpu.make_async_copy(
        mats_ref.at[pl.ds(tile * rows, rows)], weights.at[step], ready.at[step]
    )


def normed(value):
    centered = value - jnp.mean(value, -1, keepdims=True)
    scale = lax.rsqrt(jnp.mean(centered * centered, -1, keepdims=True) + norm_eps)
    return centered * scale, scale


def norm_back(grad, value, gain):
    unit, scale = normed(value)
    inner = grad * gain
    mean = jnp.mean(inner, -1, keepdims=True)
    slope = jnp.mean(inner * unit, -1, keepdims=True)
    return (
        scale * (inner - mean - unit * slope),
        jnp.sum(grad * unit, 0, keepdims=True),
        jnp.sum(grad, 0, keepdims=True),
    )


def forward_kernel(
    hot_ref,
    rows_ref,
    pos_hot_ref,
    pos_ref,
    mask_ref,
    vec_ref,
    mats_ref,
    x_out,
    a_out,
    qkv_out,
    probs_out,
    o_out,
    mid_out,
    m_out,
    u_out,
    g_out,
    hidden_out,
    final_out,
    cur,
    weights,
    ready,
):
    step = pl.program_id(0)
    layer, s = lax.div(step, STEPS), lax.rem(step, STEPS)
    low, f32 = jnp.bfloat16, jnp.float32
    width = cur.shape[1]
    head_dim = width // H


    def vec(row):
        return vec_ref[layer * STEPS + row]

    @pl.when(step == 0)
    def fetch():
        for n in range(2 * STEPS):
            tile_copy(mats_ref, weights, ready, n, n).start()

    @pl.when(step == 0)
    def embed():
        cur[...] = along_k(hot_ref[...], rows_ref[...]) + across_k(pos_hot_ref[...], pos_ref[...])

    @pl.when(s == 0)
    def first_norm():
        x_out[layer] = cur[...]
        a_out[layer] = (normed(cur[...])[0] * vec(G1) + vec(S1)).astype(low)

    tile_copy(mats_ref, weights, ready, 0, step).wait()

    @pl.when(s < 3)
    def project():
        bias = jnp.where(s == 0, vec(BQ), jnp.where(s == 2, vec(BV), 0.0))
        qkv_out[layer, s] = (across_k(a_out[layer], weights[step]) + bias).astype(low)

    @pl.when(s == 2)
    def attend():
        lanes = lax.broadcasted_iota(jnp.int32, (1, 2 * head_dim), 1)
        for pair in range(H // 2):
            cols = slice(2 * head_dim * pair, 2 * head_dim * (pair + 1))
            q, k, v = (qkv_out[layer, part, :, cols] for part in range(3))
            total = None
            for side in range(2):
                own = (lanes < head_dim) if side == 0 else (lanes >= head_dim)
                scores = across_k(jnp.where(own, q, jnp.zeros_like(q)), k) * head_dim ** (-0.5)
                scores = jnp.where(mask_ref[...] > 0.0, scores, -1000000000.0)
                shifted = jnp.exp(scores - jnp.max(scores, -1, keepdims=True))
                probs = shifted / jnp.sum(shifted, -1, keepdims=True)
                probs_out[layer, 2 * pair + side] = probs
                term = along_k(probs.astype(low), jnp.where(own, v, jnp.zeros_like(v)))
                total = term if total is None else total + term
            o_out[layer, :, cols] = total.astype(low)

    @pl.when(s == 3)
    def second_norm():
        mid = cur[...] + across_k(o_out[layer], weights[step]) + vec(BPROJ)
        mid_out[layer] = mid
        m_out[layer] = (normed(mid)[0] * vec(G2) + vec(S2)).astype(low)
        cur[...] = mid + vec(BOUT)

    @pl.when((s >= 4) & (s < 8))
    def widen():
        u = across_k(m_out[layer], weights[step]) + vec(BFC + s - 4)
        u_out[layer, s - 4] = u
        g = 0.5 * u * (1.0 + jnp.tanh(GELU_A * (u + GELU_B * (u * u * u))))
        g_out[layer, s - 4] = g.astype(low)

    @pl.when(s >= 8)
    def narrow():
        cur[...] += along_k(g_out[layer, s - 8], weights[step])

    @pl.when(step == 2 * STEPS - 1)
    def last_norm():
        hidden_out[...] = cur[...]
        final_out[...] = (normed(cur[...])[0] * vec_ref[2 * STEPS] + vec_ref[2 * STEPS + 1]).astype(low)


def forward_layers(hot, rows, pos_hot, pos, mask, vecs, mats):
    tok, width = hot.shape[0], rows.shape[1]
    low, f32 = jnp.bfloat16, jnp.float32
    shape = jax.ShapeDtypeStruct
    vmem = pl.BlockSpec(memory_space=pltpu.VMEM)
    return pl.pallas_call(
        forward_kernel,
        grid=(2 * STEPS,),
        out_shape=(
            shape((2, tok, width), f32),
            shape((2, tok, width), low),
            shape((2, 3, tok, width), low),
            shape((2, H, tok, tok), f32),
            shape((2, tok, width), low),
            shape((2, tok, width), f32),
            shape((2, tok, width), low),
            shape((2, 4, tok, width), f32),
            shape((2, 4, tok, width), low),
            shape((tok, width), f32),
            shape((tok, width), low),
        ),
        in_specs=[vmem] * 6 + [pl.BlockSpec(memory_space=pltpu.HBM)],
        out_specs=(vmem,) * 11,
        scratch_shapes=[
            pltpu.VMEM((tok, width), f32),
            pltpu.VMEM((2 * STEPS, width, width), low),
            pltpu.SemaphoreType.DMA((2 * STEPS,)),
        ],
        compiler_params=pltpu.CompilerParams(vmem_limit_bytes=58 * 2**20),
        cost_estimate=pl.CostEstimate(
            flops=2 * tok * mats.size, bytes_accessed=2 * mats.size, transcendentals=0
        ),
        name="forward_layers",
    )(hot, rows, pos_hot, pos, mask, vecs, mats)


def backward_kernel(
    grad_ref,
    hidden_ref,
    vec_ref,
    x_ref,
    a_ref,
    qkv_ref,
    probs_ref,
    o_ref,
    mid_ref,
    m_ref,
    u_ref,
    g_ref,
    hot_ref,
    mats_ref,
    dx_out,
    vec_out,
    rows_out,
    acc_out,
    cur,
    wide,
    du_s,
    dqkv_s,
    lefts,
    rights,
    right_send,
    weights,
    ready,
    send_left,
    recv_left,
    send_right,
    recv_right,
):
    step = pl.program_id(0)
    layer, s = 1 - lax.div(step, STEPS), lax.rem(step, STEPS)
    low, f32 = jnp.bfloat16, jnp.float32
    tok, width = cur.shape
    half = width // 2
    head_dim = width // H
    at, core = place()
    sibling = device_at(at, 1 - core)
    last = 2 * STEPS
    slot = lax.rem(step, 4)

    def vec(row):
        return vec_ref[layer * STEPS + row]

    def put(row, value):
        vec_out[layer * STEPS + row] = value

    def to_sibling(src, dst, send, recv):
        return pltpu.make_async_remote_copy(
            src_ref=src,
            dst_ref=dst,
            send_sem=send,
            recv_sem=recv,
            device_id=sibling,
            device_id_type=pl.DeviceIdType.MESH,
        )

    def left_copy(n):
        return to_sibling(
            lefts.at[n, pl.ds(0, tok)],
            lefts.at[n, pl.ds(tok, tok)],
            send_left.at[n],
            recv_left.at[n],
        )

    def right_copy(n):
        return to_sibling(
            right_send.at[n], rights.at[n, pl.ds(tok, tok)], send_right.at[n], recv_right.at[n]
        )

    def set_left(value):
        lefts[slot, :tok, :] = value

    def set_right(n, value):
        pl.when(step >= STEPS)(lambda: right_copy(n).wait_send())
        rights[n, :tok, :] = jnp.where(core == 0, value[:, :half], value[:, half:])
        right_send[n] = jnp.where(core == 0, value[:, half:], value[:, :half])

    @pl.when(step == 0)
    def enter():
        for n in range(last):
            tile = STEPS * (1 - n // STEPS) + TILE_ORDER[n % STEPS]
            tile_copy(mats_ref, weights, ready, tile, n).start()
        greet([sibling])
        dx, dg, ds = norm_back(grad_ref[...], hidden_ref[...], vec_ref[last])
        cur[...] = dx
        vec_out[last] = dg
        vec_out[last + 1] = ds

    @pl.when(step < last)
    def arrived():
        tile_copy(mats_ref, weights, ready, 0, step).wait()

    pl.when((step >= 4) & (step < last))(lambda: left_copy(slot).wait_send())

    @pl.when((s == 0) & (step < last))
    def begin():
        put(BOUT, jnp.sum(cur[...], 0, keepdims=True))
        set_right(0, cur[...].astype(low))
        wide[...] = cur[...].astype(low)

    @pl.when((s < 4) & (step < last))
    def through_gelu():
        dg = across_k(wide[...], weights[step])
        u = u_ref[layer, s]
        square = u * u
        t = jnp.tanh(GELU_A * (u + GELU_B * (square * u)))
        slope = 0.5 * (1.0 + t) + (0.5 * GELU_A) * u * (1.0 - t * t) * (1.0 + (3.0 * GELU_B) * square)
        du = dg * slope
        put(BFC + s, jnp.sum(du, 0, keepdims=True))
        du_s[s] = du.astype(low)
        set_left(g_ref[layer, s])

    @pl.when(s == 4)
    def begin_fc():
        set_right(1, m_ref[layer])
        dx_out[...] = jnp.zeros_like(dx_out)

    @pl.when((s >= 4) & (s < 8))
    def through_fc():
        left = du_s[s - 4]
        dx_out[...] += along_k(left, weights[step])
        set_left(left)

    @pl.when(s == 8)
    def through_attention():
        dx, dg, ds = norm_back(dx_out[...], mid_ref[layer], vec(G2))
        put(G2, dg)
        put(S2, ds)
        cur[...] = cur[...] + dx
        put(BPROJ, jnp.sum(cur[...], 0, keepdims=True))
        mid_low = cur[...].astype(low)
        set_left(mid_low)
        set_right(2, o_ref[layer])
        wide[...] = along_k(mid_low, weights[step]).astype(low)
        lanes = lax.broadcasted_iota(jnp.int32, (1, 2 * head_dim), 1)
        scale = head_dim ** (-0.5)
        for pair in range(H // 2):
            cols = slice(2 * head_dim * pair, 2 * head_dim * (pair + 1))
            q, k, v = (qkv_ref[layer, part, :, cols] for part in range(3))
            do = wide[:, cols]
            parts = [None] * 3
            for side in range(2):
                own = (lanes < head_dim) if side == 0 else (lanes >= head_dim)
                keep = lambda item, own=own: jnp.where(own, item, jnp.zeros_like(item))
                probs = probs_ref[layer, 2 * pair + side]
                do_own = keep(do)
                dprobs = across_k(do_own, v)
                dscores = probs * (dprobs - jnp.sum(probs * dprobs, -1, keepdims=True))
                dlow = (dscores * scale).astype(low)
                terms = (
                    along_k(dlow, keep(k)),
                    over_rows(dlow, keep(q)),
                    over_rows(probs.astype(low), do_own),
                )
                parts = [
                    term if held is None else held + term for held, term in zip(parts, terms)
                ]
            for part in range(3):
                dqkv_s[part, :, cols] = parts[part].astype(low)
            vec_out[layer * STEPS + BQ, :, cols] = jnp.sum(parts[0], 0, keepdims=True)
            vec_out[layer * STEPS + BV, :, cols] = jnp.sum(parts[2], 0, keepdims=True)

    @pl.when(s == 9)
    def begin_qkv():
        set_right(3, a_ref[layer])
        dx_out[...] = jnp.zeros_like(dx_out)

    @pl.when(s >= 9)
    def through_qkv():
        left = dqkv_s[s - 9]
        dx_out[...] += along_k(left, weights[step])
        set_left(left)

    def kind_of(at_s):
        return jnp.where(at_s < 4, 0, jnp.where(at_s < 8, 1, jnp.where(at_s == 8, 2, 3)))

    def fresh(at_s):
        return (at_s == 0) | (at_s == 4) | (at_s == 8) | (at_s == 9)

    @pl.when(step >= 2)
    def gradient():
        slot_then, s_then = lax.rem(step - 2, 4), lax.rem(step - 2, STEPS)
        kind = kind_of(s_then)
        left_copy(slot_then).wait_recv()
        pl.when(fresh(s_then))(lambda: right_copy(kind).wait_recv())
        grad = over_rows(lefts[slot_then], rights[kind])
        acc_out[0] = grad.astype(low).reshape(acc_out.shape[1:])

    @pl.when(step < last)
    def share():
        left_copy(slot).start()
        pl.when(fresh(s))(lambda: right_copy(kind_of(s)).start())

    @pl.when(s == STEPS - 1)
    def end_layer():
        dx, dg, ds = norm_back(dx_out[...], x_ref[layer], vec(G1))
        put(G1, dg)
        put(S1, ds)
        cur[...] = cur[...] + dx

    @pl.when(step == last + 1)
    def leave():
        dx_out[...] = cur[...]
        rows = over_rows(hot_ref[...], cur[...].astype(low)).astype(low)
        rows_out[...] = rows.reshape(rows_out.shape)
        for n in range(4):
            left_copy(n).wait_send()
            right_copy(n).wait_send()


def backward_layers(grad, hidden, vecs, saved, hot, mats):
    tok, width = grad.shape
    low, f32 = jnp.bfloat16, jnp.float32
    shape = jax.ShapeDtypeStruct
    vmem = pl.BlockSpec(memory_space=pltpu.VMEM)
    hbm = pl.BlockSpec(memory_space=pltpu.HBM)
    half, part = width // 2, 48
    granules = width // part

    def tile(i):
        i = jnp.clip(i - 2, 0, 2 * STEPS - 1)
        layer, s = 1 - i // STEPS, i % STEPS
        return (
            layer,
            jnp.where(s < 4, 8 + s, jnp.where(s < 8, s, jnp.where(s == 8, 3, s - 9))),
            0,
            0,
        )

    return pl.pallas_call(
        backward_kernel,
        grid=(2 * STEPS + 2,),
        out_shape=(
            shape((tok, width), f32),
            shape((2 * STEPS + 2, 1, width), f32),
            shape((RING, 2, 32, width), low),
            shape((2, STEPS * granules, part, half), low),
        ),
        in_specs=[vmem] * 13 + [hbm],
        out_specs=(vmem, vmem, vmem, pl.BlockSpec((1, granules, part, half), tile)),
        scratch_shapes=[
            pltpu.VMEM((tok, width), f32),
            pltpu.VMEM((tok, width), low),
            pltpu.VMEM((4, tok, width), low),
            pltpu.VMEM((3, tok, width), low),
            pltpu.VMEM((4, 2 * tok, width), low),
            pltpu.VMEM((4, 2 * tok, half), low),
            pltpu.VMEM((4, tok, half), low),
            pltpu.VMEM((2 * STEPS, width, width), low),
            pltpu.SemaphoreType.DMA((2 * STEPS,)),
            pltpu.SemaphoreType.DMA((4,)),
            pltpu.SemaphoreType.DMA((4,)),
            pltpu.SemaphoreType.DMA((4,)),
            pltpu.SemaphoreType.DMA((4,)),
        ],
        compiler_params=pltpu.CompilerParams(
            collective_id=4, has_side_effects=True, vmem_limit_bytes=60 * 2**20
        ),
        cost_estimate=pl.CostEstimate(
            flops=4 * tok * mats.size, bytes_accessed=2 * mats.size, transcendentals=0
        ),
        name="backward_layers",
    )(grad, hidden, vecs, *saved, hot, mats)


def doc_info(doc_lens, tok_count, total_docs):
    doc_ends = jnp.cumsum(doc_lens)
    places = jnp.arange(tok_count, dtype=jnp.int32)
    seg_ids = jnp.sum((places[:, None] >= doc_ends[None, :]).astype(jnp.int32), 1)
    one_hot = seg_ids[:, None] == jnp.arange(doc_lens.shape[0], dtype=jnp.int32)[None, :]
    starts = doc_ends - doc_lens
    pos_ids = places - jnp.sum(jnp.where(one_hot, starts[None, :], 0), 1)
    doc_len = jnp.sum(jnp.where(one_hot, doc_lens[None, :], 0), 1)
    weights = 1.0 / (doc_len.astype(jnp.float32) * total_docs)
    return (seg_ids, pos_ids, weights)


def device_rise(first, count, devices):
    places = first + jnp.arange(count, dtype=jnp.int32)
    return 1.0 + 2.0 * places.astype(jnp.float32) / (devices - 1)


def contract(left, right, left_dim, right_dim):
    return lax.dot_general(
        left, right, (((left_dim,), (right_dim,)), ((), ())), preferred_element_type=jnp.float32
    )


def renew(weight, moment, average, grad, factor):
    clipped = factor * grad
    moment_next = momentum_coef * moment + clipped
    weight_next = weight - learn_rate * (clipped + momentum_coef * moment_next)
    average_next = ema_decay * average + (1.0 - ema_decay) * weight_next
    return (moment_next, weight_next, average_next, weight_next.astype(jnp.bfloat16))


SMALL_ROWS, LANES = 16, 128


def pack_small(values):
    room = SMALL_ROWS * LANES - values.shape[-1]
    pads = [(0, 0)] * (values.ndim - 1) + [(0, room)]
    return jnp.pad(values, pads).reshape(values.shape[:-1] + (SMALL_ROWS, LANES))


def per_device(
    token_ids,
    targets,
    lengths,
    embed_table,
    embed_moment,
    embed_average,
    blocks,
    block_moment,
    block_average,
    pos_table,
    pos_moment,
    pos_average,
    vectors,
    vector_moment,
    vector_average,
):
    devices = lax.axis_size(("dp", "vocab"))
    vocab_count = lax.axis_size("vocab")
    dp_count = lax.axis_size("dp")
    vocab_at = lax.axis_index("vocab")
    data_at = lax.axis_index("dp")
    tok = token_ids.shape[0]
    own_rows, width = embed_table.shape
    capacity = max(2, 2 * tok // devices)
    low = jnp.bfloat16
    blocks, block_moment, block_average = (
        jnp.transpose(item, (0, 2, 1)) for item in (blocks, block_moment, block_average)
    )
    pos_rows, pos_cols = pos_table.shape
    vec_own = vectors.shape[0]
    pad_rows = -own_rows % 16
    table_padded = jnp.pad(embed_table, ((0, pad_rows), (0, 0))).astype(low)
    slot_rows = own_rows + pad_rows

    table_slice = lax.all_gather(table_padded, "dp", axis=0, tiled=True)
    target_owners = targets // own_rows
    codes = (
        (target_owners % vocab_count) * (dp_count * slot_rows)
        + (target_owners // vocab_count) * slot_rows
        + targets % own_rows
    )

    owners = token_ids // own_rows
    tokens = jnp.arange(tok, dtype=jnp.int32)
    rank = jnp.sum((owners[:, None] == owners[None, :]) & (tokens[None, :] < tokens[:, None]), 1)
    slot_count = devices * capacity
    slots = jnp.arange(slot_count, dtype=jnp.int32)
    arrival = (
        (owners % 8) * 32 + (owners // 8 % RING) * 8 + (owners // 32) * capacity + rank
    )
    slot_hot = (arrival[:, None] == slots[None, :]).astype(low)
    hot = lambda condition: condition.astype(ml_dtypes.bfloat16)
    line, step = np.arange(slot_count), np.arange(tok)
    spread = hot(line[:, None] // capacity == np.arange(devices)[None, :])
    earlier = hot(step[:, None] < step[None, :])
    slot_number = np.broadcast_to((line % capacity).astype(np.float32)[:, None], (slot_count, tok)).copy()
    by_owner = line % 64 // 16 * 2 + line // 64 * 8 + line % 16 // 2 * 32 + line % capacity
    swap = hot(by_owner[:, None] == line[None, :])
    values = jnp.concatenate([jnp.transpose(pos_table).reshape(-1), vectors]).astype(low)
    small = jnp.concatenate(
        [
            jnp.pad(values, (0, IDS_ROW * LANES - values.shape[0])).reshape(IDS_ROW, LANES),
            jnp.stack([token_ids // 256, token_ids % 256]).astype(low),
            jnp.zeros((SMALL_ROWS - IDS_ROW - 2, LANES), low),
        ]
    )
    mats_all, small_all, returned_rows, asked = gather_weights(
        blocks, small, table_padded, spread, earlier, slot_number, swap.T.copy()
    )
    small_all = small_all.reshape(devices, -1)
    pos_low_t = small_all[:, : pos_rows * pos_cols].reshape(width, pos_rows)
    vecs_all = (
        small_all[:, pos_rows * pos_cols : pos_rows * pos_cols + vec_own]
        .reshape(-1)
        .astype(jnp.float32)
    )
    lens_group = lengths[0]
    seg_group, pos_group, weight_group = jax.vmap(
        partial(doc_info, tok_count=tok, total_docs=devices * lens_group.shape[1])
    )(lens_group)
    weight_group = weight_group * device_rise(data_at * vocab_count, vocab_count, devices)[:, None]
    seg_ids = lax.dynamic_index_in_dim(seg_group, vocab_at, 0, keepdims=False)
    pos_ids = lax.dynamic_index_in_dim(pos_group, vocab_at, 0, keepdims=False)
    places = jnp.arange(tok, dtype=jnp.int32)
    attn_mask = (seg_ids[:, None] == seg_ids[None, :]) & (places[None, :] <= places[:, None])

    pos_hot = (pos_ids[:, None] == jnp.arange(pos_rows, dtype=jnp.int32)[None, :]).astype(low)
    vec_rows = vecs_all.reshape(-1, 1, width)
    *saved, hidden, final_low = forward_layers(
        slot_hot,
        returned_rows,
        pos_hot,
        pos_low_t,
        attn_mask.astype(jnp.float32),
        vec_rows,
        mats_all,
    )
    grad_final, table_part, token_losses = head(
        final_low, jnp.broadcast_to(codes[None, :], (8, tok)), weight_group, table_slice
    )
    table_part = lax.psum_scatter(table_part, "dp", scatter_dimension=0, tiled=True)
    grad_hidden, grad_vecs, rows_back, grad_acc = backward_layers(
        grad_final, hidden, vec_rows, saved, slot_hot, mats_all
    )
    grad_pos = lax.dot_general(
        grad_hidden,
        pos_hot.astype(jnp.float32),
        (((0,), (0,)), ((), ())),
        precision=lax.Precision.HIGHEST,
    )
    small_grads = pack_small(
        jnp.concatenate(
            [grad_pos.reshape(devices, -1), grad_vecs.reshape(devices, -1)], 1
        )
    )
    mats_shard, small_shard, back_grads = reduce_weights(grad_acc.reshape(2, RING, RING, RING, 3, 48, width // 2), small_grads, rows_back, swap)
    both_sums, table_grad = sum_all(
        table_part,
        asked,
        back_grads.reshape(slot_count, width),
        mats_shard,
        small_shard,
        token_losses,
    )
    small_shard = small_shard.reshape(-1)
    pos_shard = small_shard[: pos_rows * pos_cols].reshape(pos_cols, pos_rows)
    vec_shard = small_shard[pos_rows * pos_cols : pos_rows * pos_cols + vec_own]
    loss_sum, squares = both_sums[0, 0], both_sums[1, 0]
    grad_norm = jnp.sqrt(squares)
    factor = clip_bound / jnp.maximum(grad_norm, clip_bound)
    own_shape = blocks.shape
    flat = lambda item: item.reshape(-1, width)
    embed_out, block_out = update(
        both_sums,
        (embed_table, embed_moment, embed_average, table_grad),
        (flat(blocks), flat(block_moment), flat(block_average), flat(mats_shard)),
    )
    block_out = tuple(
        jnp.transpose(item.reshape(own_shape), (0, 2, 1)) for item in block_out
    )
    pos_out = renew(
        jnp.transpose(pos_table),
        jnp.transpose(pos_moment),
        jnp.transpose(pos_average),
        pos_shard,
        factor,
    )
    pos_out = tuple(jnp.transpose(item) for item in pos_out)
    vector_out = renew(vectors, vector_moment, vector_average, vec_shard, factor)
    return (loss_sum, grad_norm) + tuple(embed_out) + block_out + pos_out + vector_out


def solution(mesh):
    table = P(("dp", "vocab"), None)
    cols = P(None, None, ("dp", "vocab"))
    pos = P(None, ("dp", "vocab"))
    vec = P(("dp", "vocab"))
    return jax.shard_map(
        per_device,
        mesh=mesh,
        in_specs=(vec, vec, P("dp", None, None))
        + (table,) * 3
        + (cols,) * 3
        + (pos,) * 3
        + (vec,) * 3,
        out_specs=(P(), P()) + (table,) * 4 + (cols,) * 4 + (pos,) * 4 + (vec,) * 4,
        check_vma=False,
    )
```
